32 devices in a mesh: expert: 16 (over z, y, x), tensor: 2 (over core).
Axes of the slice: x: 2, y: 2, z: 4, core: 2. Of those that a mesh axis runs over, the one named last changes fastest.
Arguments:
- attn_out: bfloat16 [512, 4096], P('expert', 'tensor'), may hold values from -6 to 6
- out_weight: bfloat16 [4096, 2048], P('tensor'), may hold values from -0.09375 to 0.09375
- residual: bfloat16 [512, 2048], P(('expert', 'tensor')), may hold values from -6 to 6
- attn_gain: float32 [2048], replicated, may hold values from 0.1 to 1.9
- expert_ids: int32 [512, 8], P('expert'), may hold values from 0 to 31, all different within a row; in each aligned block of 32 rows (0 to 31, 32 to 63, ...) at most 12 rows name the same one
- route_weights: float32 [512, 8], P('expert'), may hold values from 0.05 to 0.3
- w_gate: bfloat16 [16, 2048, 1536], P('expert', None, 'tensor'), may hold values from -0.125 to 0.125
- w_up: bfloat16 [16, 2048, 1536], P('expert', None, 'tensor'), may hold values from -0.125 to 0.125
- w_down: bfloat16 [16, 1536, 2048], P('expert', 'tensor'), may hold values from -0.21875 to 0.21875
- input_gain: float32 [2048], replicated, may hold values from 0.1 to 1.9
- q_weight: bfloat16 [2048, 4096], P('expert', 'tensor'), may hold values from -0.125 to 0.125
- kv_weight: bfloat16 [2048, 1024], P('expert', 'tensor'), may hold values from -0.125 to 0.125
- q_gain: float32 [128], replicated, may hold values from 0.1 to 1.9
- k_gain: float32 [128], replicated, may hold values from 0.1 to 1.9
Outputs:
- next_residual: bfloat16 [512, 2048], P(('expert', 'tensor'))
- queries: bfloat16 [512, 4096], P('expert', 'tensor')
- keys_values: bfloat16 [512, 1024], P('expert', 'tensor')
The draws below stay inside these ranges and needn't reach their ends.
Inputs may be any that keep to these rules, and one draw needn't show every extreme that they name: `expert_ids`: each row names 8 different experts. In each aligned block of 32 rows no expert is named by more than 12 rows, and in some block one expert is named by exactly 12 rows.
All inputs are finite; a program needn't handle non-finite values.
Results may differ from the reference program's by a relative error of at most 0.012.
Values may be sent and summed in bfloat16 or wider, within the bound.
No kernel may reach another device: no remote copies, remote signals or barrier semaphores. Data moves between devices by JAX's collectives and lax.ppermute only.
A program may use at most 64 MiB of HBM per device.

```python
import math
import jax
import jax.numpy as jnp
import numpy as np
from jax import lax

D = 2048
FF = 768
HEADS = 32
KV_HEADS = 4
HEAD_DIM = 128
TOP = 8
EXPERTS = 32
GROUP = 32
TOKENS = 512
CAP = 12
SHARE = 1
FF_DEV = 768
N_EXPERT = 16


def levels(stream_key, dims, pieces, low, top_value):
    level, own = 1.0, jax.random.fold_in(stream_key, 6)
    for position, blocks in pieces:
        heights = jnp.exp(jax.random.uniform(jax.random.fold_in(own, position), (blocks,), jnp.float32, low / len(pieces), top_value / len(pieces)))
        level = level * jnp.repeat(heights, dims[position] // blocks).reshape([-1 if axis == position else 1 for axis in range(len(dims))])
    return level


def shared_out(stream_key, own, number, rows, count, top, most, slope):
    ranking = jax.random.permutation(stream_key, count)
    packed, usual = load_shares(count, rows * top, most, slope, True), load_shares(count, rows * top, most, slope, False)
    places = jnp.arange(count)

    def named(tallies, offset_by):
        used = int((tallies > 0).sum())
        fixed = max(1, used // 4)
        shifted = fixed + (places - fixed + offset_by * (used - fixed)) % max(1, count - fixed)
        return jnp.zeros((count,), jnp.int32).at[ranking[jnp.where(places < fixed, places, shifted)]].set(jnp.asarray(tallies, jnp.int32))

    tallies = jnp.where(number % 4 == 0, named(packed, number // 4), named(usual, number - number // 4 - 1))
    mixed = jax.random.permutation(jax.random.fold_in(own, 3), count)
    donor, receiver = mixed[0:count // 2 * 2:2], mixed[1:count // 2 * 2:2]
    margin = jnp.minimum(tallies[donor] - 1, most - tallies[receiver]) // 2
    margin = jnp.where((donor == ranking[0]) | (receiver == ranking[0]) | (tallies[receiver] == 0), 0, jnp.maximum(margin, 0))
    shifted = jax.random.randint(jax.random.fold_in(own, 4), (count // 2,), 0, 1 << 20) % (margin + 1)
    tallies = tallies.at[donor].add(-shifted).at[receiver].add(shifted)
    labels = jnp.searchsorted(jnp.cumsum(tallies), jnp.arange(rows * top), side="right").astype(jnp.int32)
    listing = labels.reshape(top, rows).T
    listing = listing[jax.random.permutation(jax.random.fold_in(own, 1), rows)]
    offset_by = jax.random.randint(jax.random.fold_in(own, 2), (rows, 1), 0, top)
    return jnp.take_along_axis(listing, (jnp.arange(top)[None, :] + offset_by) % top, axis=1)


def load_shares(count, total, most, slope, full):
    portions = [(1 << 20) // math.isqrt(rank ** slope) + 1 for rank in range(1, count + 1)]
    largest = most if full else min(most, max(-(-total // count), total * portions[0] // sum(portions)))
    least = 1 if total - largest >= count - 1 else 0
    holding, spare = [largest] + [least] * (count - 1), total - largest - least * (count - 1)
    while spare > 0:
        movable = [i for i in range(1, count) if holding[i] < largest] or [i for i in range(1, count) if holding[i] < most]
        pool, left = sum([portions[i] for i in movable]), spare
        for i in movable:
            extra = min(most - holding[i], max(1, left * portions[i] // pool), spare)
            holding[i] = holding[i] + extra
            spare = spare - extra
    return np.array(holding)


def centred(stream_key, shape, deviation, bound, cuts=(), kind=jnp.bfloat16):
    array = deviation * jax.random.normal(stream_key, shape, jnp.float32)
    if cuts:
        array = array * levels(stream_key, shape, cuts, -0.22, 0.18)
    return jnp.clip(array, -bound, bound).astype(kind)


def setup_inputs(seed: int = 0) -> dict:
    streams_of = jax.random.split(jax.random.key(seed), 15)
    attn_out = centred(streams_of[0], (TOKENS, HEADS * HEAD_DIM), 1.0, 6.0, ((0, 16), (1, 2)))
    out_weight = centred(streams_of[1], (HEADS * HEAD_DIM, D), (HEADS * HEAD_DIM) ** -0.5, 0.09375, ((0, 2),))
    residual = centred(streams_of[2], (TOKENS, D), 1.0, 6.0, ((0, 32),))
    attn_gain = jnp.clip(1.0 + 0.18 * jax.random.normal(streams_of[3], (D,), jnp.float32), 0.1, 1.9)
    expert_ids_keys = jax.random.split(jax.random.fold_in(streams_of[4], 1), TOKENS // GROUP)
    expert_ids_turns = jax.random.permutation(jax.random.fold_in(streams_of[4], 3), TOKENS // GROUP)
    expert_ids = jax.vmap(lambda own, number: shared_out(jax.random.fold_in(streams_of[4], 2), own, number, GROUP, EXPERTS, TOP, CAP, 2))(expert_ids_keys, expert_ids_turns).reshape((TOKENS, TOP))
    route_weights = jnp.clip(0.05 + 0.25 * jax.random.uniform(streams_of[5], (TOKENS, TOP), jnp.float32) ** levels(streams_of[5], (TOKENS, TOP), ((0, 16),), -0.2, 0.2), 0.05, 0.3)
    w_gate = centred(streams_of[6], (EXPERTS // 2, D, 2 * FF), D ** -0.5, 0.125, ((0, 16), (2, 2)))
    w_up = centred(streams_of[7], (EXPERTS // 2, D, 2 * FF), D ** -0.5, 0.125, ((0, 16), (2, 2)))
    w_down = centred(streams_of[8], (EXPERTS // 2, 2 * FF, D), FF ** -0.5, 0.21875, ((0, 16), (1, 2)))
    input_gain = jnp.clip(1.0 + 0.18 * jax.random.normal(streams_of[9], (D,), jnp.float32), 0.1, 1.9)
    q_weight = centred(streams_of[10], (D, HEADS * HEAD_DIM), D ** -0.5, 0.125, ((0, 16), (1, 2)))
    kv_weight = centred(streams_of[11], (D, 2 * KV_HEADS * HEAD_DIM), D ** -0.5, 0.125, ((0, 16), (1, 2)))
    q_gain = jnp.clip(1.0 + 0.18 * jax.random.normal(streams_of[12], (HEAD_DIM,), jnp.float32), 0.1, 1.9)
    k_gain = jnp.clip(1.0 + 0.18 * jax.random.normal(streams_of[13], (HEAD_DIM,), jnp.float32), 0.1, 1.9)
    return dict(attn_out=attn_out, out_weight=out_weight, residual=residual, attn_gain=attn_gain, expert_ids=expert_ids, route_weights=route_weights, w_gate=w_gate, w_up=w_up, w_down=w_down, input_gain=input_gain, q_weight=q_weight, kv_weight=kv_weight, q_gain=q_gain, k_gain=k_gain)


EPSILON = 1e-06

def normalize(values, gain):
    return values * lax.rsqrt(lax.optimization_barrier(jnp.mean(values * values, axis=-1, keepdims=True)) + EPSILON) * gain

def block_slots(ids_block, weight_block, base):
    flat = ids_block.reshape(-1)
    onehot = (flat[:, None] == jnp.arange(EXPERTS, dtype=jnp.int32)[None, :]).astype(jnp.int32)
    earlier = (jnp.cumsum(onehot, axis=0) - onehot).astype(jnp.int32)
    rank = lax.optimization_barrier(jnp.sum(earlier * onehot, axis=1)).astype(jnp.int32)
    dest = (flat * CAP + rank).astype(jnp.int32)
    rows = (base + jnp.arange(GROUP * TOP, dtype=jnp.int32) // TOP).astype(jnp.int32)
    slot_row = jnp.full((EXPERTS * CAP,), TOKENS, jnp.int32).at[dest].set(rows)
    slot_weight = jnp.zeros((EXPERTS * CAP,), jnp.float32).at[dest].set(weight_block.reshape(-1))
    return (slot_row, slot_weight)

def reference(attn_out, out_weight, residual, attn_gain, expert_ids, route_weights, w_gate, w_up, w_down, input_gain, q_weight, kv_weight, q_gain, k_gain):
    attn = jnp.dot(attn_out, out_weight, preferred_element_type=jnp.float32)
    first_residual = (residual.astype(jnp.float32) + attn).astype(jnp.bfloat16)
    normed = normalize(first_residual.astype(jnp.float32), attn_gain).astype(jnp.bfloat16)
    bases = (jnp.arange(N_EXPERT, dtype=jnp.int32) * GROUP).astype(jnp.int32)
    slot_row, slot_weight = jax.vmap(block_slots)(expert_ids.reshape(N_EXPERT, GROUP, TOP), route_weights.reshape(N_EXPERT, GROUP, TOP), bases)
    slot_row = jnp.transpose(slot_row.reshape(N_EXPERT, EXPERTS, CAP), (1, 0, 2)).reshape(EXPERTS, N_EXPERT * CAP)
    slot_weight = jnp.transpose(slot_weight.reshape(N_EXPERT, EXPERTS, CAP), (1, 0, 2)).reshape(EXPERTS, N_EXPERT * CAP)
    padded = jnp.concatenate([normed, jnp.zeros((1, D), jnp.bfloat16)], axis=0)
    zero = jnp.zeros((), jnp.int32)

    def one_expert(total, inputs):
        index, rows_index, weights = inputs
        pair = (index // 2).astype(jnp.int32)
        side = (index % 2).astype(jnp.int32)
        gate_w = lax.dynamic_slice(w_gate, (pair, zero, (side * FF).astype(jnp.int32)), (1, D, FF))[0]
        up_w = lax.dynamic_slice(w_up, (pair, zero, (side * FF).astype(jnp.int32)), (1, D, FF))[0]
        down_w = lax.dynamic_slice(w_down, (pair, (side * FF).astype(jnp.int32), zero), (1, FF, D))[0]
        rows = jnp.take(padded, rows_index, axis=0)
        gate = jnp.dot(rows, gate_w, preferred_element_type=jnp.float32)
        up = jnp.dot(rows, up_w, preferred_element_type=jnp.float32)
        act = (jax.nn.silu(gate) * up).astype(jnp.bfloat16)
        act_groups = act.reshape(-1, SHARE, FF_DEV).astype(jnp.float32)
        down_groups = down_w.reshape(SHARE, FF_DEV, D).astype(jnp.float32)
        parts = jnp.einsum('nsf,sfd->nsd', act_groups, down_groups).astype(jnp.bfloat16)
        summed = lax.optimization_barrier(jnp.sum(parts.astype(jnp.float32), axis=1))
        total = total.at[rows_index].add(weights[:, None] * summed)
        return (total, None)
    start = jnp.zeros((TOKENS + 1, D), jnp.float32)
    moe, unused = lax.scan(one_expert, start, (jnp.arange(EXPERTS, dtype=jnp.int32), slot_row, slot_weight))
    moe = moe[:TOKENS]
    next_residual = (first_residual.astype(jnp.float32) + moe).astype(jnp.bfloat16)
    next_normed = normalize(next_residual.astype(jnp.float32), input_gain).astype(jnp.bfloat16)
    query_raw = jnp.dot(next_normed, q_weight, preferred_element_type=jnp.float32)
    queries = normalize(query_raw.reshape(TOKENS, HEADS, HEAD_DIM), q_gain).reshape(TOKENS, HEADS * HEAD_DIM).astype(jnp.bfloat16)
    kv_raw = jnp.dot(next_normed, kv_weight, preferred_element_type=jnp.float32)
    keys = normalize(kv_raw[:, :KV_HEADS * HEAD_DIM].reshape(TOKENS, KV_HEADS, HEAD_DIM), k_gain).reshape(TOKENS, KV_HEADS * HEAD_DIM)
    keys_values = jnp.concatenate([keys, kv_raw[:, KV_HEADS * HEAD_DIM:]], axis=1).astype(jnp.bfloat16)
    return (next_residual, queries, keys_values)
```

```python
import functools

import jax
import jax.numpy as jnp
from jax import lax
from jax.experimental import pallas as pl
from jax.experimental.pallas import tpu as pltpu
from jax.sharding import PartitionSpec as P

KV_HEADS = 4
TOP = 8
PLANE = 4
META = 128


EPSILON = 1e-06


def normalize(values, gain):
    return values * lax.rsqrt(jnp.mean(values * values, axis=-1, keepdims=True) + EPSILON) * gain


def out_projection_kernel(chunk, pos_ref, a_ref, w_ref, mine_ref, theirs_ref, w_buf, sems):
    depth, width = w_buf.shape
    count = width // chunk
    half = mine_ref.shape[0]
    copies = []
    for i in range(count):
        cols = pl.ds(i * chunk, chunk)
        copies.append(pltpu.make_async_copy(w_ref.at[:, cols], w_buf.at[:, cols], sems.at[i]))
    for copy in copies:
        copy.start()
    tensor = pos_ref[1]
    own_rows = pl.ds(pl.multiple_of(tensor * half, half), half)
    other_rows = pl.ds(pl.multiple_of((1 - tensor) * half, half), half)
    own = a_ref[own_rows, :]
    other = a_ref[other_rows, :]
    both = jnp.concatenate([own, other], axis=0)
    for i in range(count):
        copies[i].wait()
        cols = pl.ds(i * chunk, chunk)
        product = jnp.dot(both, w_buf[:, cols], preferred_element_type=jnp.float32)
        mine_ref[:, cols] = product[:half]
        theirs_ref[:, cols] = product[half:]


def out_projection(pos, attn_out, out_weight):
    rows, depth = attn_out.shape
    width = out_weight.shape[1]
    chunk = 256
    half = jax.ShapeDtypeStruct((rows // 2, width), jnp.float32)
    return pl.pallas_call(
        functools.partial(out_projection_kernel, chunk),
        out_shape=(half, half),
        in_specs=[
            pl.BlockSpec(memory_space=pltpu.SMEM),
            pl.BlockSpec(memory_space=pltpu.VMEM),
            pl.BlockSpec(memory_space=pl.ANY),
        ],
        out_specs=(pl.BlockSpec(memory_space=pltpu.VMEM), pl.BlockSpec(memory_space=pltpu.VMEM)),
        scratch_shapes=[
            pltpu.VMEM((depth, width), jnp.bfloat16),
            pltpu.SemaphoreType.DMA((width // chunk,)),
        ],
        compiler_params=pltpu.CompilerParams(vmem_limit_bytes=24 << 20),
        cost_estimate=pl.CostEstimate(
            flops=2 * rows * depth * width, bytes_accessed=2 * depth * width, transcendentals=0
        ),
        name="out_projection",
    )(pos, attn_out, out_weight)


def first_norm_kernel(
    slices, pos_ref, mine_ref, theirs_ref, residual_ref, gain_ref, meta_ref, tokens_ref, *slice_refs
):
    width = residual_ref.shape[1]
    part = width // slices
    first = (residual_ref[...].astype(jnp.float32) + (mine_ref[...] + theirs_ref[...])).astype(
        jnp.bfloat16
    )
    tokens_ref[:, :width] = normalize(first.astype(jnp.float32), gain_ref[...]).astype(jnp.bfloat16)
    tokens_ref[:, width:] = meta_ref[...]
    for d in range(slices):
        for j in range(slices):

            @pl.when((pos_ref[0] ^ d) == j)
            def _(d=d, j=j):
                slice_refs[d][...] = first[:, j * part : (j + 1) * part]


def first_norm(pos, mine, theirs, residual, gain, meta, slices):
    rows, width = residual.shape
    vmem = pl.BlockSpec(memory_space=pltpu.VMEM)
    return pl.pallas_call(
        functools.partial(first_norm_kernel, slices),
        out_shape=(jax.ShapeDtypeStruct((rows, width + META), jnp.bfloat16),)
        + (jax.ShapeDtypeStruct((rows, width // slices), jnp.bfloat16),) * slices,
        in_specs=[pl.BlockSpec(memory_space=pltpu.SMEM)] + [vmem] * 5,
        out_specs=(vmem,) * (1 + slices),
        name="first_norm",
    )(pos, mine, theirs, residual, gain, meta)


def expert_kernel(blocks, chunk, pos_ref, *refs):
    block_refs = refs[:blocks]
    weight_refs = refs[blocks : blocks + 6]
    rest = refs[blocks + 6 :]
    out_refs, (x_buf, gate_buf, up_buf, down_buf, act_buf, sems) = rest[:PLANE], rest[PLANE:]
    width, hidden = gate_buf.shape[1], gate_buf.shape[2]
    rows = block_refs[0].shape[0]
    per = hidden // chunk
    gate_copies, down_copies = [], []
    for side in range(2):
        gate_ref, up_ref, down_ref = weight_refs[3 * side : 3 * side + 3]
        for i in range(per):
            cols = pl.ds(i * chunk, chunk)
            at = side * per + i
            pair = (
                pltpu.make_async_copy(
                    gate_ref.at[0, :, cols], gate_buf.at[side, :, cols], sems.at[0, at]
                ),
                pltpu.make_async_copy(
                    up_ref.at[0, :, cols], up_buf.at[side, :, cols], sems.at[1, at]
                ),
            )
            gate_copies.append(pair)
    for side in range(2):
        down_ref = weight_refs[3 * side + 2]
        for i in range(per):
            at = side * per + i
            down_copies.append(
                pltpu.make_async_copy(
                    down_ref.at[0, pl.ds(i * chunk, chunk), :],
                    down_buf.at[pl.ds(at * chunk, chunk), :],
                    sems.at[2, at],
                )
            )
    for pair in gate_copies:
        pair[0].start()
        pair[1].start()
    for copy in down_copies:
        copy.start()
    for i in range(blocks):
        x_buf[i * rows : (i + 1) * rows, :] = block_refs[i][...]
    meta = x_buf[:, width:].astype(jnp.float32)
    lane = lax.broadcasted_iota(jnp.int32, meta.shape, 1)
    for side in range(2):
        expert = pos_ref[2 + side]
        chosen = (lane == expert) | (lane == expert + META // 2)
        route = jnp.sum(jnp.where(chosen, meta, 0.0), axis=1, keepdims=True)
        for i in range(per):
            at = side * per + i
            gate_copies[at][0].wait()
            gate_copies[at][1].wait()
            cols = pl.ds(i * chunk, chunk)
            x = x_buf[:, :width]
            gate = jnp.dot(x, gate_buf[side, :, cols], preferred_element_type=jnp.float32)
            up = jnp.dot(x, up_buf[side, :, cols], preferred_element_type=jnp.float32)
            act = gate / (1.0 + jnp.exp(-gate)) * up * route
            act_buf[:, at * chunk : (at + 1) * chunk] = act.astype(jnp.bfloat16)
    for copy in down_copies:
        copy.wait()
    step = width // 4
    group = blocks // PLANE * rows
    for j in range(4):
        cols = pl.ds(j * step, step)
        out = jnp.dot(act_buf[...], down_buf[:, cols], preferred_element_type=jnp.float32)
        for k in range(PLANE):
            out_refs[k][:, cols] = out[k * group : (k + 1) * group].astype(jnp.bfloat16)


def experts(pos, blocks, weights):
    rows, extended = blocks[0].shape
    width, hidden = weights[0].shape[1:]
    chunk = 256
    total = rows * len(blocks)
    vmem = pl.BlockSpec(memory_space=pltpu.VMEM)
    return pl.pallas_call(
        functools.partial(expert_kernel, len(blocks), chunk),
        out_shape=(jax.ShapeDtypeStruct((total // PLANE, width), jnp.bfloat16),) * PLANE,
        in_specs=[pl.BlockSpec(memory_space=pltpu.SMEM)]
        + [vmem] * len(blocks)
        + [pl.BlockSpec(memory_space=pl.ANY)] * 6,
        out_specs=(vmem,) * PLANE,
        scratch_shapes=[
            pltpu.VMEM((total, extended), jnp.bfloat16),
            pltpu.VMEM((2, width, hidden), jnp.bfloat16),
            pltpu.VMEM((2, width, hidden), jnp.bfloat16),
            pltpu.VMEM((2 * hidden, width), jnp.bfloat16),
            pltpu.VMEM((total, 2 * hidden), jnp.bfloat16),
            pltpu.SemaphoreType.DMA((3, 2 * (hidden // chunk))),
        ],
        compiler_params=pltpu.CompilerParams(vmem_limit_bytes=40 << 20),
        cost_estimate=pl.CostEstimate(
            flops=12 * total * width * hidden,
            bytes_accessed=12 * width * hidden,
            transcendentals=2 * total * hidden,
        ),
        name="experts",
    )(pos, *blocks, *weights)


def plane_sum_kernel(slices, pos_ref, *refs):
    in_refs, out_refs = refs[:PLANE], refs[PLANE:]
    rows, width = in_refs[0].shape
    part = width // slices
    block = rows // slices
    total = in_refs[0][...].astype(jnp.float32)
    for ref in in_refs[1:]:
        total = total + ref[...].astype(jnp.float32)
    total = total.astype(jnp.bfloat16)
    for d in range(slices):
        for j in range(slices):

            @pl.when((pos_ref[0] ^ d) == j)
            def _(d=d, j=j):
                for i in range(slices):
                    out_refs[d][i * block : (i + 1) * block, :] = total[
                        (d ^ i) * block : ((d ^ i) + 1) * block, j * part : (j + 1) * part
                    ]


def plane_sum(pos, parts, slices):
    rows, width = parts[0].shape
    vmem = pl.BlockSpec(memory_space=pltpu.VMEM)
    return pl.pallas_call(
        functools.partial(plane_sum_kernel, slices),
        out_shape=(jax.ShapeDtypeStruct((rows, width // slices), jnp.bfloat16),) * slices,
        in_specs=[pl.BlockSpec(memory_space=pltpu.SMEM)] + [vmem] * PLANE,
        out_specs=(vmem,) * slices,
        name="plane_sum",
    )(pos, *parts)


def second_norm_kernel(slices, *refs):
    parts, firsts, gain_ref = refs[:slices], refs[slices : 2 * slices], refs[2 * slices]
    scaled_ref, next_refs = refs[2 * slices + 1], refs[2 * slices + 2 :]
    rows, part = firsts[0].shape
    total = parts[0][...].astype(jnp.float32)
    for ref in parts[1:]:
        total = total + ref[...].astype(jnp.float32)
    lane = lax.broadcasted_iota(jnp.int32, (rows, META), 1)
    for d in range(slices):
        at = slice(d * rows, (d + 1) * rows)
        following = (firsts[d][...].astype(jnp.float32) + total[at]).astype(jnp.bfloat16)
        next_refs[d][...] = following
        wide = following.astype(jnp.float32)
        scaled_ref[at, :part] = (wide * gain_ref[...]).astype(jnp.bfloat16)
        squares = jnp.sum(wide * wide, axis=1, keepdims=True)
        high = squares.astype(jnp.bfloat16).astype(jnp.float32)
        low = squares - high
        scaled_ref[at, part:] = jnp.where(
            lane == 0, high, jnp.where(lane == 1, low, 0.0)
        ).astype(jnp.bfloat16)


def second_norm(parts, firsts, gain):
    slices = len(parts)
    rows, part = firsts[0].shape
    vmem = pl.BlockSpec(memory_space=pltpu.VMEM)
    return pl.pallas_call(
        functools.partial(second_norm_kernel, slices),
        out_shape=(jax.ShapeDtypeStruct((slices * rows, part + META), jnp.bfloat16),)
        + (jax.ShapeDtypeStruct((rows, part), jnp.bfloat16),) * slices,
        in_specs=[vmem] * (2 * slices + 1),
        out_specs=(vmem,) * (1 + slices),
        name="second_norm",
    )(*parts, *firsts, gain)


def projection_kernel(slices, pos_ref, mine_ref, theirs_ref, q_ref, kv_ref, *out_refs):
    rows, extended = mine_ref.shape
    part = extended - META
    block = rows // slices
    q_cols, kv_cols = q_ref.shape[1], kv_ref.shape[1]
    both = jnp.concatenate([mine_ref[:, :part], theirs_ref[:, :part]], axis=0)
    starts = [(q_ref, i, i) for i in range(0, q_cols, kv_cols)] + [(kv_ref, 0, q_cols)]
    tensor = pos_ref[1]
    own = pl.ds(pl.multiple_of(tensor * block, block), block)
    other = pl.ds(pl.multiple_of((1 - tensor) * block, block), block)
    for weight_ref, source, target in starts:
        product = jnp.dot(
            both, weight_ref[:, source : source + kv_cols], preferred_element_type=jnp.float32
        ).astype(jnp.bfloat16)
        for d in range(slices):
            cols = slice(target, target + kv_cols)
            out_refs[d][own, cols] = product[d * block : (d + 1) * block]
            out_refs[d][other, cols] = product[rows + d * block : rows + (d + 1) * block]
    for d in range(slices):
        out_refs[d][own, q_cols + kv_cols :] = mine_ref[d * block : (d + 1) * block, part:]
        out_refs[d][other, q_cols + kv_cols :] = theirs_ref[d * block : (d + 1) * block, part:]


def projection(pos, mine, theirs, q_weight, kv_weight, slices):
    rows = mine.shape[0]
    cols = q_weight.shape[1] + kv_weight.shape[1]
    vmem = pl.BlockSpec(memory_space=pltpu.VMEM)
    return pl.pallas_call(
        functools.partial(projection_kernel, slices),
        out_shape=(jax.ShapeDtypeStruct((2 * rows // slices, cols + META), jnp.bfloat16),) * slices,
        in_specs=[pl.BlockSpec(memory_space=pltpu.SMEM)] + [vmem] * 4,
        out_specs=(vmem,) * slices,
        compiler_params=pltpu.CompilerParams(vmem_limit_bytes=24 << 20),
        cost_estimate=pl.CostEstimate(
            flops=4 * rows * q_weight.shape[0] * cols,
            bytes_accessed=2 * q_weight.shape[0] * cols,
            transcendentals=0,
        ),
        name="qkv_projection",
    )(pos, mine, theirs, q_weight, kv_weight)


def head_norm_kernel(slices, width, pos_ref, *refs):
    parts, q_gain_ref, k_gain_ref = refs[:slices], refs[slices], refs[slices + 1]
    q_ref, kv_ref = refs[slices + 2 :]
    q_cols, kv_cols = q_ref.shape[1], kv_ref.shape[1]
    head = q_gain_ref.shape[1]

    def total(cols):
        value = parts[0][:, cols].astype(jnp.float32)
        for ref in parts[1:]:
            value = value + ref[:, cols].astype(jnp.float32)
        return value

    squares = jnp.sum(total(slice(q_cols + kv_cols, None)), axis=1, keepdims=True)
    scale = lax.rsqrt(squares / width + EPSILON)
    for h in range(q_cols // head):
        cols = slice(h * head, (h + 1) * head)
        q_ref[:, cols] = normalize(total(cols) * scale, q_gain_ref[...]).astype(jnp.bfloat16)
    for h in range(kv_cols // head):
        cols = slice(h * head, (h + 1) * head)
        raw = total(slice(q_cols + h * head, q_cols + (h + 1) * head)) * scale
        is_key = pos_ref[1] * (kv_cols // head) + h < KV_HEADS
        kv_ref[:, cols] = jnp.where(is_key, normalize(raw, k_gain_ref[...]), raw).astype(
            jnp.bfloat16
        )


def head_norm(pos, parts, q_gain, k_gain, q_cols, kv_cols, width):
    slices = len(parts)
    rows = parts[0].shape[0]
    vmem = pl.BlockSpec(memory_space=pltpu.VMEM)
    return pl.pallas_call(
        functools.partial(head_norm_kernel, slices, width),
        out_shape=(
            jax.ShapeDtypeStruct((rows, q_cols), jnp.bfloat16),
            jax.ShapeDtypeStruct((rows, kv_cols), jnp.bfloat16),
        ),
        in_specs=[pl.BlockSpec(memory_space=pltpu.SMEM)] + [vmem] * (slices + 2),
        out_specs=(vmem, vmem),
        name="head_norm",
    )(pos, *parts, q_gain, k_gain)


def assemble_kernel(slices, pos_ref, *refs):
    out_ref = refs[slices]
    part = refs[0].shape[1]
    for d in range(slices):
        at = pl.multiple_of((pos_ref[0] ^ d) * part, part)
        out_ref[:, pl.ds(at, part)] = refs[d][...]


def assemble(pos, parts):
    slices = len(parts)
    rows, part = parts[0].shape
    vmem = pl.BlockSpec(memory_space=pltpu.VMEM)
    return pl.pallas_call(
        functools.partial(assemble_kernel, slices),
        out_shape=jax.ShapeDtypeStruct((rows, slices * part), jnp.bfloat16),
        in_specs=[pl.BlockSpec(memory_space=pltpu.SMEM)] + [vmem] * slices,
        out_specs=vmem,
        name="assemble_residual",
    )(pos, *parts)


def per_device_dense(
    attn_out,
    out_weight,
    residual,
    attn_gain,
    expert_ids,
    route_weights,
    w_gate,
    w_up,
    w_down,
    input_gain,
    q_weight,
    kv_weight,
    q_gain,
    k_gain,
):
    n_expert = lax.axis_size("expert")
    depth = n_expert // PLANE
    all_experts = 2 * n_expert
    width = residual.shape[1]
    rows = residual.shape[0]
    expert_index = lax.axis_index("expert").astype(jnp.int32)
    tensor_index = lax.axis_index("tensor").astype(jnp.int32)
    z_index = expert_index // PLANE
    pos = jnp.stack(
        [
            z_index,
            tensor_index,
            2 * expert_index + tensor_index,
            2 * expert_index + 1 - tensor_index,
        ]
    )

    def to_core(value):
        return lax.ppermute(value, "tensor", [(0, 1), (1, 0)])

    def to_expert(value, offset):
        return lax.ppermute(value, "expert", [(i, i ^ offset) for i in range(n_expert)])

    def to_z(value, d):
        return to_expert(value, d * PLANE) if d else value

    def to_plane(value, d):
        return to_expert(value, d) if d else value

    planes = [list(range(i, i + PLANE)) for i in range(0, n_expert, PLANE)]
    q_rows = lax.all_gather(q_weight, "expert", axis=0, tiled=True, axis_index_groups=planes)
    kv_rows = lax.all_gather(kv_weight, "expert", axis=0, tiled=True, axis_index_groups=planes)
    weights = (w_gate, w_up, w_down, to_core(w_gate), to_core(w_up), to_core(w_down))

    own_ids = lax.dynamic_slice_in_dim(expert_ids, tensor_index * rows, rows, 0)
    own_route = lax.dynamic_slice_in_dim(route_weights, tensor_index * rows, rows, 0)
    chosen = own_ids[:, :, None] == jnp.arange(META // 2, dtype=jnp.int32)[None, None, :]
    dense = jnp.sum(jnp.where(chosen, own_route[:, :, None], 0.0), axis=1)
    high = lax.reduce_precision(dense, 8, 7)
    meta = jnp.concatenate([high, dense - high], axis=1).astype(jnp.bfloat16)

    mine, theirs = out_projection(pos, attn_out, out_weight)
    tokens, *firsts = first_norm(
        pos, mine, to_core(theirs), residual, attn_gain[None, :], meta, depth
    )
    firsts = [to_z(firsts[d], d) for d in range(depth)]
    line = [to_z(tokens, d) for d in range(depth)]
    blocks = [to_plane(block, d) for d in range(PLANE) for block in line]
    outs = experts(pos, blocks, weights)
    outs = [to_plane(outs[d], d) for d in range(PLANE)]
    parts = plane_sum(pos, outs, depth)
    parts = [to_z(parts[d], d) for d in range(depth)]
    own_gain = lax.dynamic_slice_in_dim(input_gain, z_index * (width // depth), width // depth, 0)
    scaled, *following = second_norm(parts, firsts, own_gain[None, :])
    products = projection(pos, scaled, to_core(scaled), q_rows, kv_rows, depth)
    next_residual = assemble(pos, [to_z(following[d], d) for d in range(depth)])
    products = [to_z(products[d], d) for d in range(depth)]
    queries, keys_values = head_norm(
        pos,
        products,
        q_gain[None, :],
        k_gain[None, :],
        q_weight.shape[1],
        kv_weight.shape[1],
        width,
    )
    return (next_residual, queries, keys_values)


def per_device(
    attn_out,
    out_weight,
    residual,
    attn_gain,
    expert_ids,
    route_weights,
    w_gate,
    w_up,
    w_down,
    input_gain,
    q_weight,
    kv_weight,
    q_gain,
    k_gain,
):
    n_expert = lax.axis_size("expert")
    n_tensor = lax.axis_size("tensor")
    share = n_tensor // 2
    tensor_index = lax.axis_index("tensor")
    group_rows = attn_out.shape[0]
    width = residual.shape[1]
    half = tensor_index // share
    capacity = 3 * group_rows * TOP // (4 * n_expert)
    all_experts = 2 * n_expert
    attn_rows = lax.psum_scatter(
        jnp.dot(attn_out, out_weight, preferred_element_type=jnp.float32),
        "tensor",
        scatter_dimension=0,
        tiled=True,
    )
    first_residual = (residual.astype(jnp.float32) + attn_rows).astype(jnp.bfloat16)
    normed = normalize(first_residual.astype(jnp.float32), attn_gain).astype(jnp.bfloat16)
    group_normed = lax.all_gather(normed, "tensor", axis=0, tiled=True)
    flat_ids = expert_ids.reshape(-1)
    onehot = (flat_ids[:, None] == jnp.arange(all_experts, dtype=jnp.int32)[None, :]).astype(
        jnp.int32
    )
    earlier = jnp.cumsum(onehot, axis=0) - onehot
    rank = jnp.sum(earlier * onehot, axis=1)
    dest = flat_ids * capacity + rank
    row_owner = jnp.arange(flat_ids.shape[0], dtype=jnp.int32) // TOP
    slot_row = jnp.full((all_experts * capacity,), group_rows, jnp.int32).at[dest].set(row_owner)
    slot_weight = (
        jnp.zeros((all_experts * capacity,), jnp.float32).at[dest].set(route_weights.reshape(-1))
    )
    own_slots = lax.dynamic_index_in_dim(
        slot_row.reshape(n_expert, 2, capacity), half, 1, keepdims=False
    )
    own_weights = lax.dynamic_index_in_dim(
        slot_weight.reshape(n_expert, 2, capacity), half, 1, keepdims=False
    )
    padded_rows = jnp.concatenate([group_normed, jnp.zeros((1, width), jnp.bfloat16)], axis=0)
    gate_w = w_gate[0]
    up_w = w_up[0]
    down_w = w_down[0]
    outgoing = jnp.take(padded_rows, own_slots, axis=0)
    arrived = lax.all_to_all(outgoing, "expert", split_axis=0, concat_axis=0, tiled=True)
    flat = arrived.reshape(-1, width)
    gate = jnp.dot(flat, gate_w, preferred_element_type=jnp.float32)
    up = jnp.dot(flat, up_w, preferred_element_type=jnp.float32)
    act = (jax.nn.silu(gate) * up).astype(jnp.bfloat16)
    part = jnp.dot(act, down_w, preferred_element_type=jnp.float32).astype(jnp.bfloat16)
    send_part = part.reshape(arrived.shape)
    returned = lax.all_to_all(send_part, "expert", split_axis=0, concat_axis=0, tiled=True)
    weighted = own_weights.reshape(-1)[:, None] * returned.reshape(-1, width).astype(jnp.float32)
    term = (
        jnp.zeros((group_rows + 1, width), jnp.float32)
        .at[own_slots.reshape(-1)]
        .add(weighted)[:group_rows]
    )
    expert_sum = lax.psum_scatter(
        term.astype(jnp.bfloat16), "tensor", scatter_dimension=0, tiled=True
    ).astype(jnp.float32)
    next_residual = (first_residual.astype(jnp.float32) + expert_sum).astype(jnp.bfloat16)
    own_normed = normalize(next_residual.astype(jnp.float32), input_gain).astype(jnp.bfloat16)
    next_normed = lax.all_gather(own_normed, "tensor", axis=0, tiled=True)
    query_cols = q_weight.shape[1]
    kv_cols = kv_weight.shape[1]
    query_raw = jnp.dot(
        next_normed,
        lax.all_gather(q_weight, "expert", axis=0, tiled=True),
        preferred_element_type=jnp.float32,
    )
    kv_raw = jnp.dot(
        next_normed,
        lax.all_gather(kv_weight, "expert", axis=0, tiled=True),
        preferred_element_type=jnp.float32,
    )
    head_size = q_gain.shape[0]
    queries = (
        normalize(query_raw.reshape(group_rows, -1, head_size), q_gain)
        .reshape(group_rows, query_cols)
        .astype(jnp.bfloat16)
    )
    heads_here = kv_cols // head_size
    head_number = tensor_index * heads_here + jnp.arange(heads_here, dtype=jnp.int32)
    is_key = head_number < KV_HEADS
    kv_shaped = kv_raw.reshape(group_rows, heads_here, head_size)
    keys_values = (
        jnp.where(is_key[None, :, None], normalize(kv_shaped, k_gain), kv_shaped)
        .reshape(group_rows, kv_cols)
        .astype(jnp.bfloat16)
    )
    return (next_residual, queries, keys_values)


def solution(mesh):
    small = mesh.shape["tensor"] == 2 and mesh.shape["expert"] == 4 * PLANE
    return jax.shard_map(
        per_device_dense if small else per_device,
        mesh=mesh,
        in_specs=(
            P("expert", "tensor"),
            P("tensor", None),
            P(("expert", "tensor"), None),
            P(),
            P("expert", None),
            P("expert", None),
            P("expert", None, "tensor"),
            P("expert", None, "tensor"),
            P("expert", "tensor", None),
            P(),
            P("expert", "tensor"),
            P("expert", "tensor"),
            P(),
            P(),
        ),
        out_specs=(P(("expert", "tensor"), None), P("expert", "tensor"), P("expert", "tensor")),
        check_vma=False,
    )
```

```python
import functools

import jax
import jax.numpy as jnp
from jax import lax
from jax.experimental import pallas as pl
from jax.experimental.pallas import tpu as pltpu
from jax.sharding import PartitionSpec as P

KV_HEADS = 4
TOP = 8
PLANE = 4
META = 128


EPSILON = 1e-06

VMEM = pl.BlockSpec(memory_space=pltpu.VMEM)
HBM = pl.BlockSpec(memory_space=pltpu.HBM)


def normalize(values, gain):
    return values * lax.rsqrt(jnp.mean(values * values, axis=-1, keepdims=True) + EPSILON) * gain


def params(mebibytes):
    return pltpu.CompilerParams(vmem_limit_bytes=mebibytes << 20)


def lanes(start, size):
    return pl.ds(pl.multiple_of(start, size), size)


def out_projection_kernel(chunk, a_hbm, w_hbm, mine_ref, theirs_ref, a_buf, w_buf, a_sem, sems):
    width = w_buf.shape[1]
    count = width // chunk
    half = mine_ref.shape[0]
    a_copy = pltpu.make_async_copy(a_hbm, a_buf, a_sem)
    a_copy.start()
    copies = []
    for i in range(count):
        cols = pl.ds(i * chunk, chunk)
        copies.append(pltpu.make_async_copy(w_hbm.at[:, cols], w_buf.at[:, cols], sems.at[i]))
    for copy in copies:
        copy.start()
    tensor = lax.axis_index("tensor")
    a_copy.wait()
    own = a_buf[lanes(tensor * half, half), :]
    other = a_buf[lanes((1 - tensor) * half, half), :]
    both = jnp.concatenate([own, other], axis=0)
    for i in range(count):
        copies[i].wait()
        cols = pl.ds(i * chunk, chunk)
        product = jnp.dot(both, w_buf[:, cols], preferred_element_type=jnp.float32)
        mine_ref[:, cols] = product[:half]
        theirs_ref[:, cols] = product[half:]


def out_projection(attn_out, out_weight):
    rows, depth = attn_out.shape
    width = out_weight.shape[1]
    chunk = 256
    half = jax.ShapeDtypeStruct((rows // 2, width), jnp.float32)
    return pl.pallas_call(
        functools.partial(out_projection_kernel, chunk),
        out_shape=(half, half),
        in_specs=[HBM, HBM],
        out_specs=(VMEM, VMEM),
        scratch_shapes=[
            pltpu.VMEM((rows, depth), jnp.bfloat16),
            pltpu.VMEM((depth, width), jnp.bfloat16),
            pltpu.SemaphoreType.DMA,
            pltpu.SemaphoreType.DMA((width // chunk,)),
        ],
        compiler_params=params(14),
        cost_estimate=pl.CostEstimate(
            flops=2 * rows * depth * width, bytes_accessed=2 * depth * width, transcendentals=0
        ),
        name="out_projection",
    )(attn_out, out_weight)


def first_norm_kernel(
    depth, mine_ref, theirs_ref, residual_ref, gain_ref, meta_ref, tokens_ref, *refs
):
    slice_refs, first_ref = refs[:PLANE], refs[PLANE]
    rows, width = residual_ref.shape
    sub = width // (PLANE * depth)
    first = (residual_ref[...].astype(jnp.float32) + (mine_ref[...] + theirs_ref[...])).astype(
        jnp.bfloat16
    )
    first_ref[...] = first
    tokens_ref[:, :width] = normalize(first.astype(jnp.float32), gain_ref[...]).astype(jnp.bfloat16)
    tokens_ref[:, width:] = meta_ref[...]
    plane = lax.axis_index("expert") % PLANE
    for d in range(PLANE):
        for z in range(depth):
            slice_refs[d][z * rows : (z + 1) * rows, :] = first_ref[
                :, lanes((z * PLANE + (plane ^ d)) * sub, sub)
            ]


def first_norm(mine, theirs, residual, gain, meta, depth):
    rows, width = residual.shape
    piece = jax.ShapeDtypeStruct((depth * rows, width // (PLANE * depth)), jnp.bfloat16)
    return pl.pallas_call(
        functools.partial(first_norm_kernel, depth),
        out_shape=(jax.ShapeDtypeStruct((rows, width + META), jnp.bfloat16),) + (piece,) * PLANE,
        in_specs=[VMEM] * 5,
        out_specs=(VMEM,) * (1 + PLANE),
        scratch_shapes=[pltpu.VMEM((rows, width), jnp.bfloat16)],
        compiler_params=params(2),
        name="first_norm",
    )(mine, theirs, residual, gain, meta)


def pack_kernel(depth, *refs):
    line, pieces, out_refs = refs[:depth], refs[depth : depth + PLANE - 1], refs[depth + PLANE - 1 :]
    rows, extended = line[0].shape
    for ref, piece in zip(out_refs, pieces):
        for z in range(depth):
            ref[z * rows : (z + 1) * rows, :extended] = line[z][...]
        ref[:, extended:] = piece[...]


def pack(line, pieces):
    depth = len(line)
    rows, extended = line[0].shape
    shape = jax.ShapeDtypeStruct((depth * rows, extended + pieces[0].shape[1]), jnp.bfloat16)
    return pl.pallas_call(
        functools.partial(pack_kernel, depth),
        out_shape=(shape,) * (PLANE - 1),
        in_specs=[VMEM] * (depth + PLANE - 1),
        out_specs=(VMEM,) * (PLANE - 1),
        compiler_params=params(2),
        name="pack_tokens",
    )(*line, *pieces)


def expert_kernel(depth, chunk, *refs):
    line, packed = refs[:depth], refs[depth : depth + PLANE - 1]
    at = depth + PLANE - 1
    weight_refs, out_refs = refs[at : at + 6], refs[at + 6 : at + 6 + PLANE]
    x_buf, gate_buf, up_buf, down_buf, act_buf, sems = refs[at + 6 + PLANE :]
    width, hidden = gate_buf.shape[1], gate_buf.shape[2]
    rows, extended = line[0].shape
    per = hidden // chunk
    gate_copies, down_copies = [], []
    for side in range(2):
        gate_ref, up_ref, down_ref = weight_refs[3 * side : 3 * side + 3]
        for i in range(per):
            cols = pl.ds(i * chunk, chunk)
            j = side * per + i
            gate_copies.append(
                (
                    pltpu.make_async_copy(
                        gate_ref.at[0, :, cols], gate_buf.at[side, :, cols], sems.at[0, j]
                    ),
                    pltpu.make_async_copy(
                        up_ref.at[0, :, cols], up_buf.at[side, :, cols], sems.at[1, j]
                    ),
                )
            )
            down_copies.append(
                pltpu.make_async_copy(
                    down_ref.at[0, pl.ds(i * chunk, chunk), :],
                    down_buf.at[pl.ds(j * chunk, chunk), :],
                    sems.at[2, j],
                )
            )
    for pair in gate_copies:
        pair[0].start()
        pair[1].start()
    for copy in down_copies:
        copy.start()
    group = depth * rows
    for z in range(depth):
        x_buf[z * rows : (z + 1) * rows, :] = line[z][...]
    for d in range(1, PLANE):
        x_buf[d * group : (d + 1) * group, :] = packed[d - 1][:, :extended]
    meta = x_buf[:, width:].astype(jnp.float32)
    lane = lax.broadcasted_iota(jnp.int32, meta.shape, 1)
    chip = lax.axis_index("expert")
    tensor = lax.axis_index("tensor")
    for side in range(2):
        expert = 2 * chip + (tensor if side == 0 else 1 - tensor)
        chosen = (lane == expert) | (lane == expert + META // 2)
        route = jnp.sum(jnp.where(chosen, meta, 0.0), axis=1, keepdims=True)
        for i in range(per):
            j = side * per + i
            gate_copies[j][0].wait()
            gate_copies[j][1].wait()
            cols = pl.ds(i * chunk, chunk)
            x = x_buf[:, :width]
            gate = jnp.dot(x, gate_buf[side, :, cols], preferred_element_type=jnp.float32)
            up = jnp.dot(x, up_buf[side, :, cols], preferred_element_type=jnp.float32)
            act = gate / (1.0 + jnp.exp(-gate)) * up * route
            act_buf[:, j * chunk : (j + 1) * chunk] = act.astype(jnp.bfloat16)
    for copy in down_copies:
        copy.wait()
    sub = width // (PLANE * depth)
    plane = chip % PLANE
    for d in range(PLANE):
        weight = jnp.concatenate(
            [
                down_buf[:, lanes((z * PLANE + (plane ^ d)) * sub, sub)]
                for z in range(depth)
            ],
            axis=1,
        )
        out = jnp.dot(act_buf[...], weight, preferred_element_type=jnp.float32)
        for k in range(PLANE):
            out_refs[d][k * group : (k + 1) * group, :] = out[
                (d ^ k) * group : ((d ^ k) + 1) * group
            ].astype(jnp.bfloat16)


def experts(line, packed, weights):
    depth = len(line)
    rows, extended = line[0].shape
    width, hidden = weights[0].shape[1:]
    chunk = 256
    total = rows * depth * PLANE
    return pl.pallas_call(
        functools.partial(expert_kernel, depth, chunk),
        out_shape=(jax.ShapeDtypeStruct((total, width // PLANE), jnp.bfloat16),) * PLANE,
        in_specs=[VMEM] * (depth + PLANE - 1) + [HBM] * 6,
        out_specs=(VMEM,) * PLANE,
        scratch_shapes=[
            pltpu.VMEM((total, extended), jnp.bfloat16),
            pltpu.VMEM((2, width, hidden), jnp.bfloat16),
            pltpu.VMEM((2, width, hidden), jnp.bfloat16),
            pltpu.VMEM((2 * hidden, width), jnp.bfloat16),
            pltpu.VMEM((total, 2 * hidden), jnp.bfloat16),
            pltpu.SemaphoreType.DMA((3, 2 * (hidden // chunk))),
        ],
        compiler_params=params(32),
        cost_estimate=pl.CostEstimate(
            flops=12 * total * width * hidden,
            bytes_accessed=12 * width * hidden,
            transcendentals=2 * total * hidden,
        ),
        name="experts",
    )(*line, *packed, *weights)


def plane_sum_kernel(depth, *refs):
    in_refs, out_refs = refs[:PLANE], refs[PLANE:]
    rows = in_refs[0].shape[0] // (PLANE * depth)
    for d in range(PLANE):
        for z in range(depth):
            start = (d * depth + z) * rows
            at = slice(start, start + rows)
            total = in_refs[0][at, :].astype(jnp.float32)
            for ref in in_refs[1:]:
                total = total + ref[at, :].astype(jnp.float32)
            out_refs[z][d * rows : (d + 1) * rows, :] = total.astype(jnp.bfloat16)


def plane_sum(parts, depth):
    rows, part = parts[0].shape
    return pl.pallas_call(
        functools.partial(plane_sum_kernel, depth),
        out_shape=(jax.ShapeDtypeStruct((rows // depth, part), jnp.bfloat16),) * depth,
        in_specs=[VMEM] * PLANE,
        out_specs=(VMEM,) * depth,
        compiler_params=params(4),
        name="plane_sum",
    )(*parts)


def second_norm_kernel(depth, *refs):
    parts, first_ref, packed = refs[:depth], refs[depth], refs[depth + 1 : depth + PLANE]
    gain_ref, scaled_ref, next_ref = refs[depth + PLANE :]
    rows = first_ref.shape[0] // depth
    sub = first_ref.shape[1]
    part = depth * sub
    lane = lax.broadcasted_iota(jnp.int32, (rows, META), 1)
    plane = lax.axis_index("expert") % PLANE
    gain = jnp.concatenate(
        [gain_ref[:, lanes((z * PLANE + plane) * sub, sub)] for z in range(depth)], axis=1
    )
    for d in range(PLANE):
        at = slice(d * rows, (d + 1) * rows)
        total = parts[0][at, :].astype(jnp.float32)
        for ref in parts[1:]:
            total = total + ref[at, :].astype(jnp.float32)
        source = first_ref if d == 0 else packed[d - 1]
        skip = source.shape[1] - sub
        first = jnp.concatenate(
            [source[z * rows : (z + 1) * rows, skip:] for z in range(depth)], axis=1
        )
        following = (first.astype(jnp.float32) + total).astype(jnp.bfloat16)
        next_ref[at, :] = following
        wide = following.astype(jnp.float32)
        scaled_ref[at, :part] = (wide * gain).astype(jnp.bfloat16)
        squares = jnp.sum(wide * wide, axis=1, keepdims=True)
        high = squares.astype(jnp.bfloat16).astype(jnp.float32)
        low = squares - high
        scaled_ref[at, part:] = jnp.where(
            lane == 0, high, jnp.where(lane == 1, low, 0.0)
        ).astype(jnp.bfloat16)


def second_norm(parts, first, packed, gain):
    depth = len(parts)
    rows, part = parts[0].shape
    return pl.pallas_call(
        functools.partial(second_norm_kernel, depth),
        out_shape=(
            jax.ShapeDtypeStruct((rows, part + META), jnp.bfloat16),
            jax.ShapeDtypeStruct((rows, part), jnp.bfloat16),
        ),
        in_specs=[VMEM] * (depth + PLANE + 1),
        out_specs=(VMEM, VMEM),
        compiler_params=params(4),
        name="second_norm",
    )(*parts, first, *packed, gain)


def projection_kernel(chunk, mine_ref, theirs_ref, next_ref, w_hbm, *refs):
    out_refs, (w_buf, sems) = refs[:PLANE], refs[PLANE:]
    cols = w_buf.shape[1]
    copies = []
    for i in range(cols // chunk):
        at = pl.ds(i * chunk, chunk)
        copies.append(pltpu.make_async_copy(w_hbm.at[:, at], w_buf.at[:, at], sems.at[i]))
    for copy in copies:
        copy.start()
    rows, extended = mine_ref.shape
    part = extended - META
    block = rows // PLANE
    tensor = lax.axis_index("tensor")
    own = lanes(tensor * block, block)
    other = lanes((1 - tensor) * block, block)
    for d in range(PLANE):
        at = slice(d * block, (d + 1) * block)
        out_refs[d][own, cols : cols + META] = mine_ref[at, part:]
        out_refs[d][other, cols : cols + META] = theirs_ref[at, part:]
        out_refs[d][:block, cols + META :] = next_ref[at, : part // 2]
        out_refs[d][block:, cols + META :] = next_ref[at, part // 2 :]
    both = jnp.concatenate([mine_ref[:, :part], theirs_ref[:, :part]], axis=0)
    for i in range(cols // chunk):
        copies[i].wait()
        at = slice(i * chunk, (i + 1) * chunk)
        product = jnp.dot(both, w_buf[:, at], preferred_element_type=jnp.float32).astype(
            jnp.bfloat16
        )
        for d in range(PLANE):
            out_refs[d][own, at] = product[d * block : (d + 1) * block]
            out_refs[d][other, at] = product[rows + d * block : rows + (d + 1) * block]


def projection(mine, theirs, following, weight):
    rows, part = following.shape
    cols = weight.shape[1]
    chunk = 512
    shape = jax.ShapeDtypeStruct((2 * rows // PLANE, cols + META + part // 2), jnp.bfloat16)
    return pl.pallas_call(
        functools.partial(projection_kernel, chunk),
        out_shape=(shape,) * PLANE,
        in_specs=[VMEM] * 3 + [HBM],
        out_specs=(VMEM,) * PLANE,
        scratch_shapes=[
            pltpu.VMEM((part, cols), jnp.bfloat16),
            pltpu.SemaphoreType.DMA((cols // chunk,)),
        ],
        compiler_params=params(8),
        cost_estimate=pl.CostEstimate(
            flops=4 * rows * part * cols, bytes_accessed=2 * part * cols, transcendentals=0
        ),
        name="qkv_projection",
    )(mine, theirs, following, weight)


def head_norm_kernel(depth, *refs):
    parts, q_gain_ref, k_gain_ref = refs[:PLANE], refs[PLANE], refs[PLANE + 1]
    next_ref, q_ref, kv_ref = refs[PLANE + 2 :]
    width = next_ref.shape[1]
    q_cols, kv_cols = q_ref.shape[1], kv_ref.shape[1]
    cols = q_cols + kv_cols
    head = q_gain_ref.shape[1]

    def total(at):
        value = parts[0][:, at].astype(jnp.float32)
        for ref in parts[1:]:
            value = value + ref[:, at].astype(jnp.float32)
        return value

    squares = jnp.sum(total(slice(cols, cols + META)), axis=1, keepdims=True)
    scale = lax.rsqrt(squares / width + EPSILON)
    for h in range(q_cols // head):
        at = slice(h * head, (h + 1) * head)
        q_ref[:, at] = normalize(total(at) * scale, q_gain_ref[...]).astype(jnp.bfloat16)
    tensor = lax.axis_index("tensor")
    for h in range(kv_cols // head):
        at = slice(h * head, (h + 1) * head)
        raw = total(slice(q_cols + h * head, q_cols + (h + 1) * head)) * scale
        is_key = tensor * (kv_cols // head) + h < KV_HEADS
        kv_ref[:, at] = jnp.where(is_key, normalize(raw, k_gain_ref[...]), raw).astype(
            jnp.bfloat16
        )
    plane = lax.axis_index("expert") % PLANE
    rows = next_ref.shape[0]
    sub = width // (PLANE * depth)
    for d in range(PLANE):
        for z in range(depth):
            top = z * sub * 2 // (depth * sub)
            start = cols + META + z * sub - top * (depth * sub // 2)
            next_ref[:, lanes((z * PLANE + (plane ^ d)) * sub, sub)] = parts[d][
                top * rows : (top + 1) * rows, start : start + sub
            ]


def head_norm(parts, q_gain, k_gain, q_cols, kv_cols, rows, width, depth):
    both = parts[0].shape[0]
    return pl.pallas_call(
        functools.partial(head_norm_kernel, depth),
        out_shape=(
            jax.ShapeDtypeStruct((rows, width), jnp.bfloat16),
            jax.ShapeDtypeStruct((both, q_cols), jnp.bfloat16),
            jax.ShapeDtypeStruct((both, kv_cols), jnp.bfloat16),
        ),
        in_specs=[VMEM] * (PLANE + 2),
        out_specs=(VMEM, VMEM, VMEM),
        compiler_params=params(4),
        name="head_norm",
    )(*parts, q_gain, k_gain)


def per_device_dense(
    attn_out,
    out_weight,
    residual,
    attn_gain,
    expert_ids,
    route_weights,
    w_gate,
    w_up,
    w_down,
    input_gain,
    q_weight,
    kv_weight,
    q_gain,
    k_gain,
):
    n_expert = lax.axis_size("expert")
    depth = n_expert // PLANE
    rows, width = residual.shape
    tensor_index = lax.axis_index("tensor").astype(jnp.int32)

    def to_core(value):
        return lax.ppermute(value, "tensor", [(0, 1), (1, 0)])

    def to_expert(value, offset):
        return lax.ppermute(value, "expert", [(i, i ^ offset) for i in range(n_expert)])

    def to_z(values):
        return [to_expert(v, d * PLANE) if d else v for d, v in enumerate(values)]

    def to_plane(values):
        return [to_expert(v, d) if d else v for d, v in enumerate(values)]

    lines = [list(range(i, n_expert, PLANE)) for i in range(PLANE)]
    qkv = lax.all_gather(
        jnp.concatenate([q_weight, kv_weight], axis=1),
        "expert",
        axis=0,
        tiled=True,
        axis_index_groups=lines,
    )
    weights = (w_gate, w_up, w_down, to_core(w_gate), to_core(w_up), to_core(w_down))

    own_ids = lax.dynamic_slice_in_dim(expert_ids, tensor_index * rows, rows, 0)
    own_route = lax.dynamic_slice_in_dim(route_weights, tensor_index * rows, rows, 0)
    chosen = own_ids[:, :, None] == jnp.arange(META // 2, dtype=jnp.int32)[None, None, :]
    dense = jnp.sum(jnp.where(chosen, own_route[:, :, None], 0.0), axis=1)
    high = lax.reduce_precision(dense, 8, 7)
    meta = jnp.concatenate([high, dense - high], axis=1).astype(jnp.bfloat16)

    mine, theirs = out_projection(attn_out, out_weight)
    tokens, *firsts = first_norm(
        mine, to_core(theirs), residual, attn_gain[None, :], meta, depth
    )
    line = to_z([tokens] * depth)
    packed = to_plane([None, *pack(line, firsts[1:])])[1:]
    parts = plane_sum(to_plane(experts(line, packed, weights)), depth)
    scaled, following = second_norm(to_z(parts), firsts[0], packed, input_gain[None, :])
    products = to_plane(projection(scaled, to_core(scaled), following, qkv))
    return head_norm(
        products,
        q_gain[None, :],
        k_gain[None, :],
        q_weight.shape[1],
        kv_weight.shape[1],
        rows,
        width,
        depth,
    )


def per_device(
    attn_out,
    out_weight,
    residual,
    attn_gain,
    expert_ids,
    route_weights,
    w_gate,
    w_up,
    w_down,
    input_gain,
    q_weight,
    kv_weight,
    q_gain,
    k_gain,
):
    n_expert = lax.axis_size("expert")
    n_tensor = lax.axis_size("tensor")
    share = n_tensor // 2
    tensor_index = lax.axis_index("tensor")
    group_rows = attn_out.shape[0]
    width = residual.shape[1]
    half = tensor_index // share
    capacity = 3 * group_rows * TOP // (4 * n_expert)
    all_experts = 2 * n_expert
    attn_rows = lax.psum_scatter(
        jnp.dot(attn_out, out_weight, preferred_element_type=jnp.float32),
        "tensor",
        scatter_dimension=0,
        tiled=True,
    )
    first_residual = (residual.astype(jnp.float32) + attn_rows).astype(jnp.bfloat16)
    normed = normalize(first_residual.astype(jnp.float32), attn_gain).astype(jnp.bfloat16)
    group_normed = lax.all_gather(normed, "tensor", axis=0, tiled=True)
    flat_ids = expert_ids.reshape(-1)
    onehot = (flat_ids[:, None] == jnp.arange(all_experts, dtype=jnp.int32)[None, :]).astype(
        jnp.int32
    )
    earlier = jnp.cumsum(onehot, axis=0) - onehot
    rank = jnp.sum(earlier * onehot, axis=1)
    dest = flat_ids * capacity + rank
    row_owner = jnp.arange(flat_ids.shape[0], dtype=jnp.int32) // TOP
    slot_row = jnp.full((all_experts * capacity,), group_rows, jnp.int32).at[dest].set(row_owner)
    slot_weight = (
        jnp.zeros((all_experts * capacity,), jnp.float32).at[dest].set(route_weights.reshape(-1))
    )
    own_slots = lax.dynamic_index_in_dim(
        slot_row.reshape(n_expert, 2, capacity), half, 1, keepdims=False
    )
    own_weights = lax.dynamic_index_in_dim(
        slot_weight.reshape(n_expert, 2, capacity), half, 1, keepdims=False
    )
    padded_rows = jnp.concatenate([group_normed, jnp.zeros((1, width), jnp.bfloat16)], axis=0)
    gate_w = w_gate[0]
    up_w = w_up[0]
    down_w = w_down[0]
    outgoing = jnp.take(padded_rows, own_slots, axis=0)
    arrived = lax.all_to_all(outgoing, "expert", split_axis=0, concat_axis=0, tiled=True)
    flat = arrived.reshape(-1, width)
    gate = jnp.dot(flat, gate_w, preferred_element_type=jnp.float32)
    up = jnp.dot(flat, up_w, preferred_element_type=jnp.float32)
    act = (jax.nn.silu(gate) * up).astype(jnp.bfloat16)
    part = jnp.dot(act, down_w, preferred_element_type=jnp.float32).astype(jnp.bfloat16)
    send_part = part.reshape(arrived.shape)
    returned = lax.all_to_all(send_part, "expert", split_axis=0, concat_axis=0, tiled=True)
    weighted = own_weights.reshape(-1)[:, None] * returned.reshape(-1, width).astype(jnp.float32)
    term = (
        jnp.zeros((group_rows + 1, width), jnp.float32)
        .at[own_slots.reshape(-1)]
        .add(weighted)[:group_rows]
    )
    expert_sum = lax.psum_scatter(
        term.astype(jnp.bfloat16), "tensor", scatter_dimension=0, tiled=True
    ).astype(jnp.float32)
    next_residual = (first_residual.astype(jnp.float32) + expert_sum).astype(jnp.bfloat16)
    own_normed = normalize(next_residual.astype(jnp.float32), input_gain).astype(jnp.bfloat16)
    next_normed = lax.all_gather(own_normed, "tensor", axis=0, tiled=True)
    query_cols = q_weight.shape[1]
    kv_cols = kv_weight.shape[1]
    query_raw = jnp.dot(
        next_normed,
        lax.all_gather(q_weight, "expert", axis=0, tiled=True),
        preferred_element_type=jnp.float32,
    )
    kv_raw = jnp.dot(
        next_normed,
        lax.all_gather(kv_weight, "expert", axis=0, tiled=True),
        preferred_element_type=jnp.float32,
    )
    head_size = q_gain.shape[0]
    queries = (
        normalize(query_raw.reshape(group_rows, -1, head_size), q_gain)
        .reshape(group_rows, query_cols)
        .astype(jnp.bfloat16)
    )
    heads_here = kv_cols // head_size
    head_number = tensor_index * heads_here + jnp.arange(heads_here, dtype=jnp.int32)
    is_key = head_number < KV_HEADS
    kv_shaped = kv_raw.reshape(group_rows, heads_here, head_size)
    keys_values = (
        jnp.where(is_key[None, :, None], normalize(kv_shaped, k_gain), kv_shaped)
        .reshape(group_rows, kv_cols)
        .astype(jnp.bfloat16)
    )
    return (next_residual, queries, keys_values)


def solution(mesh):
    small = mesh.shape["tensor"] == 2 and mesh.shape["expert"] == 4 * PLANE
    return jax.shard_map(
        per_device_dense if small else per_device,
        mesh=mesh,
        in_specs=(
            P("expert", "tensor"),
            P("tensor", None),
            P(("expert", "tensor"), None),
            P(),
            P("expert", None),
            P("expert", None),
            P("expert", None, "tensor"),
            P("expert", None, "tensor"),
            P("expert", "tensor", None),
            P(),
            P("expert", "tensor"),
            P("expert", "tensor"),
            P(),
            P(),
        ),
        out_specs=(P(("expert", "tensor"), None), P("expert", "tensor"), P("expert", "tensor")),
        check_vma=False,
    )
```

```python
import functools

import jax
import jax.numpy as jnp
from jax import lax
from jax.experimental import pallas as pl
from jax.experimental.pallas import tpu as pltpu
from jax.sharding import PartitionSpec as P

KV_HEADS = 4
TOP = 8
PLANE = 4
META = 128


EPSILON = 1e-06

VMEM = pl.BlockSpec(memory_space=pltpu.VMEM)
HBM = pl.BlockSpec(memory_space=pltpu.HBM)


def normalize(values, gain):
    return values * lax.rsqrt(jnp.mean(values * values, axis=-1, keepdims=True) + EPSILON) * gain


def params(mebibytes):
    return pltpu.CompilerParams(vmem_limit_bytes=mebibytes << 20)


def lanes(start, size):
    return pl.ds(pl.multiple_of(start, size), size)


def out_projection_kernel(
    chunk, start, side_count, a_hbm, w_hbm, *refs
):
    side_refs, (mine_ref, theirs_ref) = refs[:side_count], refs[side_count : side_count + 2]
    joined = refs[side_count + 2 : -5]
    a_buf, w_buf, a_sem, sems, side_sems = refs[-5:]
    width = w_buf.shape[1]
    count = width // chunk
    half = mine_ref.shape[0]
    a_copy = pltpu.make_async_copy(a_hbm, a_buf, a_sem)
    a_copy.start()
    copies = []
    for i in range(count):
        copies.append(
            pltpu.make_async_copy(
                w_hbm.at[:, pl.ds(start + i * chunk, chunk)],
                w_buf.at[:, pl.ds(i * chunk, chunk)],
                sems.at[i],
            )
        )
    for copy in copies:
        copy.start()
    side_copies, at = [], 0
    for i, ref in enumerate(side_refs):
        cols = ref.shape[1]
        side_copies.append(
            pltpu.make_async_copy(ref, joined[0].at[:, pl.ds(at, cols)], side_sems.at[i])
        )
        at += cols
    for copy in side_copies:
        copy.start()
    tensor = lax.axis_index("tensor")
    a_copy.wait()
    own = a_buf[lanes(tensor * half, half), :]
    other = a_buf[lanes((1 - tensor) * half, half), :]
    both = jnp.concatenate([own, other], axis=0)
    for i in range(count):
        copies[i].wait()
        cols = pl.ds(i * chunk, chunk)
        product = jnp.dot(both, w_buf[:, cols], preferred_element_type=jnp.float32)
        mine_ref[:, cols] = product[:half]
        theirs_ref[:, cols] = product[half:]
    for copy in side_copies:
        copy.wait()


def out_projection(attn_out, out_weight, start, width, side=()):
    rows, depth = attn_out.shape
    chunk = 256
    half = jax.ShapeDtypeStruct((rows // 2, width), jnp.float32)
    joined = ()
    if side:
        cols = sum(array.shape[1] for array in side)
        joined = (jax.ShapeDtypeStruct((side[0].shape[0], cols), side[0].dtype),)
    return pl.pallas_call(
        functools.partial(out_projection_kernel, chunk, start, len(side)),
        out_shape=(half, half) + joined,
        in_specs=[HBM, HBM] + [HBM] * len(side),
        out_specs=(VMEM, VMEM) + (HBM,) * len(joined),
        scratch_shapes=[
            pltpu.VMEM((rows, depth), jnp.bfloat16),
            pltpu.VMEM((depth, width), jnp.bfloat16),
            pltpu.SemaphoreType.DMA,
            pltpu.SemaphoreType.DMA((width // chunk,)),
            pltpu.SemaphoreType.DMA((2,)),
        ],
        compiler_params=params(60),
        cost_estimate=pl.CostEstimate(
            flops=2 * rows * depth * width, bytes_accessed=2 * depth * width, transcendentals=0
        ),
        name="out_projection",
    )(attn_out, out_weight, *side)


def first_norm_kernel(depth, count, *refs):
    mine, theirs = refs[:count], refs[count : 2 * count]
    residual_ref, gain_ref, meta_ref, tokens_ref = refs[2 * count : 2 * count + 4]
    slice_refs, first_ref = refs[2 * count + 4 : -1], refs[-1]
    rows, width = residual_ref.shape
    sub = width // (PLANE * depth)
    start = 0
    for mine_ref, theirs_ref in zip(mine, theirs):
        cols = slice(start, start + mine_ref.shape[1])
        start += mine_ref.shape[1]
        first_ref[:, cols] = (
            residual_ref[:, cols].astype(jnp.float32) + (mine_ref[...] + theirs_ref[...])
        ).astype(jnp.bfloat16)
    first = first_ref[...]
    tokens_ref[:, :width] = normalize(first.astype(jnp.float32), gain_ref[...]).astype(jnp.bfloat16)
    tokens_ref[:, width:] = meta_ref[...]
    plane = lax.axis_index("expert") % PLANE
    for d in range(PLANE):
        for z in range(depth):
            slice_refs[d][z * rows : (z + 1) * rows, :] = first_ref[
                :, lanes((z * PLANE + (plane ^ d)) * sub, sub)
            ]


def first_norm(mine, theirs, residual, gain, meta, depth):
    rows, width = residual.shape
    piece = jax.ShapeDtypeStruct((depth * rows, width // (PLANE * depth)), jnp.bfloat16)
    return pl.pallas_call(
        functools.partial(first_norm_kernel, depth, len(mine)),
        out_shape=(jax.ShapeDtypeStruct((rows, width + META), jnp.bfloat16),) + (piece,) * PLANE,
        in_specs=[VMEM] * (2 * len(mine) + 3),
        out_specs=(VMEM,) * (1 + PLANE),
        scratch_shapes=[pltpu.VMEM((rows, width), jnp.bfloat16)],
        compiler_params=params(2),
        name="first_norm",
    )(*mine, *theirs, residual, gain, meta)


def pack_kernel(depth, *refs):
    line, pieces, out_refs = refs[:depth], refs[depth : depth + PLANE - 1], refs[depth + PLANE - 1 :]
    rows, extended = line[0].shape
    for ref, piece in zip(out_refs, pieces):
        for z in range(depth):
            ref[z * rows : (z + 1) * rows, :extended] = line[z][...]
        ref[:, extended:] = piece[...]


def pack(line, pieces):
    depth = len(line)
    rows, extended = line[0].shape
    shape = jax.ShapeDtypeStruct((depth * rows, extended + pieces[0].shape[1]), jnp.bfloat16)
    return pl.pallas_call(
        functools.partial(pack_kernel, depth),
        out_shape=(shape,) * (PLANE - 1),
        in_specs=[VMEM] * (depth + PLANE - 1),
        out_specs=(VMEM,) * (PLANE - 1),
        compiler_params=params(2),
        name="pack_tokens",
    )(*line, *pieces)


def load_kernel(*refs):
    sources, targets, sems = refs[:3], refs[-4:-1], refs[-1]
    copies = [
        pltpu.make_async_copy(source, target, sems.at[i])
        for i, (source, target) in enumerate(zip(sources, targets))
    ]
    for copy in copies:
        copy.start()
    for copy in copies:
        copy.wait()


def load(weights, after):
    size = sum(w.size for w in weights)
    return pl.pallas_call(
        load_kernel,
        out_shape=tuple(jax.ShapeDtypeStruct(w.shape, w.dtype) for w in weights),
        in_specs=[HBM] * 3 + [pl.BlockSpec(memory_space=pl.ANY)] * len(after),
        out_specs=(VMEM,) * 3,
        scratch_shapes=[pltpu.SemaphoreType.DMA((3,))],
        compiler_params=params(46),
        cost_estimate=pl.CostEstimate(flops=0, bytes_accessed=4 * size, transcendentals=0),
        name="load_weights",
    )(*weights, *after)


def expert_kernel(depth, chunk, *refs):
    line, packed = refs[:depth], refs[depth : depth + PLANE - 1]
    at = depth + PLANE - 1
    own_gate, own_up, own_down, gate_hbm, up_hbm, down_hbm = refs[at : at + 6]
    out_refs = refs[at + 6 : at + 6 + PLANE]
    x_buf, gate_buf, up_buf, down_buf, act_buf, sems = refs[at + 6 + PLANE :]
    width, hidden = gate_buf.shape[1:]
    rows, extended = line[0].shape
    per = hidden // chunk
    gate_copies = []
    for i in range(per):
        cols = pl.ds(i * chunk, chunk)
        gate_copies.append(
            (
                pltpu.make_async_copy(
                    gate_hbm.at[:, :, cols], gate_buf.at[:, :, cols], sems.at[i]
                ),
                pltpu.make_async_copy(
                    up_hbm.at[:, :, cols], up_buf.at[:, :, cols], sems.at[per + i]
                ),
            )
        )
    down_copy = pltpu.make_async_copy(down_hbm, down_buf, sems.at[2 * per])
    for pair in gate_copies:
        pair[0].start()
        pair[1].start()
    down_copy.start()
    group = depth * rows
    for z in range(depth):
        x_buf[z * rows : (z + 1) * rows, :] = line[z][...]
    for d in range(1, PLANE):
        x_buf[d * group : (d + 1) * group, :] = packed[d - 1][:, :extended]
    meta = x_buf[:, width:].astype(jnp.float32)
    lane = lax.broadcasted_iota(jnp.int32, meta.shape, 1)
    chip = lax.axis_index("expert")
    tensor = lax.axis_index("tensor")
    for side in range(2):
        expert = 2 * chip + (tensor if side == 0 else 1 - tensor)
        chosen = (lane == expert) | (lane == expert + META // 2)
        route = jnp.sum(jnp.where(chosen, meta, 0.0), axis=1, keepdims=True)
        gate_ref, up_ref = (own_gate, own_up) if side == 0 else (gate_buf, up_buf)
        for i in range(per):
            if side == 1:
                gate_copies[i][0].wait()
                gate_copies[i][1].wait()
            cols = pl.ds(i * chunk, chunk)
            x = x_buf[:, :width]
            gate = jnp.dot(x, gate_ref[0, :, cols], preferred_element_type=jnp.float32)
            up = jnp.dot(x, up_ref[0, :, cols], preferred_element_type=jnp.float32)
            act = gate / (1.0 + jnp.exp(-gate)) * up * route
            start = side * hidden + i * chunk
            act_buf[:, start : start + chunk] = act.astype(jnp.bfloat16)
    down_copy.wait()
    sub = width // (PLANE * depth)
    plane = chip % PLANE
    for d in range(PLANE):
        out = 0.0
        for side, ref in enumerate((own_down, down_buf)):
            weight = jnp.concatenate(
                [ref[0, :, lanes((z * PLANE + (plane ^ d)) * sub, sub)] for z in range(depth)],
                axis=1,
            )
            out = out + jnp.dot(
                act_buf[:, side * hidden : (side + 1) * hidden],
                weight,
                preferred_element_type=jnp.float32,
            )
        for k in range(PLANE):
            out_refs[d][k * group : (k + 1) * group, :] = out[
                (d ^ k) * group : ((d ^ k) + 1) * group
            ].astype(jnp.bfloat16)


def experts(line, packed, own, other):
    depth = len(line)
    rows, extended = line[0].shape
    width, hidden = own[0].shape[1:]
    chunk = 256
    total = rows * depth * PLANE
    return pl.pallas_call(
        functools.partial(expert_kernel, depth, chunk),
        out_shape=(jax.ShapeDtypeStruct((total, width // PLANE), jnp.bfloat16),) * PLANE,
        in_specs=[VMEM] * (depth + PLANE + 2) + [HBM] * 3,
        out_specs=(VMEM,) * PLANE,
        scratch_shapes=[
            pltpu.VMEM((total, extended), jnp.bfloat16),
            pltpu.VMEM((1, width, hidden), jnp.bfloat16),
            pltpu.VMEM((1, width, hidden), jnp.bfloat16),
            pltpu.VMEM((1, hidden, width), jnp.bfloat16),
            pltpu.VMEM((total, 2 * hidden), jnp.bfloat16),
            pltpu.SemaphoreType.DMA((2 * (hidden // chunk) + 1,)),
        ],
        compiler_params=params(46),
        cost_estimate=pl.CostEstimate(
            flops=12 * total * width * hidden,
            bytes_accessed=12 * width * hidden,
            transcendentals=2 * total * hidden,
        ),
        name="experts",
    )(*line, *packed, *own, *other)


def plane_sum_kernel(depth, *refs):
    in_refs, out_refs = refs[:PLANE], refs[PLANE:]
    rows = in_refs[0].shape[0] // (PLANE * depth)
    for d in range(PLANE):
        for z in range(depth):
            start = (d * depth + z) * rows
            at = slice(start, start + rows)
            total = in_refs[0][at, :].astype(jnp.float32)
            for ref in in_refs[1:]:
                total = total + ref[at, :].astype(jnp.float32)
            out_refs[z][d * rows : (d + 1) * rows, :] = total.astype(jnp.bfloat16)


def plane_sum(parts, depth):
    rows, part = parts[0].shape
    return pl.pallas_call(
        functools.partial(plane_sum_kernel, depth),
        out_shape=(jax.ShapeDtypeStruct((rows // depth, part), jnp.bfloat16),) * depth,
        in_specs=[VMEM] * PLANE,
        out_specs=(VMEM,) * depth,
        compiler_params=params(4),
        name="plane_sum",
    )(*parts)


def second_norm_kernel(depth, *refs):
    parts, first_ref, packed = refs[:depth], refs[depth], refs[depth + 1 : depth + PLANE]
    gain_ref, scaled_ref, next_ref = refs[depth + PLANE :]
    rows = first_ref.shape[0] // depth
    sub = first_ref.shape[1]
    part = depth * sub
    lane = lax.broadcasted_iota(jnp.int32, (rows, META), 1)
    plane = lax.axis_index("expert") % PLANE
    gain = jnp.concatenate(
        [gain_ref[:, lanes((z * PLANE + plane) * sub, sub)] for z in range(depth)], axis=1
    )
    for d in range(PLANE):
        at = slice(d * rows, (d + 1) * rows)
        total = parts[0][at, :].astype(jnp.float32)
        for ref in parts[1:]:
            total = total + ref[at, :].astype(jnp.float32)
        source = first_ref if d == 0 else packed[d - 1]
        skip = source.shape[1] - sub
        first = jnp.concatenate(
            [source[z * rows : (z + 1) * rows, skip:] for z in range(depth)], axis=1
        )
        following = (first.astype(jnp.float32) + total).astype(jnp.bfloat16)
        next_ref[at, :] = following
        wide = following.astype(jnp.float32)
        scaled_ref[at, :part] = (wide * gain).astype(jnp.bfloat16)
        squares = jnp.sum(wide * wide, axis=1, keepdims=True)
        high = squares.astype(jnp.bfloat16).astype(jnp.float32)
        low = squares - high
        scaled_ref[at, part:] = jnp.where(
            lane == 0, high, jnp.where(lane == 1, low, 0.0)
        ).astype(jnp.bfloat16)


def second_norm(parts, first, packed, gain):
    depth = len(parts)
    rows, part = parts[0].shape
    return pl.pallas_call(
        functools.partial(second_norm_kernel, depth),
        out_shape=(
            jax.ShapeDtypeStruct((rows, part + META), jnp.bfloat16),
            jax.ShapeDtypeStruct((rows, part), jnp.bfloat16),
        ),
        in_specs=[VMEM] * (depth + PLANE + 1),
        out_specs=(VMEM, VMEM),
        compiler_params=params(4),
        name="second_norm",
    )(*parts, first, *packed, gain)


def projection_kernel(chunk, mine_ref, theirs_ref, next_ref, w_hbm, *refs):
    out_refs, (w_buf, sems) = refs[:PLANE], refs[PLANE:]
    cols = w_buf.shape[1]
    copies = []
    for i in range(cols // chunk):
        at = pl.ds(i * chunk, chunk)
        copies.append(pltpu.make_async_copy(w_hbm.at[:, at], w_buf.at[:, at], sems.at[i]))
    for copy in copies:
        copy.start()
    rows, extended = mine_ref.shape
    part = extended - META
    block = rows // PLANE
    tensor = lax.axis_index("tensor")
    own = lanes(tensor * block, block)
    other = lanes((1 - tensor) * block, block)
    for d in range(PLANE):
        at = slice(d * block, (d + 1) * block)
        out_refs[d][own, cols : cols + META] = mine_ref[at, part:]
        out_refs[d][other, cols : cols + META] = theirs_ref[at, part:]
        out_refs[d][:block, cols + META :] = next_ref[at, : part // 2]
        out_refs[d][block:, cols + META :] = next_ref[at, part // 2 :]
    both = jnp.concatenate([mine_ref[:, :part], theirs_ref[:, :part]], axis=0)
    for i in range(cols // chunk):
        copies[i].wait()
        at = slice(i * chunk, (i + 1) * chunk)
        product = jnp.dot(both, w_buf[:, at], preferred_element_type=jnp.float32).astype(
            jnp.bfloat16
        )
        for d in range(PLANE):
            out_refs[d][own, at] = product[d * block : (d + 1) * block]
            out_refs[d][other, at] = product[rows + d * block : rows + (d + 1) * block]


def projection(mine, theirs, following, weight):
    rows, part = following.shape
    cols = weight.shape[1]
    chunk = 512
    shape = jax.ShapeDtypeStruct((2 * rows // PLANE, cols + META + part // 2), jnp.bfloat16)
    return pl.pallas_call(
        functools.partial(projection_kernel, chunk),
        out_shape=(shape,) * PLANE,
        in_specs=[VMEM] * 3 + [HBM],
        out_specs=(VMEM,) * PLANE,
        scratch_shapes=[
            pltpu.VMEM((part, cols), jnp.bfloat16),
            pltpu.SemaphoreType.DMA((cols // chunk,)),
        ],
        compiler_params=params(58),
        cost_estimate=pl.CostEstimate(
            flops=4 * rows * part * cols, bytes_accessed=2 * part * cols, transcendentals=0
        ),
        name="qkv_projection",
    )(mine, theirs, following, weight)


def head_norm_kernel(depth, *refs):
    parts, q_gain_ref, k_gain_ref = refs[:PLANE], refs[PLANE], refs[PLANE + 1]
    next_ref, q_ref, kv_ref = refs[PLANE + 2 :]
    width = next_ref.shape[1]
    q_cols, kv_cols = q_ref.shape[1], kv_ref.shape[1]
    cols = q_cols + kv_cols
    head = q_gain_ref.shape[1]

    def total(at):
        value = parts[0][:, at].astype(jnp.float32)
        for ref in parts[1:]:
            value = value + ref[:, at].astype(jnp.float32)
        return value

    squares = jnp.sum(total(slice(cols, cols + META)), axis=1, keepdims=True)
    scale = lax.rsqrt(squares / width + EPSILON)
    for h in range(q_cols // head):
        at = slice(h * head, (h + 1) * head)
        q_ref[:, at] = normalize(total(at) * scale, q_gain_ref[...]).astype(jnp.bfloat16)
    tensor = lax.axis_index("tensor")
    for h in range(kv_cols // head):
        at = slice(h * head, (h + 1) * head)
        raw = total(slice(q_cols + h * head, q_cols + (h + 1) * head)) * scale
        is_key = tensor * (kv_cols // head) + h < KV_HEADS
        kv_ref[:, at] = jnp.where(is_key, normalize(raw, k_gain_ref[...]), raw).astype(
            jnp.bfloat16
        )
    plane = lax.axis_index("expert") % PLANE
    rows = next_ref.shape[0]
    sub = width // (PLANE * depth)
    for d in range(PLANE):
        for z in range(depth):
            top = z * sub * 2 // (depth * sub)
            start = cols + META + z * sub - top * (depth * sub // 2)
            next_ref[:, lanes((z * PLANE + (plane ^ d)) * sub, sub)] = parts[d][
                top * rows : (top + 1) * rows, start : start + sub
            ]


def head_norm(parts, q_gain, k_gain, q_cols, kv_cols, rows, width, depth):
    both = parts[0].shape[0]
    return pl.pallas_call(
        functools.partial(head_norm_kernel, depth),
        out_shape=(
            jax.ShapeDtypeStruct((rows, width), jnp.bfloat16),
            jax.ShapeDtypeStruct((both, q_cols), jnp.bfloat16),
            jax.ShapeDtypeStruct((both, kv_cols), jnp.bfloat16),
        ),
        in_specs=[VMEM] * (PLANE + 2),
        out_specs=(VMEM, VMEM, VMEM),
        compiler_params=params(4),
        name="head_norm",
    )(*parts, q_gain, k_gain)


def per_device_dense(
    attn_out,
    out_weight,
    residual,
    attn_gain,
    expert_ids,
    route_weights,
    w_gate,
    w_up,
    w_down,
    input_gain,
    q_weight,
    kv_weight,
    q_gain,
    k_gain,
):
    n_expert = lax.axis_size("expert")
    depth = n_expert // PLANE
    rows, width = residual.shape
    tensor_index = lax.axis_index("tensor").astype(jnp.int32)

    def to_core(value):
        return lax.ppermute(value, "tensor", [(0, 1), (1, 0)])

    def to_expert(value, offset):
        return lax.ppermute(value, "expert", [(i, i ^ offset) for i in range(n_expert)])

    def to_z(values):
        return [to_expert(v, d * PLANE) if d else v for d, v in enumerate(values)]

    def to_plane(values):
        return [to_expert(v, d) if d else v for d, v in enumerate(values)]

    own_ids = lax.dynamic_slice_in_dim(expert_ids, tensor_index * rows, rows, 0)
    own_route = lax.dynamic_slice_in_dim(route_weights, tensor_index * rows, rows, 0)
    chosen = own_ids[:, :, None] == jnp.arange(META // 2, dtype=jnp.int32)[None, None, :]
    dense = jnp.sum(jnp.where(chosen, own_route[:, :, None], 0.0), axis=1)
    high = lax.reduce_precision(dense, 8, 7)
    meta = jnp.concatenate([high, dense - high], axis=1).astype(jnp.bfloat16)

    first_cols = width // 4
    mine_a, theirs_a, qkv_rows = out_projection(
        attn_out, out_weight, 0, first_cols, (q_weight, kv_weight)
    )
    lines = [list(range(i, n_expert, PLANE)) for i in range(PLANE)]
    qkv = lax.all_gather(qkv_rows, "expert", axis=0, tiled=True, axis_index_groups=lines)
    mine_b, theirs_b = out_projection(attn_out, out_weight, first_cols, width - first_cols)
    theirs = (to_core(theirs_a), to_core(theirs_b))
    tokens, *firsts = first_norm(
        (mine_a, mine_b), theirs, residual, attn_gain[None, :], meta, depth
    )
    own = (w_gate, w_up, w_down)
    other = [to_core(w) for w in lax.optimization_barrier((*own, tokens))[:3]]
    line = to_z([tokens] * depth)
    sent = pack(line, firsts[1:])
    packed = to_plane([None, *sent])[1:]
    own = load(own, sent)
    parts = plane_sum(to_plane(experts(line, packed, own, other)), depth)
    scaled, following = second_norm(to_z(parts), firsts[0], packed, input_gain[None, :])
    products = to_plane(projection(scaled, to_core(scaled), following, qkv))
    return head_norm(
        products,
        q_gain[None, :],
        k_gain[None, :],
        q_weight.shape[1],
        kv_weight.shape[1],
        rows,
        width,
        depth,
    )


def per_device(
    attn_out,
    out_weight,
    residual,
    attn_gain,
    expert_ids,
    route_weights,
    w_gate,
    w_up,
    w_down,
    input_gain,
    q_weight,
    kv_weight,
    q_gain,
    k_gain,
):
    n_expert = lax.axis_size("expert")
    n_tensor = lax.axis_size("tensor")
    share = n_tensor // 2
    tensor_index = lax.axis_index("tensor")
    group_rows = attn_out.shape[0]
    width = residual.shape[1]
    half = tensor_index // share
    capacity = 3 * group_rows * TOP // (4 * n_expert)
    all_experts = 2 * n_expert
    attn_rows = lax.psum_scatter(
        jnp.dot(attn_out, out_weight, preferred_element_type=jnp.float32),
        "tensor",
        scatter_dimension=0,
        tiled=True,
    )
    first_residual = (residual.astype(jnp.float32) + attn_rows).astype(jnp.bfloat16)
    normed = normalize(first_residual.astype(jnp.float32), attn_gain).astype(jnp.bfloat16)
    group_normed = lax.all_gather(normed, "tensor", axis=0, tiled=True)
    flat_ids = expert_ids.reshape(-1)
    onehot = (flat_ids[:, None] == jnp.arange(all_experts, dtype=jnp.int32)[None, :]).astype(
        jnp.int32
    )
    earlier = jnp.cumsum(onehot, axis=0) - onehot
    rank = jnp.sum(earlier * onehot, axis=1)
    dest = flat_ids * capacity + rank
    row_owner = jnp.arange(flat_ids.shape[0], dtype=jnp.int32) // TOP
    slot_row = jnp.full((all_experts * capacity,), group_rows, jnp.int32).at[dest].set(row_owner)
    slot_weight = (
        jnp.zeros((all_experts * capacity,), jnp.float32).at[dest].set(route_weights.reshape(-1))
    )
    own_slots = lax.dynamic_index_in_dim(
        slot_row.reshape(n_expert, 2, capacity), half, 1, keepdims=False
    )
    own_weights = lax.dynamic_index_in_dim(
        slot_weight.reshape(n_expert, 2, capacity), half, 1, keepdims=False
    )
    padded_rows = jnp.concatenate([group_normed, jnp.zeros((1, width), jnp.bfloat16)], axis=0)
    gate_w = w_gate[0]
    up_w = w_up[0]
    down_w = w_down[0]
    outgoing = jnp.take(padded_rows, own_slots, axis=0)
    arrived = lax.all_to_all(outgoing, "expert", split_axis=0, concat_axis=0, tiled=True)
    flat = arrived.reshape(-1, width)
    gate = jnp.dot(flat, gate_w, preferred_element_type=jnp.float32)
    up = jnp.dot(flat, up_w, preferred_element_type=jnp.float32)
    act = (jax.nn.silu(gate) * up).astype(jnp.bfloat16)
    part = jnp.dot(act, down_w, preferred_element_type=jnp.float32).astype(jnp.bfloat16)
    send_part = part.reshape(arrived.shape)
    returned = lax.all_to_all(send_part, "expert", split_axis=0, concat_axis=0, tiled=True)
    weighted = own_weights.reshape(-1)[:, None] * returned.reshape(-1, width).astype(jnp.float32)
    term = (
        jnp.zeros((group_rows + 1, width), jnp.float32)
        .at[own_slots.reshape(-1)]
        .add(weighted)[:group_rows]
    )
    expert_sum = lax.psum_scatter(
        term.astype(jnp.bfloat16), "tensor", scatter_dimension=0, tiled=True
    ).astype(jnp.float32)
    next_residual = (first_residual.astype(jnp.float32) + expert_sum).astype(jnp.bfloat16)
    own_normed = normalize(next_residual.astype(jnp.float32), input_gain).astype(jnp.bfloat16)
    next_normed = lax.all_gather(own_normed, "tensor", axis=0, tiled=True)
    query_cols = q_weight.shape[1]
    kv_cols = kv_weight.shape[1]
    query_raw = jnp.dot(
        next_normed,
        lax.all_gather(q_weight, "expert", axis=0, tiled=True),
        preferred_element_type=jnp.float32,
    )
    kv_raw = jnp.dot(
        next_normed,
        lax.all_gather(kv_weight, "expert", axis=0, tiled=True),
        preferred_element_type=jnp.float32,
    )
    head_size = q_gain.shape[0]
    queries = (
        normalize(query_raw.reshape(group_rows, -1, head_size), q_gain)
        .reshape(group_rows, query_cols)
        .astype(jnp.bfloat16)
    )
    heads_here = kv_cols // head_size
    head_number = tensor_index * heads_here + jnp.arange(heads_here, dtype=jnp.int32)
    is_key = head_number < KV_HEADS
    kv_shaped = kv_raw.reshape(group_rows, heads_here, head_size)
    keys_values = (
        jnp.where(is_key[None, :, None], normalize(kv_shaped, k_gain), kv_shaped)
        .reshape(group_rows, kv_cols)
        .astype(jnp.bfloat16)
    )
    return (next_residual, queries, keys_values)


def solution(mesh):
    small = mesh.shape["tensor"] == 2 and mesh.shape["expert"] == 4 * PLANE
    return jax.shard_map(
        per_device_dense if small else per_device,
        mesh=mesh,
        in_specs=(
            P("expert", "tensor"),
            P("tensor", None),
            P(("expert", "tensor"), None),
            P(),
            P("expert", None),
            P("expert", None),
            P("expert", None, "tensor"),
            P("expert", None, "tensor"),
            P("expert", "tensor", None),
            P(),
            P("expert", "tensor"),
            P("expert", "tensor"),
            P(),
            P(),
        ),
        out_specs=(P(("expert", "tensor"), None), P("expert", "tensor"), P("expert", "tensor")),
        check_vma=False,
    )
```

```python
import functools

import jax
import jax.numpy as jnp
from jax import lax
from jax.experimental import pallas as pl
from jax.experimental.pallas import tpu as pltpu
from jax.sharding import PartitionSpec as P

KV_HEADS = 4
TOP = 8
PLANE = 4
META = 128


EPSILON = 1e-06

SMALL = pl.CostEstimate(flops=0, bytes_accessed=0, transcendentals=0)
VMEM = pl.BlockSpec(memory_space=pltpu.VMEM)
HBM = pl.BlockSpec(memory_space=pltpu.HBM)


def normalize(values, gain):
    return values * lax.rsqrt(jnp.mean(values * values, axis=-1, keepdims=True) + EPSILON) * gain


def params(mebibytes):
    return pltpu.CompilerParams(vmem_limit_bytes=mebibytes << 20)


def lanes(start, size):
    return pl.ds(pl.multiple_of(start, size), size)


def in_hbm(value):
    return pltpu.with_memory_space_constraint(value, pltpu.HBM)


def in_vmem(value):
    return pltpu.with_memory_space_constraint(value, pltpu.VMEM)


def out_projection_kernel(chunk, a_hbm, w_hbm, mine_ref, theirs_ref, a_buf, w_buf, a_sem, sems):
    depth = w_buf.shape[0]
    count = depth // chunk
    half = mine_ref.shape[0]
    a_copy = pltpu.make_async_copy(a_hbm, a_buf, a_sem)
    a_copy.start()
    copies = []
    for i in range(count):
        rows = pl.ds(i * chunk, chunk)
        copies.append(pltpu.make_async_copy(w_hbm.at[rows], w_buf.at[rows], sems.at[i]))
    for copy in copies:
        copy.start()
    tensor = lax.axis_index("tensor")
    own = lanes(tensor * half, half)
    other = lanes((1 - tensor) * half, half)
    a_copy.wait()
    for i in range(count):
        copies[i].wait()
        at = pl.ds(i * chunk, chunk)
        both = jnp.concatenate([a_buf[own, at], a_buf[other, at]], axis=0)
        product = jnp.dot(both, w_buf[at, :], preferred_element_type=jnp.float32)
        if i == 0:
            mine_ref[...] = product[:half]
            theirs_ref[...] = product[half:]
        else:
            mine_ref[...] += product[:half]
            theirs_ref[...] += product[half:]


def out_projection(attn_out, out_weight):
    rows, depth = attn_out.shape
    width = out_weight.shape[1]
    chunk = 256
    half = pltpu.VMEM((rows // 2, width), jnp.float32)
    return pl.pallas_call(
        functools.partial(out_projection_kernel, chunk),
        out_shape=(half, half),
        in_specs=[HBM, HBM],
        out_specs=(VMEM, VMEM),
        scratch_shapes=[
            pltpu.VMEM((rows, depth), jnp.bfloat16),
            pltpu.VMEM((depth, width), jnp.bfloat16),
            pltpu.SemaphoreType.DMA,
            pltpu.SemaphoreType.DMA((depth // chunk,)),
        ],
        compiler_params=params(14),
        cost_estimate=SMALL,
        name="out_projection",
    )(in_hbm(attn_out), in_hbm(out_weight))


def first_norm_kernel(depth, count, *refs):
    mine, theirs = refs[:count], refs[count : 2 * count]
    residual_ref, gain_ref, meta_ref, tokens_ref = refs[2 * count : 2 * count + 4]
    slice_refs, first_ref = refs[2 * count + 4 : -1], refs[-1]
    rows, width = residual_ref.shape
    sub = width // (PLANE * depth)
    start = 0
    for mine_ref, theirs_ref in zip(mine, theirs):
        cols = slice(start, start + mine_ref.shape[1])
        start += mine_ref.shape[1]
        first_ref[:, cols] = (
            residual_ref[:, cols].astype(jnp.float32) + (mine_ref[...] + theirs_ref[...])
        ).astype(jnp.bfloat16)
    first = first_ref[...]
    tokens_ref[:, :width] = normalize(first.astype(jnp.float32), gain_ref[...]).astype(jnp.bfloat16)
    tokens_ref[:, width:] = meta_ref[...]
    plane = lax.axis_index("expert") % PLANE
    for d in range(PLANE):
        for z in range(depth):
            slice_refs[d][z * rows : (z + 1) * rows, :] = first_ref[
                :, lanes((z * PLANE + (plane ^ d)) * sub, sub)
            ]


def first_norm(mine, theirs, residual, gain, meta, depth):
    rows, width = residual.shape
    piece = jax.ShapeDtypeStruct((depth * rows, width // (PLANE * depth)), jnp.bfloat16)
    return pl.pallas_call(
        functools.partial(first_norm_kernel, depth, len(mine)),
        out_shape=(jax.ShapeDtypeStruct((rows, width + META), jnp.bfloat16),) + (piece,) * PLANE,
        in_specs=[VMEM] * (2 * len(mine) + 3),
        out_specs=(VMEM,) * (1 + PLANE),
        scratch_shapes=[pltpu.VMEM((rows, width), jnp.bfloat16)],
        compiler_params=params(2),
        name="first_norm",
    )(*mine, *theirs, residual, gain, meta)


def pack_kernel(depth, *refs):
    line, pieces, out_refs = refs[:depth], refs[depth : depth + PLANE - 1], refs[depth + PLANE - 1 :]
    rows, extended = line[0].shape
    for ref, piece in zip(out_refs, pieces):
        for z in range(depth):
            ref[z * rows : (z + 1) * rows, :extended] = line[z][...]
        ref[:, extended:] = piece[...]


def pack(line, pieces):
    depth = len(line)
    rows, extended = line[0].shape
    shape = jax.ShapeDtypeStruct((depth * rows, extended + pieces[0].shape[1]), jnp.bfloat16)
    return pl.pallas_call(
        functools.partial(pack_kernel, depth),
        out_shape=(shape,) * (PLANE - 1),
        in_specs=[VMEM] * (depth + PLANE - 1),
        out_specs=(VMEM,) * (PLANE - 1),
        compiler_params=params(2),
        name="pack_tokens",
    )(*line, *pieces)


def load_kernel(*refs):
    sources, targets, sems = refs[:3], refs[-4:-1], refs[-1]
    copies = [
        pltpu.make_async_copy(source, target, sems.at[i])
        for i, (source, target) in enumerate(zip(sources, targets))
    ]
    for copy in copies:
        copy.start()
    for copy in copies:
        copy.wait()


def load(weights, after):
    size = sum(w.size for w in weights)
    return pl.pallas_call(
        load_kernel,
        out_shape=tuple(pltpu.VMEM(w.shape, w.dtype) for w in weights),
        in_specs=[HBM] * 3 + [pl.BlockSpec(memory_space=pl.ANY)] * len(after),
        out_specs=(VMEM,) * 3,
        scratch_shapes=[pltpu.SemaphoreType.DMA((3,))],
        compiler_params=params(2),
        cost_estimate=SMALL,
        name="load_weights",
    )(*map(in_hbm, weights), *after)


def expert_kernel(depth, chunk, *refs):
    line, packed = refs[:depth], refs[depth : depth + PLANE - 1]
    at = depth + PLANE - 1
    sides = (refs[at : at + 3], refs[at + 3 : at + 6])
    out_refs = refs[at + 6 : at + 6 + PLANE]
    x_buf, act_buf = refs[at + 6 + PLANE :]
    width, hidden = sides[0][0].shape[1:]
    rows, extended = line[0].shape
    group = depth * rows
    for z in range(depth):
        x_buf[z * rows : (z + 1) * rows, :] = line[z][...]
    for d in range(1, PLANE):
        x_buf[d * group : (d + 1) * group, :] = packed[d - 1][:, :extended]
    meta = x_buf[:, width:].astype(jnp.float32)
    lane = lax.broadcasted_iota(jnp.int32, meta.shape, 1)
    chip = lax.axis_index("expert")
    tensor = lax.axis_index("tensor")
    for side, (gate_ref, up_ref, _) in enumerate(sides):
        expert = 2 * chip + (tensor if side == 0 else 1 - tensor)
        chosen = (lane == expert) | (lane == expert + META // 2)
        route = jnp.sum(jnp.where(chosen, meta, 0.0), axis=1, keepdims=True)
        for i in range(hidden // chunk):
            cols = pl.ds(i * chunk, chunk)
            x = x_buf[:, :width]
            gate = jnp.dot(x, gate_ref[0, :, cols], preferred_element_type=jnp.float32)
            up = jnp.dot(x, up_ref[0, :, cols], preferred_element_type=jnp.float32)
            act = gate / (1.0 + jnp.exp(-gate)) * up * route
            start = side * hidden + i * chunk
            act_buf[:, start : start + chunk] = act.astype(jnp.bfloat16)
    sub = width // (PLANE * depth)
    plane = chip % PLANE
    for d in range(PLANE):
        out = 0.0
        for side in range(2):
            down_ref = sides[side][2]
            weight = jnp.concatenate(
                [
                    down_ref[0, :, lanes((z * PLANE + (plane ^ d)) * sub, sub)]
                    for z in range(depth)
                ],
                axis=1,
            )
            out = out + jnp.dot(
                act_buf[:, side * hidden : (side + 1) * hidden],
                weight,
                preferred_element_type=jnp.float32,
            )
        for k in range(PLANE):
            out_refs[d][k * group : (k + 1) * group, :] = out[
                (d ^ k) * group : ((d ^ k) + 1) * group
            ].astype(jnp.bfloat16)


def experts(line, packed, own, other):
    depth = len(line)
    rows, extended = line[0].shape
    width, hidden = own[0].shape[1:]
    chunk = 256
    total = rows * depth * PLANE
    return pl.pallas_call(
        functools.partial(expert_kernel, depth, chunk),
        out_shape=(pltpu.VMEM((total, width // PLANE), jnp.bfloat16),) * PLANE,
        in_specs=[VMEM] * (depth + PLANE + 5),
        out_specs=(VMEM,) * PLANE,
        scratch_shapes=[
            pltpu.VMEM((total, extended), jnp.bfloat16),
            pltpu.VMEM((total, 2 * hidden), jnp.bfloat16),
        ],
        compiler_params=params(16),
        cost_estimate=SMALL,
        name="experts",
    )(*line, *packed, *own, *map(in_vmem, other))


def plane_sum_kernel(depth, *refs):
    in_refs, out_refs = refs[:PLANE], refs[PLANE:]
    rows = in_refs[0].shape[0] // (PLANE * depth)
    for d in range(PLANE):
        for z in range(depth):
            start = (d * depth + z) * rows
            at = slice(start, start + rows)
            total = in_refs[0][at, :].astype(jnp.float32)
            for ref in in_refs[1:]:
                total = total + ref[at, :].astype(jnp.float32)
            out_refs[z][d * rows : (d + 1) * rows, :] = total.astype(jnp.bfloat16)


def plane_sum(parts, depth):
    rows, part = parts[0].shape
    return pl.pallas_call(
        functools.partial(plane_sum_kernel, depth),
        out_shape=(jax.ShapeDtypeStruct((rows // depth, part), jnp.bfloat16),) * depth,
        in_specs=[VMEM] * PLANE,
        out_specs=(VMEM,) * depth,
        compiler_params=params(4),
        name="plane_sum",
    )(*parts)


def second_norm_kernel(depth, *refs):
    parts, first_ref, packed = refs[:depth], refs[depth], refs[depth + 1 : depth + PLANE]
    gain_ref, scaled_ref, next_ref = refs[depth + PLANE :]
    rows = first_ref.shape[0] // depth
    sub = first_ref.shape[1]
    part = depth * sub
    lane = lax.broadcasted_iota(jnp.int32, (rows, META), 1)
    plane = lax.axis_index("expert") % PLANE
    gain = jnp.concatenate(
        [gain_ref[:, lanes((z * PLANE + plane) * sub, sub)] for z in range(depth)], axis=1
    )
    for d in range(PLANE):
        at = slice(d * rows, (d + 1) * rows)
        total = parts[0][at, :].astype(jnp.float32)
        for ref in parts[1:]:
            total = total + ref[at, :].astype(jnp.float32)
        source = first_ref if d == 0 else packed[d - 1]
        skip = source.shape[1] - sub
        first = jnp.concatenate(
            [source[z * rows : (z + 1) * rows, skip:] for z in range(depth)], axis=1
        )
        following = (first.astype(jnp.float32) + total).astype(jnp.bfloat16)
        next_ref[at, :] = following
        wide = following.astype(jnp.float32)
        scaled_ref[at, :part] = (wide * gain).astype(jnp.bfloat16)
        squares = jnp.sum(wide * wide, axis=1, keepdims=True)
        high = squares.astype(jnp.bfloat16).astype(jnp.float32)
        low = squares - high
        scaled_ref[at, part:] = jnp.where(
            lane == 0, high, jnp.where(lane == 1, low, 0.0)
        ).astype(jnp.bfloat16)


def second_norm(parts, first, packed, gain):
    depth = len(parts)
    rows, part = parts[0].shape
    return pl.pallas_call(
        functools.partial(second_norm_kernel, depth),
        out_shape=(
            jax.ShapeDtypeStruct((rows, part + META), jnp.bfloat16),
            jax.ShapeDtypeStruct((rows, part), jnp.bfloat16),
        ),
        in_specs=[VMEM] * (depth + PLANE + 1),
        out_specs=(VMEM, VMEM),
        compiler_params=params(4),
        name="second_norm",
    )(*parts, first, *packed, gain)


def projection_kernel(chunk, mine_ref, theirs_ref, next_ref, w_hbm, *refs):
    out_refs, (w_buf, sems) = refs[:PLANE], refs[PLANE:]
    cols = w_buf.shape[1]
    copies = []
    for i in range(sems.shape[0]):
        at = lanes(i * META, META)
        copies.append(pltpu.make_async_copy(w_hbm.at[at], w_buf.at[at], sems.at[i]))
    for copy in copies:
        copy.start()
    rows, extended = mine_ref.shape
    part = extended - META
    block = rows // PLANE
    tensor = lax.axis_index("tensor")
    own = lanes(tensor * block, block)
    other = lanes((1 - tensor) * block, block)
    for d in range(PLANE):
        at = slice(d * block, (d + 1) * block)
        out_refs[d][own, cols : cols + META] = mine_ref[at, part:]
        out_refs[d][other, cols : cols + META] = theirs_ref[at, part:]
        out_refs[d][:block, cols + META :] = next_ref[at, : part // 2]
        out_refs[d][block:, cols + META :] = next_ref[at, part // 2 :]
    both = jnp.concatenate([mine_ref[:, :part], theirs_ref[:, :part]], axis=0)
    for copy in copies:
        copy.wait()
    for i in range(cols // chunk):
        at = slice(i * chunk, (i + 1) * chunk)
        product = jnp.dot(both, w_buf[:, at], preferred_element_type=jnp.float32).astype(
            jnp.bfloat16
        )
        for d in range(PLANE):
            out_refs[d][own, at] = product[d * block : (d + 1) * block]
            out_refs[d][other, at] = product[rows + d * block : rows + (d + 1) * block]


def projection(mine, theirs, following, weight):
    rows, part = following.shape
    cols = weight.shape[1]
    chunk = 512
    shape = pltpu.VMEM((2 * rows // PLANE, cols + META + part // 2), jnp.bfloat16)
    return pl.pallas_call(
        functools.partial(projection_kernel, chunk),
        out_shape=(shape,) * PLANE,
        in_specs=[VMEM] * 3 + [HBM],
        out_specs=(VMEM,) * PLANE,
        scratch_shapes=[
            pltpu.VMEM((part, cols), jnp.bfloat16),
            pltpu.SemaphoreType.DMA((part // META,)),
        ],
        compiler_params=params(8),
        cost_estimate=SMALL,
        name="qkv_projection",
    )(mine, theirs, following, in_hbm(weight))


def head_norm_kernel(depth, *refs):
    parts, q_gain_ref, k_gain_ref = refs[:PLANE], refs[PLANE], refs[PLANE + 1]
    next_ref, q_ref, kv_ref = refs[PLANE + 2 :]
    width = next_ref.shape[1]
    q_cols, kv_cols = q_ref.shape[1], kv_ref.shape[1]
    cols = q_cols + kv_cols
    head = q_gain_ref.shape[1]

    def total(at):
        value = parts[0][:, at].astype(jnp.float32)
        for ref in parts[1:]:
            value = value + ref[:, at].astype(jnp.float32)
        return value

    squares = jnp.sum(total(slice(cols, cols + META)), axis=1, keepdims=True)
    scale = lax.rsqrt(squares / width + EPSILON)
    for h in range(q_cols // head):
        at = slice(h * head, (h + 1) * head)
        q_ref[:, at] = normalize(total(at) * scale, q_gain_ref[...]).astype(jnp.bfloat16)
    tensor = lax.axis_index("tensor")
    for h in range(kv_cols // head):
        at = slice(h * head, (h + 1) * head)
        raw = total(slice(q_cols + h * head, q_cols + (h + 1) * head)) * scale
        is_key = tensor * (kv_cols // head) + h < KV_HEADS
        kv_ref[:, at] = jnp.where(is_key, normalize(raw, k_gain_ref[...]), raw).astype(
            jnp.bfloat16
        )
    plane = lax.axis_index("expert") % PLANE
    rows = next_ref.shape[0]
    sub = width // (PLANE * depth)
    for d in range(PLANE):
        for z in range(depth):
            top = z * sub * 2 // (depth * sub)
            start = cols + META + z * sub - top * (depth * sub // 2)
            next_ref[:, lanes((z * PLANE + (plane ^ d)) * sub, sub)] = parts[d][
                top * rows : (top + 1) * rows, start : start + sub
            ]


def head_norm(parts, q_gain, k_gain, q_cols, kv_cols, rows, width, depth):
    both = parts[0].shape[0]
    return pl.pallas_call(
        functools.partial(head_norm_kernel, depth),
        out_shape=(
            jax.ShapeDtypeStruct((rows, width), jnp.bfloat16),
            jax.ShapeDtypeStruct((both, q_cols), jnp.bfloat16),
            jax.ShapeDtypeStruct((both, kv_cols), jnp.bfloat16),
        ),
        in_specs=[VMEM] * (PLANE + 2),
        out_specs=(VMEM, VMEM, VMEM),
        compiler_params=params(4),
        name="head_norm",
    )(*parts, q_gain, k_gain)


def per_device_dense(
    attn_out,
    out_weight,
    residual,
    attn_gain,
    expert_ids,
    route_weights,
    w_gate,
    w_up,
    w_down,
    input_gain,
    q_weight,
    kv_weight,
    q_gain,
    k_gain,
):
    n_expert = lax.axis_size("expert")
    depth = n_expert // PLANE
    rows, width = residual.shape
    tensor_index = lax.axis_index("tensor").astype(jnp.int32)

    def to_core(value):
        return lax.ppermute(value, "tensor", [(0, 1), (1, 0)])

    def to_expert(value, offset):
        return lax.ppermute(value, "expert", [(i, i ^ offset) for i in range(n_expert)])

    def to_z(values):
        return [to_expert(v, d * PLANE) if d else v for d, v in enumerate(values)]

    def to_plane(values):
        return [to_expert(v, d) if d else v for d, v in enumerate(values)]

    own_ids = lax.dynamic_slice_in_dim(expert_ids, tensor_index * rows, rows, 0)
    own_route = lax.dynamic_slice_in_dim(route_weights, tensor_index * rows, rows, 0)
    chosen = own_ids[:, :, None] == jnp.arange(META // 2, dtype=jnp.int32)[None, None, :]
    dense = jnp.sum(jnp.where(chosen, own_route[:, :, None], 0.0), axis=1)
    high = lax.reduce_precision(dense, 8, 7)
    meta = jnp.concatenate([high, dense - high], axis=1).astype(jnp.bfloat16)

    lines = [list(range(i, n_expert, PLANE)) for i in range(PLANE)]
    qkv = lax.all_gather(
        jnp.concatenate([q_weight, kv_weight], axis=1),
        "expert",
        axis=0,
        tiled=True,
        axis_index_groups=lines,
    )
    other = [to_core(w_gate), to_core(w_up), to_core(w_down)]
    mine, theirs = out_projection(attn_out, out_weight)
    tokens, *firsts = first_norm(
        (mine,), (to_core(theirs),), residual, attn_gain[None, :], meta, depth
    )
    line = to_z([tokens] * depth)
    sent = pack(line, firsts[1:])
    packed = to_plane([None, *sent])[1:]
    own = load((w_gate, w_up, w_down), sent)
    parts = plane_sum(to_plane(experts(line, packed, own, other)), depth)
    scaled, following = second_norm(to_z(parts), firsts[0], packed, input_gain[None, :])
    products = to_plane(projection(scaled, to_core(scaled), following, qkv))
    return head_norm(
        products,
        q_gain[None, :],
        k_gain[None, :],
        q_weight.shape[1],
        kv_weight.shape[1],
        rows,
        width,
        depth,
    )


def per_device(
    attn_out,
    out_weight,
    residual,
    attn_gain,
    expert_ids,
    route_weights,
    w_gate,
    w_up,
    w_down,
    input_gain,
    q_weight,
    kv_weight,
    q_gain,
    k_gain,
):
    n_expert = lax.axis_size("expert")
    n_tensor = lax.axis_size("tensor")
    share = n_tensor // 2
    tensor_index = lax.axis_index("tensor")
    group_rows = attn_out.shape[0]
    width = residual.shape[1]
    half = tensor_index // share
    capacity = 3 * group_rows * TOP // (4 * n_expert)
    all_experts = 2 * n_expert
    attn_rows = lax.psum_scatter(
        jnp.dot(attn_out, out_weight, preferred_element_type=jnp.float32),
        "tensor",
        scatter_dimension=0,
        tiled=True,
    )
    first_residual = (residual.astype(jnp.float32) + attn_rows).astype(jnp.bfloat16)
    normed = normalize(first_residual.astype(jnp.float32), attn_gain).astype(jnp.bfloat16)
    group_normed = lax.all_gather(normed, "tensor", axis=0, tiled=True)
    flat_ids = expert_ids.reshape(-1)
    onehot = (flat_ids[:, None] == jnp.arange(all_experts, dtype=jnp.int32)[None, :]).astype(
        jnp.int32
    )
    earlier = jnp.cumsum(onehot, axis=0) - onehot
    rank = jnp.sum(earlier * onehot, axis=1)
    dest = flat_ids * capacity + rank
    row_owner = jnp.arange(flat_ids.shape[0], dtype=jnp.int32) // TOP
    slot_row = jnp.full((all_experts * capacity,), group_rows, jnp.int32).at[dest].set(row_owner)
    slot_weight = (
        jnp.zeros((all_experts * capacity,), jnp.float32).at[dest].set(route_weights.reshape(-1))
    )
    own_slots = lax.dynamic_index_in_dim(
        slot_row.reshape(n_expert, 2, capacity), half, 1, keepdims=False
    )
    own_weights = lax.dynamic_index_in_dim(
        slot_weight.reshape(n_expert, 2, capacity), half, 1, keepdims=False
    )
    padded_rows = jnp.concatenate([group_normed, jnp.zeros((1, width), jnp.bfloat16)], axis=0)
    gate_w = w_gate[0]
    up_w = w_up[0]
    down_w = w_down[0]
    outgoing = jnp.take(padded_rows, own_slots, axis=0)
    arrived = lax.all_to_all(outgoing, "expert", split_axis=0, concat_axis=0, tiled=True)
    flat = arrived.reshape(-1, width)
    gate = jnp.dot(flat, gate_w, preferred_element_type=jnp.float32)
    up = jnp.dot(flat, up_w, preferred_element_type=jnp.float32)
    act = (jax.nn.silu(gate) * up).astype(jnp.bfloat16)
    part = jnp.dot(act, down_w, preferred_element_type=jnp.float32).astype(jnp.bfloat16)
    send_part = part.reshape(arrived.shape)
    returned = lax.all_to_all(send_part, "expert", split_axis=0, concat_axis=0, tiled=True)
    weighted = own_weights.reshape(-1)[:, None] * returned.reshape(-1, width).astype(jnp.float32)
    term = (
        jnp.zeros((group_rows + 1, width), jnp.float32)
        .at[own_slots.reshape(-1)]
        .add(weighted)[:group_rows]
    )
    expert_sum = lax.psum_scatter(
        term.astype(jnp.bfloat16), "tensor", scatter_dimension=0, tiled=True
    ).astype(jnp.float32)
    next_residual = (first_residual.astype(jnp.float32) + expert_sum).astype(jnp.bfloat16)
    own_normed = normalize(next_residual.astype(jnp.float32), input_gain).astype(jnp.bfloat16)
    next_normed = lax.all_gather(own_normed, "tensor", axis=0, tiled=True)
    query_cols = q_weight.shape[1]
    kv_cols = kv_weight.shape[1]
    query_raw = jnp.dot(
        next_normed,
        lax.all_gather(q_weight, "expert", axis=0, tiled=True),
        preferred_element_type=jnp.float32,
    )
    kv_raw = jnp.dot(
        next_normed,
        lax.all_gather(kv_weight, "expert", axis=0, tiled=True),
        preferred_element_type=jnp.float32,
    )
    head_size = q_gain.shape[0]
    queries = (
        normalize(query_raw.reshape(group_rows, -1, head_size), q_gain)
        .reshape(group_rows, query_cols)
        .astype(jnp.bfloat16)
    )
    heads_here = kv_cols // head_size
    head_number = tensor_index * heads_here + jnp.arange(heads_here, dtype=jnp.int32)
    is_key = head_number < KV_HEADS
    kv_shaped = kv_raw.reshape(group_rows, heads_here, head_size)
    keys_values = (
        jnp.where(is_key[None, :, None], normalize(kv_shaped, k_gain), kv_shaped)
        .reshape(group_rows, kv_cols)
        .astype(jnp.bfloat16)
    )
    return (next_residual, queries, keys_values)


def solution(mesh):
    small = mesh.shape["tensor"] == 2 and mesh.shape["expert"] == 4 * PLANE
    return jax.shard_map(
        per_device_dense if small else per_device,
        mesh=mesh,
        in_specs=(
            P("expert", "tensor"),
            P("tensor", None),
            P(("expert", "tensor"), None),
            P(),
            P("expert", None),
            P("expert", None),
            P("expert", None, "tensor"),
            P("expert", None, "tensor"),
            P("expert", "tensor", None),
            P(),
            P("expert", "tensor"),
            P("expert", "tensor"),
            P(),
            P(),
        ),
        out_specs=(P(("expert", "tensor"), None), P("expert", "tensor"), P("expert", "tensor")),
        check_vma=False,
    )
```

```python
import functools

import jax
import jax.numpy as jnp
from jax import lax
from jax.experimental import pallas as pl
from jax.experimental.pallas import tpu as pltpu
from jax.sharding import PartitionSpec as P

KV_HEADS = 4
TOP = 8
PLANE = 4
META = 128


EPSILON = 1e-06

SMALL = pl.CostEstimate(flops=0, bytes_accessed=0, transcendentals=0)
VMEM = pl.BlockSpec(memory_space=pltpu.VMEM)
HBM = pl.BlockSpec(memory_space=pltpu.HBM)


def normalize(values, gain):
    return values * lax.rsqrt(jnp.mean(values * values, axis=-1, keepdims=True) + EPSILON) * gain


def params(mebibytes):
    return pltpu.CompilerParams(vmem_limit_bytes=mebibytes << 20)


def lanes(start, size):
    return pl.ds(pl.multiple_of(start, size), size)


def in_hbm(value):
    return pltpu.with_memory_space_constraint(value, pltpu.HBM)


def in_vmem(value):
    return pltpu.with_memory_space_constraint(value, pltpu.VMEM)


def out_projection_kernel(chunk, a_hbm, w_hbm, mine_ref, theirs_ref, a_buf, w_buf, a_sem, sems):
    depth = w_buf.shape[0]
    count = depth // chunk
    half = mine_ref.shape[0]
    a_copy = pltpu.make_async_copy(a_hbm, a_buf, a_sem)
    a_copy.start()
    copies = []
    for i in range(count):
        rows = pl.ds(i * chunk, chunk)
        copies.append(pltpu.make_async_copy(w_hbm.at[rows], w_buf.at[rows], sems.at[i]))
    for copy in copies:
        copy.start()
    tensor = lax.axis_index("tensor")
    own = lanes(tensor * half, half)
    other = lanes((1 - tensor) * half, half)
    a_copy.wait()
    for i in range(count):
        copies[i].wait()
        at = pl.ds(i * chunk, chunk)
        both = jnp.concatenate([a_buf[own, at], a_buf[other, at]], axis=0)
        product = jnp.dot(both, w_buf[at, :], preferred_element_type=jnp.float32)
        if i == 0:
            mine_ref[...] = product[:half]
            theirs_ref[...] = product[half:]
        else:
            mine_ref[...] += product[:half]
            theirs_ref[...] += product[half:]


def out_projection(attn_out, out_weight):
    rows, depth = attn_out.shape
    width = out_weight.shape[1]
    chunk = 256
    half = pltpu.VMEM((rows // 2, width), jnp.float32)
    return pl.pallas_call(
        functools.partial(out_projection_kernel, chunk),
        out_shape=(half, half),
        in_specs=[HBM, HBM],
        out_specs=(VMEM, VMEM),
        scratch_shapes=[
            pltpu.VMEM((rows, depth), jnp.bfloat16),
            pltpu.VMEM((depth, width), jnp.bfloat16),
            pltpu.SemaphoreType.DMA,
            pltpu.SemaphoreType.DMA((depth // chunk,)),
        ],
        compiler_params=params(14),
        cost_estimate=SMALL,
        name="out_projection",
    )(in_hbm(attn_out), in_hbm(out_weight))


def first_norm_kernel(depth, count, *refs):
    mine, theirs = refs[:count], refs[count : 2 * count]
    residual_ref, gain_ref, meta_ref, tokens_ref = refs[2 * count : 2 * count + 4]
    slice_refs, first_ref = refs[2 * count + 4 : -1], refs[-1]
    rows, width = residual_ref.shape
    sub = width // (PLANE * depth)
    start = 0
    for mine_ref, theirs_ref in zip(mine, theirs):
        cols = slice(start, start + mine_ref.shape[1])
        start += mine_ref.shape[1]
        first_ref[:, cols] = (
            residual_ref[:, cols].astype(jnp.float32) + (mine_ref[...] + theirs_ref[...])
        ).astype(jnp.bfloat16)
    first = first_ref[...]
    tokens_ref[:, :width] = normalize(first.astype(jnp.float32), gain_ref[...]).astype(jnp.bfloat16)
    tokens_ref[:, width:] = meta_ref[...]
    plane = lax.axis_index("expert") % PLANE
    for d in range(PLANE):
        for z in range(depth):
            slice_refs[d][z * rows : (z + 1) * rows, :] = first_ref[
                :, lanes((z * PLANE + (plane ^ d)) * sub, sub)
            ]


def first_norm(mine, theirs, residual, gain, meta, depth):
    rows, width = residual.shape
    piece = jax.ShapeDtypeStruct((depth * rows, width // (PLANE * depth)), jnp.bfloat16)
    return pl.pallas_call(
        functools.partial(first_norm_kernel, depth, len(mine)),
        out_shape=(jax.ShapeDtypeStruct((rows, width + META), jnp.bfloat16),) + (piece,) * PLANE,
        in_specs=[VMEM] * (2 * len(mine) + 3),
        out_specs=(VMEM,) * (1 + PLANE),
        scratch_shapes=[pltpu.VMEM((rows, width), jnp.bfloat16)],
        compiler_params=params(2),
        name="first_norm",
    )(*mine, *theirs, residual, gain, meta)


def pack_kernel(depth, *refs):
    line, pieces, out_refs = refs[:depth], refs[depth : depth + PLANE], refs[depth + PLANE :]
    rows, extended = line[0].shape
    for ref, piece in zip(out_refs, pieces):
        for z in range(depth):
            ref[z * rows : (z + 1) * rows, :extended] = line[z][...]
        ref[:, extended:] = piece[...]


def pack(line, pieces):
    depth = len(line)
    rows, extended = line[0].shape
    shape = pltpu.VMEM((depth * rows, extended + pieces[0].shape[1]), jnp.bfloat16)
    return pl.pallas_call(
        functools.partial(pack_kernel, depth),
        out_shape=(shape,) * PLANE,
        in_specs=[VMEM] * (depth + PLANE),
        out_specs=(VMEM,) * PLANE,
        compiler_params=params(2),
        name="pack_tokens",
    )(*line, *pieces)


def load_kernel(*refs):
    sources, targets, sems = refs[:3], refs[-4:-1], refs[-1]
    copies = [
        pltpu.make_async_copy(source, target, sems.at[i])
        for i, (source, target) in enumerate(zip(sources, targets))
    ]
    for copy in copies:
        copy.start()
    for copy in copies:
        copy.wait()


def load(weights, after):
    size = sum(w.size for w in weights)
    return pl.pallas_call(
        load_kernel,
        out_shape=tuple(pltpu.VMEM(w.shape, w.dtype) for w in weights),
        in_specs=[HBM] * 3 + [pl.BlockSpec(memory_space=pl.ANY)] * len(after),
        out_specs=(VMEM,) * 3,
        scratch_shapes=[pltpu.SemaphoreType.DMA((3,))],
        compiler_params=params(2),
        cost_estimate=SMALL,
        name="load_weights",
    )(*map(in_hbm, weights), *after)


def expert_kernel(depth, chunk, count, *refs):
    block_refs, (gate_ref, up_ref, down_ref) = refs[:count], refs[count : count + 3]
    mine_ref, theirs_ref, x_buf, act_buf = refs[count + 3 :]
    width, hidden = gate_ref.shape[1:]
    extended = x_buf.shape[1]
    start = 0
    for ref in block_refs:
        rows = ref.shape[0]
        x_buf[start : start + rows, :] = ref[:, :extended]
        start += rows
    meta = x_buf[:, width:].astype(jnp.float32)
    lane = lax.broadcasted_iota(jnp.int32, meta.shape, 1)
    chip = lax.axis_index("expert")
    expert = 2 * chip + lax.axis_index("tensor")
    chosen = (lane == expert) | (lane == expert + META // 2)
    route = 0.5 * jnp.sum(jnp.where(chosen, meta, 0.0), axis=1, keepdims=True)
    for i in range(hidden // chunk):
        cols = pl.ds(i * chunk, chunk)
        x = x_buf[:, :width]
        gate = jnp.dot(x, gate_ref[0, :, cols], preferred_element_type=jnp.float32)
        up = jnp.dot(x, up_ref[0, :, cols], preferred_element_type=jnp.float32)
        act = gate * (1.0 + jnp.tanh(0.5 * gate)) * (up * route)
        act_buf[:, i * chunk : (i + 1) * chunk] = act.astype(jnp.bfloat16)
    sub = width // (PLANE * depth)
    part = sub * depth
    half = mine_ref.shape[0]
    plane = chip % PLANE
    for d in range(PLANE):
        weight = jnp.concatenate(
            [down_ref[0, :, lanes((z * PLANE + (plane ^ d)) * sub, sub)] for z in range(depth)],
            axis=1,
        )
        out = jnp.dot(act_buf[...], weight, preferred_element_type=jnp.float32)
        cols = slice(d * part, (d + 1) * part)
        mine_ref[:, cols] = out[:half].astype(jnp.bfloat16)
        theirs_ref[:, cols] = out[half:].astype(jnp.bfloat16)


def experts(blocks, weights, depth):
    width, hidden = weights[0].shape[1:]
    chunk = 256
    extended = width + META
    total = sum(block.shape[0] for block in blocks)
    half = pltpu.VMEM((total // 2, width), jnp.bfloat16)
    return pl.pallas_call(
        functools.partial(expert_kernel, depth, chunk, len(blocks)),
        out_shape=(half, half),
        in_specs=[VMEM] * (len(blocks) + 3),
        out_specs=(VMEM, VMEM),
        scratch_shapes=[
            pltpu.VMEM((total, extended), jnp.bfloat16),
            pltpu.VMEM((total, hidden), jnp.bfloat16),
        ],
        compiler_params=params(16),
        cost_estimate=pl.CostEstimate(
            flops=6 * total * width * hidden, bytes_accessed=0, transcendentals=0
        ),
        name="experts",
    )(*blocks, *weights)


def chip_sum_kernel(mine_ref, theirs_ref, *out_refs):
    part = out_refs[0].shape[1]
    for d, ref in enumerate(out_refs):
        at = slice(d * part, (d + 1) * part)
        total = mine_ref[:, at].astype(jnp.float32) + theirs_ref[:, at].astype(jnp.float32)
        ref[...] = total.astype(jnp.bfloat16)


def chip_sum(mine, theirs):
    rows, width = mine.shape
    return pl.pallas_call(
        chip_sum_kernel,
        out_shape=(pltpu.VMEM((rows, width // PLANE), jnp.bfloat16),) * PLANE,
        in_specs=[VMEM] * 2,
        out_specs=(VMEM,) * PLANE,
        compiler_params=params(2),
        name="chip_sum",
    )(mine, theirs)


def plane_sum_kernel(depth, *refs):
    halves, out_refs = (refs[:PLANE], refs[PLANE : 2 * PLANE]), refs[2 * PLANE :]
    group = halves[0][0].shape[0] // 2
    rows = group // depth
    for k in range(PLANE):
        for z in range(depth):
            total = 0.0
            for d in range(PLANE):
                block = k ^ d
                start = block % 2 * group + z * rows
                part = halves[block // 2][d][start : start + rows, :]
                total = total + part.astype(jnp.float32)
            out_refs[z][k * rows : (k + 1) * rows, :] = total.astype(jnp.bfloat16)


def plane_sum(first, second, depth):
    rows, part = first[0].shape
    return pl.pallas_call(
        functools.partial(plane_sum_kernel, depth),
        out_shape=(pltpu.VMEM((2 * rows // depth, part), jnp.bfloat16),) * depth,
        in_specs=[VMEM] * (2 * PLANE),
        out_specs=(VMEM,) * depth,
        compiler_params=params(4),
        name="plane_sum",
    )(*first, *second)


def second_norm_kernel(depth, *refs):
    parts, packed = refs[:depth], refs[depth : depth + PLANE]
    gain_ref, scaled_ref, next_ref = refs[depth + PLANE :]
    rows = packed[0].shape[0] // depth
    part = parts[0].shape[1]
    sub = part // depth
    lane = lax.broadcasted_iota(jnp.int32, (rows, META), 1)
    plane = lax.axis_index("expert") % PLANE
    gain = jnp.concatenate(
        [gain_ref[:, lanes((z * PLANE + plane) * sub, sub)] for z in range(depth)], axis=1
    )
    for d in range(PLANE):
        at = slice(d * rows, (d + 1) * rows)
        total = parts[0][at, :].astype(jnp.float32)
        for ref in parts[1:]:
            total = total + ref[at, :].astype(jnp.float32)
        source = packed[d]
        skip = source.shape[1] - sub
        first = jnp.concatenate(
            [source[z * rows : (z + 1) * rows, skip:] for z in range(depth)], axis=1
        )
        following = (first.astype(jnp.float32) + total).astype(jnp.bfloat16)
        next_ref[at, :] = following
        wide = following.astype(jnp.float32)
        scaled_ref[at, :part] = (wide * gain).astype(jnp.bfloat16)
        squares = jnp.sum(wide * wide, axis=1, keepdims=True)
        high = squares.astype(jnp.bfloat16).astype(jnp.float32)
        low = squares - high
        scaled_ref[at, part:] = jnp.where(
            lane == 0, high, jnp.where(lane == 1, low, 0.0)
        ).astype(jnp.bfloat16)


def second_norm(parts, packed, gain):
    depth = len(parts)
    rows, part = parts[0].shape
    return pl.pallas_call(
        functools.partial(second_norm_kernel, depth),
        out_shape=(
            jax.ShapeDtypeStruct((rows, part + META), jnp.bfloat16),
            jax.ShapeDtypeStruct((rows, part), jnp.bfloat16),
        ),
        in_specs=[VMEM] * (depth + PLANE + 1),
        out_specs=(VMEM, VMEM),
        compiler_params=params(4),
        name="second_norm",
    )(*parts, *packed, gain)


def projection_kernel(chunk, mine_ref, theirs_ref, next_ref, w_hbm, *refs):
    out_refs, (w_buf, sems) = refs[:PLANE], refs[PLANE:]
    cols = w_buf.shape[1]
    copies = []
    for i in range(sems.shape[0]):
        at = lanes(i * META, META)
        copies.append(pltpu.make_async_copy(w_hbm.at[at], w_buf.at[at], sems.at[i]))
    for copy in copies:
        copy.start()
    rows, extended = mine_ref.shape
    part = extended - META
    block = rows // PLANE
    tensor = lax.axis_index("tensor")
    own = lanes(tensor * block, block)
    other = lanes((1 - tensor) * block, block)
    for d in range(PLANE):
        at = slice(d * block, (d + 1) * block)
        out_refs[d][own, cols : cols + META] = mine_ref[at, part:]
        out_refs[d][other, cols : cols + META] = theirs_ref[at, part:]
        out_refs[d][:block, cols + META :] = next_ref[at, : part // 2]
        out_refs[d][block:, cols + META :] = next_ref[at, part // 2 :]
    both = jnp.concatenate([mine_ref[:, :part], theirs_ref[:, :part]], axis=0)
    for copy in copies:
        copy.wait()
    for i in range(cols // chunk):
        at = slice(i * chunk, (i + 1) * chunk)
        product = jnp.dot(both, w_buf[:, at], preferred_element_type=jnp.float32).astype(
            jnp.bfloat16
        )
        for d in range(PLANE):
            out_refs[d][own, at] = product[d * block : (d + 1) * block]
            out_refs[d][other, at] = product[rows + d * block : rows + (d + 1) * block]


def projection(mine, theirs, following, weight):
    rows, part = following.shape
    cols = weight.shape[1]
    chunk = 512
    shape = pltpu.VMEM((2 * rows // PLANE, cols + META + part // 2), jnp.bfloat16)
    return pl.pallas_call(
        functools.partial(projection_kernel, chunk),
        out_shape=(shape,) * PLANE,
        in_specs=[VMEM] * 3 + [HBM],
        out_specs=(VMEM,) * PLANE,
        scratch_shapes=[
            pltpu.VMEM((part, cols), jnp.bfloat16),
            pltpu.SemaphoreType.DMA((part // META,)),
        ],
        compiler_params=params(8),
        cost_estimate=SMALL,
        name="qkv_projection",
    )(mine, theirs, following, in_hbm(weight))


def head_norm_kernel(depth, *refs):
    parts, q_gain_ref, k_gain_ref = refs[:PLANE], refs[PLANE], refs[PLANE + 1]
    next_ref, q_ref, kv_ref = refs[PLANE + 2 :]
    width = next_ref.shape[1]
    q_cols, kv_cols = q_ref.shape[1], kv_ref.shape[1]
    cols = q_cols + kv_cols
    head = q_gain_ref.shape[1]

    def total(at):
        value = parts[0][:, at].astype(jnp.float32)
        for ref in parts[1:]:
            value = value + ref[:, at].astype(jnp.float32)
        return value

    squares = jnp.sum(total(slice(cols, cols + META)), axis=1, keepdims=True)
    scale = lax.rsqrt(squares / width + EPSILON)
    for h in range(q_cols // head):
        at = slice(h * head, (h + 1) * head)
        q_ref[:, at] = normalize(total(at) * scale, q_gain_ref[...]).astype(jnp.bfloat16)
    tensor = lax.axis_index("tensor")
    for h in range(kv_cols // head):
        at = slice(h * head, (h + 1) * head)
        raw = total(slice(q_cols + h * head, q_cols + (h + 1) * head)) * scale
        is_key = tensor * (kv_cols // head) + h < KV_HEADS
        kv_ref[:, at] = jnp.where(is_key, normalize(raw, k_gain_ref[...]), raw).astype(
            jnp.bfloat16
        )
    plane = lax.axis_index("expert") % PLANE
    rows = next_ref.shape[0]
    sub = width // (PLANE * depth)
    for d in range(PLANE):
        for z in range(depth):
            top = z * sub * 2 // (depth * sub)
            start = cols + META + z * sub - top * (depth * sub // 2)
            next_ref[:, lanes((z * PLANE + (plane ^ d)) * sub, sub)] = parts[d][
                top * rows : (top + 1) * rows, start : start + sub
            ]


def head_norm(parts, q_gain, k_gain, q_cols, kv_cols, rows, width, depth):
    both = parts[0].shape[0]
    return pl.pallas_call(
        functools.partial(head_norm_kernel, depth),
        out_shape=(
            jax.ShapeDtypeStruct((rows, width), jnp.bfloat16),
            jax.ShapeDtypeStruct((both, q_cols), jnp.bfloat16),
            jax.ShapeDtypeStruct((both, kv_cols), jnp.bfloat16),
        ),
        in_specs=[VMEM] * (PLANE + 2),
        out_specs=(VMEM, VMEM, VMEM),
        compiler_params=params(4),
        name="head_norm",
    )(*parts, q_gain, k_gain)


def per_device_dense(
    attn_out,
    out_weight,
    residual,
    attn_gain,
    expert_ids,
    route_weights,
    w_gate,
    w_up,
    w_down,
    input_gain,
    q_weight,
    kv_weight,
    q_gain,
    k_gain,
):
    n_expert = lax.axis_size("expert")
    depth = n_expert // PLANE
    rows, width = residual.shape
    tensor_index = lax.axis_index("tensor").astype(jnp.int32)

    def to_core(value):
        return lax.ppermute(value, "tensor", [(0, 1), (1, 0)])

    def to_expert(value, offset):
        return lax.ppermute(value, "expert", [(i, i ^ offset) for i in range(n_expert)])

    def to_z(values):
        return [to_expert(v, d * PLANE) if d else v for d, v in enumerate(values)]

    def to_plane(values):
        return [to_expert(v, d) if d else v for d, v in enumerate(values)]

    own_ids = lax.dynamic_slice_in_dim(expert_ids, tensor_index * rows, rows, 0)
    own_route = lax.dynamic_slice_in_dim(route_weights, tensor_index * rows, rows, 0)
    chosen = own_ids[:, :, None] == jnp.arange(META // 2, dtype=jnp.int32)[None, None, :]
    dense = jnp.sum(jnp.where(chosen, own_route[:, :, None], 0.0), axis=1)
    high = lax.reduce_precision(dense, 8, 7)
    meta = jnp.concatenate([high, dense - high], axis=1).astype(jnp.bfloat16)

    lines = [list(range(i, n_expert, PLANE)) for i in range(PLANE)]
    qkv = lax.all_gather(
        jnp.concatenate([q_weight, kv_weight], axis=1),
        "expert",
        axis=0,
        tiled=True,
        axis_index_groups=lines,
    )
    mine, theirs = out_projection(attn_out, out_weight)
    tokens, *firsts = first_norm(
        (mine,), (to_core(theirs),), residual, attn_gain[None, :], meta, depth
    )
    weights = load((w_gate, w_up, w_down), (tokens,))
    line = to_z([tokens] * depth)
    packed = to_plane(pack(line, firsts))
    near, far = packed[:2], packed[2:]
    sums = []
    for blocks in (near, far):
        mine, theirs = experts((*blocks, *map(to_core, blocks)), weights, depth)
        sums.append(to_plane(chip_sum(mine, to_core(theirs))))
    parts = plane_sum(*sums, depth)
    scaled, following = second_norm(to_z(parts), packed, input_gain[None, :])
    products = to_plane(projection(scaled, to_core(scaled), following, qkv))
    return head_norm(
        products,
        q_gain[None, :],
        k_gain[None, :],
        q_weight.shape[1],
        kv_weight.shape[1],
        rows,
        width,
        depth,
    )


def per_device(
    attn_out,
    out_weight,
    residual,
    attn_gain,
    expert_ids,
    route_weights,
    w_gate,
    w_up,
    w_down,
    input_gain,
    q_weight,
    kv_weight,
    q_gain,
    k_gain,
):
    n_expert = lax.axis_size("expert")
    n_tensor = lax.axis_size("tensor")
    share = n_tensor // 2
    tensor_index = lax.axis_index("tensor")
    group_rows = attn_out.shape[0]
    width = residual.shape[1]
    half = tensor_index // share
    capacity = 3 * group_rows * TOP // (4 * n_expert)
    all_experts = 2 * n_expert
    attn_rows = lax.psum_scatter(
        jnp.dot(attn_out, out_weight, preferred_element_type=jnp.float32),
        "tensor",
        scatter_dimension=0,
        tiled=True,
    )
    first_residual = (residual.astype(jnp.float32) + attn_rows).astype(jnp.bfloat16)
    normed = normalize(first_residual.astype(jnp.float32), attn_gain).astype(jnp.bfloat16)
    group_normed = lax.all_gather(normed, "tensor", axis=0, tiled=True)
    flat_ids = expert_ids.reshape(-1)
    onehot = (flat_ids[:, None] == jnp.arange(all_experts, dtype=jnp.int32)[None, :]).astype(
        jnp.int32
    )
    earlier = jnp.cumsum(onehot, axis=0) - onehot
    rank = jnp.sum(earlier * onehot, axis=1)
    dest = flat_ids * capacity + rank
    row_owner = jnp.arange(flat_ids.shape[0], dtype=jnp.int32) // TOP
    slot_row = jnp.full((all_experts * capacity,), group_rows, jnp.int32).at[dest].set(row_owner)
    slot_weight = (
        jnp.zeros((all_experts * capacity,), jnp.float32).at[dest].set(route_weights.reshape(-1))
    )
    own_slots = lax.dynamic_index_in_dim(
        slot_row.reshape(n_expert, 2, capacity), half, 1, keepdims=False
    )
    own_weights = lax.dynamic_index_in_dim(
        slot_weight.reshape(n_expert, 2, capacity), half, 1, keepdims=False
    )
    padded_rows = jnp.concatenate([group_normed, jnp.zeros((1, width), jnp.bfloat16)], axis=0)
    gate_w = w_gate[0]
    up_w = w_up[0]
    down_w = w_down[0]
    outgoing = jnp.take(padded_rows, own_slots, axis=0)
    arrived = lax.all_to_all(outgoing, "expert", split_axis=0, concat_axis=0, tiled=True)
    flat = arrived.reshape(-1, width)
    gate = jnp.dot(flat, gate_w, preferred_element_type=jnp.float32)
    up = jnp.dot(flat, up_w, preferred_element_type=jnp.float32)
    act = (jax.nn.silu(gate) * up).astype(jnp.bfloat16)
    part = jnp.dot(act, down_w, preferred_element_type=jnp.float32).astype(jnp.bfloat16)
    send_part = part.reshape(arrived.shape)
    returned = lax.all_to_all(send_part, "expert", split_axis=0, concat_axis=0, tiled=True)
    weighted = own_weights.reshape(-1)[:, None] * returned.reshape(-1, width).astype(jnp.float32)
    term = (
        jnp.zeros((group_rows + 1, width), jnp.float32)
        .at[own_slots.reshape(-1)]
        .add(weighted)[:group_rows]
    )
    expert_sum = lax.psum_scatter(
        term.astype(jnp.bfloat16), "tensor", scatter_dimension=0, tiled=True
    ).astype(jnp.float32)
    next_residual = (first_residual.astype(jnp.float32) + expert_sum).astype(jnp.bfloat16)
    own_normed = normalize(next_residual.astype(jnp.float32), input_gain).astype(jnp.bfloat16)
    next_normed = lax.all_gather(own_normed, "tensor", axis=0, tiled=True)
    query_cols = q_weight.shape[1]
    kv_cols = kv_weight.shape[1]
    query_raw = jnp.dot(
        next_normed,
        lax.all_gather(q_weight, "expert", axis=0, tiled=True),
        preferred_element_type=jnp.float32,
    )
    kv_raw = jnp.dot(
        next_normed,
        lax.all_gather(kv_weight, "expert", axis=0, tiled=True),
        preferred_element_type=jnp.float32,
    )
    head_size = q_gain.shape[0]
    queries = (
        normalize(query_raw.reshape(group_rows, -1, head_size), q_gain)
        .reshape(group_rows, query_cols)
        .astype(jnp.bfloat16)
    )
    heads_here = kv_cols // head_size
    head_number = tensor_index * heads_here + jnp.arange(heads_here, dtype=jnp.int32)
    is_key = head_number < KV_HEADS
    kv_shaped = kv_raw.reshape(group_rows, heads_here, head_size)
    keys_values = (
        jnp.where(is_key[None, :, None], normalize(kv_shaped, k_gain), kv_shaped)
        .reshape(group_rows, kv_cols)
        .astype(jnp.bfloat16)
    )
    return (next_residual, queries, keys_values)


def solution(mesh):
    small = mesh.shape["tensor"] == 2 and mesh.shape["expert"] == 4 * PLANE
    return jax.shard_map(
        per_device_dense if small else per_device,
        mesh=mesh,
        in_specs=(
            P("expert", "tensor"),
            P("tensor", None),
            P(("expert", "tensor"), None),
            P(),
            P("expert", None),
            P("expert", None),
            P("expert", None, "tensor"),
            P("expert", None, "tensor"),
            P("expert", "tensor", None),
            P(),
            P("expert", "tensor"),
            P("expert", "tensor"),
            P(),
            P(),
        ),
        out_specs=(P(("expert", "tensor"), None), P("expert", "tensor"), P("expert", "tensor")),
        check_vma=False,
    )
```

```python
import functools

import jax
import jax.numpy as jnp
from jax import lax
from jax.experimental import pallas as pl
from jax.experimental.pallas import tpu as pltpu
from jax.sharding import PartitionSpec as P

KV_HEADS = 4
TOP = 8
PLANE = 4
META = 128


EPSILON = 1e-06

SMALL = pl.CostEstimate(flops=0, bytes_accessed=0, transcendentals=0)
VMEM = pl.BlockSpec(memory_space=pltpu.VMEM)
HBM = pl.BlockSpec(memory_space=pltpu.HBM)


def normalize(values, gain):
    return values * lax.rsqrt(jnp.mean(values * values, axis=-1, keepdims=True) + EPSILON) * gain


def params(mebibytes):
    return pltpu.CompilerParams(vmem_limit_bytes=mebibytes << 20)


def lanes(start, size):
    return pl.ds(pl.multiple_of(start, size), size)


def in_hbm(value):
    return pltpu.with_memory_space_constraint(value, pltpu.HBM)


def in_vmem(value):
    return pltpu.with_memory_space_constraint(value, pltpu.VMEM)


def out_projection_kernel(chunk, a_hbm, w_hbm, mine_ref, theirs_ref, a_buf, w_buf, a_sem, sems):
    depth = w_buf.shape[0]
    count = depth // chunk
    half = mine_ref.shape[0]
    a_copy = pltpu.make_async_copy(a_hbm, a_buf, a_sem)
    a_copy.start()
    copies = []
    for i in range(count):
        rows = pl.ds(i * chunk, chunk)
        copies.append(pltpu.make_async_copy(w_hbm.at[rows], w_buf.at[rows], sems.at[i]))
    for copy in copies:
        copy.start()
    tensor = lax.axis_index("tensor")
    own = lanes(tensor * half, half)
    other = lanes((1 - tensor) * half, half)
    a_copy.wait()
    for i in range(count):
        copies[i].wait()
        at = pl.ds(i * chunk, chunk)
        both = jnp.concatenate([a_buf[own, at], a_buf[other, at]], axis=0)
        product = jnp.dot(both, w_buf[at, :], preferred_element_type=jnp.float32)
        if i == 0:
            mine_ref[...] = product[:half]
            theirs_ref[...] = product[half:]
        else:
            mine_ref[...] += product[:half]
            theirs_ref[...] += product[half:]


def out_projection(attn_out, out_weight):
    rows, depth = attn_out.shape
    width = out_weight.shape[1]
    chunk = 256
    half = pltpu.VMEM((rows // 2, width), jnp.float32)
    return pl.pallas_call(
        functools.partial(out_projection_kernel, chunk),
        out_shape=(half, half),
        in_specs=[HBM, HBM],
        out_specs=(VMEM, VMEM),
        scratch_shapes=[
            pltpu.VMEM((rows, depth), jnp.bfloat16),
            pltpu.VMEM((depth, width), jnp.bfloat16),
            pltpu.SemaphoreType.DMA,
            pltpu.SemaphoreType.DMA((depth // chunk,)),
        ],
        compiler_params=params(14),
        cost_estimate=SMALL,
        name="out_projection",
    )(in_hbm(attn_out), in_hbm(out_weight))


def first_norm_kernel(depth, count, *refs):
    mine, theirs = refs[:count], refs[count : 2 * count]
    residual_ref, gain_ref, meta_ref, tokens_ref = refs[2 * count : 2 * count + 4]
    slice_refs, first_ref = refs[2 * count + 4 : -1], refs[-1]
    rows, width = residual_ref.shape
    sub = width // (PLANE * depth)
    start = 0
    for mine_ref, theirs_ref in zip(mine, theirs):
        cols = slice(start, start + mine_ref.shape[1])
        start += mine_ref.shape[1]
        first_ref[:, cols] = (
            residual_ref[:, cols].astype(jnp.float32) + (mine_ref[...] + theirs_ref[...])
        ).astype(jnp.bfloat16)
    first = first_ref[...]
    tokens_ref[:, :width] = normalize(first.astype(jnp.float32), gain_ref[...]).astype(jnp.bfloat16)
    tokens_ref[:, width:] = meta_ref[...]
    plane = lax.axis_index("expert") % PLANE
    for d in range(PLANE):
        for z in range(depth):
            slice_refs[d][z * rows : (z + 1) * rows, :] = first_ref[
                :, lanes((z * PLANE + (plane ^ d)) * sub, sub)
            ]


def first_norm(mine, theirs, residual, gain, meta, depth):
    rows, width = residual.shape
    piece = jax.ShapeDtypeStruct((depth * rows, width // (PLANE * depth)), jnp.bfloat16)
    return pl.pallas_call(
        functools.partial(first_norm_kernel, depth, len(mine)),
        out_shape=(jax.ShapeDtypeStruct((rows, width + META), jnp.bfloat16),) + (piece,) * PLANE,
        in_specs=[VMEM] * (2 * len(mine) + 3),
        out_specs=(VMEM,) * (1 + PLANE),
        scratch_shapes=[pltpu.VMEM((rows, width), jnp.bfloat16)],
        compiler_params=params(2),
        name="first_norm",
    )(*mine, *theirs, residual, gain, meta)


def pack_kernel(depth, *refs):
    line, pieces, out_refs = refs[:depth], refs[depth : depth + PLANE], refs[depth + PLANE :]
    rows, extended = line[0].shape
    sub = pieces[0].shape[1]
    for d, ref in enumerate(out_refs):
        for z in range(depth):
            ref[z * rows : (z + 1) * rows, :extended] = line[z][...]
        ref[:, extended : extended + sub] = pieces[d][...]
        ref[:, extended + sub :] = pieces[PLANE - 1][...]


def pack(line, pieces):
    depth = len(line)
    rows, extended = line[0].shape
    shape = pltpu.VMEM((depth * rows, extended + 2 * pieces[0].shape[1]), jnp.bfloat16)
    return pl.pallas_call(
        functools.partial(pack_kernel, depth),
        out_shape=(shape,) * (PLANE - 1),
        in_specs=[VMEM] * (depth + PLANE),
        out_specs=(VMEM,) * (PLANE - 1),
        compiler_params=params(2),
        name="pack_tokens",
    )(*line, *pieces)


def load_kernel(*refs):
    sources, targets, sems = refs[:3], refs[-4:-1], refs[-1]
    copies = [
        pltpu.make_async_copy(source, target, sems.at[i])
        for i, (source, target) in enumerate(zip(sources, targets))
    ]
    for copy in copies:
        copy.start()
    for copy in copies:
        copy.wait()


def load(weights, after):
    size = sum(w.size for w in weights)
    return pl.pallas_call(
        load_kernel,
        out_shape=tuple(pltpu.VMEM(w.shape, w.dtype) for w in weights),
        in_specs=[HBM] * 3 + [pl.BlockSpec(memory_space=pl.ANY)] * len(after),
        out_specs=(VMEM,) * 3,
        scratch_shapes=[pltpu.SemaphoreType.DMA((3,))],
        compiler_params=params(2),
        cost_estimate=SMALL,
        name="load_weights",
    )(*map(in_hbm, weights), *after)


def expert_kernel(depth, chunk, count, *refs):
    block_refs, (gate_ref, up_ref, down_ref) = refs[:count], refs[count : count + 3]
    mine_ref, *theirs_refs, x_buf, act_buf = refs[count + 3 :]
    width, hidden = gate_ref.shape[1:]
    extended = x_buf.shape[1]
    start = 0
    for ref in block_refs:
        rows = ref.shape[0]
        x_buf[start : start + rows, :] = ref[:, :extended]
        start += rows
    meta = x_buf[:, width:].astype(jnp.float32)
    lane = lax.broadcasted_iota(jnp.int32, meta.shape, 1)
    chip = lax.axis_index("expert")
    expert = 2 * chip + lax.axis_index("tensor")
    chosen = (lane == expert) | (lane == expert + META // 2)
    route = 0.5 * jnp.sum(jnp.where(chosen, meta, 0.0), axis=1, keepdims=True)
    for i in range(hidden // chunk):
        cols = pl.ds(i * chunk, chunk)
        x = x_buf[:, :width]
        gate = jnp.dot(x, gate_ref[0, :, cols], preferred_element_type=jnp.float32)
        up = jnp.dot(x, up_ref[0, :, cols], preferred_element_type=jnp.float32)
        act = gate * (1.0 + jnp.tanh(0.5 * gate)) * (up * route)
        act_buf[:, i * chunk : (i + 1) * chunk] = act.astype(jnp.bfloat16)
    sub = width // (PLANE * depth)
    part = sub * depth
    half = mine_ref.shape[0]
    plane = chip % PLANE
    for d in range(PLANE):
        weight = jnp.concatenate(
            [down_ref[0, :, lanes((z * PLANE + (plane ^ d)) * sub, sub)] for z in range(depth)],
            axis=1,
        )
        out = jnp.dot(act_buf[...], weight, preferred_element_type=jnp.float32)
        cols = slice(d * part, (d + 1) * part)
        mine_ref[:, cols] = out[:half].astype(jnp.bfloat16)
        start = half
        for ref in theirs_refs:
            stop = start + ref.shape[0]
            ref[:, cols] = out[start:stop].astype(jnp.bfloat16)
            start = stop


def experts(blocks, weights, depth, pieces):
    width, hidden = weights[0].shape[1:]
    chunk = 256
    extended = width + META
    total = sum(block.shape[0] for block in blocks)
    rows = [total // 2] + [total // 2 // pieces] * pieces
    return pl.pallas_call(
        functools.partial(expert_kernel, depth, chunk, len(blocks)),
        out_shape=tuple(pltpu.VMEM((size, width), jnp.bfloat16) for size in rows),
        in_specs=[VMEM] * (len(blocks) + 3),
        out_specs=(VMEM,) * (1 + pieces),
        scratch_shapes=[
            pltpu.VMEM((total, extended), jnp.bfloat16),
            pltpu.VMEM((total, hidden), jnp.bfloat16),
        ],
        compiler_params=params(16),
        cost_estimate=pl.CostEstimate(
            flops=6 * total * width * hidden, bytes_accessed=0, transcendentals=0
        ),
        name="experts",
    )(*blocks, *weights)


def chip_sum_kernel(count, mine_ref, *refs):
    theirs, out_refs = refs[:count], refs[count:]
    part = out_refs[0].shape[1]
    start = 0
    for theirs_ref in theirs:
        rows = slice(start, start + theirs_ref.shape[0])
        start = rows.stop
        for d, ref in enumerate(out_refs):
            at = slice(d * part, (d + 1) * part)
            total = mine_ref[rows, at].astype(jnp.float32) + theirs_ref[:, at].astype(jnp.float32)
            ref[rows, :] = total.astype(jnp.bfloat16)


def chip_sum(mine, theirs):
    rows, width = mine.shape
    return pl.pallas_call(
        functools.partial(chip_sum_kernel, len(theirs)),
        out_shape=(pltpu.VMEM((rows, width // PLANE), jnp.bfloat16),) * PLANE,
        in_specs=[VMEM] * (1 + len(theirs)),
        out_specs=(VMEM,) * PLANE,
        compiler_params=params(2),
        name="chip_sum",
    )(mine, *theirs)


def plane_sum_kernel(depth, *refs):
    near, far, out_refs = refs[:PLANE], refs[PLANE : 2 * PLANE], refs[2 * PLANE :]
    group = far[0].shape[0]
    rows = group // depth
    for k in range(PLANE):
        for z in range(depth):
            total = 0.0
            for d in range(PLANE):
                block = k ^ d
                ref, skip = (far[d], 0) if block == PLANE - 1 else (near[d], block * group)
                start = skip + z * rows
                total = total + ref[start : start + rows, :].astype(jnp.float32)
            out_refs[z][k * rows : (k + 1) * rows, :] = total.astype(jnp.bfloat16)


def plane_sum(near, far, depth):
    rows, part = far[0].shape
    return pl.pallas_call(
        functools.partial(plane_sum_kernel, depth),
        out_shape=(pltpu.VMEM((PLANE * rows // depth, part), jnp.bfloat16),) * depth,
        in_specs=[VMEM] * (2 * PLANE),
        out_specs=(VMEM,) * depth,
        compiler_params=params(4),
        name="plane_sum",
    )(*near, *far)


def second_norm_kernel(depth, *refs):
    parts, packed = refs[:depth], refs[depth : depth + PLANE + 1]
    gain_ref, scaled_ref, next_ref = refs[depth + PLANE + 1 :]
    rows = packed[0].shape[0] // depth
    part = parts[0].shape[1]
    sub = part // depth
    skip = packed[0].shape[1] - 2 * sub
    lane = lax.broadcasted_iota(jnp.int32, (rows, META), 1)
    plane = lax.axis_index("expert") % PLANE
    gain = jnp.concatenate(
        [gain_ref[:, lanes((z * PLANE + plane) * sub, sub)] for z in range(depth)], axis=1
    )
    for d in range(PLANE):
        at = slice(d * rows, (d + 1) * rows)
        total = parts[0][at, :].astype(jnp.float32)
        for ref in parts[1:]:
            total = total + ref[at, :].astype(jnp.float32)
        if d < PLANE - 1:
            first = packed[d][:, skip : skip + sub]
        else:
            first = jnp.concatenate([ref[:, skip + sub :] for ref in packed[d:]], axis=0)
        first = jnp.concatenate([first[z * rows : (z + 1) * rows] for z in range(depth)], axis=1)
        following = (first.astype(jnp.float32) + total).astype(jnp.bfloat16)
        next_ref[at, :] = following
        wide = following.astype(jnp.float32)
        scaled_ref[at, :part] = (wide * gain).astype(jnp.bfloat16)
        squares = jnp.sum(wide * wide, axis=1, keepdims=True)
        high = squares.astype(jnp.bfloat16).astype(jnp.float32)
        low = squares - high
        scaled_ref[at, part:] = jnp.where(
            lane == 0, high, jnp.where(lane == 1, low, 0.0)
        ).astype(jnp.bfloat16)


def second_norm(parts, packed, gain):
    depth = len(parts)
    rows, part = parts[0].shape
    return pl.pallas_call(
        functools.partial(second_norm_kernel, depth),
        out_shape=(
            jax.ShapeDtypeStruct((rows, part + META), jnp.bfloat16),
            jax.ShapeDtypeStruct((rows, part), jnp.bfloat16),
        ),
        in_specs=[VMEM] * (depth + PLANE + 2),
        out_specs=(VMEM, VMEM),
        compiler_params=params(4),
        name="second_norm",
    )(*parts, *packed, gain)


def projection_kernel(chunk, mine_ref, theirs_ref, next_ref, w_hbm, *refs):
    out_refs, (w_buf, sems) = refs[:PLANE], refs[PLANE:]
    cols = w_buf.shape[1]
    copies = []
    for i in range(sems.shape[0]):
        at = lanes(i * META, META)
        copies.append(pltpu.make_async_copy(w_hbm.at[at], w_buf.at[at], sems.at[i]))
    for copy in copies:
        copy.start()
    rows, extended = mine_ref.shape
    part = extended - META
    block = rows // PLANE
    tensor = lax.axis_index("tensor")
    own = lanes(tensor * block, block)
    other = lanes((1 - tensor) * block, block)
    for d in range(PLANE):
        at = slice(d * block, (d + 1) * block)
        out_refs[d][own, cols : cols + META] = mine_ref[at, part:]
        out_refs[d][other, cols : cols + META] = theirs_ref[at, part:]
        out_refs[d][:block, cols + META :] = next_ref[at, : part // 2]
        out_refs[d][block:, cols + META :] = next_ref[at, part // 2 :]
    both = jnp.concatenate([mine_ref[:, :part], theirs_ref[:, :part]], axis=0)
    for copy in copies:
        copy.wait()
    for i in range(cols // chunk):
        at = slice(i * chunk, (i + 1) * chunk)
        product = jnp.dot(both, w_buf[:, at], preferred_element_type=jnp.float32).astype(
            jnp.bfloat16
        )
        for d in range(PLANE):
            out_refs[d][own, at] = product[d * block : (d + 1) * block]
            out_refs[d][other, at] = product[rows + d * block : rows + (d + 1) * block]


def projection(mine, theirs, following, weight):
    rows, part = following.shape
    cols = weight.shape[1]
    chunk = 512
    shape = pltpu.VMEM((2 * rows // PLANE, cols + META + part // 2), jnp.bfloat16)
    return pl.pallas_call(
        functools.partial(projection_kernel, chunk),
        out_shape=(shape,) * PLANE,
        in_specs=[VMEM] * 3 + [HBM],
        out_specs=(VMEM,) * PLANE,
        scratch_shapes=[
            pltpu.VMEM((part, cols), jnp.bfloat16),
            pltpu.SemaphoreType.DMA((part // META,)),
        ],
        compiler_params=params(8),
        cost_estimate=SMALL,
        name="qkv_projection",
    )(mine, theirs, following, in_hbm(weight))


def head_norm_kernel(depth, *refs):
    parts, q_gain_ref, k_gain_ref = refs[:PLANE], refs[PLANE], refs[PLANE + 1]
    next_ref, q_ref, kv_ref = refs[PLANE + 2 :]
    width = next_ref.shape[1]
    q_cols, kv_cols = q_ref.shape[1], kv_ref.shape[1]
    cols = q_cols + kv_cols
    head = q_gain_ref.shape[1]

    def total(at):
        value = parts[0][:, at].astype(jnp.float32)
        for ref in parts[1:]:
            value = value + ref[:, at].astype(jnp.float32)
        return value

    squares = jnp.sum(total(slice(cols, cols + META)), axis=1, keepdims=True)
    scale = lax.rsqrt(squares / width + EPSILON)
    for h in range(q_cols // head):
        at = slice(h * head, (h + 1) * head)
        q_ref[:, at] = normalize(total(at) * scale, q_gain_ref[...]).astype(jnp.bfloat16)
    tensor = lax.axis_index("tensor")
    for h in range(kv_cols // head):
        at = slice(h * head, (h + 1) * head)
        raw = total(slice(q_cols + h * head, q_cols + (h + 1) * head)) * scale
        is_key = tensor * (kv_cols // head) + h < KV_HEADS
        kv_ref[:, at] = jnp.where(is_key, normalize(raw, k_gain_ref[...]), raw).astype(
            jnp.bfloat16
        )
    plane = lax.axis_index("expert") % PLANE
    rows = next_ref.shape[0]
    sub = width // (PLANE * depth)
    for d in range(PLANE):
        for z in range(depth):
            top = z * sub * 2 // (depth * sub)
            start = cols + META + z * sub - top * (depth * sub // 2)
            next_ref[:, lanes((z * PLANE + (plane ^ d)) * sub, sub)] = parts[d][
                top * rows : (top + 1) * rows, start : start + sub
            ]


def head_norm(parts, q_gain, k_gain, q_cols, kv_cols, rows, width, depth):
    both = parts[0].shape[0]
    return pl.pallas_call(
        functools.partial(head_norm_kernel, depth),
        out_shape=(
            jax.ShapeDtypeStruct((rows, width), jnp.bfloat16),
            jax.ShapeDtypeStruct((both, q_cols), jnp.bfloat16),
            jax.ShapeDtypeStruct((both, kv_cols), jnp.bfloat16),
        ),
        in_specs=[VMEM] * (PLANE + 2),
        out_specs=(VMEM, VMEM, VMEM),
        compiler_params=params(4),
        name="head_norm",
    )(*parts, q_gain, k_gain)


def per_device_dense(
    attn_out,
    out_weight,
    residual,
    attn_gain,
    expert_ids,
    route_weights,
    w_gate,
    w_up,
    w_down,
    input_gain,
    q_weight,
    kv_weight,
    q_gain,
    k_gain,
):
    n_expert = lax.axis_size("expert")
    depth = n_expert // PLANE
    rows, width = residual.shape
    tensor_index = lax.axis_index("tensor").astype(jnp.int32)

    def to_core(value):
        return lax.ppermute(value, "tensor", [(0, 1), (1, 0)])

    def to_expert(value, offset):
        return lax.ppermute(value, "expert", [(i, i ^ offset) for i in range(n_expert)])

    def to_z(values):
        return [to_expert(v, d * PLANE) if d else v for d, v in enumerate(values)]

    def to_plane(values):
        return [to_expert(v, d) if d else v for d, v in enumerate(values)]

    own_ids = lax.dynamic_slice_in_dim(expert_ids, tensor_index * rows, rows, 0)
    own_route = lax.dynamic_slice_in_dim(route_weights, tensor_index * rows, rows, 0)
    chosen = own_ids[:, :, None] == jnp.arange(META // 2, dtype=jnp.int32)[None, None, :]
    dense = jnp.sum(jnp.where(chosen, own_route[:, :, None], 0.0), axis=1)
    high = lax.reduce_precision(dense, 8, 7)
    meta = jnp.concatenate([high, dense - high], axis=1).astype(jnp.bfloat16)

    lines = [list(range(i, n_expert, PLANE)) for i in range(PLANE)]
    qkv = lax.all_gather(
        jnp.concatenate([q_weight, kv_weight], axis=1),
        "expert",
        axis=0,
        tiled=True,
        axis_index_groups=lines,
    )
    mine, theirs = out_projection(attn_out, out_weight)
    tokens, *firsts = first_norm(
        (mine,), (to_core(theirs),), residual, attn_gain[None, :], meta, depth
    )
    weights = load((w_gate, w_up, w_down), (tokens,))
    line = to_z([tokens] * depth)
    *line, gate, up, down = lax.optimization_barrier((*line, *weights))
    weights = (gate, up, down)
    near = to_plane(pack(line, firsts))
    cut = near[0].shape[0] // 2
    one, two = near[1][:cut], near[2][cut:]
    far = [to_expert(one, 2), to_expert(two, 1)]
    mine, *theirs = experts((*near, *map(to_core, near)), weights, depth, len(near))
    near_sum = chip_sum(mine, list(map(to_core, theirs)))
    far_both = [*far, *map(to_core, far)]
    tied = lax.optimization_barrier((*near_sum, *far_both))
    near_sum, far_both = tied[:PLANE], tied[PLANE:]
    mine, *theirs = experts(far_both, weights, depth, 1)
    far_sum = chip_sum(mine, list(map(to_core, theirs)))
    parts = plane_sum(to_plane(near_sum), to_plane(far_sum), depth)
    scaled, following = second_norm(to_z(parts), (*near, *far), input_gain[None, :])
    products = to_plane(projection(scaled, to_core(scaled), following, qkv))
    return head_norm(
        products,
        q_gain[None, :],
        k_gain[None, :],
        q_weight.shape[1],
        kv_weight.shape[1],
        rows,
        width,
        depth,
    )


def per_device(
    attn_out,
    out_weight,
    residual,
    attn_gain,
    expert_ids,
    route_weights,
    w_gate,
    w_up,
    w_down,
    input_gain,
    q_weight,
    kv_weight,
    q_gain,
    k_gain,
):
    n_expert = lax.axis_size("expert")
    n_tensor = lax.axis_size("tensor")
    share = n_tensor // 2
    tensor_index = lax.axis_index("tensor")
    group_rows = attn_out.shape[0]
    width = residual.shape[1]
    half = tensor_index // share
    capacity = 3 * group_rows * TOP // (4 * n_expert)
    all_experts = 2 * n_expert
    attn_rows = lax.psum_scatter(
        jnp.dot(attn_out, out_weight, preferred_element_type=jnp.float32),
        "tensor",
        scatter_dimension=0,
        tiled=True,
    )
    first_residual = (residual.astype(jnp.float32) + attn_rows).astype(jnp.bfloat16)
    normed = normalize(first_residual.astype(jnp.float32), attn_gain).astype(jnp.bfloat16)
    group_normed = lax.all_gather(normed, "tensor", axis=0, tiled=True)
    flat_ids = expert_ids.reshape(-1)
    onehot = (flat_ids[:, None] == jnp.arange(all_experts, dtype=jnp.int32)[None, :]).astype(
        jnp.int32
    )
    earlier = jnp.cumsum(onehot, axis=0) - onehot
    rank = jnp.sum(earlier * onehot, axis=1)
    dest = flat_ids * capacity + rank
    row_owner = jnp.arange(flat_ids.shape[0], dtype=jnp.int32) // TOP
    slot_row = jnp.full((all_experts * capacity,), group_rows, jnp.int32).at[dest].set(row_owner)
    slot_weight = (
        jnp.zeros((all_experts * capacity,), jnp.float32).at[dest].set(route_weights.reshape(-1))
    )
    own_slots = lax.dynamic_index_in_dim(
        slot_row.reshape(n_expert, 2, capacity), half, 1, keepdims=False
    )
    own_weights = lax.dynamic_index_in_dim(
        slot_weight.reshape(n_expert, 2, capacity), half, 1, keepdims=False
    )
    padded_rows = jnp.concatenate([group_normed, jnp.zeros((1, width), jnp.bfloat16)], axis=0)
    gate_w = w_gate[0]
    up_w = w_up[0]
    down_w = w_down[0]
    outgoing = jnp.take(padded_rows, own_slots, axis=0)
    arrived = lax.all_to_all(outgoing, "expert", split_axis=0, concat_axis=0, tiled=True)
    flat = arrived.reshape(-1, width)
    gate = jnp.dot(flat, gate_w, preferred_element_type=jnp.float32)
    up = jnp.dot(flat, up_w, preferred_element_type=jnp.float32)
    act = (jax.nn.silu(gate) * up).astype(jnp.bfloat16)
    part = jnp.dot(act, down_w, preferred_element_type=jnp.float32).astype(jnp.bfloat16)
    send_part = part.reshape(arrived.shape)
    returned = lax.all_to_all(send_part, "expert", split_axis=0, concat_axis=0, tiled=True)
    weighted = own_weights.reshape(-1)[:, None] * returned.reshape(-1, width).astype(jnp.float32)
    term = (
        jnp.zeros((group_rows + 1, width), jnp.float32)
        .at[own_slots.reshape(-1)]
        .add(weighted)[:group_rows]
    )
    expert_sum = lax.psum_scatter(
        term.astype(jnp.bfloat16), "tensor", scatter_dimension=0, tiled=True
    ).astype(jnp.float32)
    next_residual = (first_residual.astype(jnp.float32) + expert_sum).astype(jnp.bfloat16)
    own_normed = normalize(next_residual.astype(jnp.float32), input_gain).astype(jnp.bfloat16)
    next_normed = lax.all_gather(own_normed, "tensor", axis=0, tiled=True)
    query_cols = q_weight.shape[1]
    kv_cols = kv_weight.shape[1]
    query_raw = jnp.dot(
        next_normed,
        lax.all_gather(q_weight, "expert", axis=0, tiled=True),
        preferred_element_type=jnp.float32,
    )
    kv_raw = jnp.dot(
        next_normed,
        lax.all_gather(kv_weight, "expert", axis=0, tiled=True),
        preferred_element_type=jnp.float32,
    )
    head_size = q_gain.shape[0]
    queries = (
        normalize(query_raw.reshape(group_rows, -1, head_size), q_gain)
        .reshape(group_rows, query_cols)
        .astype(jnp.bfloat16)
    )
    heads_here = kv_cols // head_size
    head_number = tensor_index * heads_here + jnp.arange(heads_here, dtype=jnp.int32)
    is_key = head_number < KV_HEADS
    kv_shaped = kv_raw.reshape(group_rows, heads_here, head_size)
    keys_values = (
        jnp.where(is_key[None, :, None], normalize(kv_shaped, k_gain), kv_shaped)
        .reshape(group_rows, kv_cols)
        .astype(jnp.bfloat16)
    )
    return (next_residual, queries, keys_values)


def solution(mesh):
    small = mesh.shape["tensor"] == 2 and mesh.shape["expert"] == 4 * PLANE
    return jax.shard_map(
        per_device_dense if small else per_device,
        mesh=mesh,
        in_specs=(
            P("expert", "tensor"),
            P("tensor", None),
            P(("expert", "tensor"), None),
            P(),
            P("expert", None),
            P("expert", None),
            P("expert", None, "tensor"),
            P("expert", None, "tensor"),
            P("expert", "tensor", None),
            P(),
            P("expert", "tensor"),
            P("expert", "tensor"),
            P(),
            P(),
        ),
        out_specs=(P(("expert", "tensor"), None), P("expert", "tensor"), P("expert", "tensor")),
        check_vma=False,
    )
```

```python
import functools

import jax
import jax.numpy as jnp
from jax import lax
from jax.experimental import pallas as pl
from jax.experimental.pallas import tpu as pltpu
from jax.sharding import PartitionSpec as P

KV_HEADS = 4
TOP = 8
PLANE = 4
META = 128


EPSILON = 1e-06

SMALL = pl.CostEstimate(flops=0, bytes_accessed=0, transcendentals=0)
VMEM = pl.BlockSpec(memory_space=pltpu.VMEM)
HBM = pl.BlockSpec(memory_space=pltpu.HBM)


def normalize(values, gain):
    return values * lax.rsqrt(jnp.mean(values * values, axis=-1, keepdims=True) + EPSILON) * gain


def params(mebibytes):
    return pltpu.CompilerParams(vmem_limit_bytes=mebibytes << 20)


def lanes(start, size):
    return pl.ds(pl.multiple_of(start, size), size)


def in_hbm(value):
    return pltpu.with_memory_space_constraint(value, pltpu.HBM)


def in_vmem(value):
    return pltpu.with_memory_space_constraint(value, pltpu.VMEM)


def out_projection_kernel(chunk, a_hbm, w_hbm, mine_ref, theirs_ref, a_buf, w_buf, a_sem, sems):
    depth = w_buf.shape[0]
    count = depth // chunk
    half = mine_ref.shape[0]
    a_copy = pltpu.make_async_copy(a_hbm, a_buf, a_sem)
    a_copy.start()
    copies = []
    for i in range(count):
        rows = pl.ds(i * chunk, chunk)
        copies.append(pltpu.make_async_copy(w_hbm.at[rows], w_buf.at[rows], sems.at[i]))
    for copy in copies:
        copy.start()
    tensor = lax.axis_index("tensor")
    own = lanes(tensor * half, half)
    other = lanes((1 - tensor) * half, half)
    a_copy.wait()
    for i in range(count):
        copies[i].wait()
        at = pl.ds(i * chunk, chunk)
        both = jnp.concatenate([a_buf[own, at], a_buf[other, at]], axis=0)
        product = jnp.dot(both, w_buf[at, :], preferred_element_type=jnp.float32)
        if i == 0:
            mine_ref[...] = product[:half]
            theirs_ref[...] = product[half:]
        else:
            mine_ref[...] += product[:half]
            theirs_ref[...] += product[half:]


def out_projection(attn_out, out_weight):
    rows, depth = attn_out.shape
    width = out_weight.shape[1]
    chunk = 256
    half = pltpu.VMEM((rows // 2, width), jnp.float32)
    return pl.pallas_call(
        functools.partial(out_projection_kernel, chunk),
        out_shape=(half, half),
        in_specs=[HBM, HBM],
        out_specs=(VMEM, VMEM),
        scratch_shapes=[
            pltpu.VMEM((rows, depth), jnp.bfloat16),
            pltpu.VMEM((depth, width), jnp.bfloat16),
            pltpu.SemaphoreType.DMA,
            pltpu.SemaphoreType.DMA((depth // chunk,)),
        ],
        compiler_params=params(14),
        cost_estimate=SMALL,
        name="out_projection",
    )(in_hbm(attn_out), in_hbm(out_weight))


def first_norm_kernel(depth, count, *refs):
    mine, theirs = refs[:count], refs[count : 2 * count]
    residual_ref, gain_ref, meta_ref, tokens_ref = refs[2 * count : 2 * count + 4]
    slice_refs, first_ref = refs[2 * count + 4 : -1], refs[-1]
    rows, width = residual_ref.shape
    sub = width // (PLANE * depth)
    start = 0
    for mine_ref, theirs_ref in zip(mine, theirs):
        cols = slice(start, start + mine_ref.shape[1])
        start += mine_ref.shape[1]
        first_ref[:, cols] = (
            residual_ref[:, cols].astype(jnp.float32) + (mine_ref[...] + theirs_ref[...])
        ).astype(jnp.bfloat16)
    first = first_ref[...]
    tokens_ref[:, :width] = normalize(first.astype(jnp.float32), gain_ref[...]).astype(jnp.bfloat16)
    tokens_ref[:, width:] = meta_ref[...]
    plane = lax.axis_index("expert") % PLANE
    for d in range(PLANE):
        for z in range(depth):
            slice_refs[d][z * rows : (z + 1) * rows, :] = first_ref[
                :, lanes((z * PLANE + (plane ^ d)) * sub, sub)
            ]


def first_norm(mine, theirs, residual, gain, meta, depth):
    rows, width = residual.shape
    piece = jax.ShapeDtypeStruct((depth * rows, width // (PLANE * depth)), jnp.bfloat16)
    return pl.pallas_call(
        functools.partial(first_norm_kernel, depth, len(mine)),
        out_shape=(jax.ShapeDtypeStruct((rows, width + META), jnp.bfloat16),) + (piece,) * PLANE,
        in_specs=[VMEM] * (2 * len(mine) + 3),
        out_specs=(VMEM,) * (1 + PLANE),
        scratch_shapes=[pltpu.VMEM((rows, width), jnp.bfloat16)],
        compiler_params=params(2),
        name="first_norm",
    )(*mine, *theirs, residual, gain, meta)


def pack_kernel(depth, *refs):
    line, pieces, out_refs = refs[:depth], refs[depth : depth + PLANE], refs[depth + PLANE :]
    rows, extended = line[0].shape
    sub = pieces[0].shape[1]
    for d, ref in enumerate(out_refs):
        for z in range(depth):
            ref[z * rows : (z + 1) * rows, :extended] = line[z][...]
        ref[:, extended : extended + sub] = pieces[d][...]
        ref[:, extended + sub :] = pieces[PLANE - 1][...]


def pack(line, pieces):
    depth = len(line)
    rows, extended = line[0].shape
    shape = pltpu.VMEM((depth * rows, extended + 2 * pieces[0].shape[1]), jnp.bfloat16)
    return pl.pallas_call(
        functools.partial(pack_kernel, depth),
        out_shape=(shape,) * (PLANE - 1),
        in_specs=[VMEM] * (depth + PLANE),
        out_specs=(VMEM,) * (PLANE - 1),
        compiler_params=params(2),
        name="pack_tokens",
    )(*line, *pieces)


def load_kernel(*refs):
    sources, targets, sems = refs[:3], refs[-4:-1], refs[-1]
    copies = [
        pltpu.make_async_copy(source, target, sems.at[i])
        for i, (source, target) in enumerate(zip(sources, targets))
    ]
    for copy in copies:
        copy.start()
    for copy in copies:
        copy.wait()


def load(weights, after):
    size = sum(w.size for w in weights)
    return pl.pallas_call(
        load_kernel,
        out_shape=tuple(pltpu.VMEM(w.shape, w.dtype) for w in weights),
        in_specs=[HBM] * 3 + [pl.BlockSpec(memory_space=pl.ANY)] * len(after),
        out_specs=(VMEM,) * 3,
        scratch_shapes=[pltpu.SemaphoreType.DMA((3,))],
        compiler_params=params(2),
        cost_estimate=SMALL,
        name="load_weights",
    )(*map(in_hbm, weights), *after)


def expert_kernel(depth, chunk, count, *refs):
    block_refs, (gate_ref, up_ref, down_ref) = refs[:count], refs[count : count + 3]
    mine_ref, *theirs_refs, x_buf, act_buf = refs[count + 3 :]
    width, hidden = gate_ref.shape[1:]
    extended = x_buf.shape[1]
    start = 0
    for ref in block_refs:
        rows = ref.shape[0]
        x_buf[start : start + rows, :] = ref[:, :extended]
        start += rows
    meta = x_buf[:, width:].astype(jnp.float32)
    lane = lax.broadcasted_iota(jnp.int32, meta.shape, 1)
    chip = lax.axis_index("expert")
    expert = 2 * chip + lax.axis_index("tensor")
    chosen = (lane == expert) | (lane == expert + META // 2)
    route = 0.5 * jnp.sum(jnp.where(chosen, meta, 0.0), axis=1, keepdims=True)
    for i in range(hidden // chunk):
        cols = pl.ds(i * chunk, chunk)
        x = x_buf[:, :width]
        gate = jnp.dot(x, gate_ref[0, :, cols], preferred_element_type=jnp.float32)
        up = jnp.dot(x, up_ref[0, :, cols], preferred_element_type=jnp.float32)
        act = gate * (1.0 + jnp.tanh(0.5 * gate)) * (up * route)
        act_buf[:, i * chunk : (i + 1) * chunk] = act.astype(jnp.bfloat16)
    sub = width // (PLANE * depth)
    part = sub * depth
    half = mine_ref.shape[0]
    plane = chip % PLANE
    for d in range(PLANE):
        weight = jnp.concatenate(
            [down_ref[0, :, lanes((z * PLANE + (plane ^ d)) * sub, sub)] for z in range(depth)],
            axis=1,
        )
        out = jnp.dot(act_buf[...], weight, preferred_element_type=jnp.float32)
        cols = slice(d * part, (d + 1) * part)
        mine_ref[:, cols] = out[:half].astype(jnp.bfloat16)
        start = half
        for ref in theirs_refs:
            stop = start + ref.shape[0]
            ref[:, cols] = out[start:stop].astype(jnp.bfloat16)
            start = stop


def experts(blocks, weights, depth, pieces):
    width, hidden = weights[0].shape[1:]
    chunk = 256
    extended = width + META
    total = sum(block.shape[0] for block in blocks)
    rows = [total // 2] + [total // 2 // pieces] * pieces
    return pl.pallas_call(
        functools.partial(expert_kernel, depth, chunk, len(blocks)),
        out_shape=tuple(pltpu.VMEM((size, width), jnp.bfloat16) for size in rows),
        in_specs=[VMEM] * (len(blocks) + 3),
        out_specs=(VMEM,) * (1 + pieces),
        scratch_shapes=[
            pltpu.VMEM((total, extended), jnp.bfloat16),
            pltpu.VMEM((total, hidden), jnp.bfloat16),
        ],
        compiler_params=params(16),
        cost_estimate=pl.CostEstimate(
            flops=6 * total * width * hidden, bytes_accessed=0, transcendentals=0
        ),
        name="experts",
    )(*blocks, *weights)


def chip_sum_kernel(count, mine_ref, *refs):
    theirs, out_refs = refs[:count], refs[count:]
    part = out_refs[0].shape[1]
    start = 0
    for theirs_ref in theirs:
        rows = slice(start, start + theirs_ref.shape[0])
        start = rows.stop
        for d, ref in enumerate(out_refs):
            at = slice(d * part, (d + 1) * part)
            total = mine_ref[rows, at].astype(jnp.float32) + theirs_ref[:, at].astype(jnp.float32)
            ref[rows, :] = total.astype(jnp.bfloat16)


def chip_sum(mine, theirs):
    rows, width = mine.shape
    return pl.pallas_call(
        functools.partial(chip_sum_kernel, len(theirs)),
        out_shape=(pltpu.VMEM((rows, width // PLANE), jnp.bfloat16),) * PLANE,
        in_specs=[VMEM] * (1 + len(theirs)),
        out_specs=(VMEM,) * PLANE,
        compiler_params=params(2),
        name="chip_sum",
    )(mine, *theirs)


def plane_sum_kernel(depth, *refs):
    near, far, out_refs = refs[:PLANE], refs[PLANE : 2 * PLANE], refs[2 * PLANE :]
    group = far[0].shape[0]
    rows = group // depth
    for k in range(PLANE):
        for z in range(depth):
            total = 0.0
            for d in range(PLANE):
                block = k ^ d
                ref, skip = (far[d], 0) if block == PLANE - 1 else (near[d], block * group)
                start = skip + z * rows
                total = total + ref[start : start + rows, :].astype(jnp.float32)
            out_refs[z][k * rows : (k + 1) * rows, :] = total.astype(jnp.bfloat16)


def plane_sum(near, far, depth):
    rows, part = far[0].shape
    return pl.pallas_call(
        functools.partial(plane_sum_kernel, depth),
        out_shape=(pltpu.VMEM((PLANE * rows // depth, part), jnp.bfloat16),) * depth,
        in_specs=[VMEM] * (2 * PLANE),
        out_specs=(VMEM,) * depth,
        compiler_params=params(4),
        name="plane_sum",
    )(*near, *far)


def second_norm_kernel(depth, *refs):
    parts, packed = refs[:depth], refs[depth : depth + PLANE + 1]
    gain_ref, scaled_ref, next_ref = refs[depth + PLANE + 1 :]
    rows = packed[0].shape[0] // depth
    part = parts[0].shape[1]
    sub = part // depth
    skip = packed[0].shape[1] - 2 * sub
    lane = lax.broadcasted_iota(jnp.int32, (rows, META), 1)
    plane = lax.axis_index("expert") % PLANE
    gain = jnp.concatenate(
        [gain_ref[:, lanes((z * PLANE + plane) * sub, sub)] for z in range(depth)], axis=1
    )
    for d in range(PLANE):
        at = slice(d * rows, (d + 1) * rows)
        total = parts[0][at, :].astype(jnp.float32)
        for ref in parts[1:]:
            total = total + ref[at, :].astype(jnp.float32)
        if d < PLANE - 1:
            first = packed[d][:, skip : skip + sub]
        else:
            first = jnp.concatenate([ref[:, skip + sub :] for ref in packed[d:]], axis=0)
        first = jnp.concatenate([first[z * rows : (z + 1) * rows] for z in range(depth)], axis=1)
        following = (first.astype(jnp.float32) + total).astype(jnp.bfloat16)
        next_ref[at, :] = following
        wide = following.astype(jnp.float32)
        scaled_ref[at, :part] = (wide * gain).astype(jnp.bfloat16)
        squares = jnp.sum(wide * wide, axis=1, keepdims=True)
        high = squares.astype(jnp.bfloat16).astype(jnp.float32)
        low = squares - high
        scaled_ref[at, part:] = jnp.where(
            lane == 0, high, jnp.where(lane == 1, low, 0.0)
        ).astype(jnp.bfloat16)


def second_norm(parts, packed, gain):
    depth = len(parts)
    rows, part = parts[0].shape
    return pl.pallas_call(
        functools.partial(second_norm_kernel, depth),
        out_shape=(
            jax.ShapeDtypeStruct((rows, part + META), jnp.bfloat16),
            jax.ShapeDtypeStruct((rows, part), jnp.bfloat16),
        ),
        in_specs=[VMEM] * (depth + PLANE + 2),
        out_specs=(VMEM, VMEM),
        compiler_params=params(4),
        name="second_norm",
    )(*parts, *packed, gain)


def projection_kernel(chunk, mine_ref, theirs_ref, next_ref, w_hbm, *refs):
    out_refs, (w_buf, sems) = refs[:PLANE], refs[PLANE:]
    cols = w_buf.shape[1]
    copies = []
    for i in range(sems.shape[0]):
        at = lanes(i * META, META)
        copies.append(pltpu.make_async_copy(w_hbm.at[at], w_buf.at[at], sems.at[i]))
    for copy in copies:
        copy.start()
    rows, extended = mine_ref.shape
    part = extended - META
    block = rows // PLANE
    tensor = lax.axis_index("tensor")
    own = lanes(tensor * block, block)
    other = lanes((1 - tensor) * block, block)
    for d in range(PLANE):
        at = slice(d * block, (d + 1) * block)
        out_refs[d][own, cols : cols + META] = mine_ref[at, part:]
        out_refs[d][other, cols : cols + META] = theirs_ref[at, part:]
        out_refs[d][:block, cols + META :] = next_ref[at, : part // 2]
        out_refs[d][block:, cols + META :] = next_ref[at, part // 2 :]
    both = jnp.concatenate([mine_ref[:, :part], theirs_ref[:, :part]], axis=0)
    for copy in copies:
        copy.wait()
    for i in range(cols // chunk):
        at = slice(i * chunk, (i + 1) * chunk)
        product = jnp.dot(both, w_buf[:, at], preferred_element_type=jnp.float32).astype(
            jnp.bfloat16
        )
        for d in range(PLANE):
            out_refs[d][own, at] = product[d * block : (d + 1) * block]
            out_refs[d][other, at] = product[rows + d * block : rows + (d + 1) * block]


def projection(mine, theirs, following, weight):
    rows, part = following.shape
    cols = weight.shape[1]
    chunk = 512
    shape = pltpu.VMEM((2 * rows // PLANE, cols + META + part // 2), jnp.bfloat16)
    return pl.pallas_call(
        functools.partial(projection_kernel, chunk),
        out_shape=(shape,) * PLANE,
        in_specs=[VMEM] * 3 + [HBM],
        out_specs=(VMEM,) * PLANE,
        scratch_shapes=[
            pltpu.VMEM((part, cols), jnp.bfloat16),
            pltpu.SemaphoreType.DMA((part // META,)),
        ],
        compiler_params=params(8),
        cost_estimate=SMALL,
        name="qkv_projection",
    )(mine, theirs, following, in_hbm(weight))


def head_norm_kernel(depth, *refs):
    parts, q_gain_ref, k_gain_ref = refs[:PLANE], refs[PLANE], refs[PLANE + 1]
    next_ref, q_ref, kv_ref = refs[PLANE + 2 :]
    width = next_ref.shape[1]
    q_cols, kv_cols = q_ref.shape[1], kv_ref.shape[1]
    cols = q_cols + kv_cols
    head = q_gain_ref.shape[1]

    def total(at):
        value = parts[0][:, at].astype(jnp.float32)
        for ref in parts[1:]:
            value = value + ref[:, at].astype(jnp.float32)
        return value

    squares = jnp.sum(total(slice(cols, cols + META)), axis=1, keepdims=True)
    scale = lax.rsqrt(squares / width + EPSILON)
    for h in range(q_cols // head):
        at = slice(h * head, (h + 1) * head)
        q_ref[:, at] = normalize(total(at) * scale, q_gain_ref[...]).astype(jnp.bfloat16)
    tensor = lax.axis_index("tensor")
    for h in range(kv_cols // head):
        at = slice(h * head, (h + 1) * head)
        raw = total(slice(q_cols + h * head, q_cols + (h + 1) * head)) * scale
        is_key = tensor * (kv_cols // head) + h < KV_HEADS
        kv_ref[:, at] = jnp.where(is_key, normalize(raw, k_gain_ref[...]), raw).astype(
            jnp.bfloat16
        )
    plane = lax.axis_index("expert") % PLANE
    rows = next_ref.shape[0]
    sub = width // (PLANE * depth)
    for d in range(PLANE):
        for z in range(depth):
            top = z * sub * 2 // (depth * sub)
            start = cols + META + z * sub - top * (depth * sub // 2)
            next_ref[:, lanes((z * PLANE + (plane ^ d)) * sub, sub)] = parts[d][
                top * rows : (top + 1) * rows, start : start + sub
            ]


def head_norm(parts, q_gain, k_gain, q_cols, kv_cols, rows, width, depth):
    both = parts[0].shape[0]
    return pl.pallas_call(
        functools.partial(head_norm_kernel, depth),
        out_shape=(
            jax.ShapeDtypeStruct((rows, width), jnp.bfloat16),
            jax.ShapeDtypeStruct((both, q_cols), jnp.bfloat16),
            jax.ShapeDtypeStruct((both, kv_cols), jnp.bfloat16),
        ),
        in_specs=[VMEM] * (PLANE + 2),
        out_specs=(VMEM, VMEM, VMEM),
        compiler_params=params(4),
        name="head_norm",
    )(*parts, q_gain, k_gain)


def per_device_dense(
    attn_out,
    out_weight,
    residual,
    attn_gain,
    expert_ids,
    route_weights,
    w_gate,
    w_up,
    w_down,
    input_gain,
    q_weight,
    kv_weight,
    q_gain,
    k_gain,
):
    n_expert = lax.axis_size("expert")
    depth = n_expert // PLANE
    rows, width = residual.shape
    tensor_index = lax.axis_index("tensor").astype(jnp.int32)

    def to_core(value):
        return lax.ppermute(value, "tensor", [(0, 1), (1, 0)])

    def to_expert(value, offset):
        return lax.ppermute(value, "expert", [(i, i ^ offset) for i in range(n_expert)])

    def to_z(values):
        return [to_expert(v, d * PLANE) if d else v for d, v in enumerate(values)]

    def to_plane(values):
        return [to_expert(v, d) if d else v for d, v in enumerate(values)]

    own_ids = lax.dynamic_slice_in_dim(expert_ids, tensor_index * rows, rows, 0)
    own_route = lax.dynamic_slice_in_dim(route_weights, tensor_index * rows, rows, 0)
    chosen = own_ids[:, :, None] == jnp.arange(META // 2, dtype=jnp.int32)[None, None, :]
    dense = jnp.sum(jnp.where(chosen, own_route[:, :, None], 0.0), axis=1)
    high = lax.reduce_precision(dense, 8, 7)
    meta = jnp.concatenate([high, dense - high], axis=1).astype(jnp.bfloat16)

    lines = [list(range(i, n_expert, PLANE)) for i in range(PLANE)]
    joined = jnp.concatenate([q_weight, kv_weight], axis=1)
    mine, theirs = out_projection(attn_out, out_weight)
    tokens, *firsts = first_norm(
        (mine,), (to_core(theirs),), residual, attn_gain[None, :], meta, depth
    )
    weights = load((w_gate, w_up, w_down), (tokens, joined))
    line = to_z([tokens] * depth)
    *line, joined, gate, up, down = lax.optimization_barrier((*line, joined, *weights))
    qkv = lax.all_gather(joined, "expert", axis=0, tiled=True, axis_index_groups=lines)
    weights = (gate, up, down)
    near = to_plane(pack(line, firsts))
    cut = near[0].shape[0] // 2
    one, two = near[1][:cut], near[2][cut:]
    far = [to_expert(one, 2), to_expert(two, 1)]
    mine, *theirs = experts((*near, *map(to_core, near)), weights, depth, len(near))
    near_sum = chip_sum(mine, list(map(to_core, theirs)))
    far_both = [*far, *map(to_core, far)]
    tied = lax.optimization_barrier((*near_sum, *far_both))
    near_sum, far_both = tied[:PLANE], tied[PLANE:]
    mine, *theirs = experts(far_both, weights, depth, 1)
    far_sum = chip_sum(mine, list(map(to_core, theirs)))
    parts = plane_sum(to_plane(near_sum), to_plane(far_sum), depth)
    scaled, following = second_norm(to_z(parts), (*near, *far), input_gain[None, :])
    products = to_plane(projection(scaled, to_core(scaled), following, qkv))
    return head_norm(
        products,
        q_gain[None, :],
        k_gain[None, :],
        q_weight.shape[1],
        kv_weight.shape[1],
        rows,
        width,
        depth,
    )


def per_device(
    attn_out,
    out_weight,
    residual,
    attn_gain,
    expert_ids,
    route_weights,
    w_gate,
    w_up,
    w_down,
    input_gain,
    q_weight,
    kv_weight,
    q_gain,
    k_gain,
):
    n_expert = lax.axis_size("expert")
    n_tensor = lax.axis_size("tensor")
    share = n_tensor // 2
    tensor_index = lax.axis_index("tensor")
    group_rows = attn_out.shape[0]
    width = residual.shape[1]
    half = tensor_index // share
    capacity = 3 * group_rows * TOP // (4 * n_expert)
    all_experts = 2 * n_expert
    attn_rows = lax.psum_scatter(
        jnp.dot(attn_out, out_weight, preferred_element_type=jnp.float32),
        "tensor",
        scatter_dimension=0,
        tiled=True,
    )
    first_residual = (residual.astype(jnp.float32) + attn_rows).astype(jnp.bfloat16)
    normed = normalize(first_residual.astype(jnp.float32), attn_gain).astype(jnp.bfloat16)
    group_normed = lax.all_gather(normed, "tensor", axis=0, tiled=True)
    flat_ids = expert_ids.reshape(-1)
    onehot = (flat_ids[:, None] == jnp.arange(all_experts, dtype=jnp.int32)[None, :]).astype(
        jnp.int32
    )
    earlier = jnp.cumsum(onehot, axis=0) - onehot
    rank = jnp.sum(earlier * onehot, axis=1)
    dest = flat_ids * capacity + rank
    row_owner = jnp.arange(flat_ids.shape[0], dtype=jnp.int32) // TOP
    slot_row = jnp.full((all_experts * capacity,), group_rows, jnp.int32).at[dest].set(row_owner)
    slot_weight = (
        jnp.zeros((all_experts * capacity,), jnp.float32).at[dest].set(route_weights.reshape(-1))
    )
    own_slots = lax.dynamic_index_in_dim(
        slot_row.reshape(n_expert, 2, capacity), half, 1, keepdims=False
    )
    own_weights = lax.dynamic_index_in_dim(
        slot_weight.reshape(n_expert, 2, capacity), half, 1, keepdims=False
    )
    padded_rows = jnp.concatenate([group_normed, jnp.zeros((1, width), jnp.bfloat16)], axis=0)
    gate_w = w_gate[0]
    up_w = w_up[0]
    down_w = w_down[0]
    outgoing = jnp.take(padded_rows, own_slots, axis=0)
    arrived = lax.all_to_all(outgoing, "expert", split_axis=0, concat_axis=0, tiled=True)
    flat = arrived.reshape(-1, width)
    gate = jnp.dot(flat, gate_w, preferred_element_type=jnp.float32)
    up = jnp.dot(flat, up_w, preferred_element_type=jnp.float32)
    act = (jax.nn.silu(gate) * up).astype(jnp.bfloat16)
    part = jnp.dot(act, down_w, preferred_element_type=jnp.float32).astype(jnp.bfloat16)
    send_part = part.reshape(arrived.shape)
    returned = lax.all_to_all(send_part, "expert", split_axis=0, concat_axis=0, tiled=True)
    weighted = own_weights.reshape(-1)[:, None] * returned.reshape(-1, width).astype(jnp.float32)
    term = (
        jnp.zeros((group_rows + 1, width), jnp.float32)
        .at[own_slots.reshape(-1)]
        .add(weighted)[:group_rows]
    )
    expert_sum = lax.psum_scatter(
        term.astype(jnp.bfloat16), "tensor", scatter_dimension=0, tiled=True
    ).astype(jnp.float32)
    next_residual = (first_residual.astype(jnp.float32) + expert_sum).astype(jnp.bfloat16)
    own_normed = normalize(next_residual.astype(jnp.float32), input_gain).astype(jnp.bfloat16)
    next_normed = lax.all_gather(own_normed, "tensor", axis=0, tiled=True)
    query_cols = q_weight.shape[1]
    kv_cols = kv_weight.shape[1]
    query_raw = jnp.dot(
        next_normed,
        lax.all_gather(q_weight, "expert", axis=0, tiled=True),
        preferred_element_type=jnp.float32,
    )
    kv_raw = jnp.dot(
        next_normed,
        lax.all_gather(kv_weight, "expert", axis=0, tiled=True),
        preferred_element_type=jnp.float32,
    )
    head_size = q_gain.shape[0]
    queries = (
        normalize(query_raw.reshape(group_rows, -1, head_size), q_gain)
        .reshape(group_rows, query_cols)
        .astype(jnp.bfloat16)
    )
    heads_here = kv_cols // head_size
    head_number = tensor_index * heads_here + jnp.arange(heads_here, dtype=jnp.int32)
    is_key = head_number < KV_HEADS
    kv_shaped = kv_raw.reshape(group_rows, heads_here, head_size)
    keys_values = (
        jnp.where(is_key[None, :, None], normalize(kv_shaped, k_gain), kv_shaped)
        .reshape(group_rows, kv_cols)
        .astype(jnp.bfloat16)
    )
    return (next_residual, queries, keys_values)


def solution(mesh):
    small = mesh.shape["tensor"] == 2 and mesh.shape["expert"] == 4 * PLANE
    return jax.shard_map(
        per_device_dense if small else per_device,
        mesh=mesh,
        in_specs=(
            P("expert", "tensor"),
            P("tensor", None),
            P(("expert", "tensor"), None),
            P(),
            P("expert", None),
            P("expert", None),
            P("expert", None, "tensor"),
            P("expert", None, "tensor"),
            P("expert", "tensor", None),
            P(),
            P("expert", "tensor"),
            P("expert", "tensor"),
            P(),
            P(),
        ),
        out_specs=(P(("expert", "tensor"), None), P("expert", "tensor"), P("expert", "tensor")),
        check_vma=False,
    )
```

```python
import functools

import jax
import jax.numpy as jnp
from jax import lax
from jax.experimental import pallas as pl
from jax.experimental.pallas import tpu as pltpu
from jax.sharding import PartitionSpec as P

KV_HEADS = 4
TOP = 8
PLANE = 4
META = 128


EPSILON = 1e-06

SMALL = pl.CostEstimate(flops=0, bytes_accessed=0, transcendentals=0)
VMEM = pl.BlockSpec(memory_space=pltpu.VMEM)
HBM = pl.BlockSpec(memory_space=pltpu.HBM)


def normalize(values, gain):
    return values * lax.rsqrt(jnp.mean(values * values, axis=-1, keepdims=True) + EPSILON) * gain


def params(mebibytes):
    return pltpu.CompilerParams(vmem_limit_bytes=mebibytes << 20)


def lanes(start, size):
    return pl.ds(pl.multiple_of(start, size), size)


def in_hbm(value):
    return pltpu.with_memory_space_constraint(value, pltpu.HBM)


def in_vmem(value):
    return pltpu.with_memory_space_constraint(value, pltpu.VMEM)


def out_projection_kernel(chunk, a_hbm, w_hbm, mine_ref, theirs_ref, a_buf, w_buf, a_sem, sems):
    depth = w_buf.shape[0]
    count = depth // chunk
    half = mine_ref.shape[0]
    a_copy = pltpu.make_async_copy(a_hbm, a_buf, a_sem)
    a_copy.start()
    copies = []
    for i in range(count):
        rows = pl.ds(i * chunk, chunk)
        copies.append(pltpu.make_async_copy(w_hbm.at[rows], w_buf.at[rows], sems.at[i]))
    for copy in copies:
        copy.start()
    tensor = lax.axis_index("tensor")
    own = lanes(tensor * half, half)
    other = lanes((1 - tensor) * half, half)
    a_copy.wait()
    for i in range(count):
        copies[i].wait()
        at = pl.ds(i * chunk, chunk)
        both = jnp.concatenate([a_buf[own, at], a_buf[other, at]], axis=0)
        product = jnp.dot(both, w_buf[at, :], preferred_element_type=jnp.float32)
        if i == 0:
            mine_ref[...] = product[:half]
            theirs_ref[...] = product[half:]
        else:
            mine_ref[...] += product[:half]
            theirs_ref[...] += product[half:]


def out_projection(attn_out, out_weight):
    rows, depth = attn_out.shape
    width = out_weight.shape[1]
    chunk = 256
    half = pltpu.VMEM((rows // 2, width), jnp.float32)
    return pl.pallas_call(
        functools.partial(out_projection_kernel, chunk),
        out_shape=(half, half),
        in_specs=[HBM, HBM],
        out_specs=(VMEM, VMEM),
        scratch_shapes=[
            pltpu.VMEM((rows, depth), jnp.bfloat16),
            pltpu.VMEM((depth, width), jnp.bfloat16),
            pltpu.SemaphoreType.DMA,
            pltpu.SemaphoreType.DMA((depth // chunk,)),
        ],
        compiler_params=params(14),
        cost_estimate=SMALL,
        name="out_projection",
    )(in_hbm(attn_out), in_hbm(out_weight))


def first_norm_kernel(depth, count, *refs):
    mine, theirs = refs[:count], refs[count : 2 * count]
    residual_ref, gain_ref, meta_ref, tokens_ref = refs[2 * count : 2 * count + 4]
    slice_refs, first_ref = refs[2 * count + 4 : -1], refs[-1]
    rows, width = residual_ref.shape
    sub = width // (PLANE * depth)
    start = 0
    for mine_ref, theirs_ref in zip(mine, theirs):
        cols = slice(start, start + mine_ref.shape[1])
        start += mine_ref.shape[1]
        first_ref[:, cols] = (
            residual_ref[:, cols].astype(jnp.float32) + (mine_ref[...] + theirs_ref[...])
        ).astype(jnp.bfloat16)
    first = first_ref[...]
    tokens_ref[:, :width] = normalize(first.astype(jnp.float32), gain_ref[...]).astype(jnp.bfloat16)
    tokens_ref[:, width:] = meta_ref[...]
    plane = lax.axis_index("expert") % PLANE
    for d in range(PLANE):
        for z in range(depth):
            slice_refs[d][z * rows : (z + 1) * rows, :] = first_ref[
                :, lanes((z * PLANE + (plane ^ d)) * sub, sub)
            ]


def first_norm(mine, theirs, residual, gain, meta, depth):
    rows, width = residual.shape
    piece = jax.ShapeDtypeStruct((depth * rows, width // (PLANE * depth)), jnp.bfloat16)
    return pl.pallas_call(
        functools.partial(first_norm_kernel, depth, len(mine)),
        out_shape=(jax.ShapeDtypeStruct((rows, width + META), jnp.bfloat16),) + (piece,) * PLANE,
        in_specs=[VMEM] * (2 * len(mine) + 3),
        out_specs=(VMEM,) * (1 + PLANE),
        scratch_shapes=[pltpu.VMEM((rows, width), jnp.bfloat16)],
        compiler_params=params(2),
        name="first_norm",
    )(*mine, *theirs, residual, gain, meta)


def pack_kernel(depth, *refs):
    line, pieces, out_refs = refs[:depth], refs[depth : depth + PLANE], refs[depth + PLANE :]
    rows, extended = line[0].shape
    sub = pieces[0].shape[1]
    for d, ref in enumerate(out_refs):
        for z in range(depth):
            ref[z * rows : (z + 1) * rows, :extended] = line[z][...]
        ref[:, extended : extended + sub] = pieces[d][...]
        ref[:, extended + sub :] = pieces[PLANE - 1][...]


def pack(line, pieces):
    depth = len(line)
    rows, extended = line[0].shape
    shape = pltpu.VMEM((depth * rows, extended + 2 * pieces[0].shape[1]), jnp.bfloat16)
    return pl.pallas_call(
        functools.partial(pack_kernel, depth),
        out_shape=(shape,) * (PLANE - 1),
        in_specs=[VMEM] * (depth + PLANE),
        out_specs=(VMEM,) * (PLANE - 1),
        compiler_params=params(2),
        name="pack_tokens",
    )(*line, *pieces)


def load_kernel(*refs):
    sources, targets, sems = refs[:3], refs[-4:-1], refs[-1]
    copies = [
        pltpu.make_async_copy(source, target, sems.at[i])
        for i, (source, target) in enumerate(zip(sources, targets))
    ]
    for copy in copies:
        copy.start()
    for copy in copies:
        copy.wait()


def load(weights, after):
    size = sum(w.size for w in weights)
    return pl.pallas_call(
        load_kernel,
        out_shape=tuple(pltpu.VMEM(w.shape, w.dtype) for w in weights),
        in_specs=[HBM] * 3 + [pl.BlockSpec(memory_space=pl.ANY)] * len(after),
        out_specs=(VMEM,) * 3,
        scratch_shapes=[pltpu.SemaphoreType.DMA((3,))],
        compiler_params=params(2),
        cost_estimate=SMALL,
        name="load_weights",
    )(*map(in_hbm, weights), *after)


def expert_kernel(depth, chunk, count, *refs):
    block_refs, (gate_ref, up_ref, down_ref) = refs[:count], refs[count : count + 3]
    mine_ref, *theirs_refs, x_buf, act_buf = refs[count + 3 :]
    width, hidden = gate_ref.shape[1:]
    extended = x_buf.shape[1]
    start = 0
    for ref in block_refs:
        rows = ref.shape[0]
        x_buf[start : start + rows, :] = ref[:, :extended]
        start += rows
    meta = x_buf[:, width:].astype(jnp.float32)
    lane = lax.broadcasted_iota(jnp.int32, meta.shape, 1)
    chip = lax.axis_index("expert")
    expert = 2 * chip + lax.axis_index("tensor")
    chosen = (lane == expert) | (lane == expert + META // 2)
    route = 0.5 * jnp.sum(jnp.where(chosen, meta, 0.0), axis=1, keepdims=True)
    for i in range(hidden // chunk):
        cols = pl.ds(i * chunk, chunk)
        x = x_buf[:, :width]
        gate = jnp.dot(x, gate_ref[0, :, cols], preferred_element_type=jnp.float32)
        up = jnp.dot(x, up_ref[0, :, cols], preferred_element_type=jnp.float32)
        act = gate * (1.0 + jnp.tanh(0.5 * gate)) * (up * route)
        act_buf[:, i * chunk : (i + 1) * chunk] = act.astype(jnp.bfloat16)
    sub = width // (PLANE * depth)
    part = sub * depth
    half = mine_ref.shape[0]
    plane = chip % PLANE
    for d in range(PLANE):
        weight = jnp.concatenate(
            [down_ref[0, :, lanes((z * PLANE + (plane ^ d)) * sub, sub)] for z in range(depth)],
            axis=1,
        )
        out = jnp.dot(act_buf[...], weight, preferred_element_type=jnp.float32)
        cols = slice(d * part, (d + 1) * part)
        mine_ref[:, cols] = out[:half].astype(jnp.bfloat16)
        start = half
        for ref in theirs_refs:
            stop = start + ref.shape[0]
            ref[:, cols] = out[start:stop].astype(jnp.bfloat16)
            start = stop


def experts(blocks, weights, depth, pieces):
    width, hidden = weights[0].shape[1:]
    chunk = 256
    extended = width + META
    total = sum(block.shape[0] for block in blocks)
    rows = [total // 2] + [total // 2 // pieces] * pieces
    return pl.pallas_call(
        functools.partial(expert_kernel, depth, chunk, len(blocks)),
        out_shape=tuple(pltpu.VMEM((size, width), jnp.bfloat16) for size in rows),
        in_specs=[VMEM] * (len(blocks) + 3),
        out_specs=(VMEM,) * (1 + pieces),
        scratch_shapes=[
            pltpu.VMEM((total, extended), jnp.bfloat16),
            pltpu.VMEM((total, hidden), jnp.bfloat16),
        ],
        compiler_params=params(16),
        cost_estimate=pl.CostEstimate(
            flops=6 * total * width * hidden, bytes_accessed=0, transcendentals=0
        ),
        name="experts",
    )(*blocks, *weights)


def chip_sum_kernel(count, mine_ref, *refs):
    theirs, out_refs = refs[:count], refs[count:]
    part = out_refs[0].shape[1]
    start = 0
    for theirs_ref in theirs:
        rows = slice(start, start + theirs_ref.shape[0])
        start = rows.stop
        for d, ref in enumerate(out_refs):
            at = slice(d * part, (d + 1) * part)
            total = mine_ref[rows, at].astype(jnp.float32) + theirs_ref[:, at].astype(jnp.float32)
            ref[rows, :] = total.astype(jnp.bfloat16)


def chip_sum(mine, theirs):
    rows, width = mine.shape
    return pl.pallas_call(
        functools.partial(chip_sum_kernel, len(theirs)),
        out_shape=(pltpu.VMEM((rows, width // PLANE), jnp.bfloat16),) * PLANE,
        in_specs=[VMEM] * (1 + len(theirs)),
        out_specs=(VMEM,) * PLANE,
        compiler_params=params(2),
        name="chip_sum",
    )(mine, *theirs)


def plane_sum_kernel(depth, *refs):
    near, far, out_refs = refs[:PLANE], refs[PLANE : 2 * PLANE], refs[2 * PLANE :]
    group = far[0].shape[0]
    rows = group // depth
    for k in range(PLANE):
        for z in range(depth):
            total = 0.0
            for d in range(PLANE):
                block = k ^ d
                ref, skip = (far[d], 0) if block == PLANE - 1 else (near[d], block * group)
                start = skip + z * rows
                total = total + ref[start : start + rows, :].astype(jnp.float32)
            out_refs[z][k * rows : (k + 1) * rows, :] = total.astype(jnp.bfloat16)


def plane_sum(near, far, depth):
    rows, part = far[0].shape
    return pl.pallas_call(
        functools.partial(plane_sum_kernel, depth),
        out_shape=(pltpu.VMEM((PLANE * rows // depth, part), jnp.bfloat16),) * depth,
        in_specs=[VMEM] * (2 * PLANE),
        out_specs=(VMEM,) * depth,
        compiler_params=params(4),
        name="plane_sum",
    )(*near, *far)


def second_norm_kernel(depth, *refs):
    parts, packed = refs[:depth], refs[depth : depth + PLANE + 1]
    gain_ref, scaled_ref, next_ref = refs[depth + PLANE + 1 :]
    rows = packed[0].shape[0] // depth
    part = parts[0].shape[1]
    sub = part // depth
    skip = packed[0].shape[1] - 2 * sub
    lane = lax.broadcasted_iota(jnp.int32, (rows, META), 1)
    plane = lax.axis_index("expert") % PLANE
    gain = jnp.concatenate(
        [gain_ref[:, lanes((z * PLANE + plane) * sub, sub)] for z in range(depth)], axis=1
    )
    for d in range(PLANE):
        at = slice(d * rows, (d + 1) * rows)
        total = parts[0][at, :].astype(jnp.float32)
        for ref in parts[1:]:
            total = total + ref[at, :].astype(jnp.float32)
        if d < PLANE - 1:
            first = packed[d][:, skip : skip + sub]
        else:
            first = jnp.concatenate([ref[:, skip + sub :] for ref in packed[d:]], axis=0)
        first = jnp.concatenate([first[z * rows : (z + 1) * rows] for z in range(depth)], axis=1)
        following = (first.astype(jnp.float32) + total).astype(jnp.bfloat16)
        next_ref[at, :] = following
        wide = following.astype(jnp.float32)
        scaled_ref[at, :part] = (wide * gain).astype(jnp.bfloat16)
        squares = jnp.sum(wide * wide, axis=1, keepdims=True)
        high = squares.astype(jnp.bfloat16).astype(jnp.float32)
        low = squares - high
        scaled_ref[at, part:] = jnp.where(
            lane == 0, high, jnp.where(lane == 1, low, 0.0)
        ).astype(jnp.bfloat16)


def second_norm(parts, packed, gain):
    depth = len(parts)
    rows, part = parts[0].shape
    return pl.pallas_call(
        functools.partial(second_norm_kernel, depth),
        out_shape=(
            jax.ShapeDtypeStruct((rows, part + META), jnp.bfloat16),
            jax.ShapeDtypeStruct((rows, part), jnp.bfloat16),
        ),
        in_specs=[VMEM] * (depth + PLANE + 2),
        out_specs=(VMEM, VMEM),
        compiler_params=params(4),
        name="second_norm",
    )(*parts, *packed, gain)


def projection_kernel(chunk, mine_ref, theirs_ref, next_ref, w_hbm, *refs):
    out_refs, (w_buf, sems) = refs[:PLANE], refs[PLANE:]
    cols = w_buf.shape[1]
    copies = []
    for i in range(sems.shape[0]):
        at = lanes(i * META, META)
        copies.append(pltpu.make_async_copy(w_hbm.at[at], w_buf.at[at], sems.at[i]))
    for copy in copies:
        copy.start()
    rows, extended = mine_ref.shape
    part = extended - META
    block = rows // PLANE
    tensor = lax.axis_index("tensor")
    own = lanes(tensor * block, block)
    other = lanes((1 - tensor) * block, block)
    for d in range(PLANE):
        at = slice(d * block, (d + 1) * block)
        out_refs[d][own, cols : cols + META] = mine_ref[at, part:]
        out_refs[d][other, cols : cols + META] = theirs_ref[at, part:]
        out_refs[d][:block, cols + META :] = next_ref[at, : part // 2]
        out_refs[d][block:, cols + META :] = next_ref[at, part // 2 :]
    both = jnp.concatenate([mine_ref[:, :part], theirs_ref[:, :part]], axis=0)
    for copy in copies:
        copy.wait()
    for i in range(cols // chunk):
        at = slice(i * chunk, (i + 1) * chunk)
        product = jnp.dot(both, w_buf[:, at], preferred_element_type=jnp.float32).astype(
            jnp.bfloat16
        )
        for d in range(PLANE):
            out_refs[d][own, at] = product[d * block : (d + 1) * block]
            out_refs[d][other, at] = product[rows + d * block : rows + (d + 1) * block]


def projection(mine, theirs, following, weight):
    rows, part = following.shape
    cols = weight.shape[1]
    chunk = 512
    shape = pltpu.VMEM((2 * rows // PLANE, cols + META + part // 2), jnp.bfloat16)
    return pl.pallas_call(
        functools.partial(projection_kernel, chunk),
        out_shape=(shape,) * PLANE,
        in_specs=[VMEM] * 3 + [HBM],
        out_specs=(VMEM,) * PLANE,
        scratch_shapes=[
            pltpu.VMEM((part, cols), jnp.bfloat16),
            pltpu.SemaphoreType.DMA((part // META,)),
        ],
        compiler_params=params(8),
        cost_estimate=SMALL,
        name="qkv_projection",
    )(mine, theirs, following, in_hbm(weight))


def head_norm_kernel(depth, *refs):
    parts, q_gain_ref, k_gain_ref = refs[:PLANE], refs[PLANE], refs[PLANE + 1]
    next_ref, q_ref, kv_ref = refs[PLANE + 2 :]
    width = next_ref.shape[1]
    q_cols, kv_cols = q_ref.shape[1], kv_ref.shape[1]
    cols = q_cols + kv_cols
    head = q_gain_ref.shape[1]

    def total(at):
        value = parts[0][:, at].astype(jnp.float32)
        for ref in parts[1:]:
            value = value + ref[:, at].astype(jnp.float32)
        return value

    squares = jnp.sum(total(slice(cols, cols + META)), axis=1, keepdims=True)
    scale = lax.rsqrt(squares / width + EPSILON)
    for h in range(q_cols // head):
        at = slice(h * head, (h + 1) * head)
        q_ref[:, at] = normalize(total(at) * scale, q_gain_ref[...]).astype(jnp.bfloat16)
    tensor = lax.axis_index("tensor")
    for h in range(kv_cols // head):
        at = slice(h * head, (h + 1) * head)
        raw = total(slice(q_cols + h * head, q_cols + (h + 1) * head)) * scale
        is_key = tensor * (kv_cols // head) + h < KV_HEADS
        kv_ref[:, at] = jnp.where(is_key, normalize(raw, k_gain_ref[...]), raw).astype(
            jnp.bfloat16
        )
    plane = lax.axis_index("expert") % PLANE
    rows = next_ref.shape[0]
    sub = width // (PLANE * depth)
    for d in range(PLANE):
        for z in range(depth):
            top = z * sub * 2 // (depth * sub)
            start = cols + META + z * sub - top * (depth * sub // 2)
            next_ref[:, lanes((z * PLANE + (plane ^ d)) * sub, sub)] = parts[d][
                top * rows : (top + 1) * rows, start : start + sub
            ]


def head_norm(parts, q_gain, k_gain, q_cols, kv_cols, rows, width, depth):
    both = parts[0].shape[0]
    return pl.pallas_call(
        functools.partial(head_norm_kernel, depth),
        out_shape=(
            jax.ShapeDtypeStruct((rows, width), jnp.bfloat16),
            jax.ShapeDtypeStruct((both, q_cols), jnp.bfloat16),
            jax.ShapeDtypeStruct((both, kv_cols), jnp.bfloat16),
        ),
        in_specs=[VMEM] * (PLANE + 2),
        out_specs=(VMEM, VMEM, VMEM),
        compiler_params=params(4),
        name="head_norm",
    )(*parts, q_gain, k_gain)


def per_device_dense(
    attn_out,
    out_weight,
    residual,
    attn_gain,
    expert_ids,
    route_weights,
    w_gate,
    w_up,
    w_down,
    input_gain,
    q_weight,
    kv_weight,
    q_gain,
    k_gain,
):
    n_expert = lax.axis_size("expert")
    depth = n_expert // PLANE
    rows, width = residual.shape
    tensor_index = lax.axis_index("tensor").astype(jnp.int32)

    def to_core(value):
        return lax.ppermute(value, "tensor", [(0, 1), (1, 0)])

    def to_expert(value, offset):
        return lax.ppermute(value, "expert", [(i, i ^ offset) for i in range(n_expert)])

    def to_z(values):
        return [to_expert(v, d * PLANE) if d else v for d, v in enumerate(values)]

    def to_plane(values):
        return [to_expert(v, d) if d else v for d, v in enumerate(values)]

    own_ids = lax.dynamic_slice_in_dim(expert_ids, tensor_index * rows, rows, 0)
    own_route = lax.dynamic_slice_in_dim(route_weights, tensor_index * rows, rows, 0)
    chosen = own_ids[:, :, None] == jnp.arange(META // 2, dtype=jnp.int32)[None, None, :]
    dense = jnp.sum(jnp.where(chosen, own_route[:, :, None], 0.0), axis=1)
    high = lax.reduce_precision(dense, 8, 7)
    meta = jnp.concatenate([high, dense - high], axis=1).astype(jnp.bfloat16)

    lines = [list(range(i, n_expert, PLANE)) for i in range(PLANE)]
    mine, theirs = out_projection(attn_out, out_weight)
    mine, q_own, kv_own = lax.optimization_barrier((mine, q_weight, kv_weight))
    joined = jnp.concatenate([q_own, kv_own], axis=1)
    tokens, *firsts = first_norm(
        (mine,), (to_core(theirs),), residual, attn_gain[None, :], meta, depth
    )
    tokens, joined = lax.optimization_barrier((tokens, joined))
    qkv = lax.all_gather(joined, "expert", axis=0, tiled=True, axis_index_groups=lines)
    weights = load((w_gate, w_up, w_down), (tokens,))
    line = to_z([tokens] * depth)
    *line, gate, up, down = lax.optimization_barrier((*line, *weights))
    weights = (gate, up, down)
    near = to_plane(pack(line, firsts))
    cut = near[0].shape[0] // 2
    one, two = near[1][:cut], near[2][cut:]
    far = [to_expert(one, 2), to_expert(two, 1)]
    mine, *theirs = experts((*near, *map(to_core, near)), weights, depth, len(near))
    near_sum = chip_sum(mine, list(map(to_core, theirs)))
    far_both = [*far, *map(to_core, far)]
    tied = lax.optimization_barrier((*near_sum, *far_both))
    near_sum, far_both = tied[:PLANE], tied[PLANE:]
    mine, *theirs = experts(far_both, weights, depth, 1)
    far_sum = chip_sum(mine, list(map(to_core, theirs)))
    parts = plane_sum(to_plane(near_sum), to_plane(far_sum), depth)
    scaled, following = second_norm(to_z(parts), (*near, *far), input_gain[None, :])
    products = to_plane(projection(scaled, to_core(scaled), following, qkv))
    return head_norm(
        products,
        q_gain[None, :],
        k_gain[None, :],
        q_weight.shape[1],
        kv_weight.shape[1],
        rows,
        width,
        depth,
    )


def per_device(
    attn_out,
    out_weight,
    residual,
    attn_gain,
    expert_ids,
    route_weights,
    w_gate,
    w_up,
    w_down,
    input_gain,
    q_weight,
    kv_weight,
    q_gain,
    k_gain,
):
    n_expert = lax.axis_size("expert")
    n_tensor = lax.axis_size("tensor")
    share = n_tensor // 2
    tensor_index = lax.axis_index("tensor")
    group_rows = attn_out.shape[0]
    width = residual.shape[1]
    half = tensor_index // share
    capacity = 3 * group_rows * TOP // (4 * n_expert)
    all_experts = 2 * n_expert
    attn_rows = lax.psum_scatter(
        jnp.dot(attn_out, out_weight, preferred_element_type=jnp.float32),
        "tensor",
        scatter_dimension=0,
        tiled=True,
    )
    first_residual = (residual.astype(jnp.float32) + attn_rows).astype(jnp.bfloat16)
    normed = normalize(first_residual.astype(jnp.float32), attn_gain).astype(jnp.bfloat16)
    group_normed = lax.all_gather(normed, "tensor", axis=0, tiled=True)
    flat_ids = expert_ids.reshape(-1)
    onehot = (flat_ids[:, None] == jnp.arange(all_experts, dtype=jnp.int32)[None, :]).astype(
        jnp.int32
    )
    earlier = jnp.cumsum(onehot, axis=0) - onehot
    rank = jnp.sum(earlier * onehot, axis=1)
    dest = flat_ids * capacity + rank
    row_owner = jnp.arange(flat_ids.shape[0], dtype=jnp.int32) // TOP
    slot_row = jnp.full((all_experts * capacity,), group_rows, jnp.int32).at[dest].set(row_owner)
    slot_weight = (
        jnp.zeros((all_experts * capacity,), jnp.float32).at[dest].set(route_weights.reshape(-1))
    )
    own_slots = lax.dynamic_index_in_dim(
        slot_row.reshape(n_expert, 2, capacity), half, 1, keepdims=False
    )
    own_weights = lax.dynamic_index_in_dim(
        slot_weight.reshape(n_expert, 2, capacity), half, 1, keepdims=False
    )
    padded_rows = jnp.concatenate([group_normed, jnp.zeros((1, width), jnp.bfloat16)], axis=0)
    gate_w = w_gate[0]
    up_w = w_up[0]
    down_w = w_down[0]
    outgoing = jnp.take(padded_rows, own_slots, axis=0)
    arrived = lax.all_to_all(outgoing, "expert", split_axis=0, concat_axis=0, tiled=True)
    flat = arrived.reshape(-1, width)
    gate = jnp.dot(flat, gate_w, preferred_element_type=jnp.float32)
    up = jnp.dot(flat, up_w, preferred_element_type=jnp.float32)
    act = (jax.nn.silu(gate) * up).astype(jnp.bfloat16)
    part = jnp.dot(act, down_w, preferred_element_type=jnp.float32).astype(jnp.bfloat16)
    send_part = part.reshape(arrived.shape)
    returned = lax.all_to_all(send_part, "expert", split_axis=0, concat_axis=0, tiled=True)
    weighted = own_weights.reshape(-1)[:, None] * returned.reshape(-1, width).astype(jnp.float32)
    term = (
        jnp.zeros((group_rows + 1, width), jnp.float32)
        .at[own_slots.reshape(-1)]
        .add(weighted)[:group_rows]
    )
    expert_sum = lax.psum_scatter(
        term.astype(jnp.bfloat16), "tensor", scatter_dimension=0, tiled=True
    ).astype(jnp.float32)
    next_residual = (first_residual.astype(jnp.float32) + expert_sum).astype(jnp.bfloat16)
    own_normed = normalize(next_residual.astype(jnp.float32), input_gain).astype(jnp.bfloat16)
    next_normed = lax.all_gather(own_normed, "tensor", axis=0, tiled=True)
    query_cols = q_weight.shape[1]
    kv_cols = kv_weight.shape[1]
    query_raw = jnp.dot(
        next_normed,
        lax.all_gather(q_weight, "expert", axis=0, tiled=True),
        preferred_element_type=jnp.float32,
    )
    kv_raw = jnp.dot(
        next_normed,
        lax.all_gather(kv_weight, "expert", axis=0, tiled=True),
        preferred_element_type=jnp.float32,
    )
    head_size = q_gain.shape[0]
    queries = (
        normalize(query_raw.reshape(group_rows, -1, head_size), q_gain)
        .reshape(group_rows, query_cols)
        .astype(jnp.bfloat16)
    )
    heads_here = kv_cols // head_size
    head_number = tensor_index * heads_here + jnp.arange(heads_here, dtype=jnp.int32)
    is_key = head_number < KV_HEADS
    kv_shaped = kv_raw.reshape(group_rows, heads_here, head_size)
    keys_values = (
        jnp.where(is_key[None, :, None], normalize(kv_shaped, k_gain), kv_shaped)
        .reshape(group_rows, kv_cols)
        .astype(jnp.bfloat16)
    )
    return (next_residual, queries, keys_values)


def solution(mesh):
    small = mesh.shape["tensor"] == 2 and mesh.shape["expert"] == 4 * PLANE
    return jax.shard_map(
        per_device_dense if small else per_device,
        mesh=mesh,
        in_specs=(
            P("expert", "tensor"),
            P("tensor", None),
            P(("expert", "tensor"), None),
            P(),
            P("expert", None),
            P("expert", None),
            P("expert", None, "tensor"),
            P("expert", None, "tensor"),
            P("expert", "tensor", None),
            P(),
            P("expert", "tensor"),
            P("expert", "tensor"),
            P(),
            P(),
        ),
        out_specs=(P(("expert", "tensor"), None), P("expert", "tensor"), P("expert", "tensor")),
        check_vma=False,
    )
```

```python
import functools

import jax
import jax.numpy as jnp
from jax import lax
from jax.experimental import pallas as pl
from jax.experimental.pallas import tpu as pltpu
from jax.sharding import PartitionSpec as P

KV_HEADS = 4
TOP = 8
PLANE = 4
META = 128


EPSILON = 1e-06

SMALL = pl.CostEstimate(flops=0, bytes_accessed=0, transcendentals=0)
VMEM = pl.BlockSpec(memory_space=pltpu.VMEM)
HBM = pl.BlockSpec(memory_space=pltpu.HBM)


def normalize(values, gain):
    return values * lax.rsqrt(jnp.mean(values * values, axis=-1, keepdims=True) + EPSILON) * gain


def params(mebibytes):
    return pltpu.CompilerParams(vmem_limit_bytes=mebibytes << 20)


def lanes(start, size):
    return pl.ds(pl.multiple_of(start, size), size)


def in_hbm(value):
    return pltpu.with_memory_space_constraint(value, pltpu.HBM)


def in_vmem(value):
    return pltpu.with_memory_space_constraint(value, pltpu.VMEM)


def out_projection_kernel(chunk, a_hbm, w_hbm, mine_ref, theirs_ref, a_buf, w_buf, a_sem, sems):
    depth = w_buf.shape[0]
    count = depth // chunk
    half = mine_ref.shape[0]
    a_copy = pltpu.make_async_copy(a_hbm, a_buf, a_sem)
    a_copy.start()
    copies = []
    for i in range(count):
        rows = pl.ds(i * chunk, chunk)
        copies.append(pltpu.make_async_copy(w_hbm.at[rows], w_buf.at[rows], sems.at[i]))
    for copy in copies:
        copy.start()
    tensor = lax.axis_index("tensor")
    own = lanes(tensor * half, half)
    other = lanes((1 - tensor) * half, half)
    a_copy.wait()
    for i in range(count):
        copies[i].wait()
        at = pl.ds(i * chunk, chunk)
        both = jnp.concatenate([a_buf[own, at], a_buf[other, at]], axis=0)
        product = jnp.dot(both, w_buf[at, :], preferred_element_type=jnp.float32)
        if i == 0:
            mine_ref[...] = product[:half]
            theirs_ref[...] = product[half:]
        else:
            mine_ref[...] += product[:half]
            theirs_ref[...] += product[half:]


def out_projection(attn_out, out_weight):
    rows, depth = attn_out.shape
    width = out_weight.shape[1]
    chunk = 256
    half = pltpu.VMEM((rows // 2, width), jnp.float32)
    return pl.pallas_call(
        functools.partial(out_projection_kernel, chunk),
        out_shape=(half, half),
        in_specs=[HBM, HBM],
        out_specs=(VMEM, VMEM),
        scratch_shapes=[
            pltpu.VMEM((rows, depth), jnp.bfloat16),
            pltpu.VMEM((depth, width), jnp.bfloat16),
            pltpu.SemaphoreType.DMA,
            pltpu.SemaphoreType.DMA((depth // chunk,)),
        ],
        compiler_params=params(14),
        cost_estimate=SMALL,
        name="out_projection",
    )(in_hbm(attn_out), in_hbm(out_weight))


def first_norm_kernel(depth, count, *refs):
    mine, theirs = refs[:count], refs[count : 2 * count]
    residual_ref, gain_ref, meta_ref, tokens_ref = refs[2 * count : 2 * count + 4]
    slice_refs, first_ref = refs[2 * count + 4 : -1], refs[-1]
    rows, width = residual_ref.shape
    sub = width // (PLANE * depth)
    start = 0
    for mine_ref, theirs_ref in zip(mine, theirs):
        cols = slice(start, start + mine_ref.shape[1])
        start += mine_ref.shape[1]
        first_ref[:, cols] = (
            residual_ref[:, cols].astype(jnp.float32) + (mine_ref[...] + theirs_ref[...])
        ).astype(jnp.bfloat16)
    first = first_ref[...]
    tokens_ref[:, :width] = normalize(first.astype(jnp.float32), gain_ref[...]).astype(jnp.bfloat16)
    tokens_ref[:, width:] = meta_ref[...]
    plane = lax.axis_index("expert") % PLANE
    for d in range(PLANE):
        for z in range(depth):
            slice_refs[d][z * rows : (z + 1) * rows, :] = first_ref[
                :, lanes((z * PLANE + (plane ^ d)) * sub, sub)
            ]


def first_norm(mine, theirs, residual, gain, meta, depth):
    rows, width = residual.shape
    piece = jax.ShapeDtypeStruct((depth * rows, width // (PLANE * depth)), jnp.bfloat16)
    return pl.pallas_call(
        functools.partial(first_norm_kernel, depth, len(mine)),
        out_shape=(jax.ShapeDtypeStruct((rows, width + META), jnp.bfloat16),) + (piece,) * PLANE,
        in_specs=[VMEM] * (2 * len(mine) + 3),
        out_specs=(VMEM,) * (1 + PLANE),
        scratch_shapes=[pltpu.VMEM((rows, width), jnp.bfloat16)],
        compiler_params=params(2),
        name="first_norm",
    )(*mine, *theirs, residual, gain, meta)


def pack_kernel(depth, *refs):
    line, pieces, out_refs = refs[:depth], refs[depth : depth + PLANE], refs[depth + PLANE :]
    rows, extended = line[0].shape
    sub = pieces[0].shape[1]
    for d, ref in enumerate(out_refs):
        for z in range(depth):
            ref[z * rows : (z + 1) * rows, :extended] = line[z][...]
        ref[:, extended : extended + sub] = pieces[d][...]
        ref[:, extended + sub :] = pieces[PLANE - 1][...]


def pack(line, pieces):
    depth = len(line)
    rows, extended = line[0].shape
    shape = pltpu.VMEM((depth * rows, extended + 2 * pieces[0].shape[1]), jnp.bfloat16)
    return pl.pallas_call(
        functools.partial(pack_kernel, depth),
        out_shape=(shape,) * (PLANE - 1),
        in_specs=[VMEM] * (depth + PLANE),
        out_specs=(VMEM,) * (PLANE - 1),
        compiler_params=params(2),
        name="pack_tokens",
    )(*line, *pieces)


def load_kernel(*refs):
    sources, targets, sems = refs[:3], refs[-4:-1], refs[-1]
    copies = [
        pltpu.make_async_copy(source, target, sems.at[i])
        for i, (source, target) in enumerate(zip(sources, targets))
    ]
    for copy in copies:
        copy.start()
    for copy in copies:
        copy.wait()


def load(weights, after):
    size = sum(w.size for w in weights)
    return pl.pallas_call(
        load_kernel,
        out_shape=tuple(pltpu.VMEM(w.shape, w.dtype) for w in weights),
        in_specs=[HBM] * 3 + [pl.BlockSpec(memory_space=pl.ANY)] * len(after),
        out_specs=(VMEM,) * 3,
        scratch_shapes=[pltpu.SemaphoreType.DMA((3,))],
        compiler_params=params(2),
        cost_estimate=SMALL,
        name="load_weights",
    )(*map(in_hbm, weights), *after)


def expert_kernel(depth, chunk, count, *refs):
    block_refs, (gate_ref, up_ref, down_ref) = refs[:count], refs[count : count + 3]
    mine_ref, *theirs_refs, x_buf, act_buf = refs[count + 3 :]
    width, hidden = gate_ref.shape[1:]
    extended = x_buf.shape[1]
    start = 0
    for ref in block_refs:
        rows = ref.shape[0]
        x_buf[start : start + rows, :] = ref[:, :extended]
        start += rows
    meta = x_buf[:, width:].astype(jnp.float32)
    lane = lax.broadcasted_iota(jnp.int32, meta.shape, 1)
    chip = lax.axis_index("expert")
    expert = 2 * chip + lax.axis_index("tensor")
    chosen = (lane == expert) | (lane == expert + META // 2)
    route = 0.5 * jnp.sum(jnp.where(chosen, meta, 0.0), axis=1, keepdims=True)
    for i in range(hidden // chunk):
        cols = pl.ds(i * chunk, chunk)
        x = x_buf[:, :width]
        gate = jnp.dot(x, gate_ref[0, :, cols], preferred_element_type=jnp.float32)
        up = jnp.dot(x, up_ref[0, :, cols], preferred_element_type=jnp.float32)
        act = gate * (1.0 + jnp.tanh(0.5 * gate)) * (up * route)
        act_buf[:, i * chunk : (i + 1) * chunk] = act.astype(jnp.bfloat16)
    sub = width // (PLANE * depth)
    part = sub * depth
    half = mine_ref.shape[0]
    plane = chip % PLANE
    for d in range(PLANE):
        weight = jnp.concatenate(
            [down_ref[0, :, lanes((z * PLANE + (plane ^ d)) * sub, sub)] for z in range(depth)],
            axis=1,
        )
        out = jnp.dot(act_buf[...], weight, preferred_element_type=jnp.float32)
        cols = slice(d * part, (d + 1) * part)
        mine_ref[:, cols] = out[:half].astype(jnp.bfloat16)
        start = half
        for ref in theirs_refs:
            stop = start + ref.shape[0]
            ref[:, cols] = out[start:stop].astype(jnp.bfloat16)
            start = stop


def experts(blocks, weights, depth, pieces):
    width, hidden = weights[0].shape[1:]
    chunk = 256
    extended = width + META
    total = sum(block.shape[0] for block in blocks)
    rows = [total // 2] + [total // 2 // pieces] * pieces
    return pl.pallas_call(
        functools.partial(expert_kernel, depth, chunk, len(blocks)),
        out_shape=tuple(pltpu.VMEM((size, width), jnp.bfloat16) for size in rows),
        in_specs=[VMEM] * (len(blocks) + 3),
        out_specs=(VMEM,) * (1 + pieces),
        scratch_shapes=[
            pltpu.VMEM((total, extended), jnp.bfloat16),
            pltpu.VMEM((total, hidden), jnp.bfloat16),
        ],
        compiler_params=params(16),
        cost_estimate=pl.CostEstimate(
            flops=6 * total * width * hidden, bytes_accessed=0, transcendentals=0
        ),
        name="experts",
    )(*blocks, *weights)


def chip_sum_kernel(count, mine_ref, *refs):
    theirs, out_refs = refs[:count], refs[count:]
    part = out_refs[0].shape[1]
    start = 0
    for theirs_ref in theirs:
        rows = slice(start, start + theirs_ref.shape[0])
        start = rows.stop
        for d, ref in enumerate(out_refs):
            at = slice(d * part, (d + 1) * part)
            total = mine_ref[rows, at].astype(jnp.float32) + theirs_ref[:, at].astype(jnp.float32)
            ref[rows, :] = total.astype(jnp.bfloat16)


def chip_sum(mine, theirs):
    rows, width = mine.shape
    return pl.pallas_call(
        functools.partial(chip_sum_kernel, len(theirs)),
        out_shape=(pltpu.VMEM((rows, width // PLANE), jnp.bfloat16),) * PLANE,
        in_specs=[VMEM] * (1 + len(theirs)),
        out_specs=(VMEM,) * PLANE,
        compiler_params=params(2),
        name="chip_sum",
    )(mine, *theirs)


def plane_sum_kernel(depth, *refs):
    near, far, out_refs = refs[:PLANE], refs[PLANE : 2 * PLANE], refs[2 * PLANE :]
    group = far[0].shape[0]
    rows = group // depth
    for k in range(PLANE):
        for z in range(depth):
            total = 0.0
            for d in range(PLANE):
                block = k ^ d
                ref, skip = (far[d], 0) if block == PLANE - 1 else (near[d], block * group)
                start = skip + z * rows
                total = total + ref[start : start + rows, :].astype(jnp.float32)
            out_refs[z][k * rows : (k + 1) * rows, :] = total.astype(jnp.bfloat16)


def plane_sum(near, far, depth):
    rows, part = far[0].shape
    return pl.pallas_call(
        functools.partial(plane_sum_kernel, depth),
        out_shape=(pltpu.VMEM((PLANE * rows // depth, part), jnp.bfloat16),) * depth,
        in_specs=[VMEM] * (2 * PLANE),
        out_specs=(VMEM,) * depth,
        compiler_params=params(4),
        name="plane_sum",
    )(*near, *far)


def second_norm_kernel(depth, *refs):
    parts, packed = refs[:depth], refs[depth : depth + PLANE + 1]
    gain_ref, scaled_ref, next_ref = refs[depth + PLANE + 1 :]
    rows = packed[0].shape[0] // depth
    part = parts[0].shape[1]
    sub = part // depth
    skip = packed[0].shape[1] - 2 * sub
    lane = lax.broadcasted_iota(jnp.int32, (rows, META), 1)
    plane = lax.axis_index("expert") % PLANE
    gain = jnp.concatenate(
        [gain_ref[:, lanes((z * PLANE + plane) * sub, sub)] for z in range(depth)], axis=1
    )
    for d in range(PLANE):
        at = slice(d * rows, (d + 1) * rows)
        total = parts[0][at, :].astype(jnp.float32)
        for ref in parts[1:]:
            total = total + ref[at, :].astype(jnp.float32)
        if d < PLANE - 1:
            first = packed[d][:, skip : skip + sub]
        else:
            first = jnp.concatenate([ref[:, skip + sub :] for ref in packed[d:]], axis=0)
        first = jnp.concatenate([first[z * rows : (z + 1) * rows] for z in range(depth)], axis=1)
        following = (first.astype(jnp.float32) + total).astype(jnp.bfloat16)
        next_ref[at, :] = following
        wide = following.astype(jnp.float32)
        scaled_ref[at, :part] = (wide * gain).astype(jnp.bfloat16)
        squares = jnp.sum(wide * wide, axis=1, keepdims=True)
        high = squares.astype(jnp.bfloat16).astype(jnp.float32)
        low = squares - high
        scaled_ref[at, part:] = jnp.where(
            lane == 0, high, jnp.where(lane == 1, low, 0.0)
        ).astype(jnp.bfloat16)


def second_norm(parts, packed, gain):
    depth = len(parts)
    rows, part = parts[0].shape
    return pl.pallas_call(
        functools.partial(second_norm_kernel, depth),
        out_shape=(
            jax.ShapeDtypeStruct((rows, part + META), jnp.bfloat16),
            jax.ShapeDtypeStruct((rows, part), jnp.bfloat16),
        ),
        in_specs=[VMEM] * (depth + PLANE + 2),
        out_specs=(VMEM, VMEM),
        compiler_params=params(4),
        name="second_norm",
    )(*parts, *packed, gain)


def projection_kernel(chunk, mine_ref, theirs_ref, next_ref, *refs):
    halves, out_refs, (w_buf, sems) = refs[:2], refs[2 : 2 + PLANE], refs[2 + PLANE :]
    cols = w_buf.shape[1]
    copies = []
    piece = w_buf.shape[0] // sems.shape[0]
    for i in range(sems.shape[0]):
        source = halves[i % 2].at[pl.ds(i // 2 * piece, piece)]
        target = w_buf.at[pl.ds(i * piece, piece)]
        copies.append(pltpu.make_async_copy(source, target, sems.at[i]))
    for copy in copies:
        copy.start()
    rows, extended = mine_ref.shape
    part = extended - META
    block = rows // PLANE
    tensor = lax.axis_index("tensor")
    own = lanes(tensor * block, block)
    other = lanes((1 - tensor) * block, block)
    for d in range(PLANE):
        at = slice(d * block, (d + 1) * block)
        out_refs[d][own, cols : cols + META] = mine_ref[at, part:]
        out_refs[d][other, cols : cols + META] = theirs_ref[at, part:]
        out_refs[d][:block, cols + META :] = next_ref[at, : part // 2]
        out_refs[d][block:, cols + META :] = next_ref[at, part // 2 :]
    both = jnp.concatenate([mine_ref[:, :part], theirs_ref[:, :part]], axis=0)
    for copy in copies:
        copy.wait()
    for i in range(cols // chunk):
        at = slice(i * chunk, (i + 1) * chunk)
        product = jnp.dot(both, w_buf[:, at], preferred_element_type=jnp.float32).astype(
            jnp.bfloat16
        )
        for d in range(PLANE):
            out_refs[d][own, at] = product[d * block : (d + 1) * block]
            out_refs[d][other, at] = product[rows + d * block : rows + (d + 1) * block]


def projection(mine, theirs, following, weight, depth):
    rows, part = following.shape
    cols = weight[0].shape[1]
    chunk = 512
    shape = pltpu.VMEM((2 * rows // PLANE, cols + META + part // 2), jnp.bfloat16)
    return pl.pallas_call(
        functools.partial(projection_kernel, chunk),
        out_shape=(shape,) * PLANE,
        in_specs=[VMEM] * 3 + [HBM] * 2,
        out_specs=(VMEM,) * PLANE,
        scratch_shapes=[
            pltpu.VMEM((part, cols), jnp.bfloat16),
            pltpu.SemaphoreType.DMA((2 * depth,)),
        ],
        compiler_params=params(8),
        cost_estimate=SMALL,
        name="qkv_projection",
    )(mine, theirs, following, *map(in_hbm, weight))


def head_norm_kernel(depth, *refs):
    parts, q_gain_ref, k_gain_ref = refs[:PLANE], refs[PLANE], refs[PLANE + 1]
    next_ref, q_ref, kv_ref = refs[PLANE + 2 :]
    width = next_ref.shape[1]
    q_cols, kv_cols = q_ref.shape[1], kv_ref.shape[1]
    cols = q_cols + kv_cols
    head = q_gain_ref.shape[1]

    def total(at):
        value = parts[0][:, at].astype(jnp.float32)
        for ref in parts[1:]:
            value = value + ref[:, at].astype(jnp.float32)
        return value

    squares = jnp.sum(total(slice(cols, cols + META)), axis=1, keepdims=True)
    scale = lax.rsqrt(squares / width + EPSILON)
    for h in range(q_cols // head):
        at = slice(h * head, (h + 1) * head)
        q_ref[:, at] = normalize(total(at) * scale, q_gain_ref[...]).astype(jnp.bfloat16)
    tensor = lax.axis_index("tensor")
    for h in range(kv_cols // head):
        at = slice(h * head, (h + 1) * head)
        raw = total(slice(q_cols + h * head, q_cols + (h + 1) * head)) * scale
        is_key = tensor * (kv_cols // head) + h < KV_HEADS
        kv_ref[:, at] = jnp.where(is_key, normalize(raw, k_gain_ref[...]), raw).astype(
            jnp.bfloat16
        )
    plane = lax.axis_index("expert") % PLANE
    rows = next_ref.shape[0]
    sub = width // (PLANE * depth)
    for d in range(PLANE):
        for z in range(depth):
            top = z * sub * 2 // (depth * sub)
            start = cols + META + z * sub - top * (depth * sub // 2)
            next_ref[:, lanes((z * PLANE + (plane ^ d)) * sub, sub)] = parts[d][
                top * rows : (top + 1) * rows, start : start + sub
            ]


def head_norm(parts, q_gain, k_gain, q_cols, kv_cols, rows, width, depth):
    both = parts[0].shape[0]
    return pl.pallas_call(
        functools.partial(head_norm_kernel, depth),
        out_shape=(
            jax.ShapeDtypeStruct((rows, width), jnp.bfloat16),
            jax.ShapeDtypeStruct((both, q_cols), jnp.bfloat16),
            jax.ShapeDtypeStruct((both, kv_cols), jnp.bfloat16),
        ),
        in_specs=[VMEM] * (PLANE + 2),
        out_specs=(VMEM, VMEM, VMEM),
        compiler_params=params(4),
        name="head_norm",
    )(*parts, q_gain, k_gain)


def per_device_dense(
    attn_out,
    out_weight,
    residual,
    attn_gain,
    expert_ids,
    route_weights,
    w_gate,
    w_up,
    w_down,
    input_gain,
    q_weight,
    kv_weight,
    q_gain,
    k_gain,
):
    n_expert = lax.axis_size("expert")
    depth = n_expert // PLANE
    rows, width = residual.shape
    tensor_index = lax.axis_index("tensor").astype(jnp.int32)

    def to_core(value):
        return lax.ppermute(value, "tensor", [(0, 1), (1, 0)])

    def to_expert(value, offset):
        return lax.ppermute(value, "expert", [(i, i ^ offset) for i in range(n_expert)])

    def to_z(values):
        return [to_expert(v, d * PLANE) if d else v for d, v in enumerate(values)]

    def to_plane(values):
        return [to_expert(v, d) if d else v for d, v in enumerate(values)]

    own_ids = lax.dynamic_slice_in_dim(expert_ids, tensor_index * rows, rows, 0)
    own_route = lax.dynamic_slice_in_dim(route_weights, tensor_index * rows, rows, 0)
    chosen = own_ids[:, :, None] == jnp.arange(META // 2, dtype=jnp.int32)[None, None, :]
    dense = jnp.sum(jnp.where(chosen, own_route[:, :, None], 0.0), axis=1)
    high = lax.reduce_precision(dense, 8, 7)
    meta = jnp.concatenate([high, dense - high], axis=1).astype(jnp.bfloat16)

    lines = [list(range(i, n_expert, PLANE)) for i in range(PLANE)]
    mine, theirs = out_projection(attn_out, out_weight)
    mine, q_own, kv_own = lax.optimization_barrier((mine, q_weight, kv_weight))
    middle = q_own.shape[0] // 2
    joined = [
        jnp.concatenate([q_own[at], kv_own[at]], axis=1)
        for at in (slice(None, middle), slice(middle, None))
    ]
    tokens, *firsts = first_norm(
        (mine,), (to_core(theirs),), residual, attn_gain[None, :], meta, depth
    )
    tokens, *joined = lax.optimization_barrier((tokens, *joined))
    qkv = [
        lax.all_gather(rows, "expert", axis=0, tiled=True, axis_index_groups=lines)
        for rows in joined
    ]
    weights = load((w_gate, w_up, w_down), (tokens,))
    line = to_z([tokens] * depth)
    *line, gate, up, down = lax.optimization_barrier((*line, *weights))
    weights = (gate, up, down)
    near = to_plane(pack(line, firsts))
    cut = near[0].shape[0] // 2
    one, two = near[1][:cut], near[2][cut:]
    far = [to_expert(one, 2), to_expert(two, 1)]
    mine, *theirs = experts((*near, *map(to_core, near)), weights, depth, len(near))
    near_sum = chip_sum(mine, list(map(to_core, theirs)))
    far_both = [*far, *map(to_core, far)]
    tied = lax.optimization_barrier((*near_sum, *far_both))
    near_sum, far_both = tied[:PLANE], tied[PLANE:]
    mine, *theirs = experts(far_both, weights, depth, 1)
    far_sum = chip_sum(mine, list(map(to_core, theirs)))
    parts = plane_sum(to_plane(near_sum), to_plane(far_sum), depth)
    scaled, following = second_norm(to_z(parts), (*near, *far), input_gain[None, :])
    products = to_plane(projection(scaled, to_core(scaled), following, qkv, depth))
    return head_norm(
        products,
        q_gain[None, :],
        k_gain[None, :],
        q_weight.shape[1],
        kv_weight.shape[1],
        rows,
        width,
        depth,
    )


def per_device(
    attn_out,
    out_weight,
    residual,
    attn_gain,
    expert_ids,
    route_weights,
    w_gate,
    w_up,
    w_down,
    input_gain,
    q_weight,
    kv_weight,
    q_gain,
    k_gain,
):
    n_expert = lax.axis_size("expert")
    n_tensor = lax.axis_size("tensor")
    share = n_tensor // 2
    tensor_index = lax.axis_index("tensor")
    group_rows = attn_out.shape[0]
    width = residual.shape[1]
    half = tensor_index // share
    capacity = 3 * group_rows * TOP // (4 * n_expert)
    all_experts = 2 * n_expert
    attn_rows = lax.psum_scatter(
        jnp.dot(attn_out, out_weight, preferred_element_type=jnp.float32),
        "tensor",
        scatter_dimension=0,
        tiled=True,
    )
    first_residual = (residual.astype(jnp.float32) + attn_rows).astype(jnp.bfloat16)
    normed = normalize(first_residual.astype(jnp.float32), attn_gain).astype(jnp.bfloat16)
    group_normed = lax.all_gather(normed, "tensor", axis=0, tiled=True)
    flat_ids = expert_ids.reshape(-1)
    onehot = (flat_ids[:, None] == jnp.arange(all_experts, dtype=jnp.int32)[None, :]).astype(
        jnp.int32
    )
    earlier = jnp.cumsum(onehot, axis=0) - onehot
    rank = jnp.sum(earlier * onehot, axis=1)
    dest = flat_ids * capacity + rank
    row_owner = jnp.arange(flat_ids.shape[0], dtype=jnp.int32) // TOP
    slot_row = jnp.full((all_experts * capacity,), group_rows, jnp.int32).at[dest].set(row_owner)
    slot_weight = (
        jnp.zeros((all_experts * capacity,), jnp.float32).at[dest].set(route_weights.reshape(-1))
    )
    own_slots = lax.dynamic_index_in_dim(
        slot_row.reshape(n_expert, 2, capacity), half, 1, keepdims=False
    )
    own_weights = lax.dynamic_index_in_dim(
        slot_weight.reshape(n_expert, 2, capacity), half, 1, keepdims=False
    )
    padded_rows = jnp.concatenate([group_normed, jnp.zeros((1, width), jnp.bfloat16)], axis=0)
    gate_w = w_gate[0]
    up_w = w_up[0]
    down_w = w_down[0]
    outgoing = jnp.take(padded_rows, own_slots, axis=0)
    arrived = lax.all_to_all(outgoing, "expert", split_axis=0, concat_axis=0, tiled=True)
    flat = arrived.reshape(-1, width)
    gate = jnp.dot(flat, gate_w, preferred_element_type=jnp.float32)
    up = jnp.dot(flat, up_w, preferred_element_type=jnp.float32)
    act = (jax.nn.silu(gate) * up).astype(jnp.bfloat16)
    part = jnp.dot(act, down_w, preferred_element_type=jnp.float32).astype(jnp.bfloat16)
    send_part = part.reshape(arrived.shape)
    returned = lax.all_to_all(send_part, "expert", split_axis=0, concat_axis=0, tiled=True)
    weighted = own_weights.reshape(-1)[:, None] * returned.reshape(-1, width).astype(jnp.float32)
    term = (
        jnp.zeros((group_rows + 1, width), jnp.float32)
        .at[own_slots.reshape(-1)]
        .add(weighted)[:group_rows]
    )
    expert_sum = lax.psum_scatter(
        term.astype(jnp.bfloat16), "tensor", scatter_dimension=0, tiled=True
    ).astype(jnp.float32)
    next_residual = (first_residual.astype(jnp.float32) + expert_sum).astype(jnp.bfloat16)
    own_normed = normalize(next_residual.astype(jnp.float32), input_gain).astype(jnp.bfloat16)
    next_normed = lax.all_gather(own_normed, "tensor", axis=0, tiled=True)
    query_cols = q_weight.shape[1]
    kv_cols = kv_weight.shape[1]
    query_raw = jnp.dot(
        next_normed,
        lax.all_gather(q_weight, "expert", axis=0, tiled=True),
        preferred_element_type=jnp.float32,
    )
    kv_raw = jnp.dot(
        next_normed,
        lax.all_gather(kv_weight, "expert", axis=0, tiled=True),
        preferred_element_type=jnp.float32,
    )
    head_size = q_gain.shape[0]
    queries = (
        normalize(query_raw.reshape(group_rows, -1, head_size), q_gain)
        .reshape(group_rows, query_cols)
        .astype(jnp.bfloat16)
    )
    heads_here = kv_cols // head_size
    head_number = tensor_index * heads_here + jnp.arange(heads_here, dtype=jnp.int32)
    is_key = head_number < KV_HEADS
    kv_shaped = kv_raw.reshape(group_rows, heads_here, head_size)
    keys_values = (
        jnp.where(is_key[None, :, None], normalize(kv_shaped, k_gain), kv_shaped)
        .reshape(group_rows, kv_cols)
        .astype(jnp.bfloat16)
    )
    return (next_residual, queries, keys_values)


def solution(mesh):
    small = mesh.shape["tensor"] == 2 and mesh.shape["expert"] == 4 * PLANE
    return jax.shard_map(
        per_device_dense if small else per_device,
        mesh=mesh,
        in_specs=(
            P("expert", "tensor"),
            P("tensor", None),
            P(("expert", "tensor"), None),
            P(),
            P("expert", None),
            P("expert", None),
            P("expert", None, "tensor"),
            P("expert", None, "tensor"),
            P("expert", "tensor", None),
            P(),
            P("expert", "tensor"),
            P("expert", "tensor"),
            P(),
            P(),
        ),
        out_specs=(P(("expert", "tensor"), None), P("expert", "tensor"), P("expert", "tensor")),
        check_vma=False,
    )
```

```python
import functools

import jax
import jax.numpy as jnp
from jax import lax
from jax.experimental import pallas as pl
from jax.experimental.pallas import tpu as pltpu
from jax.sharding import PartitionSpec as P

KV_HEADS = 4
TOP = 8
PLANE = 4
META = 128


EPSILON = 1e-06

SMALL = pl.CostEstimate(flops=0, bytes_accessed=0, transcendentals=0)
VMEM = pl.BlockSpec(memory_space=pltpu.VMEM)
HBM = pl.BlockSpec(memory_space=pltpu.HBM)


def normalize(values, gain):
    return values * lax.rsqrt(jnp.mean(values * values, axis=-1, keepdims=True) + EPSILON) * gain


def params(mebibytes):
    return pltpu.CompilerParams(vmem_limit_bytes=mebibytes << 20)


def lanes(start, size):
    return pl.ds(pl.multiple_of(start, size), size)


def in_hbm(value):
    return pltpu.with_memory_space_constraint(value, pltpu.HBM)


def in_vmem(value):
    return pltpu.with_memory_space_constraint(value, pltpu.VMEM)


def out_projection_kernel(
    chunk, a_hbm, w_hbm, mine_ref, left_ref, right_ref, a_buf, w_buf, a_sem, sems
):
    depth = w_buf.shape[0]
    count = depth // chunk
    half = mine_ref.shape[0]
    a_copy = pltpu.make_async_copy(a_hbm, a_buf, a_sem)
    a_copy.start()
    copies = []
    for i in range(count):
        rows = pl.ds(i * chunk, chunk)
        copies.append(pltpu.make_async_copy(w_hbm.at[rows], w_buf.at[rows], sems.at[i]))
    for copy in copies:
        copy.start()
    tensor = lax.axis_index("tensor")
    own = lanes(tensor * half, half)
    other = lanes((1 - tensor) * half, half)
    a_copy.wait()
    for i in range(count):
        copies[i].wait()
        at = pl.ds(i * chunk, chunk)
        both = jnp.concatenate([a_buf[own, at], a_buf[other, at]], axis=0)
        product = jnp.dot(both, w_buf[at, :], preferred_element_type=jnp.float32)
        middle = left_ref.shape[1]
        if i == 0:
            mine_ref[...] = product[:half]
            left_ref[...] = product[half:, :middle]
            right_ref[...] = product[half:, middle:]
        else:
            mine_ref[...] += product[:half]
            left_ref[...] += product[half:, :middle]
            right_ref[...] += product[half:, middle:]


def out_projection(attn_out, out_weight):
    rows, depth = attn_out.shape
    width = out_weight.shape[1]
    chunk = 256
    half = pltpu.VMEM((rows // 2, width), jnp.float32)
    quarter = pltpu.VMEM((rows // 2, width // 2), jnp.float32)
    return pl.pallas_call(
        functools.partial(out_projection_kernel, chunk),
        out_shape=(half, quarter, quarter),
        in_specs=[HBM, HBM],
        out_specs=(VMEM,) * 3,
        scratch_shapes=[
            pltpu.VMEM((rows, depth), jnp.bfloat16),
            pltpu.VMEM((depth, width), jnp.bfloat16),
            pltpu.SemaphoreType.DMA,
            pltpu.SemaphoreType.DMA((depth // chunk,)),
        ],
        compiler_params=params(14),
        cost_estimate=SMALL,
        name="out_projection",
    )(in_hbm(attn_out), in_hbm(out_weight))


def first_norm_kernel(depth, mine_ref, left_ref, right_ref, *refs):
    residual_ref, gain_ref, meta_ref, tokens_ref = refs[:4]
    slice_refs, first_ref = refs[4:-1], refs[-1]
    rows, width = residual_ref.shape
    sub = width // (PLANE * depth)
    middle = left_ref.shape[1]
    for ref, cols in ((left_ref, slice(None, middle)), (right_ref, slice(middle, None))):
        first_ref[:, cols] = (
            residual_ref[:, cols].astype(jnp.float32) + (mine_ref[:, cols] + ref[...])
        ).astype(jnp.bfloat16)
    first = first_ref[...]
    tokens_ref[:, :width] = normalize(first.astype(jnp.float32), gain_ref[...]).astype(jnp.bfloat16)
    tokens_ref[:, width:] = meta_ref[...]
    plane = lax.axis_index("expert") % PLANE
    for d in range(PLANE):
        for z in range(depth):
            slice_refs[d][z * rows : (z + 1) * rows, :] = first_ref[
                :, lanes((z * PLANE + (plane ^ d)) * sub, sub)
            ]


def first_norm(mine, left, right, residual, gain, meta, depth):
    rows, width = residual.shape
    piece = jax.ShapeDtypeStruct((depth * rows, width // (PLANE * depth)), jnp.bfloat16)
    return pl.pallas_call(
        functools.partial(first_norm_kernel, depth),
        out_shape=(jax.ShapeDtypeStruct((rows, width + META), jnp.bfloat16),) + (piece,) * PLANE,
        in_specs=[VMEM] * 6,
        out_specs=(VMEM,) * (1 + PLANE),
        scratch_shapes=[pltpu.VMEM((rows, width), jnp.bfloat16)],
        compiler_params=params(2),
        name="first_norm",
    )(mine, left, right, residual, gain, meta)


def pack_kernel(depth, *refs):
    line, pieces, out_refs = refs[:depth], refs[depth : depth + PLANE], refs[depth + PLANE :]
    rows, extended = line[0].shape
    sub = pieces[0].shape[1]
    for d, ref in enumerate(out_refs):
        for z in range(depth):
            ref[z * rows : (z + 1) * rows, :extended] = line[z][...]
        ref[:, extended : extended + sub] = pieces[d][...]
        ref[:, extended + sub :] = pieces[PLANE - 1][...]


def pack(line, pieces):
    depth = len(line)
    rows, extended = line[0].shape
    shape = pltpu.VMEM((depth * rows, extended + 2 * pieces[0].shape[1]), jnp.bfloat16)
    return pl.pallas_call(
        functools.partial(pack_kernel, depth),
        out_shape=(shape,) * (PLANE - 1),
        in_specs=[VMEM] * (depth + PLANE),
        out_specs=(VMEM,) * (PLANE - 1),
        compiler_params=params(2),
        name="pack_tokens",
    )(*line, *pieces)


def load_kernel(*refs):
    sources, targets, sems = refs[:3], refs[-4:-1], refs[-1]
    copies = [
        pltpu.make_async_copy(source, target, sems.at[i])
        for i, (source, target) in enumerate(zip(sources, targets))
    ]
    for copy in copies:
        copy.start()
    for copy in copies:
        copy.wait()


def load(weights, after):
    size = sum(w.size for w in weights)
    return pl.pallas_call(
        load_kernel,
        out_shape=tuple(pltpu.VMEM(w.shape, w.dtype) for w in weights),
        in_specs=[HBM] * 3 + [pl.BlockSpec(memory_space=pl.ANY)] * len(after),
        out_specs=(VMEM,) * 3,
        scratch_shapes=[pltpu.SemaphoreType.DMA((3,))],
        compiler_params=params(2),
        cost_estimate=SMALL,
        name="load_weights",
    )(*map(in_hbm, weights), *after)


def expert_kernel(depth, chunk, count, *refs):
    block_refs, (gate_ref, up_ref, down_ref) = refs[:count], refs[count : count + 3]
    mine_ref, *theirs_refs, x_buf, act_buf = refs[count + 3 :]
    width, hidden = gate_ref.shape[1:]
    extended = x_buf.shape[1]
    start = 0
    for ref in block_refs:
        rows = ref.shape[0]
        x_buf[start : start + rows, :] = ref[:, :extended]
        start += rows
    meta = x_buf[:, width:].astype(jnp.float32)
    lane = lax.broadcasted_iota(jnp.int32, meta.shape, 1)
    chip = lax.axis_index("expert")
    expert = 2 * chip + lax.axis_index("tensor")
    chosen = (lane == expert) | (lane == expert + META // 2)
    route = 0.5 * jnp.sum(jnp.where(chosen, meta, 0.0), axis=1, keepdims=True)
    for i in range(hidden // chunk):
        cols = pl.ds(i * chunk, chunk)
        x = x_buf[:, :width]
        gate = jnp.dot(x, gate_ref[0, :, cols], preferred_element_type=jnp.float32)
        up = jnp.dot(x, up_ref[0, :, cols], preferred_element_type=jnp.float32)
        act = gate * (1.0 + jnp.tanh(0.5 * gate)) * (up * route)
        act_buf[:, i * chunk : (i + 1) * chunk] = act.astype(jnp.bfloat16)
    sub = width // (PLANE * depth)
    part = sub * depth
    half = mine_ref.shape[0]
    plane = chip % PLANE
    for d in range(PLANE):
        weight = jnp.concatenate(
            [down_ref[0, :, lanes((z * PLANE + (plane ^ d)) * sub, sub)] for z in range(depth)],
            axis=1,
        )
        out = jnp.dot(act_buf[...], weight, preferred_element_type=jnp.float32)
        cols = slice(d * part, (d + 1) * part)
        mine_ref[:, cols] = out[:half].astype(jnp.bfloat16)
        start = half
        for ref in theirs_refs:
            stop = start + ref.shape[0]
            ref[:, cols] = out[start:stop].astype(jnp.bfloat16)
            start = stop


def experts(blocks, weights, depth, pieces):
    width, hidden = weights[0].shape[1:]
    chunk = 256
    extended = width + META
    total = sum(block.shape[0] for block in blocks)
    rows = [total // 2] + [total // 2 // pieces] * pieces
    return pl.pallas_call(
        functools.partial(expert_kernel, depth, chunk, len(blocks)),
        out_shape=tuple(pltpu.VMEM((size, width), jnp.bfloat16) for size in rows),
        in_specs=[VMEM] * (len(blocks) + 3),
        out_specs=(VMEM,) * (1 + pieces),
        scratch_shapes=[
            pltpu.VMEM((total, extended), jnp.bfloat16),
            pltpu.VMEM((total, hidden), jnp.bfloat16),
        ],
        compiler_params=params(16),
        cost_estimate=pl.CostEstimate(
            flops=6 * total * width * hidden, bytes_accessed=0, transcendentals=0
        ),
        name="experts",
    )(*blocks, *weights)


def chip_sum_kernel(count, mine_ref, *refs):
    theirs, out_refs = refs[:count], refs[count:]
    part = out_refs[0].shape[1]
    start = 0
    for theirs_ref in theirs:
        rows = slice(start, start + theirs_ref.shape[0])
        start = rows.stop
        for d, ref in enumerate(out_refs):
            at = slice(d * part, (d + 1) * part)
            total = mine_ref[rows, at].astype(jnp.float32) + theirs_ref[:, at].astype(jnp.float32)
            ref[rows, :] = total.astype(jnp.bfloat16)


def chip_sum(mine, theirs):
    rows, width = mine.shape
    return pl.pallas_call(
        functools.partial(chip_sum_kernel, len(theirs)),
        out_shape=(pltpu.VMEM((rows, width // PLANE), jnp.bfloat16),) * PLANE,
        in_specs=[VMEM] * (1 + len(theirs)),
        out_specs=(VMEM,) * PLANE,
        compiler_params=params(2),
        name="chip_sum",
    )(mine, *theirs)


def plane_sum_kernel(depth, *refs):
    near, far, out_refs = refs[:PLANE], refs[PLANE : 2 * PLANE], refs[2 * PLANE :]
    group = far[0].shape[0]
    rows = group // depth
    for k in range(PLANE):
        for z in range(depth):
            total = 0.0
            for d in range(PLANE):
                block = k ^ d
                ref, skip = (far[d], 0) if block == PLANE - 1 else (near[d], block * group)
                start = skip + z * rows
                total = total + ref[start : start + rows, :].astype(jnp.float32)
            out_refs[z][k * rows : (k + 1) * rows, :] = total.astype(jnp.bfloat16)


def plane_sum(near, far, depth):
    rows, part = far[0].shape
    return pl.pallas_call(
        functools.partial(plane_sum_kernel, depth),
        out_shape=(pltpu.VMEM((PLANE * rows // depth, part), jnp.bfloat16),) * depth,
        in_specs=[VMEM] * (2 * PLANE),
        out_specs=(VMEM,) * depth,
        compiler_params=params(4),
        name="plane_sum",
    )(*near, *far)


def second_norm_kernel(depth, *refs):
    parts, packed = refs[:depth], refs[depth : depth + PLANE + 1]
    gain_ref, scaled_ref, next_ref = refs[depth + PLANE + 1 :]
    rows = packed[0].shape[0] // depth
    part = parts[0].shape[1]
    sub = part // depth
    skip = packed[0].shape[1] - 2 * sub
    lane = lax.broadcasted_iota(jnp.int32, (rows, META), 1)
    plane = lax.axis_index("expert") % PLANE
    gain = jnp.concatenate(
        [gain_ref[:, lanes((z * PLANE + plane) * sub, sub)] for z in range(depth)], axis=1
    )
    for d in range(PLANE):
        at = slice(d * rows, (d + 1) * rows)
        total = parts[0][at, :].astype(jnp.float32)
        for ref in parts[1:]:
            total = total + ref[at, :].astype(jnp.float32)
        if d < PLANE - 1:
            first = packed[d][:, skip : skip + sub]
        else:
            first = jnp.concatenate([ref[:, skip + sub :] for ref in packed[d:]], axis=0)
        first = jnp.concatenate([first[z * rows : (z + 1) * rows] for z in range(depth)], axis=1)
        following = (first.astype(jnp.float32) + total).astype(jnp.bfloat16)
        next_ref[at, :] = following
        wide = following.astype(jnp.float32)
        scaled_ref[at, :part] = (wide * gain).astype(jnp.bfloat16)
        squares = jnp.sum(wide * wide, axis=1, keepdims=True)
        high = squares.astype(jnp.bfloat16).astype(jnp.float32)
        low = squares - high
        scaled_ref[at, part:] = jnp.where(
            lane == 0, high, jnp.where(lane == 1, low, 0.0)
        ).astype(jnp.bfloat16)


def second_norm(parts, packed, gain):
    depth = len(parts)
    rows, part = parts[0].shape
    return pl.pallas_call(
        functools.partial(second_norm_kernel, depth),
        out_shape=(
            jax.ShapeDtypeStruct((rows, part + META), jnp.bfloat16),
            jax.ShapeDtypeStruct((rows, part), jnp.bfloat16),
        ),
        in_specs=[VMEM] * (depth + PLANE + 2),
        out_specs=(VMEM, VMEM),
        compiler_params=params(4),
        name="second_norm",
    )(*parts, *packed, gain)


def projection_kernel(chunk, mine_ref, theirs_ref, next_ref, q_hbm, *refs):
    kv_refs, out_refs = refs[: q_hbm.shape[0] // META], refs[-PLANE - 3 : -3]
    q_buf, kv_buf, sems = refs[-3:]
    depth = len(kv_refs)
    rows, extended = mine_ref.shape
    part = extended - META
    sub = part // depth
    q_cols, kv_cols = q_buf.shape[1], kv_buf.shape[1]
    cols = q_cols + kv_cols
    copies = []
    for i in range(depth):
        at = lanes(i * sub, sub)
        copies.append(pltpu.make_async_copy(q_hbm.at[at], q_buf.at[at], sems.at[i]))
    for copy in copies:
        copy.start()
    line = lax.axis_index("expert") // PLANE
    for d, ref in enumerate(kv_refs):
        kv_buf[lanes((line ^ d) * sub, sub), :] = ref[...]
    block = rows // PLANE
    tensor = lax.axis_index("tensor")
    own = lanes(tensor * block, block)
    other = lanes((1 - tensor) * block, block)
    for d in range(PLANE):
        at = slice(d * block, (d + 1) * block)
        out_refs[d][own, cols : cols + META] = mine_ref[at, part:]
        out_refs[d][other, cols : cols + META] = theirs_ref[at, part:]
        out_refs[d][:block, cols + META :] = next_ref[at, : part // 2]
        out_refs[d][block:, cols + META :] = next_ref[at, part // 2 :]
    both = jnp.concatenate([mine_ref[:, :part], theirs_ref[:, :part]], axis=0)

    def multiply(weight, target):
        product = jnp.dot(both, weight, preferred_element_type=jnp.float32).astype(jnp.bfloat16)
        at = slice(target, target + weight.shape[1])
        for d in range(PLANE):
            out_refs[d][own, at] = product[d * block : (d + 1) * block]
            out_refs[d][other, at] = product[rows + d * block : rows + (d + 1) * block]

    multiply(kv_buf[...], q_cols)
    for copy in copies:
        copy.wait()
    for start in range(0, q_cols, chunk):
        multiply(q_buf[:, start : start + chunk], start)


def projection(mine, theirs, following, q_weight, kv_weights):
    rows, part = following.shape
    q_cols, kv_cols = q_weight.shape[1], kv_weights[0].shape[1]
    chunk = 512
    shape = pltpu.VMEM((2 * rows // PLANE, q_cols + kv_cols + META + part // 2), jnp.bfloat16)
    return pl.pallas_call(
        functools.partial(projection_kernel, chunk),
        out_shape=(shape,) * PLANE,
        in_specs=[VMEM] * 3 + [HBM] + [VMEM] * len(kv_weights),
        out_specs=(VMEM,) * PLANE,
        scratch_shapes=[
            pltpu.VMEM((part, q_cols), jnp.bfloat16),
            pltpu.VMEM((part, kv_cols), jnp.bfloat16),
            pltpu.SemaphoreType.DMA((len(kv_weights),)),
        ],
        compiler_params=params(8),
        cost_estimate=SMALL,
        name="qkv_projection",
    )(mine, theirs, following, in_hbm(q_weight), *kv_weights)


def head_norm_kernel(depth, *refs):
    parts, q_gain_ref, k_gain_ref = refs[:PLANE], refs[PLANE], refs[PLANE + 1]
    next_ref, q_ref, kv_ref = refs[PLANE + 2 :]
    width = next_ref.shape[1]
    q_cols, kv_cols = q_ref.shape[1], kv_ref.shape[1]
    cols = q_cols + kv_cols
    head = q_gain_ref.shape[1]

    def total(at):
        value = parts[0][:, at].astype(jnp.float32)
        for ref in parts[1:]:
            value = value + ref[:, at].astype(jnp.float32)
        return value

    squares = jnp.sum(total(slice(cols, cols + META)), axis=1, keepdims=True)
    scale = lax.rsqrt(squares / width + EPSILON)
    for h in range(q_cols // head):
        at = slice(h * head, (h + 1) * head)
        q_ref[:, at] = normalize(total(at) * scale, q_gain_ref[...]).astype(jnp.bfloat16)
    tensor = lax.axis_index("tensor")
    for h in range(kv_cols // head):
        at = slice(h * head, (h + 1) * head)
        raw = total(slice(q_cols + h * head, q_cols + (h + 1) * head)) * scale
        is_key = tensor * (kv_cols // head) + h < KV_HEADS
        kv_ref[:, at] = jnp.where(is_key, normalize(raw, k_gain_ref[...]), raw).astype(
            jnp.bfloat16
        )
    plane = lax.axis_index("expert") % PLANE
    rows = next_ref.shape[0]
    sub = width // (PLANE * depth)
    for d in range(PLANE):
        for z in range(depth):
            top = z * sub * 2 // (depth * sub)
            start = cols + META + z * sub - top * (depth * sub // 2)
            next_ref[:, lanes((z * PLANE + (plane ^ d)) * sub, sub)] = parts[d][
                top * rows : (top + 1) * rows, start : start + sub
            ]


def head_norm(parts, q_gain, k_gain, q_cols, kv_cols, rows, width, depth):
    both = parts[0].shape[0]
    return pl.pallas_call(
        functools.partial(head_norm_kernel, depth),
        out_shape=(
            jax.ShapeDtypeStruct((rows, width), jnp.bfloat16),
            jax.ShapeDtypeStruct((both, q_cols), jnp.bfloat16),
            jax.ShapeDtypeStruct((both, kv_cols), jnp.bfloat16),
        ),
        in_specs=[VMEM] * (PLANE + 2),
        out_specs=(VMEM, VMEM, VMEM),
        compiler_params=params(4),
        name="head_norm",
    )(*parts, q_gain, k_gain)


def per_device_dense(
    attn_out,
    out_weight,
    residual,
    attn_gain,
    expert_ids,
    route_weights,
    w_gate,
    w_up,
    w_down,
    input_gain,
    q_weight,
    kv_weight,
    q_gain,
    k_gain,
):
    n_expert = lax.axis_size("expert")
    depth = n_expert // PLANE
    rows, width = residual.shape
    tensor_index = lax.axis_index("tensor").astype(jnp.int32)

    def to_core(value):
        return lax.ppermute(value, "tensor", [(0, 1), (1, 0)])

    def to_expert(value, offset):
        return lax.ppermute(value, "expert", [(i, i ^ offset) for i in range(n_expert)])

    def to_z(values):
        return [to_expert(v, d * PLANE) if d else v for d, v in enumerate(values)]

    def to_plane(values):
        return [to_expert(v, d) if d else v for d, v in enumerate(values)]

    own_ids = lax.dynamic_slice_in_dim(expert_ids, tensor_index * rows, rows, 0)
    own_route = lax.dynamic_slice_in_dim(route_weights, tensor_index * rows, rows, 0)
    chosen = own_ids[:, :, None] == jnp.arange(META // 2, dtype=jnp.int32)[None, None, :]
    dense = jnp.sum(jnp.where(chosen, own_route[:, :, None], 0.0), axis=1)
    high = lax.reduce_precision(dense, 8, 7)
    meta = jnp.concatenate([high, dense - high], axis=1).astype(jnp.bfloat16)

    lines = [list(range(i, n_expert, PLANE)) for i in range(PLANE)]
    kv_rows = [kv_weight, to_expert(kv_weight, PLANE), to_expert(kv_weight, 2 * PLANE)]
    mine, left, right = out_projection(attn_out, out_weight)
    mine, left, right, *kv_rows = lax.optimization_barrier(
        (mine, to_core(left), to_core(right), *kv_rows)
    )
    tokens, *firsts = first_norm(
        mine, left, right, residual, attn_gain[None, :], meta, depth
    )
    tokens, q_own = lax.optimization_barrier((tokens, q_weight))
    q_rows = lax.all_gather(q_own, "expert", axis=0, tiled=True, axis_index_groups=lines)
    kv_rows.append(to_expert(kv_rows[2], PLANE))
    weights = load((w_gate, w_up, w_down), (tokens,))
    line = to_z([tokens] * depth)
    *line, kv_rows[3], gate, up, down = lax.optimization_barrier((*line, kv_rows[3], *weights))
    weights = (gate, up, down)
    near = to_plane(pack(line, firsts))
    cut = near[0].shape[0] // 2
    one, two = near[1][:cut], near[2][cut:]
    far = [to_expert(one, 2), to_expert(two, 1)]
    mine, *theirs = experts((*near, *map(to_core, near)), weights, depth, len(near))
    near_sum = chip_sum(mine, list(map(to_core, theirs)))
    far_both = [*far, *map(to_core, far)]
    tied = lax.optimization_barrier((*near_sum, *far_both))
    near_sum, far_both = tied[:PLANE], tied[PLANE:]
    near_parts = to_plane(near_sum)
    mine, *theirs = experts(far_both, weights, depth, 2)
    tied = lax.optimization_barrier((mine, *map(to_core, theirs), *near_parts))
    mine, theirs, near_parts = tied[0], tied[1:-PLANE], tied[-PLANE:]
    far_sum = chip_sum(mine, theirs)
    parts = plane_sum(near_parts, to_plane(far_sum), depth)
    scaled, following = second_norm(to_z(parts), (*near, *far), input_gain[None, :])
    products = to_plane(projection(scaled, to_core(scaled), following, q_rows, kv_rows))
    return head_norm(
        products,
        q_gain[None, :],
        k_gain[None, :],
        q_weight.shape[1],
        kv_weight.shape[1],
        rows,
        width,
        depth,
    )


def per_device(
    attn_out,
    out_weight,
    residual,
    attn_gain,
    expert_ids,
    route_weights,
    w_gate,
    w_up,
    w_down,
    input_gain,
    q_weight,
    kv_weight,
    q_gain,
    k_gain,
):
    n_expert = lax.axis_size("expert")
    n_tensor = lax.axis_size("tensor")
    share = n_tensor // 2
    tensor_index = lax.axis_index("tensor")
    group_rows = attn_out.shape[0]
    width = residual.shape[1]
    half = tensor_index // share
    capacity = 3 * group_rows * TOP // (4 * n_expert)
    all_experts = 2 * n_expert
    attn_rows = lax.psum_scatter(
        jnp.dot(attn_out, out_weight, preferred_element_type=jnp.float32),
        "tensor",
        scatter_dimension=0,
        tiled=True,
    )
    first_residual = (residual.astype(jnp.float32) + attn_rows).astype(jnp.bfloat16)
    normed = normalize(first_residual.astype(jnp.float32), attn_gain).astype(jnp.bfloat16)
    group_normed = lax.all_gather(normed, "tensor", axis=0, tiled=True)
    flat_ids = expert_ids.reshape(-1)
    onehot = (flat_ids[:, None] == jnp.arange(all_experts, dtype=jnp.int32)[None, :]).astype(
        jnp.int32
    )
    earlier = jnp.cumsum(onehot, axis=0) - onehot
    rank = jnp.sum(earlier * onehot, axis=1)
    dest = flat_ids * capacity + rank
    row_owner = jnp.arange(flat_ids.shape[0], dtype=jnp.int32) // TOP
    slot_row = jnp.full((all_experts * capacity,), group_rows, jnp.int32).at[dest].set(row_owner)
    slot_weight = (
        jnp.zeros((all_experts * capacity,), jnp.float32).at[dest].set(route_weights.reshape(-1))
    )
    own_slots = lax.dynamic_index_in_dim(
        slot_row.reshape(n_expert, 2, capacity), half, 1, keepdims=False
    )
    own_weights = lax.dynamic_index_in_dim(
        slot_weight.reshape(n_expert, 2, capacity), half, 1, keepdims=False
    )
    padded_rows = jnp.concatenate([group_normed, jnp.zeros((1, width), jnp.bfloat16)], axis=0)
    gate_w = w_gate[0]
    up_w = w_up[0]
    down_w = w_down[0]
    outgoing = jnp.take(padded_rows, own_slots, axis=0)
    arrived = lax.all_to_all(outgoing, "expert", split_axis=0, concat_axis=0, tiled=True)
    flat = arrived.reshape(-1, width)
    gate = jnp.dot(flat, gate_w, preferred_element_type=jnp.float32)
    up = jnp.dot(flat, up_w, preferred_element_type=jnp.float32)
    act = (jax.nn.silu(gate) * up).astype(jnp.bfloat16)
    part = jnp.dot(act, down_w, preferred_element_type=jnp.float32).astype(jnp.bfloat16)
    send_part = part.reshape(arrived.shape)
    returned = lax.all_to_all(send_part, "expert", split_axis=0, concat_axis=0, tiled=True)
    weighted = own_weights.reshape(-1)[:, None] * returned.reshape(-1, width).astype(jnp.float32)
    term = (
        jnp.zeros((group_rows + 1, width), jnp.float32)
        .at[own_slots.reshape(-1)]
        .add(weighted)[:group_rows]
    )
    expert_sum = lax.psum_scatter(
        term.astype(jnp.bfloat16), "tensor", scatter_dimension=0, tiled=True
    ).astype(jnp.float32)
    next_residual = (first_residual.astype(jnp.float32) + expert_sum).astype(jnp.bfloat16)
    own_normed = normalize(next_residual.astype(jnp.float32), input_gain).astype(jnp.bfloat16)
    next_normed = lax.all_gather(own_normed, "tensor", axis=0, tiled=True)
    query_cols = q_weight.shape[1]
    kv_cols = kv_weight.shape[1]
    query_raw = jnp.dot(
        next_normed,
        lax.all_gather(q_weight, "expert", axis=0, tiled=True),
        preferred_element_type=jnp.float32,
    )
    kv_raw = jnp.dot(
        next_normed,
        lax.all_gather(kv_weight, "expert", axis=0, tiled=True),
        preferred_element_type=jnp.float32,
    )
    head_size = q_gain.shape[0]
    queries = (
        normalize(query_raw.reshape(group_rows, -1, head_size), q_gain)
        .reshape(group_rows, query_cols)
        .astype(jnp.bfloat16)
    )
    heads_here = kv_cols // head_size
    head_number = tensor_index * heads_here + jnp.arange(heads_here, dtype=jnp.int32)
    is_key = head_number < KV_HEADS
    kv_shaped = kv_raw.reshape(group_rows, heads_here, head_size)
    keys_values = (
        jnp.where(is_key[None, :, None], normalize(kv_shaped, k_gain), kv_shaped)
        .reshape(group_rows, kv_cols)
        .astype(jnp.bfloat16)
    )
    return (next_residual, queries, keys_values)


def solution(mesh):
    small = mesh.shape["tensor"] == 2 and mesh.shape["expert"] == 4 * PLANE
    return jax.shard_map(
        per_device_dense if small else per_device,
        mesh=mesh,
        in_specs=(
            P("expert", "tensor"),
            P("tensor", None),
            P(("expert", "tensor"), None),
            P(),
            P("expert", None),
            P("expert", None),
            P("expert", None, "tensor"),
            P("expert", None, "tensor"),
            P("expert", "tensor", None),
            P(),
            P("expert", "tensor"),
            P("expert", "tensor"),
            P(),
            P(),
        ),
        out_specs=(P(("expert", "tensor"), None), P("expert", "tensor"), P("expert", "tensor")),
        check_vma=False,
    )
```

```python
import functools

import jax
import jax.numpy as jnp
from jax import lax
from jax.experimental import pallas as pl
from jax.experimental.pallas import tpu as pltpu
from jax.sharding import PartitionSpec as P

KV_HEADS = 4
TOP = 8
PLANE = 4
META = 128


EPSILON = 1e-06

SMALL = pl.CostEstimate(flops=0, bytes_accessed=0, transcendentals=0)
VMEM = pl.BlockSpec(memory_space=pltpu.VMEM)
HBM = pl.BlockSpec(memory_space=pltpu.HBM)


def normalize(values, gain):
    return values * lax.rsqrt(jnp.mean(values * values, axis=-1, keepdims=True) + EPSILON) * gain


def params(mebibytes):
    return pltpu.CompilerParams(vmem_limit_bytes=mebibytes << 20)


def lanes(start, size):
    return pl.ds(pl.multiple_of(start, size), size)


def in_hbm(value):
    return pltpu.with_memory_space_constraint(value, pltpu.HBM)


def in_vmem(value):
    return pltpu.with_memory_space_constraint(value, pltpu.VMEM)


def out_projection_kernel(chunk, a_hbm, w_hbm, mine_ref, theirs_ref, a_buf, w_buf, a_sem, sems):
    depth = w_buf.shape[0]
    count = depth // chunk
    half = mine_ref.shape[0]
    a_copy = pltpu.make_async_copy(a_hbm, a_buf, a_sem)
    a_copy.start()
    copies = []
    for i in range(count):
        rows = pl.ds(i * chunk, chunk)
        copies.append(pltpu.make_async_copy(w_hbm.at[rows], w_buf.at[rows], sems.at[i]))
    for copy in copies:
        copy.start()
    tensor = lax.axis_index("tensor")
    own = lanes(tensor * half, half)
    other = lanes((1 - tensor) * half, half)
    a_copy.wait()
    for i in range(count):
        copies[i].wait()
        at = pl.ds(i * chunk, chunk)
        both = jnp.concatenate([a_buf[own, at], a_buf[other, at]], axis=0)
        product = jnp.dot(both, w_buf[at, :], preferred_element_type=jnp.float32)
        if i == 0:
            mine_ref[...] = product[:half]
            theirs_ref[...] = product[half:]
        else:
            mine_ref[...] += product[:half]
            theirs_ref[...] += product[half:]


def out_projection(attn_out, out_weight):
    rows, depth = attn_out.shape
    width = out_weight.shape[1]
    chunk = 256
    half = pltpu.VMEM((rows // 2, width), jnp.float32)
    return pl.pallas_call(
        functools.partial(out_projection_kernel, chunk),
        out_shape=(half, half),
        in_specs=[HBM, HBM],
        out_specs=(VMEM, VMEM),
        scratch_shapes=[
            pltpu.VMEM((rows, depth), jnp.bfloat16),
            pltpu.VMEM((depth, width), jnp.bfloat16),
            pltpu.SemaphoreType.DMA,
            pltpu.SemaphoreType.DMA((depth // chunk,)),
        ],
        compiler_params=params(14),
        cost_estimate=SMALL,
        name="out_projection",
    )(in_hbm(attn_out), in_hbm(out_weight))


def first_norm_kernel(depth, count, *refs):
    mine, theirs = refs[:count], refs[count : 2 * count]
    residual_ref, gain_ref, meta_ref, tokens_ref = refs[2 * count : 2 * count + 4]
    slice_refs, first_ref = refs[2 * count + 4 : -1], refs[-1]
    rows, width = residual_ref.shape
    sub = width // (PLANE * depth)
    start = 0
    for mine_ref, theirs_ref in zip(mine, theirs):
        cols = slice(start, start + mine_ref.shape[1])
        start += mine_ref.shape[1]
        first_ref[:, cols] = (
            residual_ref[:, cols].astype(jnp.float32) + (mine_ref[...] + theirs_ref[...])
        ).astype(jnp.bfloat16)
    first = first_ref[...]
    tokens_ref[:, :width] = normalize(first.astype(jnp.float32), gain_ref[...]).astype(jnp.bfloat16)
    tokens_ref[:, width:] = meta_ref[...]
    plane = lax.axis_index("expert") % PLANE
    for d in range(PLANE):
        for z in range(depth):
            slice_refs[d][z * rows : (z + 1) * rows, :] = first_ref[
                :, lanes((z * PLANE + (plane ^ d)) * sub, sub)
            ]


def first_norm(mine, theirs, residual, gain, meta, depth):
    rows, width = residual.shape
    piece = jax.ShapeDtypeStruct((depth * rows, width // (PLANE * depth)), jnp.bfloat16)
    return pl.pallas_call(
        functools.partial(first_norm_kernel, depth, len(mine)),
        out_shape=(jax.ShapeDtypeStruct((rows, width + META), jnp.bfloat16),) + (piece,) * PLANE,
        in_specs=[VMEM] * (2 * len(mine) + 3),
        out_specs=(VMEM,) * (1 + PLANE),
        scratch_shapes=[pltpu.VMEM((rows, width), jnp.bfloat16)],
        compiler_params=params(2),
        name="first_norm",
    )(*mine, *theirs, residual, gain, meta)


def pack_kernel(depth, *refs):
    line, pieces, out_refs = refs[:depth], refs[depth : depth + PLANE], refs[depth + PLANE :]
    rows, extended = line[0].shape
    sub = pieces[0].shape[1]
    for d, ref in enumerate(out_refs):
        for z in range(depth):
            ref[z * rows : (z + 1) * rows, :extended] = line[z][...]
        ref[:, extended : extended + sub] = pieces[d][...]
        ref[:, extended + sub :] = pieces[PLANE - 1][...]


def pack(line, pieces):
    depth = len(line)
    rows, extended = line[0].shape
    shape = pltpu.VMEM((depth * rows, extended + 2 * pieces[0].shape[1]), jnp.bfloat16)
    return pl.pallas_call(
        functools.partial(pack_kernel, depth),
        out_shape=(shape,) * (PLANE - 1),
        in_specs=[VMEM] * (depth + PLANE),
        out_specs=(VMEM,) * (PLANE - 1),
        compiler_params=params(2),
        name="pack_tokens",
    )(*line, *pieces)


def load_kernel(count, *refs):
    sources, targets, sems = refs[:count], refs[-count - 1 : -1], refs[-1]
    copies = [
        pltpu.make_async_copy(source, target, sems.at[i])
        for i, (source, target) in enumerate(zip(sources, targets))
    ]
    for copy in copies:
        copy.start()
    for copy in copies:
        copy.wait()


def load(weights, after):
    count = len(weights)
    return pl.pallas_call(
        functools.partial(load_kernel, count),
        out_shape=tuple(pltpu.VMEM(w.shape, w.dtype) for w in weights),
        in_specs=[HBM] * count + [pl.BlockSpec(memory_space=pl.ANY)] * len(after),
        out_specs=(VMEM,) * count,
        scratch_shapes=[pltpu.SemaphoreType.DMA((count,))],
        compiler_params=params(2),
        cost_estimate=SMALL,
        name="load_weights",
    )(*map(in_hbm, weights), *after)


def expert_kernel(depth, chunk, count, *refs):
    block_refs, (gate_ref, up_ref, down_ref) = refs[:count], refs[count : count + 3]
    mine_ref, *theirs_refs, x_buf, act_buf = refs[count + 3 :]
    width, hidden = gate_ref.shape[1:]
    extended = x_buf.shape[1]
    start = 0
    for ref in block_refs:
        rows = ref.shape[0]
        x_buf[start : start + rows, :] = ref[:, :extended]
        start += rows
    meta = x_buf[:, width:].astype(jnp.float32)
    lane = lax.broadcasted_iota(jnp.int32, meta.shape, 1)
    chip = lax.axis_index("expert")
    expert = 2 * chip + lax.axis_index("tensor")
    chosen = (lane == expert) | (lane == expert + META // 2)
    route = 0.5 * jnp.sum(jnp.where(chosen, meta, 0.0), axis=1, keepdims=True)
    for i in range(hidden // chunk):
        cols = pl.ds(i * chunk, chunk)
        x = x_buf[:, :width]
        gate = jnp.dot(x, gate_ref[0, :, cols], preferred_element_type=jnp.float32)
        up = jnp.dot(x, up_ref[0, :, cols], preferred_element_type=jnp.float32)
        act = gate * (1.0 + jnp.tanh(0.5 * gate)) * (up * route)
        act_buf[:, i * chunk : (i + 1) * chunk] = act.astype(jnp.bfloat16)
    sub = width // (PLANE * depth)
    part = sub * depth
    half = mine_ref.shape[0]
    plane = chip % PLANE
    for d in range(PLANE):
        weight = jnp.concatenate(
            [down_ref[0, :, lanes((z * PLANE + (plane ^ d)) * sub, sub)] for z in range(depth)],
            axis=1,
        )
        out = jnp.dot(act_buf[...], weight, preferred_element_type=jnp.float32)
        cols = slice(d * part, (d + 1) * part)
        mine_ref[:, cols] = out[:half].astype(jnp.bfloat16)
        start = half
        for ref in theirs_refs:
            stop = start + ref.shape[0]
            ref[:, cols] = out[start:stop].astype(jnp.bfloat16)
            start = stop


def experts(blocks, weights, depth, pieces):
    width, hidden = weights[0].shape[1:]
    chunk = 256
    extended = width + META
    total = sum(block.shape[0] for block in blocks)
    rows = [total // 2] + [total // 2 // pieces] * pieces
    return pl.pallas_call(
        functools.partial(expert_kernel, depth, chunk, len(blocks)),
        out_shape=tuple(pltpu.VMEM((size, width), jnp.bfloat16) for size in rows),
        in_specs=[VMEM] * (len(blocks) + 3),
        out_specs=(VMEM,) * (1 + pieces),
        scratch_shapes=[
            pltpu.VMEM((total, extended), jnp.bfloat16),
            pltpu.VMEM((total, hidden), jnp.bfloat16),
        ],
        compiler_params=params(16),
        cost_estimate=pl.CostEstimate(
            flops=6 * total * width * hidden, bytes_accessed=0, transcendentals=0
        ),
        name="experts",
    )(*blocks, *weights)


def chip_sum_kernel(count, mine_ref, *refs):
    theirs, out_refs = refs[:count], refs[count:]
    part = out_refs[0].shape[1]
    start = 0
    for theirs_ref in theirs:
        rows = slice(start, start + theirs_ref.shape[0])
        start = rows.stop
        for d, ref in enumerate(out_refs):
            at = slice(d * part, (d + 1) * part)
            total = mine_ref[rows, at].astype(jnp.float32) + theirs_ref[:, at].astype(jnp.float32)
            ref[rows, :] = total.astype(jnp.bfloat16)


def chip_sum(mine, theirs):
    rows, width = mine.shape
    return pl.pallas_call(
        functools.partial(chip_sum_kernel, len(theirs)),
        out_shape=(pltpu.VMEM((rows, width // PLANE), jnp.bfloat16),) * PLANE,
        in_specs=[VMEM] * (1 + len(theirs)),
        out_specs=(VMEM,) * PLANE,
        compiler_params=params(2),
        name="chip_sum",
    )(mine, *theirs)


def plane_sum_kernel(depth, *refs):
    near, far, out_refs = refs[:PLANE], refs[PLANE : 2 * PLANE], refs[2 * PLANE :]
    group = far[0].shape[0]
    rows = group // depth
    for k in range(PLANE):
        for z in range(depth):
            total = 0.0
            for d in range(PLANE):
                block = k ^ d
                ref, skip = (far[d], 0) if block == PLANE - 1 else (near[d], block * group)
                start = skip + z * rows
                total = total + ref[start : start + rows, :].astype(jnp.float32)
            out_refs[z][k * rows : (k + 1) * rows, :] = total.astype(jnp.bfloat16)


def plane_sum(near, far, depth):
    rows, part = far[0].shape
    return pl.pallas_call(
        functools.partial(plane_sum_kernel, depth),
        out_shape=(pltpu.VMEM((PLANE * rows // depth, part), jnp.bfloat16),) * depth,
        in_specs=[VMEM] * (2 * PLANE),
        out_specs=(VMEM,) * depth,
        compiler_params=params(4),
        name="plane_sum",
    )(*near, *far)


def second_norm_kernel(depth, *refs):
    parts, packed = refs[:depth], refs[depth : depth + PLANE + 1]
    gain_ref, scaled_ref, next_ref = refs[depth + PLANE + 1 :]
    rows = packed[0].shape[0] // depth
    part = parts[0].shape[1]
    sub = part // depth
    skip = packed[0].shape[1] - 2 * sub
    lane = lax.broadcasted_iota(jnp.int32, (rows, META), 1)
    plane = lax.axis_index("expert") % PLANE
    gain = jnp.concatenate(
        [gain_ref[:, lanes((z * PLANE + plane) * sub, sub)] for z in range(depth)], axis=1
    )
    for d in range(PLANE):
        at = slice(d * rows, (d + 1) * rows)
        total = parts[0][at, :].astype(jnp.float32)
        for ref in parts[1:]:
            total = total + ref[at, :].astype(jnp.float32)
        if d < PLANE - 1:
            first = packed[d][:, skip : skip + sub]
        else:
            first = jnp.concatenate([ref[:, skip + sub :] for ref in packed[d:]], axis=0)
        first = jnp.concatenate([first[z * rows : (z + 1) * rows] for z in range(depth)], axis=1)
        following = (first.astype(jnp.float32) + total).astype(jnp.bfloat16)
        next_ref[at, :] = following
        wide = following.astype(jnp.float32)
        scaled_ref[at, :part] = (wide * gain).astype(jnp.bfloat16)
        squares = jnp.sum(wide * wide, axis=1, keepdims=True)
        high = squares.astype(jnp.bfloat16).astype(jnp.float32)
        low = squares - high
        scaled_ref[at, part:] = jnp.where(
            lane == 0, high, jnp.where(lane == 1, low, 0.0)
        ).astype(jnp.bfloat16)


def second_norm(parts, packed, gain):
    depth = len(parts)
    rows, part = parts[0].shape
    return pl.pallas_call(
        functools.partial(second_norm_kernel, depth),
        out_shape=(
            jax.ShapeDtypeStruct((rows, part + META), jnp.bfloat16),
            jax.ShapeDtypeStruct((rows, part), jnp.bfloat16),
        ),
        in_specs=[VMEM] * (depth + PLANE + 2),
        out_specs=(VMEM, VMEM),
        compiler_params=params(4),
        name="second_norm",
    )(*parts, *packed, gain)


def projection_kernel(chunk, mine_ref, theirs_ref, next_ref, q_ref, *refs):
    kv_refs, out_refs, kv_buf = refs[: -PLANE - 1], refs[-PLANE - 1 : -1], refs[-1]
    depth = len(kv_refs)
    rows, extended = mine_ref.shape
    part = extended - META
    sub = part // depth
    q_cols, kv_cols = q_ref.shape[1], kv_buf.shape[1]
    cols = q_cols + kv_cols
    line = lax.axis_index("expert") // PLANE
    for d, ref in enumerate(kv_refs):
        kv_buf[lanes((line ^ d) * sub, sub), :] = ref[...]
    block = rows // PLANE
    tensor = lax.axis_index("tensor")
    own = lanes(tensor * block, block)
    other = lanes((1 - tensor) * block, block)
    for d in range(PLANE):
        at = slice(d * block, (d + 1) * block)
        out_refs[d][own, cols : cols + META] = mine_ref[at, part:]
        out_refs[d][other, cols : cols + META] = theirs_ref[at, part:]
        out_refs[d][:block, cols + META :] = next_ref[at, : part // 2]
        out_refs[d][block:, cols + META :] = next_ref[at, part // 2 :]
    both = jnp.concatenate([mine_ref[:, :part], theirs_ref[:, :part]], axis=0)

    def multiply(weight, target):
        product = jnp.dot(both, weight, preferred_element_type=jnp.float32).astype(jnp.bfloat16)
        at = slice(target, target + weight.shape[1])
        for d in range(PLANE):
            out_refs[d][own, at] = product[d * block : (d + 1) * block]
            out_refs[d][other, at] = product[rows + d * block : rows + (d + 1) * block]

    multiply(kv_buf[...], q_cols)
    for start in range(0, q_cols, chunk):
        multiply(q_ref[:, start : start + chunk], start)


def projection(mine, theirs, following, q_weight, kv_weights):
    rows, part = following.shape
    q_cols, kv_cols = q_weight.shape[1], kv_weights[0].shape[1]
    chunk = 512
    shape = pltpu.VMEM((2 * rows // PLANE, q_cols + kv_cols + META + part // 2), jnp.bfloat16)
    return pl.pallas_call(
        functools.partial(projection_kernel, chunk),
        out_shape=(shape,) * PLANE,
        in_specs=[VMEM] * (4 + len(kv_weights)),
        out_specs=(VMEM,) * PLANE,
        scratch_shapes=[pltpu.VMEM((part, kv_cols), jnp.bfloat16)],
        compiler_params=params(8),
        cost_estimate=SMALL,
        name="qkv_projection",
    )(mine, theirs, following, q_weight, *kv_weights)


def head_norm_kernel(depth, *refs):
    parts, q_gain_ref, k_gain_ref = refs[:PLANE], refs[PLANE], refs[PLANE + 1]
    next_ref, q_ref, kv_ref = refs[PLANE + 2 :]
    width = next_ref.shape[1]
    q_cols, kv_cols = q_ref.shape[1], kv_ref.shape[1]
    cols = q_cols + kv_cols
    head = q_gain_ref.shape[1]

    def total(at):
        value = parts[0][:, at].astype(jnp.float32)
        for ref in parts[1:]:
            value = value + ref[:, at].astype(jnp.float32)
        return value

    squares = jnp.sum(total(slice(cols, cols + META)), axis=1, keepdims=True)
    scale = lax.rsqrt(squares / width + EPSILON)
    for h in range(q_cols // head):
        at = slice(h * head, (h + 1) * head)
        q_ref[:, at] = normalize(total(at) * scale, q_gain_ref[...]).astype(jnp.bfloat16)
    tensor = lax.axis_index("tensor")
    for h in range(kv_cols // head):
        at = slice(h * head, (h + 1) * head)
        raw = total(slice(q_cols + h * head, q_cols + (h + 1) * head)) * scale
        is_key = tensor * (kv_cols // head) + h < KV_HEADS
        kv_ref[:, at] = jnp.where(is_key, normalize(raw, k_gain_ref[...]), raw).astype(
            jnp.bfloat16
        )
    plane = lax.axis_index("expert") % PLANE
    rows = next_ref.shape[0]
    sub = width // (PLANE * depth)
    for d in range(PLANE):
        for z in range(depth):
            top = z * sub * 2 // (depth * sub)
            start = cols + META + z * sub - top * (depth * sub // 2)
            next_ref[:, lanes((z * PLANE + (plane ^ d)) * sub, sub)] = parts[d][
                top * rows : (top + 1) * rows, start : start + sub
            ]


def head_norm(parts, q_gain, k_gain, q_cols, kv_cols, rows, width, depth):
    both = parts[0].shape[0]
    return pl.pallas_call(
        functools.partial(head_norm_kernel, depth),
        out_shape=(
            jax.ShapeDtypeStruct((rows, width), jnp.bfloat16),
            jax.ShapeDtypeStruct((both, q_cols), jnp.bfloat16),
            jax.ShapeDtypeStruct((both, kv_cols), jnp.bfloat16),
        ),
        in_specs=[VMEM] * (PLANE + 2),
        out_specs=(VMEM, VMEM, VMEM),
        compiler_params=params(4),
        name="head_norm",
    )(*parts, q_gain, k_gain)


def per_device_dense(
    attn_out,
    out_weight,
    residual,
    attn_gain,
    expert_ids,
    route_weights,
    w_gate,
    w_up,
    w_down,
    input_gain,
    q_weight,
    kv_weight,
    q_gain,
    k_gain,
):
    n_expert = lax.axis_size("expert")
    depth = n_expert // PLANE
    rows, width = residual.shape
    tensor_index = lax.axis_index("tensor").astype(jnp.int32)

    def to_core(value):
        return lax.ppermute(value, "tensor", [(0, 1), (1, 0)])

    def to_expert(value, offset):
        return lax.ppermute(value, "expert", [(i, i ^ offset) for i in range(n_expert)])

    def to_z(values):
        return [to_expert(v, d * PLANE) if d else v for d, v in enumerate(values)]

    def to_plane(values):
        return [to_expert(v, d) if d else v for d, v in enumerate(values)]

    own_ids = lax.dynamic_slice_in_dim(expert_ids, tensor_index * rows, rows, 0)
    own_route = lax.dynamic_slice_in_dim(route_weights, tensor_index * rows, rows, 0)
    chosen = own_ids[:, :, None] == jnp.arange(META // 2, dtype=jnp.int32)[None, None, :]
    dense = jnp.sum(jnp.where(chosen, own_route[:, :, None], 0.0), axis=1)
    high = lax.reduce_precision(dense, 8, 7)
    meta = jnp.concatenate([high, dense - high], axis=1).astype(jnp.bfloat16)

    lines = [list(range(i, n_expert, PLANE)) for i in range(PLANE)]
    mine, theirs = out_projection(attn_out, out_weight)
    tokens, *firsts = first_norm(
        (mine,), (to_core(theirs),), residual, attn_gain[None, :], meta, depth
    )
    tokens, q_own = lax.optimization_barrier((tokens, q_weight))
    q_rows = lax.all_gather(q_own, "expert", axis=0, tiled=True, axis_index_groups=lines)
    weights = load((w_gate, w_up, w_down), (tokens,))
    line = to_z([tokens] * depth)
    *line, gate, up, down = lax.optimization_barrier((*line, *weights))
    weights = (gate, up, down)
    near = to_plane(pack(line, firsts))
    cut = near[0].shape[0] // 2
    one, two = near[1][:cut], near[2][cut:]
    far = [to_expert(one, 2), to_expert(two, 1)]
    mine, *theirs = experts((*near, *map(to_core, near)), weights, depth, len(near))
    near_sum = chip_sum(mine, list(map(to_core, theirs)))
    far_both = [*far, *map(to_core, far)]
    tied = lax.optimization_barrier((*near_sum, *far_both))
    near_sum, far_both = tied[:PLANE], tied[PLANE:]
    mine, *theirs = experts(far_both, weights, depth, 1)
    far_sum = chip_sum(mine, list(map(to_core, theirs)))
    *far_sum, kv_own = lax.optimization_barrier((*far_sum, kv_weight))
    kv_rows = [kv_own, to_expert(kv_own, PLANE), to_expert(kv_own, 2 * PLANE)]
    *parts, kv_rows[2] = lax.optimization_barrier(
        (*plane_sum(to_plane(near_sum), to_plane(far_sum), depth), kv_rows[2])
    )
    kv_rows.append(to_expert(kv_rows[2], PLANE))
    (q_rows,) = load((q_rows,), parts)
    parts = to_z(parts)
    *parts, q_rows = lax.optimization_barrier((*parts, q_rows))
    scaled, following = second_norm(parts, (*near, *far), input_gain[None, :])
    products = to_plane(projection(scaled, to_core(scaled), following, q_rows, kv_rows))
    return head_norm(
        products,
        q_gain[None, :],
        k_gain[None, :],
        q_weight.shape[1],
        kv_weight.shape[1],
        rows,
        width,
        depth,
    )


def per_device(
    attn_out,
    out_weight,
    residual,
    attn_gain,
    expert_ids,
    route_weights,
    w_gate,
    w_up,
    w_down,
    input_gain,
    q_weight,
    kv_weight,
    q_gain,
    k_gain,
):
    n_expert = lax.axis_size("expert")
    n_tensor = lax.axis_size("tensor")
    share = n_tensor // 2
    tensor_index = lax.axis_index("tensor")
    group_rows = attn_out.shape[0]
    width = residual.shape[1]
    half = tensor_index // share
    capacity = 3 * group_rows * TOP // (4 * n_expert)
    all_experts = 2 * n_expert
    attn_rows = lax.psum_scatter(
        jnp.dot(attn_out, out_weight, preferred_element_type=jnp.float32),
        "tensor",
        scatter_dimension=0,
        tiled=True,
    )
    first_residual = (residual.astype(jnp.float32) + attn_rows).astype(jnp.bfloat16)
    normed = normalize(first_residual.astype(jnp.float32), attn_gain).astype(jnp.bfloat16)
    group_normed = lax.all_gather(normed, "tensor", axis=0, tiled=True)
    flat_ids = expert_ids.reshape(-1)
    onehot = (flat_ids[:, None] == jnp.arange(all_experts, dtype=jnp.int32)[None, :]).astype(
        jnp.int32
    )
    earlier = jnp.cumsum(onehot, axis=0) - onehot
    rank = jnp.sum(earlier * onehot, axis=1)
    dest = flat_ids * capacity + rank
    row_owner = jnp.arange(flat_ids.shape[0], dtype=jnp.int32) // TOP
    slot_row = jnp.full((all_experts * capacity,), group_rows, jnp.int32).at[dest].set(row_owner)
    slot_weight = (
        jnp.zeros((all_experts * capacity,), jnp.float32).at[dest].set(route_weights.reshape(-1))
    )
    own_slots = lax.dynamic_index_in_dim(
        slot_row.reshape(n_expert, 2, capacity), half, 1, keepdims=False
    )
    own_weights = lax.dynamic_index_in_dim(
        slot_weight.reshape(n_expert, 2, capacity), half, 1, keepdims=False
    )
    padded_rows = jnp.concatenate([group_normed, jnp.zeros((1, width), jnp.bfloat16)], axis=0)
    gate_w = w_gate[0]
    up_w = w_up[0]
    down_w = w_down[0]
    outgoing = jnp.take(padded_rows, own_slots, axis=0)
    arrived = lax.all_to_all(outgoing, "expert", split_axis=0, concat_axis=0, tiled=True)
    flat = arrived.reshape(-1, width)
    gate = jnp.dot(flat, gate_w, preferred_element_type=jnp.float32)
    up = jnp.dot(flat, up_w, preferred_element_type=jnp.float32)
    act = (jax.nn.silu(gate) * up).astype(jnp.bfloat16)
    part = jnp.dot(act, down_w, preferred_element_type=jnp.float32).astype(jnp.bfloat16)
    send_part = part.reshape(arrived.shape)
    returned = lax.all_to_all(send_part, "expert", split_axis=0, concat_axis=0, tiled=True)
    weighted = own_weights.reshape(-1)[:, None] * returned.reshape(-1, width).astype(jnp.float32)
    term = (
        jnp.zeros((group_rows + 1, width), jnp.float32)
        .at[own_slots.reshape(-1)]
        .add(weighted)[:group_rows]
    )
    expert_sum = lax.psum_scatter(
        term.astype(jnp.bfloat16), "tensor", scatter_dimension=0, tiled=True
    ).astype(jnp.float32)
    next_residual = (first_residual.astype(jnp.float32) + expert_sum).astype(jnp.bfloat16)
    own_normed = normalize(next_residual.astype(jnp.float32), input_gain).astype(jnp.bfloat16)
    next_normed = lax.all_gather(own_normed, "tensor", axis=0, tiled=True)
    query_cols = q_weight.shape[1]
    kv_cols = kv_weight.shape[1]
    query_raw = jnp.dot(
        next_normed,
        lax.all_gather(q_weight, "expert", axis=0, tiled=True),
        preferred_element_type=jnp.float32,
    )
    kv_raw = jnp.dot(
        next_normed,
        lax.all_gather(kv_weight, "expert", axis=0, tiled=True),
        preferred_element_type=jnp.float32,
    )
    head_size = q_gain.shape[0]
    queries = (
        normalize(query_raw.reshape(group_rows, -1, head_size), q_gain)
        .reshape(group_rows, query_cols)
        .astype(jnp.bfloat16)
    )
    heads_here = kv_cols // head_size
    head_number = tensor_index * heads_here + jnp.arange(heads_here, dtype=jnp.int32)
    is_key = head_number < KV_HEADS
    kv_shaped = kv_raw.reshape(group_rows, heads_here, head_size)
    keys_values = (
        jnp.where(is_key[None, :, None], normalize(kv_shaped, k_gain), kv_shaped)
        .reshape(group_rows, kv_cols)
        .astype(jnp.bfloat16)
    )
    return (next_residual, queries, keys_values)


def solution(mesh):
    small = mesh.shape["tensor"] == 2 and mesh.shape["expert"] == 4 * PLANE
    return jax.shard_map(
        per_device_dense if small else per_device,
        mesh=mesh,
        in_specs=(
            P("expert", "tensor"),
            P("tensor", None),
            P(("expert", "tensor"), None),
            P(),
            P("expert", None),
            P("expert", None),
            P("expert", None, "tensor"),
            P("expert", None, "tensor"),
            P("expert", "tensor", None),
            P(),
            P("expert", "tensor"),
            P("expert", "tensor"),
            P(),
            P(),
        ),
        out_specs=(P(("expert", "tensor"), None), P("expert", "tensor"), P("expert", "tensor")),
        check_vma=False,
    )
```

```python
import functools

import jax
import jax.numpy as jnp
from jax import lax
from jax.experimental import pallas as pl
from jax.experimental.pallas import tpu as pltpu
from jax.sharding import PartitionSpec as P

KV_HEADS = 4
TOP = 8
PLANE = 4
META = 128


EPSILON = 1e-06

SMALL = pl.CostEstimate(flops=0, bytes_accessed=0, transcendentals=0)
VMEM = pl.BlockSpec(memory_space=pltpu.VMEM)
HBM = pl.BlockSpec(memory_space=pltpu.HBM)


def normalize(values, gain):
    return values * lax.rsqrt(jnp.mean(values * values, axis=-1, keepdims=True) + EPSILON) * gain


def params(mebibytes):
    return pltpu.CompilerParams(vmem_limit_bytes=mebibytes << 20)


def lanes(start, size):
    return pl.ds(pl.multiple_of(start, size), size)


def in_hbm(value):
    return pltpu.with_memory_space_constraint(value, pltpu.HBM)


def in_vmem(value):
    return pltpu.with_memory_space_constraint(value, pltpu.VMEM)


def out_projection_kernel(chunk, a_hbm, w_hbm, mine_ref, theirs_ref, a_buf, w_buf, a_sem, sems):
    depth = w_buf.shape[0]
    count = depth // chunk
    half = mine_ref.shape[0]
    a_copy = pltpu.make_async_copy(a_hbm, a_buf, a_sem)
    a_copy.start()
    copies = []
    for i in range(count):
        rows = pl.ds(i * chunk, chunk)
        copies.append(pltpu.make_async_copy(w_hbm.at[rows], w_buf.at[rows], sems.at[i]))
    for copy in copies:
        copy.start()
    tensor = lax.axis_index("tensor")
    own = lanes(tensor * half, half)
    other = lanes((1 - tensor) * half, half)
    a_copy.wait()
    for i in range(count):
        copies[i].wait()
        at = pl.ds(i * chunk, chunk)
        both = jnp.concatenate([a_buf[own, at], a_buf[other, at]], axis=0)
        product = jnp.dot(both, w_buf[at, :], preferred_element_type=jnp.float32)
        if i == 0:
            mine_ref[...] = product[:half]
            theirs_ref[...] = product[half:]
        else:
            mine_ref[...] += product[:half]
            theirs_ref[...] += product[half:]


def out_projection(attn_out, out_weight):
    rows, depth = attn_out.shape
    width = out_weight.shape[1]
    chunk = 256
    half = pltpu.VMEM((rows // 2, width), jnp.float32)
    return pl.pallas_call(
        functools.partial(out_projection_kernel, chunk),
        out_shape=(half, half),
        in_specs=[HBM, HBM],
        out_specs=(VMEM, VMEM),
        scratch_shapes=[
            pltpu.VMEM((rows, depth), jnp.bfloat16),
            pltpu.VMEM((depth, width), jnp.bfloat16),
            pltpu.SemaphoreType.DMA,
            pltpu.SemaphoreType.DMA((depth // chunk,)),
        ],
        compiler_params=params(14),
        cost_estimate=SMALL,
        name="out_projection",
    )(in_hbm(attn_out), in_hbm(out_weight))


def first_norm_kernel(depth, count, *refs):
    mine, theirs = refs[:count], refs[count : 2 * count]
    residual_ref, gain_ref, meta_ref, tokens_ref = refs[2 * count : 2 * count + 4]
    slice_refs, first_ref = refs[2 * count + 4 : -1], refs[-1]
    rows, width = residual_ref.shape
    sub = width // (PLANE * depth)
    start = 0
    for mine_ref, theirs_ref in zip(mine, theirs):
        cols = slice(start, start + mine_ref.shape[1])
        start += mine_ref.shape[1]
        first_ref[:, cols] = (
            residual_ref[:, cols].astype(jnp.float32) + (mine_ref[...] + theirs_ref[...])
        ).astype(jnp.bfloat16)
    first = first_ref[...]
    tokens_ref[:, :width] = normalize(first.astype(jnp.float32), gain_ref[...]).astype(jnp.bfloat16)
    tokens_ref[:, width:] = meta_ref[...]
    plane = lax.axis_index("expert") % PLANE
    for d in range(PLANE):
        for z in range(depth):
            slice_refs[d][z * rows : (z + 1) * rows, :] = first_ref[
                :, lanes((z * PLANE + (plane ^ d)) * sub, sub)
            ]


def first_norm(mine, theirs, residual, gain, meta, depth):
    rows, width = residual.shape
    piece = jax.ShapeDtypeStruct((depth * rows, width // (PLANE * depth)), jnp.bfloat16)
    return pl.pallas_call(
        functools.partial(first_norm_kernel, depth, len(mine)),
        out_shape=(jax.ShapeDtypeStruct((rows, width + META), jnp.bfloat16),) + (piece,) * PLANE,
        in_specs=[VMEM] * (2 * len(mine) + 3),
        out_specs=(VMEM,) * (1 + PLANE),
        scratch_shapes=[pltpu.VMEM((rows, width), jnp.bfloat16)],
        compiler_params=params(2),
        name="first_norm",
    )(*mine, *theirs, residual, gain, meta)


def pack_kernel(depth, *refs):
    line, pieces, out_refs = refs[:depth], refs[depth : depth + PLANE], refs[depth + PLANE :]
    rows, extended = line[0].shape
    sub = pieces[0].shape[1]
    for d, ref in enumerate(out_refs):
        for z in range(depth):
            ref[z * rows : (z + 1) * rows, :extended] = line[z][...]
        ref[:, extended : extended + sub] = pieces[d][...]
        ref[:, extended + sub :] = pieces[PLANE - 1][...]


def pack(line, pieces):
    depth = len(line)
    rows, extended = line[0].shape
    shape = pltpu.VMEM((depth * rows, extended + 2 * pieces[0].shape[1]), jnp.bfloat16)
    return pl.pallas_call(
        functools.partial(pack_kernel, depth),
        out_shape=(shape,) * (PLANE - 1),
        in_specs=[VMEM] * (depth + PLANE),
        out_specs=(VMEM,) * (PLANE - 1),
        compiler_params=params(2),
        name="pack_tokens",
    )(*line, *pieces)


def load_kernel(count, *refs):
    sources, targets, sems = refs[:count], refs[-count - 1 : -1], refs[-1]
    copies = [
        pltpu.make_async_copy(source, target, sems.at[i])
        for i, (source, target) in enumerate(zip(sources, targets))
    ]
    for copy in copies:
        copy.start()
    for copy in copies:
        copy.wait()


def load(weights, after):
    count = len(weights)
    return pl.pallas_call(
        functools.partial(load_kernel, count),
        out_shape=tuple(pltpu.VMEM(w.shape, w.dtype) for w in weights),
        in_specs=[HBM] * count + [pl.BlockSpec(memory_space=pl.ANY)] * len(after),
        out_specs=(VMEM,) * count,
        scratch_shapes=[pltpu.SemaphoreType.DMA((count,))],
        compiler_params=params(2),
        cost_estimate=SMALL,
        name="load_weights",
    )(*map(in_hbm, weights), *after)


def expert_kernel(depth, chunk, count, *refs):
    block_refs, (gate_ref, up_ref, down_ref) = refs[:count], refs[count : count + 3]
    mine_ref, *theirs_refs, x_buf, act_buf = refs[count + 3 :]
    width, hidden = gate_ref.shape[1:]
    extended = x_buf.shape[1]
    start = 0
    for ref in block_refs:
        rows = ref.shape[0]
        x_buf[start : start + rows, :] = ref[:, :extended]
        start += rows
    meta = x_buf[:, width:].astype(jnp.float32)
    lane = lax.broadcasted_iota(jnp.int32, meta.shape, 1)
    chip = lax.axis_index("expert")
    expert = 2 * chip + lax.axis_index("tensor")
    chosen = (lane == expert) | (lane == expert + META // 2)
    route = 0.5 * jnp.sum(jnp.where(chosen, meta, 0.0), axis=1, keepdims=True)
    for i in range(hidden // chunk):
        cols = pl.ds(i * chunk, chunk)
        x = x_buf[:, :width]
        gate = jnp.dot(x, gate_ref[0, :, cols], preferred_element_type=jnp.float32)
        up = jnp.dot(x, up_ref[0, :, cols], preferred_element_type=jnp.float32)
        act = gate * (1.0 + jnp.tanh(0.5 * gate)) * (up * route)
        act_buf[:, i * chunk : (i + 1) * chunk] = act.astype(jnp.bfloat16)
    sub = width // (PLANE * depth)
    part = sub * depth
    half = mine_ref.shape[0]
    plane = chip % PLANE
    for d in range(PLANE):
        weight = jnp.concatenate(
            [down_ref[0, :, lanes((z * PLANE + (plane ^ d)) * sub, sub)] for z in range(depth)],
            axis=1,
        )
        out = jnp.dot(act_buf[...], weight, preferred_element_type=jnp.float32)
        cols = slice(d * part, (d + 1) * part)
        mine_ref[:, cols] = out[:half].astype(jnp.bfloat16)
        start = half
        for ref in theirs_refs:
            stop = start + ref.shape[0]
            ref[:, cols] = out[start:stop].astype(jnp.bfloat16)
            start = stop


def experts(blocks, weights, depth, pieces):
    width, hidden = weights[0].shape[1:]
    chunk = 256
    extended = width + META
    total = sum(block.shape[0] for block in blocks)
    rows = [total // 2] + [total // 2 // pieces] * pieces
    return pl.pallas_call(
        functools.partial(expert_kernel, depth, chunk, len(blocks)),
        out_shape=tuple(pltpu.VMEM((size, width), jnp.bfloat16) for size in rows),
        in_specs=[VMEM] * (len(blocks) + 3),
        out_specs=(VMEM,) * (1 + pieces),
        scratch_shapes=[
            pltpu.VMEM((total, extended), jnp.bfloat16),
            pltpu.VMEM((total, hidden), jnp.bfloat16),
        ],
        compiler_params=params(16),
        cost_estimate=pl.CostEstimate(
            flops=6 * total * width * hidden, bytes_accessed=0, transcendentals=0
        ),
        name="experts",
    )(*blocks, *weights)


def chip_sum_kernel(count, *refs):
    mine, theirs, out_refs = refs[:2], refs[2 : 2 + count], refs[2 + count :]
    part = out_refs[0].shape[1]
    start = 0
    for own_ref in mine:
        first = start
        while start < first + own_ref.shape[0]:
            ref, theirs = theirs[0], theirs[1:]
            size = ref.shape[0]
            own = slice(start - first, start - first + size)
            for d, out_ref in enumerate(out_refs):
                at = slice(d * part, (d + 1) * part)
                total = own_ref[own, at].astype(jnp.float32) + ref[:, at].astype(jnp.float32)
                out_ref[start : start + size, :] = total.astype(jnp.bfloat16)
            start += size


def chip_sum(mine, theirs):
    rows, width = sum(value.shape[0] for value in mine), mine[0].shape[1]
    return pl.pallas_call(
        functools.partial(chip_sum_kernel, len(theirs)),
        out_shape=(pltpu.VMEM((rows, width // PLANE), jnp.bfloat16),) * PLANE,
        in_specs=[VMEM] * (2 + len(theirs)),
        out_specs=(VMEM,) * PLANE,
        compiler_params=params(4),
        name="chip_sum",
    )(*mine, *theirs)


def plane_sum_kernel(depth, *refs):
    in_refs, out_refs = refs[:PLANE], refs[PLANE:]
    group = in_refs[0].shape[0] // PLANE
    rows = group // depth
    for k in range(PLANE):
        for z in range(depth):
            total = 0.0
            for d in range(PLANE):
                start = (k ^ d) * group + z * rows
                total = total + in_refs[d][start : start + rows, :].astype(jnp.float32)
            out_refs[z][k * rows : (k + 1) * rows, :] = total.astype(jnp.bfloat16)


def plane_sum(parts, depth):
    rows, part = parts[0].shape
    return pl.pallas_call(
        functools.partial(plane_sum_kernel, depth),
        out_shape=(pltpu.VMEM((rows // depth, part), jnp.bfloat16),) * depth,
        in_specs=[VMEM] * PLANE,
        out_specs=(VMEM,) * depth,
        compiler_params=params(4),
        name="plane_sum",
    )(*parts)


def second_norm_kernel(depth, *refs):
    parts, packed = refs[:depth], refs[depth : depth + PLANE + 1]
    gain_ref, scaled_ref, next_ref = refs[depth + PLANE + 1 :]
    rows = packed[0].shape[0] // depth
    part = parts[0].shape[1]
    sub = part // depth
    skip = packed[0].shape[1] - 2 * sub
    lane = lax.broadcasted_iota(jnp.int32, (rows, META), 1)
    plane = lax.axis_index("expert") % PLANE
    gain = jnp.concatenate(
        [gain_ref[:, lanes((z * PLANE + plane) * sub, sub)] for z in range(depth)], axis=1
    )
    for d in range(PLANE):
        at = slice(d * rows, (d + 1) * rows)
        total = parts[0][at, :].astype(jnp.float32)
        for ref in parts[1:]:
            total = total + ref[at, :].astype(jnp.float32)
        if d < PLANE - 1:
            first = packed[d][:, skip : skip + sub]
        else:
            first = jnp.concatenate([ref[:, skip + sub :] for ref in packed[d:]], axis=0)
        first = jnp.concatenate([first[z * rows : (z + 1) * rows] for z in range(depth)], axis=1)
        following = (first.astype(jnp.float32) + total).astype(jnp.bfloat16)
        next_ref[at, :] = following
        wide = following.astype(jnp.float32)
        scaled_ref[at, :part] = (wide * gain).astype(jnp.bfloat16)
        squares = jnp.sum(wide * wide, axis=1, keepdims=True)
        high = squares.astype(jnp.bfloat16).astype(jnp.float32)
        low = squares - high
        scaled_ref[at, part:] = jnp.where(
            lane == 0, high, jnp.where(lane == 1, low, 0.0)
        ).astype(jnp.bfloat16)


def second_norm(parts, packed, gain):
    depth = len(parts)
    rows, part = parts[0].shape
    return pl.pallas_call(
        functools.partial(second_norm_kernel, depth),
        out_shape=(
            jax.ShapeDtypeStruct((rows, part + META), jnp.bfloat16),
            jax.ShapeDtypeStruct((rows, part), jnp.bfloat16),
        ),
        in_specs=[VMEM] * (depth + PLANE + 2),
        out_specs=(VMEM, VMEM),
        compiler_params=params(4),
        name="second_norm",
    )(*parts, *packed, gain)


def projection_kernel(chunk, mine_ref, theirs_ref, next_ref, q_ref, *refs):
    kv_refs, out_refs, kv_buf = refs[: -PLANE - 1], refs[-PLANE - 1 : -1], refs[-1]
    depth = len(kv_refs)
    rows, extended = mine_ref.shape
    part = extended - META
    sub = part // depth
    q_cols, kv_cols = q_ref.shape[1], kv_buf.shape[1]
    cols = q_cols + kv_cols
    line = lax.axis_index("expert") // PLANE
    for d, ref in enumerate(kv_refs):
        kv_buf[lanes((line ^ d) * sub, sub), :] = ref[...]
    block = rows // PLANE
    tensor = lax.axis_index("tensor")
    own = lanes(tensor * block, block)
    other = lanes((1 - tensor) * block, block)
    for d in range(PLANE):
        at = slice(d * block, (d + 1) * block)
        out_refs[d][own, cols : cols + META] = mine_ref[at, part:]
        out_refs[d][other, cols : cols + META] = theirs_ref[at, part:]
        out_refs[d][:block, cols + META :] = next_ref[at, : part // 2]
        out_refs[d][block:, cols + META :] = next_ref[at, part // 2 :]
    both = jnp.concatenate([mine_ref[:, :part], theirs_ref[:, :part]], axis=0)

    def multiply(weight, target):
        product = jnp.dot(both, weight, preferred_element_type=jnp.float32).astype(jnp.bfloat16)
        at = slice(target, target + weight.shape[1])
        for d in range(PLANE):
            out_refs[d][own, at] = product[d * block : (d + 1) * block]
            out_refs[d][other, at] = product[rows + d * block : rows + (d + 1) * block]

    multiply(kv_buf[...], q_cols)
    for start in range(0, q_cols, chunk):
        multiply(q_ref[:, start : start + chunk], start)


def projection(mine, theirs, following, q_weight, kv_weights):
    rows, part = following.shape
    q_cols, kv_cols = q_weight.shape[1], kv_weights[0].shape[1]
    chunk = 512
    shape = pltpu.VMEM((2 * rows // PLANE, q_cols + kv_cols + META + part // 2), jnp.bfloat16)
    return pl.pallas_call(
        functools.partial(projection_kernel, chunk),
        out_shape=(shape,) * PLANE,
        in_specs=[VMEM] * (4 + len(kv_weights)),
        out_specs=(VMEM,) * PLANE,
        scratch_shapes=[pltpu.VMEM((part, kv_cols), jnp.bfloat16)],
        compiler_params=params(8),
        cost_estimate=SMALL,
        name="qkv_projection",
    )(mine, theirs, following, q_weight, *kv_weights)


def head_norm_kernel(depth, *refs):
    parts, q_gain_ref, k_gain_ref = refs[:PLANE], refs[PLANE], refs[PLANE + 1]
    next_ref, q_ref, kv_ref = refs[PLANE + 2 :]
    width = next_ref.shape[1]
    q_cols, kv_cols = q_ref.shape[1], kv_ref.shape[1]
    cols = q_cols + kv_cols
    head = q_gain_ref.shape[1]

    def total(at):
        value = parts[0][:, at].astype(jnp.float32)
        for ref in parts[1:]:
            value = value + ref[:, at].astype(jnp.float32)
        return value

    squares = jnp.sum(total(slice(cols, cols + META)), axis=1, keepdims=True)
    scale = lax.rsqrt(squares / width + EPSILON)
    for h in range(q_cols // head):
        at = slice(h * head, (h + 1) * head)
        q_ref[:, at] = normalize(total(at) * scale, q_gain_ref[...]).astype(jnp.bfloat16)
    tensor = lax.axis_index("tensor")
    for h in range(kv_cols // head):
        at = slice(h * head, (h + 1) * head)
        raw = total(slice(q_cols + h * head, q_cols + (h + 1) * head)) * scale
        is_key = tensor * (kv_cols // head) + h < KV_HEADS
        kv_ref[:, at] = jnp.where(is_key, normalize(raw, k_gain_ref[...]), raw).astype(
            jnp.bfloat16
        )
    plane = lax.axis_index("expert") % PLANE
    rows = next_ref.shape[0]
    sub = width // (PLANE * depth)
    for d in range(PLANE):
        for z in range(depth):
            top = z * sub * 2 // (depth * sub)
            start = cols + META + z * sub - top * (depth * sub // 2)
            next_ref[:, lanes((z * PLANE + (plane ^ d)) * sub, sub)] = parts[d][
                top * rows : (top + 1) * rows, start : start + sub
            ]


def head_norm(parts, q_gain, k_gain, q_cols, kv_cols, rows, width, depth):
    both = parts[0].shape[0]
    return pl.pallas_call(
        functools.partial(head_norm_kernel, depth),
        out_shape=(
            jax.ShapeDtypeStruct((rows, width), jnp.bfloat16),
            jax.ShapeDtypeStruct((both, q_cols), jnp.bfloat16),
            jax.ShapeDtypeStruct((both, kv_cols), jnp.bfloat16),
        ),
        in_specs=[VMEM] * (PLANE + 2),
        out_specs=(VMEM, VMEM, VMEM),
        compiler_params=params(4),
        name="head_norm",
    )(*parts, q_gain, k_gain)


def per_device_dense(
    attn_out,
    out_weight,
    residual,
    attn_gain,
    expert_ids,
    route_weights,
    w_gate,
    w_up,
    w_down,
    input_gain,
    q_weight,
    kv_weight,
    q_gain,
    k_gain,
):
    n_expert = lax.axis_size("expert")
    depth = n_expert // PLANE
    rows, width = residual.shape
    tensor_index = lax.axis_index("tensor").astype(jnp.int32)

    def to_core(value):
        return lax.ppermute(value, "tensor", [(0, 1), (1, 0)])

    def to_expert(value, offset):
        return lax.ppermute(value, "expert", [(i, i ^ offset) for i in range(n_expert)])

    def to_z(values):
        return [to_expert(v, d * PLANE) if d else v for d, v in enumerate(values)]

    def to_plane(values):
        return [to_expert(v, d) if d else v for d, v in enumerate(values)]

    own_ids = lax.dynamic_slice_in_dim(expert_ids, tensor_index * rows, rows, 0)
    own_route = lax.dynamic_slice_in_dim(route_weights, tensor_index * rows, rows, 0)
    chosen = own_ids[:, :, None] == jnp.arange(META // 2, dtype=jnp.int32)[None, None, :]
    dense = jnp.sum(jnp.where(chosen, own_route[:, :, None], 0.0), axis=1)
    high = lax.reduce_precision(dense, 8, 7)
    meta = jnp.concatenate([high, dense - high], axis=1).astype(jnp.bfloat16)

    lines = [list(range(i, n_expert, PLANE)) for i in range(PLANE)]
    mine, theirs = out_projection(attn_out, out_weight)
    tokens, *firsts = first_norm(
        (mine,), (to_core(theirs),), residual, attn_gain[None, :], meta, depth
    )
    tokens, q_own, kv_own = lax.optimization_barrier((tokens, q_weight, kv_weight))
    q_rows = lax.all_gather(q_own, "expert", axis=0, tiled=True, axis_index_groups=lines)
    weights = load((w_gate, w_up, w_down), (tokens,))
    line = to_z([tokens] * depth)
    *line, gate, up, down, kv_own = lax.optimization_barrier((*line, *weights, kv_own))
    weights = (gate, up, down)
    kv_rows = [kv_own, to_expert(kv_own, PLANE)]
    near = to_plane(pack(line, firsts))
    near[2], kv_rows[1] = lax.optimization_barrier((near[2], kv_rows[1]))
    cut = near[0].shape[0] // 2
    one, two = near[1][:cut], near[2][cut:]
    far = [to_expert(one, 2), to_expert(two, 1)]
    near_mine, *near_theirs = experts((*near, *map(to_core, near)), weights, depth, len(near))
    theirs = list(map(to_core, near_theirs))
    near_mine, *far = lax.optimization_barrier((near_mine, *far))
    far_both = [*far, *map(to_core, far)]
    far_mine, *far_theirs = experts(far_both, weights, depth, 1)
    theirs += map(to_core, far_theirs)
    parts = to_plane(chip_sum((near_mine, far_mine), theirs))
    kv_rows.append(to_expert(kv_own, 2 * PLANE))
    *parts, kv_rows[2] = lax.optimization_barrier((*plane_sum(parts, depth), kv_rows[2]))
    kv_rows.append(to_expert(kv_rows[2], PLANE))
    (q_rows,) = load((q_rows,), parts)
    parts = to_z(parts)
    *parts, q_rows = lax.optimization_barrier((*parts, q_rows))
    scaled, following = second_norm(parts, (*near, *far), input_gain[None, :])
    products = to_plane(projection(scaled, to_core(scaled), following, q_rows, kv_rows))
    return head_norm(
        products,
        q_gain[None, :],
        k_gain[None, :],
        q_weight.shape[1],
        kv_weight.shape[1],
        rows,
        width,
        depth,
    )


def per_device(
    attn_out,
    out_weight,
    residual,
    attn_gain,
    expert_ids,
    route_weights,
    w_gate,
    w_up,
    w_down,
    input_gain,
    q_weight,
    kv_weight,
    q_gain,
    k_gain,
):
    n_expert = lax.axis_size("expert")
    n_tensor = lax.axis_size("tensor")
    share = n_tensor // 2
    tensor_index = lax.axis_index("tensor")
    group_rows = attn_out.shape[0]
    width = residual.shape[1]
    half = tensor_index // share
    capacity = 3 * group_rows * TOP // (4 * n_expert)
    all_experts = 2 * n_expert
    attn_rows = lax.psum_scatter(
        jnp.dot(attn_out, out_weight, preferred_element_type=jnp.float32),
        "tensor",
        scatter_dimension=0,
        tiled=True,
    )
    first_residual = (residual.astype(jnp.float32) + attn_rows).astype(jnp.bfloat16)
    normed = normalize(first_residual.astype(jnp.float32), attn_gain).astype(jnp.bfloat16)
    group_normed = lax.all_gather(normed, "tensor", axis=0, tiled=True)
    flat_ids = expert_ids.reshape(-1)
    onehot = (flat_ids[:, None] == jnp.arange(all_experts, dtype=jnp.int32)[None, :]).astype(
        jnp.int32
    )
    earlier = jnp.cumsum(onehot, axis=0) - onehot
    rank = jnp.sum(earlier * onehot, axis=1)
    dest = flat_ids * capacity + rank
    row_owner = jnp.arange(flat_ids.shape[0], dtype=jnp.int32) // TOP
    slot_row = jnp.full((all_experts * capacity,), group_rows, jnp.int32).at[dest].set(row_owner)
    slot_weight = (
        jnp.zeros((all_experts * capacity,), jnp.float32).at[dest].set(route_weights.reshape(-1))
    )
    own_slots = lax.dynamic_index_in_dim(
        slot_row.reshape(n_expert, 2, capacity), half, 1, keepdims=False
    )
    own_weights = lax.dynamic_index_in_dim(
        slot_weight.reshape(n_expert, 2, capacity), half, 1, keepdims=False
    )
    padded_rows = jnp.concatenate([group_normed, jnp.zeros((1, width), jnp.bfloat16)], axis=0)
    gate_w = w_gate[0]
    up_w = w_up[0]
    down_w = w_down[0]
    outgoing = jnp.take(padded_rows, own_slots, axis=0)
    arrived = lax.all_to_all(outgoing, "expert", split_axis=0, concat_axis=0, tiled=True)
    flat = arrived.reshape(-1, width)
    gate = jnp.dot(flat, gate_w, preferred_element_type=jnp.float32)
    up = jnp.dot(flat, up_w, preferred_element_type=jnp.float32)
    act = (jax.nn.silu(gate) * up).astype(jnp.bfloat16)
    part = jnp.dot(act, down_w, preferred_element_type=jnp.float32).astype(jnp.bfloat16)
    send_part = part.reshape(arrived.shape)
    returned = lax.all_to_all(send_part, "expert", split_axis=0, concat_axis=0, tiled=True)
    weighted = own_weights.reshape(-1)[:, None] * returned.reshape(-1, width).astype(jnp.float32)
    term = (
        jnp.zeros((group_rows + 1, width), jnp.float32)
        .at[own_slots.reshape(-1)]
        .add(weighted)[:group_rows]
    )
    expert_sum = lax.psum_scatter(
        term.astype(jnp.bfloat16), "tensor", scatter_dimension=0, tiled=True
    ).astype(jnp.float32)
    next_residual = (first_residual.astype(jnp.float32) + expert_sum).astype(jnp.bfloat16)
    own_normed = normalize(next_residual.astype(jnp.float32), input_gain).astype(jnp.bfloat16)
    next_normed = lax.all_gather(own_normed, "tensor", axis=0, tiled=True)
    query_cols = q_weight.shape[1]
    kv_cols = kv_weight.shape[1]
    query_raw = jnp.dot(
        next_normed,
        lax.all_gather(q_weight, "expert", axis=0, tiled=True),
        preferred_element_type=jnp.float32,
    )
    kv_raw = jnp.dot(
        next_normed,
        lax.all_gather(kv_weight, "expert", axis=0, tiled=True),
        preferred_element_type=jnp.float32,
    )
    head_size = q_gain.shape[0]
    queries = (
        normalize(query_raw.reshape(group_rows, -1, head_size), q_gain)
        .reshape(group_rows, query_cols)
        .astype(jnp.bfloat16)
    )
    heads_here = kv_cols // head_size
    head_number = tensor_index * heads_here + jnp.arange(heads_here, dtype=jnp.int32)
    is_key = head_number < KV_HEADS
    kv_shaped = kv_raw.reshape(group_rows, heads_here, head_size)
    keys_values = (
        jnp.where(is_key[None, :, None], normalize(kv_shaped, k_gain), kv_shaped)
        .reshape(group_rows, kv_cols)
        .astype(jnp.bfloat16)
    )
    return (next_residual, queries, keys_values)


def solution(mesh):
    small = mesh.shape["tensor"] == 2 and mesh.shape["expert"] == 4 * PLANE
    return jax.shard_map(
        per_device_dense if small else per_device,
        mesh=mesh,
        in_specs=(
            P("expert", "tensor"),
            P("tensor", None),
            P(("expert", "tensor"), None),
            P(),
            P("expert", None),
            P("expert", None),
            P("expert", None, "tensor"),
            P("expert", None, "tensor"),
            P("expert", "tensor", None),
            P(),
            P("expert", "tensor"),
            P("expert", "tensor"),
            P(),
            P(),
        ),
        out_specs=(P(("expert", "tensor"), None), P("expert", "tensor"), P("expert", "tensor")),
        check_vma=False,
    )
```

```python
import functools

import jax
import jax.numpy as jnp
from jax import lax
from jax.experimental import pallas as pl
from jax.experimental.pallas import tpu as pltpu
from jax.sharding import PartitionSpec as P

KV_HEADS = 4
TOP = 8
PLANE = 4
META = 128


EPSILON = 1e-06

SMALL = pl.CostEstimate(flops=0, bytes_accessed=0, transcendentals=0)
VMEM = pl.BlockSpec(memory_space=pltpu.VMEM)
HBM = pl.BlockSpec(memory_space=pltpu.HBM)


def normalize(values, gain):
    return values * lax.rsqrt(jnp.mean(values * values, axis=-1, keepdims=True) + EPSILON) * gain


def params(mebibytes):
    return pltpu.CompilerParams(vmem_limit_bytes=mebibytes << 20)


def lanes(start, size):
    return pl.ds(pl.multiple_of(start, size), size)


def in_hbm(value):
    return pltpu.with_memory_space_constraint(value, pltpu.HBM)


def in_vmem(value):
    return pltpu.with_memory_space_constraint(value, pltpu.VMEM)


def out_projection_kernel(chunk, a_hbm, w_hbm, mine_ref, theirs_ref, a_buf, w_buf, a_sem, sems):
    depth = w_buf.shape[0]
    count = depth // chunk
    half = mine_ref.shape[0]
    a_copy = pltpu.make_async_copy(a_hbm, a_buf, a_sem)
    a_copy.start()
    copies = []
    for i in range(count):
        rows = pl.ds(i * chunk, chunk)
        copies.append(pltpu.make_async_copy(w_hbm.at[rows], w_buf.at[rows], sems.at[i]))
    for copy in copies:
        copy.start()
    tensor = lax.axis_index("tensor")
    own = lanes(tensor * half, half)
    other = lanes((1 - tensor) * half, half)
    a_copy.wait()
    for i in range(count):
        copies[i].wait()
        at = pl.ds(i * chunk, chunk)
        both = jnp.concatenate([a_buf[own, at], a_buf[other, at]], axis=0)
        product = jnp.dot(both, w_buf[at, :], preferred_element_type=jnp.float32)
        if i == 0:
            mine_ref[...] = product[:half]
            theirs_ref[...] = product[half:]
        else:
            mine_ref[...] += product[:half]
            theirs_ref[...] += product[half:]


def out_projection(attn_out, out_weight):
    rows, depth = attn_out.shape
    width = out_weight.shape[1]
    chunk = 256
    half = pltpu.VMEM((rows // 2, width), jnp.float32)
    return pl.pallas_call(
        functools.partial(out_projection_kernel, chunk),
        out_shape=(half, half),
        in_specs=[HBM, HBM],
        out_specs=(VMEM, VMEM),
        scratch_shapes=[
            pltpu.VMEM((rows, depth), jnp.bfloat16),
            pltpu.VMEM((depth, width), jnp.bfloat16),
            pltpu.SemaphoreType.DMA,
            pltpu.SemaphoreType.DMA((depth // chunk,)),
        ],
        compiler_params=params(14),
        cost_estimate=SMALL,
        name="out_projection",
    )(in_hbm(attn_out), in_hbm(out_weight))


def first_norm_kernel(depth, count, *refs):
    mine, theirs = refs[:count], refs[count : 2 * count]
    residual_ref, gain_ref, meta_ref, tokens_ref = refs[2 * count : 2 * count + 4]
    slice_refs, first_ref = refs[2 * count + 4 : -1], refs[-1]
    rows, width = residual_ref.shape
    sub = width // (PLANE * depth)
    start = 0
    for mine_ref, theirs_ref in zip(mine, theirs):
        cols = slice(start, start + mine_ref.shape[1])
        start += mine_ref.shape[1]
        first_ref[:, cols] = (
            residual_ref[:, cols].astype(jnp.float32) + (mine_ref[...] + theirs_ref[...])
        ).astype(jnp.bfloat16)
    first = first_ref[...]
    tokens_ref[:, :width] = normalize(first.astype(jnp.float32), gain_ref[...]).astype(jnp.bfloat16)
    tokens_ref[:, width:] = meta_ref[...]
    plane = lax.axis_index("expert") % PLANE
    for d in range(PLANE):
        for z in range(depth):
            slice_refs[d][z * rows : (z + 1) * rows, :] = first_ref[
                :, lanes((z * PLANE + (plane ^ d)) * sub, sub)
            ]


def first_norm(mine, theirs, residual, gain, meta, depth):
    rows, width = residual.shape
    piece = jax.ShapeDtypeStruct((depth * rows, width // (PLANE * depth)), jnp.bfloat16)
    return pl.pallas_call(
        functools.partial(first_norm_kernel, depth, len(mine)),
        out_shape=(jax.ShapeDtypeStruct((rows, width + META), jnp.bfloat16),) + (piece,) * PLANE,
        in_specs=[VMEM] * (2 * len(mine) + 3),
        out_specs=(VMEM,) * (1 + PLANE),
        scratch_shapes=[pltpu.VMEM((rows, width), jnp.bfloat16)],
        compiler_params=params(2),
        name="first_norm",
    )(*mine, *theirs, residual, gain, meta)


def pack_kernel(depth, *refs):
    line, pieces, out_refs = refs[:depth], refs[depth : depth + PLANE], refs[depth + PLANE :]
    rows, extended = line[0].shape
    sub = pieces[0].shape[1]
    for d, ref in enumerate(out_refs):
        for z in range(depth):
            ref[z * rows : (z + 1) * rows, :extended] = line[z][...]
        ref[:, extended : extended + sub] = pieces[d][...]
        ref[:, extended + sub :] = pieces[PLANE - 1][...]


def pack(line, pieces):
    depth = len(line)
    rows, extended = line[0].shape
    shape = pltpu.VMEM((depth * rows, extended + 2 * pieces[0].shape[1]), jnp.bfloat16)
    return pl.pallas_call(
        functools.partial(pack_kernel, depth),
        out_shape=(shape,) * (PLANE - 1),
        in_specs=[VMEM] * (depth + PLANE),
        out_specs=(VMEM,) * (PLANE - 1),
        compiler_params=params(2),
        name="pack_tokens",
    )(*line, *pieces)


def load_kernel(count, *refs):
    sources, targets, sems = refs[:count], refs[-count - 1 : -1], refs[-1]
    copies = [
        pltpu.make_async_copy(source, target, sems.at[i])
        for i, (source, target) in enumerate(zip(sources, targets))
    ]
    for copy in copies:
        copy.start()
    for copy in copies:
        copy.wait()


def load(weights, after):
    count = len(weights)
    return pl.pallas_call(
        functools.partial(load_kernel, count),
        out_shape=tuple(pltpu.VMEM(w.shape, w.dtype) for w in weights),
        in_specs=[HBM] * count + [pl.BlockSpec(memory_space=pl.ANY)] * len(after),
        out_specs=(VMEM,) * count,
        scratch_shapes=[pltpu.SemaphoreType.DMA((count,))],
        compiler_params=params(2),
        cost_estimate=SMALL,
        name="load_weights",
    )(*map(in_hbm, weights), *after)


def expert_kernel(depth, chunk, count, *refs):
    block_refs, (gate_ref, up_ref, down_ref) = refs[:count], refs[count : count + 3]
    mine_ref, *theirs_refs, x_buf, act_buf = refs[count + 3 :]
    width, hidden = gate_ref.shape[1:]
    extended = x_buf.shape[1]
    start = 0
    for ref in block_refs:
        rows = ref.shape[0]
        x_buf[start : start + rows, :] = ref[:, :extended]
        start += rows
    meta = x_buf[:, width:].astype(jnp.float32)
    lane = lax.broadcasted_iota(jnp.int32, meta.shape, 1)
    chip = lax.axis_index("expert")
    expert = 2 * chip + lax.axis_index("tensor")
    chosen = (lane == expert) | (lane == expert + META // 2)
    route = 0.5 * jnp.sum(jnp.where(chosen, meta, 0.0), axis=1, keepdims=True)
    for i in range(hidden // chunk):
        cols = pl.ds(i * chunk, chunk)
        x = x_buf[:, :width]
        gate = jnp.dot(x, gate_ref[0, :, cols], preferred_element_type=jnp.float32)
        up = jnp.dot(x, up_ref[0, :, cols], preferred_element_type=jnp.float32)
        act = gate * (1.0 + jnp.tanh(0.5 * gate)) * (up * route)
        act_buf[:, i * chunk : (i + 1) * chunk] = act.astype(jnp.bfloat16)
    sub = width // (PLANE * depth)
    part = sub * depth
    half = mine_ref.shape[0]
    plane = chip % PLANE
    for d in range(PLANE):
        weight = jnp.concatenate(
            [down_ref[0, :, lanes((z * PLANE + (plane ^ d)) * sub, sub)] for z in range(depth)],
            axis=1,
        )
        out = jnp.dot(act_buf[...], weight, preferred_element_type=jnp.float32)
        cols = slice(d * part, (d + 1) * part)
        mine_ref[:, cols] = out[:half].astype(jnp.bfloat16)
        start = half
        for ref in theirs_refs:
            stop = start + ref.shape[0]
            ref[:, cols] = out[start:stop].astype(jnp.bfloat16)
            start = stop


def experts(blocks, weights, depth, pieces):
    width, hidden = weights[0].shape[1:]
    chunk = 256
    extended = width + META
    total = sum(block.shape[0] for block in blocks)
    rows = [total // 2] + [total // 2 // pieces] * pieces
    return pl.pallas_call(
        functools.partial(expert_kernel, depth, chunk, len(blocks)),
        out_shape=tuple(pltpu.VMEM((size, width), jnp.bfloat16) for size in rows),
        in_specs=[VMEM] * (len(blocks) + 3),
        out_specs=(VMEM,) * (1 + pieces),
        scratch_shapes=[
            pltpu.VMEM((total, extended), jnp.bfloat16),
            pltpu.VMEM((total, hidden), jnp.bfloat16),
        ],
        compiler_params=params(16),
        cost_estimate=pl.CostEstimate(
            flops=6 * total * width * hidden, bytes_accessed=0, transcendentals=0
        ),
        name="experts",
    )(*blocks, *weights)


def chip_sum_kernel(count, *refs):
    mine, theirs, out_refs = refs[:2], refs[2 : 2 + count], refs[2 + count :]
    part = out_refs[0].shape[1]
    start = 0
    for own_ref in mine:
        first = start
        while start < first + own_ref.shape[0]:
            ref, theirs = theirs[0], theirs[1:]
            size = ref.shape[0]
            own = slice(start - first, start - first + size)
            for d, out_ref in enumerate(out_refs):
                at = slice(d * part, (d + 1) * part)
                total = own_ref[own, at].astype(jnp.float32) + ref[:, at].astype(jnp.float32)
                out_ref[start : start + size, :] = total.astype(jnp.bfloat16)
            start += size


def chip_sum(mine, theirs):
    rows, width = sum(value.shape[0] for value in mine), mine[0].shape[1]
    return pl.pallas_call(
        functools.partial(chip_sum_kernel, len(theirs)),
        out_shape=(pltpu.VMEM((rows, width // PLANE), jnp.bfloat16),) * PLANE,
        in_specs=[VMEM] * (2 + len(theirs)),
        out_specs=(VMEM,) * PLANE,
        compiler_params=params(4),
        name="chip_sum",
    )(*mine, *theirs)


def plane_sum_kernel(depth, *refs):
    in_refs, out_refs = refs[:PLANE], refs[PLANE:]
    group = in_refs[0].shape[0] // PLANE
    rows = group // depth
    for k in range(PLANE):
        for z in range(depth):
            total = 0.0
            for d in range(PLANE):
                start = (k ^ d) * group + z * rows
                total = total + in_refs[d][start : start + rows, :].astype(jnp.float32)
            out_refs[z][k * rows : (k + 1) * rows, :] = total.astype(jnp.bfloat16)


def plane_sum(parts, depth):
    rows, part = parts[0].shape
    return pl.pallas_call(
        functools.partial(plane_sum_kernel, depth),
        out_shape=(pltpu.VMEM((rows // depth, part), jnp.bfloat16),) * depth,
        in_specs=[VMEM] * PLANE,
        out_specs=(VMEM,) * depth,
        compiler_params=params(4),
        name="plane_sum",
    )(*parts)


def second_norm_kernel(depth, *refs):
    parts, packed = refs[:depth], refs[depth : depth + PLANE + 1]
    gain_ref, scaled_ref, next_ref = refs[depth + PLANE + 1 :]
    rows = packed[0].shape[0] // depth
    part = parts[0].shape[1]
    sub = part // depth
    skip = packed[0].shape[1] - 2 * sub
    lane = lax.broadcasted_iota(jnp.int32, (rows, META), 1)
    plane = lax.axis_index("expert") % PLANE
    gain = jnp.concatenate(
        [gain_ref[:, lanes((z * PLANE + plane) * sub, sub)] for z in range(depth)], axis=1
    )
    for d in range(PLANE):
        at = slice(d * rows, (d + 1) * rows)
        total = parts[0][at, :].astype(jnp.float32)
        for ref in parts[1:]:
            total = total + ref[at, :].astype(jnp.float32)
        if d < PLANE - 1:
            first = packed[d][:, skip : skip + sub]
        else:
            first = jnp.concatenate([ref[:, skip + sub :] for ref in packed[d:]], axis=0)
        first = jnp.concatenate([first[z * rows : (z + 1) * rows] for z in range(depth)], axis=1)
        following = (first.astype(jnp.float32) + total).astype(jnp.bfloat16)
        next_ref[at, :] = following
        wide = following.astype(jnp.float32)
        scaled_ref[at, :part] = (wide * gain).astype(jnp.bfloat16)
        squares = jnp.sum(wide * wide, axis=1, keepdims=True)
        high = squares.astype(jnp.bfloat16).astype(jnp.float32)
        low = squares - high
        scaled_ref[at, part:] = jnp.where(
            lane == 0, high, jnp.where(lane == 1, low, 0.0)
        ).astype(jnp.bfloat16)


def second_norm(parts, packed, gain):
    depth = len(parts)
    rows, part = parts[0].shape
    return pl.pallas_call(
        functools.partial(second_norm_kernel, depth),
        out_shape=(
            jax.ShapeDtypeStruct((rows, part + META), jnp.bfloat16),
            jax.ShapeDtypeStruct((rows, part), jnp.bfloat16),
        ),
        in_specs=[VMEM] * (depth + PLANE + 2),
        out_specs=(VMEM, VMEM),
        compiler_params=params(4),
        name="second_norm",
    )(*parts, *packed, gain)


def projection_kernel(chunk, mine_ref, theirs_ref, next_ref, q_ref, *refs):
    kv_refs, out_refs, kv_buf = refs[: -PLANE - 1], refs[-PLANE - 1 : -1], refs[-1]
    depth = len(kv_refs)
    rows, extended = mine_ref.shape
    part = extended - META
    sub = part // depth
    q_cols, kv_cols = q_ref.shape[1], kv_buf.shape[1]
    cols = q_cols + kv_cols
    line = lax.axis_index("expert") // PLANE
    for d, ref in enumerate(kv_refs):
        kv_buf[lanes((line ^ d) * sub, sub), :] = ref[...]
    block = rows // PLANE
    tensor = lax.axis_index("tensor")
    own = lanes(tensor * block, block)
    other = lanes((1 - tensor) * block, block)
    for d in range(PLANE):
        at = slice(d * block, (d + 1) * block)
        out_refs[d][own, cols : cols + META] = mine_ref[at, part:]
        out_refs[d][other, cols : cols + META] = theirs_ref[at, part:]
        out_refs[d][:block, cols + META :] = next_ref[at, : part // 2]
        out_refs[d][block:, cols + META :] = next_ref[at, part // 2 :]
    both = jnp.concatenate([mine_ref[:, :part], theirs_ref[:, :part]], axis=0)

    def multiply(weight, target):
        product = jnp.dot(both, weight, preferred_element_type=jnp.float32).astype(jnp.bfloat16)
        at = slice(target, target + weight.shape[1])
        for d in range(PLANE):
            out_refs[d][own, at] = product[d * block : (d + 1) * block]
            out_refs[d][other, at] = product[rows + d * block : rows + (d + 1) * block]

    multiply(kv_buf[...], q_cols)
    for start in range(0, q_cols, chunk):
        multiply(q_ref[:, start : start + chunk], start)


def projection(mine, theirs, following, q_weight, kv_weights):
    rows, part = following.shape
    q_cols, kv_cols = q_weight.shape[1], kv_weights[0].shape[1]
    chunk = 512
    shape = pltpu.VMEM((2 * rows // PLANE, q_cols + kv_cols + META + part // 2), jnp.bfloat16)
    return pl.pallas_call(
        functools.partial(projection_kernel, chunk),
        out_shape=(shape,) * PLANE,
        in_specs=[VMEM] * (4 + len(kv_weights)),
        out_specs=(VMEM,) * PLANE,
        scratch_shapes=[pltpu.VMEM((part, kv_cols), jnp.bfloat16)],
        compiler_params=params(8),
        cost_estimate=SMALL,
        name="qkv_projection",
    )(mine, theirs, following, q_weight, *kv_weights)


def head_norm_kernel(depth, *refs):
    parts, q_gain_ref, k_gain_ref = refs[:PLANE], refs[PLANE], refs[PLANE + 1]
    next_ref, q_ref, kv_ref = refs[PLANE + 2 :]
    width = next_ref.shape[1]
    q_cols, kv_cols = q_ref.shape[1], kv_ref.shape[1]
    cols = q_cols + kv_cols
    head = q_gain_ref.shape[1]

    def total(at):
        value = parts[0][:, at].astype(jnp.float32)
        for ref in parts[1:]:
            value = value + ref[:, at].astype(jnp.float32)
        return value

    squares = jnp.sum(total(slice(cols, cols + META)), axis=1, keepdims=True)
    scale = lax.rsqrt(squares / width + EPSILON)
    for h in range(q_cols // head):
        at = slice(h * head, (h + 1) * head)
        q_ref[:, at] = normalize(total(at) * scale, q_gain_ref[...]).astype(jnp.bfloat16)
    tensor = lax.axis_index("tensor")
    for h in range(kv_cols // head):
        at = slice(h * head, (h + 1) * head)
        raw = total(slice(q_cols + h * head, q_cols + (h + 1) * head)) * scale
        is_key = tensor * (kv_cols // head) + h < KV_HEADS
        kv_ref[:, at] = jnp.where(is_key, normalize(raw, k_gain_ref[...]), raw).astype(
            jnp.bfloat16
        )
    plane = lax.axis_index("expert") % PLANE
    rows = next_ref.shape[0]
    sub = width // (PLANE * depth)
    for d in range(PLANE):
        for z in range(depth):
            top = z * sub * 2 // (depth * sub)
            start = cols + META + z * sub - top * (depth * sub // 2)
            next_ref[:, lanes((z * PLANE + (plane ^ d)) * sub, sub)] = parts[d][
                top * rows : (top + 1) * rows, start : start + sub
            ]


def head_norm(parts, q_gain, k_gain, q_cols, kv_cols, rows, width, depth):
    both = parts[0].shape[0]
    return pl.pallas_call(
        functools.partial(head_norm_kernel, depth),
        out_shape=(
            jax.ShapeDtypeStruct((rows, width), jnp.bfloat16),
            jax.ShapeDtypeStruct((both, q_cols), jnp.bfloat16),
            jax.ShapeDtypeStruct((both, kv_cols), jnp.bfloat16),
        ),
        in_specs=[VMEM] * (PLANE + 2),
        out_specs=(VMEM, VMEM, VMEM),
        compiler_params=params(4),
        name="head_norm",
    )(*parts, q_gain, k_gain)


def per_device_dense(
    attn_out,
    out_weight,
    residual,
    attn_gain,
    expert_ids,
    route_weights,
    w_gate,
    w_up,
    w_down,
    input_gain,
    q_weight,
    kv_weight,
    q_gain,
    k_gain,
):
    n_expert = lax.axis_size("expert")
    depth = n_expert // PLANE
    rows, width = residual.shape
    tensor_index = lax.axis_index("tensor").astype(jnp.int32)

    def to_core(value):
        return lax.ppermute(value, "tensor", [(0, 1), (1, 0)])

    def to_expert(value, offset):
        return lax.ppermute(value, "expert", [(i, i ^ offset) for i in range(n_expert)])

    def to_z(values):
        return [to_expert(v, d * PLANE) if d else v for d, v in enumerate(values)]

    def to_plane(values):
        return [to_expert(v, d) if d else v for d, v in enumerate(values)]

    own_ids = lax.dynamic_slice_in_dim(expert_ids, tensor_index * rows, rows, 0)
    own_route = lax.dynamic_slice_in_dim(route_weights, tensor_index * rows, rows, 0)
    chosen = own_ids[:, :, None] == jnp.arange(META // 2, dtype=jnp.int32)[None, None, :]
    dense = jnp.sum(jnp.where(chosen, own_route[:, :, None], 0.0), axis=1)
    high = lax.reduce_precision(dense, 8, 7)
    meta = jnp.concatenate([high, dense - high], axis=1).astype(jnp.bfloat16)

    lines = [list(range(i, n_expert, PLANE)) for i in range(PLANE)]
    mine, theirs = out_projection(attn_out, out_weight)
    tokens, *firsts = first_norm(
        (mine,), (to_core(theirs),), residual, attn_gain[None, :], meta, depth
    )
    tokens, q_own = lax.optimization_barrier((tokens, q_weight))
    q_rows = lax.all_gather(q_own, "expert", axis=0, tiled=True, axis_index_groups=lines)
    weights = load((w_gate, w_up, w_down), (tokens,))
    line = to_z([tokens] * depth)
    *line, gate, up, down = lax.optimization_barrier((*line, *weights))
    weights = (gate, up, down)
    near = to_plane(pack(line, firsts))
    cut = near[0].shape[0] // 2
    one, two = near[1][:cut], near[2][cut:]
    far = [to_expert(one, 2), to_expert(two, 1)]
    near_mine, *near_theirs = experts((*near, *map(to_core, near)), weights, depth, len(near))
    theirs = list(map(to_core, near_theirs))
    near_mine, *far = lax.optimization_barrier((near_mine, *far))
    far_both = [*far, *map(to_core, far)]
    far_mine, *far_theirs = experts(far_both, weights, depth, 1)
    theirs += map(to_core, far_theirs)
    *sums, kv_own = lax.optimization_barrier((*chip_sum((near_mine, far_mine), theirs), kv_weight))
    parts = to_plane(sums)
    kv_rows = [kv_own, to_expert(kv_own, PLANE), to_expert(kv_own, 2 * PLANE)]
    *parts, kv_rows[1], kv_rows[2] = lax.optimization_barrier(
        (*plane_sum(parts, depth), *kv_rows[1:])
    )
    kv_rows.append(to_expert(kv_rows[2], PLANE))
    (q_rows,) = load((q_rows,), parts)
    parts = to_z(parts)
    *parts, q_rows = lax.optimization_barrier((*parts, q_rows))
    scaled, following = second_norm(parts, (*near, *far), input_gain[None, :])
    products = to_plane(projection(scaled, to_core(scaled), following, q_rows, kv_rows))
    return head_norm(
        products,
        q_gain[None, :],
        k_gain[None, :],
        q_weight.shape[1],
        kv_weight.shape[1],
        rows,
        width,
        depth,
    )


def per_device(
    attn_out,
    out_weight,
    residual,
    attn_gain,
    expert_ids,
    route_weights,
    w_gate,
    w_up,
    w_down,
    input_gain,
    q_weight,
    kv_weight,
    q_gain,
    k_gain,
):
    n_expert = lax.axis_size("expert")
    n_tensor = lax.axis_size("tensor")
    share = n_tensor // 2
    tensor_index = lax.axis_index("tensor")
    group_rows = attn_out.shape[0]
    width = residual.shape[1]
    half = tensor_index // share
    capacity = 3 * group_rows * TOP // (4 * n_expert)
    all_experts = 2 * n_expert
    attn_rows = lax.psum_scatter(
        jnp.dot(attn_out, out_weight, preferred_element_type=jnp.float32),
        "tensor",
        scatter_dimension=0,
        tiled=True,
    )
    first_residual = (residual.astype(jnp.float32) + attn_rows).astype(jnp.bfloat16)
    normed = normalize(first_residual.astype(jnp.float32), attn_gain).astype(jnp.bfloat16)
    group_normed = lax.all_gather(normed, "tensor", axis=0, tiled=True)
    flat_ids = expert_ids.reshape(-1)
    onehot = (flat_ids[:, None] == jnp.arange(all_experts, dtype=jnp.int32)[None, :]).astype(
        jnp.int32
    )
    earlier = jnp.cumsum(onehot, axis=0) - onehot
    rank = jnp.sum(earlier * onehot, axis=1)
    dest = flat_ids * capacity + rank
    row_owner = jnp.arange(flat_ids.shape[0], dtype=jnp.int32) // TOP
    slot_row = jnp.full((all_experts * capacity,), group_rows, jnp.int32).at[dest].set(row_owner)
    slot_weight = (
        jnp.zeros((all_experts * capacity,), jnp.float32).at[dest].set(route_weights.reshape(-1))
    )
    own_slots = lax.dynamic_index_in_dim(
        slot_row.reshape(n_expert, 2, capacity), half, 1, keepdims=False
    )
    own_weights = lax.dynamic_index_in_dim(
        slot_weight.reshape(n_expert, 2, capacity), half, 1, keepdims=False
    )
    padded_rows = jnp.concatenate([group_normed, jnp.zeros((1, width), jnp.bfloat16)], axis=0)
    gate_w = w_gate[0]
    up_w = w_up[0]
    down_w = w_down[0]
    outgoing = jnp.take(padded_rows, own_slots, axis=0)
    arrived = lax.all_to_all(outgoing, "expert", split_axis=0, concat_axis=0, tiled=True)
    flat = arrived.reshape(-1, width)
    gate = jnp.dot(flat, gate_w, preferred_element_type=jnp.float32)
    up = jnp.dot(flat, up_w, preferred_element_type=jnp.float32)
    act = (jax.nn.silu(gate) * up).astype(jnp.bfloat16)
    part = jnp.dot(act, down_w, preferred_element_type=jnp.float32).astype(jnp.bfloat16)
    send_part = part.reshape(arrived.shape)
    returned = lax.all_to_all(send_part, "expert", split_axis=0, concat_axis=0, tiled=True)
    weighted = own_weights.reshape(-1)[:, None] * returned.reshape(-1, width).astype(jnp.float32)
    term = (
        jnp.zeros((group_rows + 1, width), jnp.float32)
        .at[own_slots.reshape(-1)]
        .add(weighted)[:group_rows]
    )
    expert_sum = lax.psum_scatter(
        term.astype(jnp.bfloat16), "tensor", scatter_dimension=0, tiled=True
    ).astype(jnp.float32)
    next_residual = (first_residual.astype(jnp.float32) + expert_sum).astype(jnp.bfloat16)
    own_normed = normalize(next_residual.astype(jnp.float32), input_gain).astype(jnp.bfloat16)
    next_normed = lax.all_gather(own_normed, "tensor", axis=0, tiled=True)
    query_cols = q_weight.shape[1]
    kv_cols = kv_weight.shape[1]
    query_raw = jnp.dot(
        next_normed,
        lax.all_gather(q_weight, "expert", axis=0, tiled=True),
        preferred_element_type=jnp.float32,
    )
    kv_raw = jnp.dot(
        next_normed,
        lax.all_gather(kv_weight, "expert", axis=0, tiled=True),
        preferred_element_type=jnp.float32,
    )
    head_size = q_gain.shape[0]
    queries = (
        normalize(query_raw.reshape(group_rows, -1, head_size), q_gain)
        .reshape(group_rows, query_cols)
        .astype(jnp.bfloat16)
    )
    heads_here = kv_cols // head_size
    head_number = tensor_index * heads_here + jnp.arange(heads_here, dtype=jnp.int32)
    is_key = head_number < KV_HEADS
    kv_shaped = kv_raw.reshape(group_rows, heads_here, head_size)
    keys_values = (
        jnp.where(is_key[None, :, None], normalize(kv_shaped, k_gain), kv_shaped)
        .reshape(group_rows, kv_cols)
        .astype(jnp.bfloat16)
    )
    return (next_residual, queries, keys_values)


def solution(mesh):
    small = mesh.shape["tensor"] == 2 and mesh.shape["expert"] == 4 * PLANE
    return jax.shard_map(
        per_device_dense if small else per_device,
        mesh=mesh,
        in_specs=(
            P("expert", "tensor"),
            P("tensor", None),
            P(("expert", "tensor"), None),
            P(),
            P("expert", None),
            P("expert", None),
            P("expert", None, "tensor"),
            P("expert", None, "tensor"),
            P("expert", "tensor", None),
            P(),
            P("expert", "tensor"),
            P("expert", "tensor"),
            P(),
            P(),
        ),
        out_specs=(P(("expert", "tensor"), None), P("expert", "tensor"), P("expert", "tensor")),
        check_vma=False,
    )
```

```python
import functools

import jax
import jax.numpy as jnp
from jax import lax
from jax.experimental import pallas as pl
from jax.experimental.pallas import tpu as pltpu
from jax.sharding import PartitionSpec as P

KV_HEADS = 4
TOP = 8
PLANE = 4
META = 128


EPSILON = 1e-06

SMALL = pl.CostEstimate(flops=0, bytes_accessed=0, transcendentals=0)
VMEM = pl.BlockSpec(memory_space=pltpu.VMEM)
HBM = pl.BlockSpec(memory_space=pltpu.HBM)


def normalize(values, gain):
    return values * lax.rsqrt(jnp.mean(values * values, axis=-1, keepdims=True) + EPSILON) * gain


def params(mebibytes):
    return pltpu.CompilerParams(vmem_limit_bytes=mebibytes << 20)


def lanes(start, size):
    return pl.ds(pl.multiple_of(start, size), size)


def in_hbm(value):
    return pltpu.with_memory_space_constraint(value, pltpu.HBM)


def in_vmem(value):
    return pltpu.with_memory_space_constraint(value, pltpu.VMEM)


def out_projection_kernel(chunk, a_hbm, w_hbm, mine_ref, theirs_ref, a_buf, w_buf, a_sem, sems):
    depth = w_buf.shape[0]
    count = depth // chunk
    half = mine_ref.shape[0]
    a_copy = pltpu.make_async_copy(a_hbm, a_buf, a_sem)
    a_copy.start()
    copies = []
    for i in range(count):
        rows = pl.ds(i * chunk, chunk)
        copies.append(pltpu.make_async_copy(w_hbm.at[rows], w_buf.at[rows], sems.at[i]))
    for copy in copies:
        copy.start()
    tensor = lax.axis_index("tensor")
    own = lanes(tensor * half, half)
    other = lanes((1 - tensor) * half, half)
    a_copy.wait()
    for i in range(count):
        copies[i].wait()
        at = pl.ds(i * chunk, chunk)
        both = jnp.concatenate([a_buf[own, at], a_buf[other, at]], axis=0)
        product = jnp.dot(both, w_buf[at, :], preferred_element_type=jnp.float32)
        if i == 0:
            mine_ref[...] = product[:half]
            theirs_ref[...] = product[half:]
        else:
            mine_ref[...] += product[:half]
            theirs_ref[...] += product[half:]


def out_projection(attn_out, out_weight):
    rows, depth = attn_out.shape
    width = out_weight.shape[1]
    chunk = 256
    half = pltpu.VMEM((rows // 2, width), jnp.float32)
    return pl.pallas_call(
        functools.partial(out_projection_kernel, chunk),
        out_shape=(half, half),
        in_specs=[HBM, HBM],
        out_specs=(VMEM, VMEM),
        scratch_shapes=[
            pltpu.VMEM((rows, depth), jnp.bfloat16),
            pltpu.VMEM((depth, width), jnp.bfloat16),
            pltpu.SemaphoreType.DMA,
            pltpu.SemaphoreType.DMA((depth // chunk,)),
        ],
        compiler_params=params(14),
        cost_estimate=SMALL,
        name="out_projection",
    )(in_hbm(attn_out), in_hbm(out_weight))


def first_norm_kernel(depth, count, *refs):
    mine, theirs = refs[:count], refs[count : 2 * count]
    residual_ref, gain_ref, meta_ref, tokens_ref = refs[2 * count : 2 * count + 4]
    slice_refs, first_ref = refs[2 * count + 4 : -1], refs[-1]
    rows, width = residual_ref.shape
    sub = width // (PLANE * depth)
    start = 0
    for mine_ref, theirs_ref in zip(mine, theirs):
        cols = slice(start, start + mine_ref.shape[1])
        start += mine_ref.shape[1]
        first_ref[:, cols] = (
            residual_ref[:, cols].astype(jnp.float32) + (mine_ref[...] + theirs_ref[...])
        ).astype(jnp.bfloat16)
    first = first_ref[...]
    tokens_ref[:, :width] = normalize(first.astype(jnp.float32), gain_ref[...]).astype(jnp.bfloat16)
    tokens_ref[:, width:] = meta_ref[...]
    plane = lax.axis_index("expert") % PLANE
    for d in range(PLANE):
        for z in range(depth):
            slice_refs[d][z * rows : (z + 1) * rows, :] = first_ref[
                :, lanes((z * PLANE + (plane ^ d)) * sub, sub)
            ]


def first_norm(mine, theirs, residual, gain, meta, depth):
    rows, width = residual.shape
    piece = jax.ShapeDtypeStruct((depth * rows, width // (PLANE * depth)), jnp.bfloat16)
    return pl.pallas_call(
        functools.partial(first_norm_kernel, depth, len(mine)),
        out_shape=(jax.ShapeDtypeStruct((rows, width + META), jnp.bfloat16),) + (piece,) * PLANE,
        in_specs=[VMEM] * (2 * len(mine) + 3),
        out_specs=(VMEM,) * (1 + PLANE),
        scratch_shapes=[pltpu.VMEM((rows, width), jnp.bfloat16)],
        compiler_params=params(2),
        name="first_norm",
    )(*mine, *theirs, residual, gain, meta)


def pack_kernel(depth, *refs):
    line, pieces, out_refs = refs[:depth], refs[depth : depth + PLANE], refs[depth + PLANE :]
    rows, extended = line[0].shape
    sub = pieces[0].shape[1]
    for d, ref in enumerate(out_refs):
        for z in range(depth):
            ref[z * rows : (z + 1) * rows, :extended] = line[z][...]
        ref[:, extended : extended + sub] = pieces[d][...]
        ref[:, extended + sub :] = pieces[PLANE - 1][...]


def pack(line, pieces):
    depth = len(line)
    rows, extended = line[0].shape
    shape = pltpu.VMEM((depth * rows, extended + 2 * pieces[0].shape[1]), jnp.bfloat16)
    return pl.pallas_call(
        functools.partial(pack_kernel, depth),
        out_shape=(shape,) * (PLANE - 1),
        in_specs=[VMEM] * (depth + PLANE),
        out_specs=(VMEM,) * (PLANE - 1),
        compiler_params=params(2),
        name="pack_tokens",
    )(*line, *pieces)


def load_kernel(count, *refs):
    sources, targets, sems = refs[:count], refs[-count - 1 : -1], refs[-1]
    copies = [
        pltpu.make_async_copy(source, target, sems.at[i])
        for i, (source, target) in enumerate(zip(sources, targets))
    ]
    for copy in copies:
        copy.start()
    for copy in copies:
        copy.wait()


def load(weights, after):
    count = len(weights)
    return pl.pallas_call(
        functools.partial(load_kernel, count),
        out_shape=tuple(pltpu.VMEM(w.shape, w.dtype) for w in weights),
        in_specs=[HBM] * count + [pl.BlockSpec(memory_space=pl.ANY)] * len(after),
        out_specs=(VMEM,) * count,
        scratch_shapes=[pltpu.SemaphoreType.DMA((count,))],
        compiler_params=params(2),
        cost_estimate=SMALL,
        name="load_weights",
    )(*map(in_hbm, weights), *after)


def expert_kernel(depth, chunk, count, *refs):
    block_refs, (gate_ref, up_ref, down_ref) = refs[:count], refs[count : count + 3]
    mine_ref, *theirs_refs, x_buf, act_buf = refs[count + 3 :]
    width, hidden = gate_ref.shape[1:]
    extended = x_buf.shape[1]
    start = 0
    for ref in block_refs:
        rows = ref.shape[0]
        x_buf[start : start + rows, :] = ref[:, :extended]
        start += rows
    meta = x_buf[:, width:].astype(jnp.float32)
    lane = lax.broadcasted_iota(jnp.int32, meta.shape, 1)
    chip = lax.axis_index("expert")
    expert = 2 * chip + lax.axis_index("tensor")
    chosen = (lane == expert) | (lane == expert + META // 2)
    route = 0.5 * jnp.sum(jnp.where(chosen, meta, 0.0), axis=1, keepdims=True)
    for i in range(hidden // chunk):
        cols = pl.ds(i * chunk, chunk)
        x = x_buf[:, :width]
        gate = jnp.dot(x, gate_ref[0, :, cols], preferred_element_type=jnp.float32)
        up = jnp.dot(x, up_ref[0, :, cols], preferred_element_type=jnp.float32)
        act = gate * (1.0 + jnp.tanh(0.5 * gate)) * (up * route)
        act_buf[:, i * chunk : (i + 1) * chunk] = act.astype(jnp.bfloat16)
    sub = width // (PLANE * depth)
    part = sub * depth
    half = mine_ref.shape[0]
    plane = chip % PLANE
    for d in range(PLANE):
        weight = jnp.concatenate(
            [down_ref[0, :, lanes((z * PLANE + (plane ^ d)) * sub, sub)] for z in range(depth)],
            axis=1,
        )
        out = jnp.dot(act_buf[...], weight, preferred_element_type=jnp.float32)
        cols = slice(d * part, (d + 1) * part)
        mine_ref[:, cols] = out[:half].astype(jnp.bfloat16)
        start = half
        for ref in theirs_refs:
            stop = start + ref.shape[0]
            ref[:, cols] = out[start:stop].astype(jnp.bfloat16)
            start = stop


def experts(blocks, weights, depth, pieces):
    width, hidden = weights[0].shape[1:]
    chunk = 256
    extended = width + META
    total = sum(block.shape[0] for block in blocks)
    rows = [total // 2] + [total // 2 // pieces] * pieces
    return pl.pallas_call(
        functools.partial(expert_kernel, depth, chunk, len(blocks)),
        out_shape=tuple(pltpu.VMEM((size, width), jnp.bfloat16) for size in rows),
        in_specs=[VMEM] * (len(blocks) + 3),
        out_specs=(VMEM,) * (1 + pieces),
        scratch_shapes=[
            pltpu.VMEM((total, extended), jnp.bfloat16),
            pltpu.VMEM((total, hidden), jnp.bfloat16),
        ],
        compiler_params=params(16),
        cost_estimate=pl.CostEstimate(
            flops=6 * total * width * hidden, bytes_accessed=0, transcendentals=0
        ),
        name="experts",
    )(*blocks, *weights)


def chip_sum_kernel(count, *refs):
    mine, theirs, out_refs = refs[:2], refs[2 : 2 + count], refs[2 + count :]
    part = out_refs[0].shape[1]
    start = 0
    for own_ref in mine:
        first = start
        while start < first + own_ref.shape[0]:
            ref, theirs = theirs[0], theirs[1:]
            size = ref.shape[0]
            own = slice(start - first, start - first + size)
            for d, out_ref in enumerate(out_refs):
                at = slice(d * part, (d + 1) * part)
                total = own_ref[own, at].astype(jnp.float32) + ref[:, at].astype(jnp.float32)
                out_ref[start : start + size, :] = total.astype(jnp.bfloat16)
            start += size


def chip_sum(mine, theirs):
    rows, width = sum(value.shape[0] for value in mine), mine[0].shape[1]
    return pl.pallas_call(
        functools.partial(chip_sum_kernel, len(theirs)),
        out_shape=(pltpu.VMEM((rows, width // PLANE), jnp.bfloat16),) * PLANE,
        in_specs=[VMEM] * (2 + len(theirs)),
        out_specs=(VMEM,) * PLANE,
        compiler_params=params(4),
        name="chip_sum",
    )(*mine, *theirs)


def plane_sum_kernel(depth, *refs):
    in_refs, out_refs = refs[:PLANE], refs[PLANE:]
    group = in_refs[0].shape[0] // PLANE
    rows = group // depth
    for k in range(PLANE):
        for z in range(depth):
            total = 0.0
            for d in range(PLANE):
                start = (k ^ d) * group + z * rows
                total = total + in_refs[d][start : start + rows, :].astype(jnp.float32)
            out_refs[z][k * rows : (k + 1) * rows, :] = total.astype(jnp.bfloat16)


def plane_sum(parts, depth):
    rows, part = parts[0].shape
    return pl.pallas_call(
        functools.partial(plane_sum_kernel, depth),
        out_shape=(pltpu.VMEM((rows // depth, part), jnp.bfloat16),) * depth,
        in_specs=[VMEM] * PLANE,
        out_specs=(VMEM,) * depth,
        compiler_params=params(4),
        name="plane_sum",
    )(*parts)


def second_norm_kernel(depth, *refs):
    parts, packed = refs[:depth], refs[depth : depth + PLANE + 1]
    gain_ref, scaled_ref, next_ref = refs[depth + PLANE + 1 :]
    rows = packed[0].shape[0] // depth
    part = parts[0].shape[1]
    sub = part // depth
    skip = packed[0].shape[1] - 2 * sub
    lane = lax.broadcasted_iota(jnp.int32, (rows, META), 1)
    plane = lax.axis_index("expert") % PLANE
    gain = jnp.concatenate(
        [gain_ref[:, lanes((z * PLANE + plane) * sub, sub)] for z in range(depth)], axis=1
    )
    for d in range(PLANE):
        at = slice(d * rows, (d + 1) * rows)
        total = parts[0][at, :].astype(jnp.float32)
        for ref in parts[1:]:
            total = total + ref[at, :].astype(jnp.float32)
        if d < PLANE - 1:
            first = packed[d][:, skip : skip + sub]
        else:
            first = jnp.concatenate([ref[:, skip + sub :] for ref in packed[d:]], axis=0)
        first = jnp.concatenate([first[z * rows : (z + 1) * rows] for z in range(depth)], axis=1)
        following = (first.astype(jnp.float32) + total).astype(jnp.bfloat16)
        next_ref[at, :] = following
        wide = following.astype(jnp.float32)
        scaled_ref[at, :part] = (wide * gain).astype(jnp.bfloat16)
        squares = jnp.sum(wide * wide, axis=1, keepdims=True)
        high = squares.astype(jnp.bfloat16).astype(jnp.float32)
        low = squares - high
        scaled_ref[at, part:] = jnp.where(
            lane == 0, high, jnp.where(lane == 1, low, 0.0)
        ).astype(jnp.bfloat16)


def second_norm(parts, packed, gain):
    depth = len(parts)
    rows, part = parts[0].shape
    return pl.pallas_call(
        functools.partial(second_norm_kernel, depth),
        out_shape=(
            jax.ShapeDtypeStruct((rows, part + META), jnp.bfloat16),
            jax.ShapeDtypeStruct((rows, part), jnp.bfloat16),
        ),
        in_specs=[VMEM] * (depth + PLANE + 2),
        out_specs=(VMEM, VMEM),
        compiler_params=params(4),
        name="second_norm",
    )(*parts, *packed, gain)


def projection_kernel(chunk, mine_ref, theirs_ref, next_ref, q_ref, *refs):
    kv_refs, out_refs, kv_buf = refs[: -PLANE - 1], refs[-PLANE - 1 : -1], refs[-1]
    depth = len(kv_refs)
    rows, extended = mine_ref.shape
    part = extended - META
    sub = part // depth
    q_cols, kv_cols = q_ref.shape[1], kv_buf.shape[1]
    cols = q_cols + kv_cols
    line = lax.axis_index("expert") // PLANE
    for d, ref in enumerate(kv_refs):
        kv_buf[lanes((line ^ d) * sub, sub), :] = ref[...]
    block = rows // PLANE
    tensor = lax.axis_index("tensor")
    own = lanes(tensor * block, block)
    other = lanes((1 - tensor) * block, block)
    for d in range(PLANE):
        at = slice(d * block, (d + 1) * block)
        out_refs[d][own, cols : cols + META] = mine_ref[at, part:]
        out_refs[d][other, cols : cols + META] = theirs_ref[at, part:]
        out_refs[d][:block, cols + META :] = next_ref[at, : part // 2]
        out_refs[d][block:, cols + META :] = next_ref[at, part // 2 :]
    both = jnp.concatenate([mine_ref[:, :part], theirs_ref[:, :part]], axis=0)

    def multiply(weight, target):
        product = jnp.dot(both, weight, preferred_element_type=jnp.float32).astype(jnp.bfloat16)
        at = slice(target, target + weight.shape[1])
        for d in range(PLANE):
            out_refs[d][own, at] = product[d * block : (d + 1) * block]
            out_refs[d][other, at] = product[rows + d * block : rows + (d + 1) * block]

    multiply(kv_buf[...], q_cols)
    for start in range(0, q_cols, chunk):
        multiply(q_ref[:, start : start + chunk], start)


def projection(mine, theirs, following, q_weight, kv_weights):
    rows, part = following.shape
    q_cols, kv_cols = q_weight.shape[1], kv_weights[0].shape[1]
    chunk = 512
    shape = pltpu.VMEM((2 * rows // PLANE, q_cols + kv_cols + META + part // 2), jnp.bfloat16)
    return pl.pallas_call(
        functools.partial(projection_kernel, chunk),
        out_shape=(shape,) * PLANE,
        in_specs=[VMEM] * (4 + len(kv_weights)),
        out_specs=(VMEM,) * PLANE,
        scratch_shapes=[pltpu.VMEM((part, kv_cols), jnp.bfloat16)],
        compiler_params=params(8),
        cost_estimate=SMALL,
        name="qkv_projection",
    )(mine, theirs, following, q_weight, *kv_weights)


def head_norm_kernel(depth, *refs):
    parts, q_gain_ref, k_gain_ref = refs[:PLANE], refs[PLANE], refs[PLANE + 1]
    next_ref, q_ref, kv_ref = refs[PLANE + 2 :]
    width = next_ref.shape[1]
    q_cols, kv_cols = q_ref.shape[1], kv_ref.shape[1]
    cols = q_cols + kv_cols
    head = q_gain_ref.shape[1]

    def total(at):
        value = parts[0][:, at].astype(jnp.float32)
        for ref in parts[1:]:
            value = value + ref[:, at].astype(jnp.float32)
        return value

    squares = jnp.sum(total(slice(cols, cols + META)), axis=1, keepdims=True)
    scale = lax.rsqrt(squares / width + EPSILON)
    for h in range(q_cols // head):
        at = slice(h * head, (h + 1) * head)
        q_ref[:, at] = normalize(total(at) * scale, q_gain_ref[...]).astype(jnp.bfloat16)
    tensor = lax.axis_index("tensor")
    for h in range(kv_cols // head):
        at = slice(h * head, (h + 1) * head)
        raw = total(slice(q_cols + h * head, q_cols + (h + 1) * head)) * scale
        is_key = tensor * (kv_cols // head) + h < KV_HEADS
        kv_ref[:, at] = jnp.where(is_key, normalize(raw, k_gain_ref[...]), raw).astype(
            jnp.bfloat16
        )
    plane = lax.axis_index("expert") % PLANE
    rows = next_ref.shape[0]
    sub = width // (PLANE * depth)
    for d in range(PLANE):
        for z in range(depth):
            top = z * sub * 2 // (depth * sub)
            start = cols + META + z * sub - top * (depth * sub // 2)
            next_ref[:, lanes((z * PLANE + (plane ^ d)) * sub, sub)] = parts[d][
                top * rows : (top + 1) * rows, start : start + sub
            ]


def head_norm(parts, q_gain, k_gain, q_cols, kv_cols, rows, width, depth):
    both = parts[0].shape[0]
    return pl.pallas_call(
        functools.partial(head_norm_kernel, depth),
        out_shape=(
            jax.ShapeDtypeStruct((rows, width), jnp.bfloat16),
            jax.ShapeDtypeStruct((both, q_cols), jnp.bfloat16),
            jax.ShapeDtypeStruct((both, kv_cols), jnp.bfloat16),
        ),
        in_specs=[VMEM] * (PLANE + 2),
        out_specs=(VMEM, VMEM, VMEM),
        compiler_params=params(4),
        name="head_norm",
    )(*parts, q_gain, k_gain)


def per_device_dense(
    attn_out,
    out_weight,
    residual,
    attn_gain,
    expert_ids,
    route_weights,
    w_gate,
    w_up,
    w_down,
    input_gain,
    q_weight,
    kv_weight,
    q_gain,
    k_gain,
):
    n_expert = lax.axis_size("expert")
    depth = n_expert // PLANE
    rows, width = residual.shape
    tensor_index = lax.axis_index("tensor").astype(jnp.int32)

    def to_core(value):
        return lax.ppermute(value, "tensor", [(0, 1), (1, 0)])

    def to_expert(value, offset):
        return lax.ppermute(value, "expert", [(i, i ^ offset) for i in range(n_expert)])

    def to_z(values):
        return [to_expert(v, d * PLANE) if d else v for d, v in enumerate(values)]

    def to_plane(values):
        return [to_expert(v, d) if d else v for d, v in enumerate(values)]

    own_ids = lax.dynamic_slice_in_dim(expert_ids, tensor_index * rows, rows, 0)
    own_route = lax.dynamic_slice_in_dim(route_weights, tensor_index * rows, rows, 0)
    chosen = own_ids[:, :, None] == jnp.arange(META // 2, dtype=jnp.int32)[None, None, :]
    dense = jnp.sum(jnp.where(chosen, own_route[:, :, None], 0.0), axis=1)
    high = lax.reduce_precision(dense, 8, 7)
    meta = jnp.concatenate([high, dense - high], axis=1).astype(jnp.bfloat16)

    lines = [list(range(i, n_expert, PLANE)) for i in range(PLANE)]
    mine, theirs = out_projection(attn_out, out_weight)
    mine, q_own = lax.optimization_barrier((mine, q_weight))
    q_rows = lax.all_gather(q_own, "expert", axis=0, tiled=True, axis_index_groups=lines)
    tokens, *firsts = first_norm(
        (mine,), (to_core(theirs),), residual, attn_gain[None, :], meta, depth
    )
    weights = load((w_gate, w_up, w_down), (tokens,))
    line = to_z([tokens] * depth)
    *line, gate, up, down = lax.optimization_barrier((*line, *weights))
    weights = (gate, up, down)
    near = to_plane(pack(line, firsts))
    cut = near[0].shape[0] // 2
    one, two = near[1][:cut], near[2][cut:]
    far = [to_expert(one, 2), to_expert(two, 1)]
    near_mine, *near_theirs = experts((*near, *map(to_core, near)), weights, depth, len(near))
    theirs = list(map(to_core, near_theirs))
    near_mine, *far = lax.optimization_barrier((near_mine, *far))
    far_both = [*far, *map(to_core, far)]
    far_mine, *far_theirs = experts(far_both, weights, depth, 1)
    theirs += map(to_core, far_theirs)
    *sums, kv_own = lax.optimization_barrier((*chip_sum((near_mine, far_mine), theirs), kv_weight))
    parts = to_plane(sums)
    kv_rows = [kv_own, to_expert(kv_own, PLANE), to_expert(kv_own, 2 * PLANE)]
    parts = plane_sum(parts, depth)
    kv_rows.append(to_expert(kv_rows[2], PLANE))
    (q_rows,) = load((q_rows,), parts)
    parts = to_z(parts)
    *parts, q_rows = lax.optimization_barrier((*parts, q_rows))
    scaled, following = second_norm(parts, (*near, *far), input_gain[None, :])
    products = to_plane(projection(scaled, to_core(scaled), following, q_rows, kv_rows))
    return head_norm(
        products,
        q_gain[None, :],
        k_gain[None, :],
        q_weight.shape[1],
        kv_weight.shape[1],
        rows,
        width,
        depth,
    )


def per_device(
    attn_out,
    out_weight,
    residual,
    attn_gain,
    expert_ids,
    route_weights,
    w_gate,
    w_up,
    w_down,
    input_gain,
    q_weight,
    kv_weight,
    q_gain,
    k_gain,
):
    n_expert = lax.axis_size("expert")
    n_tensor = lax.axis_size("tensor")
    share = n_tensor // 2
    tensor_index = lax.axis_index("tensor")
    group_rows = attn_out.shape[0]
    width = residual.shape[1]
    half = tensor_index // share
    capacity = 3 * group_rows * TOP // (4 * n_expert)
    all_experts = 2 * n_expert
    attn_rows = lax.psum_scatter(
        jnp.dot(attn_out, out_weight, preferred_element_type=jnp.float32),
        "tensor",
        scatter_dimension=0,
        tiled=True,
    )
    first_residual = (residual.astype(jnp.float32) + attn_rows).astype(jnp.bfloat16)
    normed = normalize(first_residual.astype(jnp.float32), attn_gain).astype(jnp.bfloat16)
    group_normed = lax.all_gather(normed, "tensor", axis=0, tiled=True)
    flat_ids = expert_ids.reshape(-1)
    onehot = (flat_ids[:, None] == jnp.arange(all_experts, dtype=jnp.int32)[None, :]).astype(
        jnp.int32
    )
    earlier = jnp.cumsum(onehot, axis=0) - onehot
    rank = jnp.sum(earlier * onehot, axis=1)
    dest = flat_ids * capacity + rank
    row_owner = jnp.arange(flat_ids.shape[0], dtype=jnp.int32) // TOP
    slot_row = jnp.full((all_experts * capacity,), group_rows, jnp.int32).at[dest].set(row_owner)
    slot_weight = (
        jnp.zeros((all_experts * capacity,), jnp.float32).at[dest].set(route_weights.reshape(-1))
    )
    own_slots = lax.dynamic_index_in_dim(
        slot_row.reshape(n_expert, 2, capacity), half, 1, keepdims=False
    )
    own_weights = lax.dynamic_index_in_dim(
        slot_weight.reshape(n_expert, 2, capacity), half, 1, keepdims=False
    )
    padded_rows = jnp.concatenate([group_normed, jnp.zeros((1, width), jnp.bfloat16)], axis=0)
    gate_w = w_gate[0]
    up_w = w_up[0]
    down_w = w_down[0]
    outgoing = jnp.take(padded_rows, own_slots, axis=0)
    arrived = lax.all_to_all(outgoing, "expert", split_axis=0, concat_axis=0, tiled=True)
    flat = arrived.reshape(-1, width)
    gate = jnp.dot(flat, gate_w, preferred_element_type=jnp.float32)
    up = jnp.dot(flat, up_w, preferred_element_type=jnp.float32)
    act = (jax.nn.silu(gate) * up).astype(jnp.bfloat16)
    part = jnp.dot(act, down_w, preferred_element_type=jnp.float32).astype(jnp.bfloat16)
    send_part = part.reshape(arrived.shape)
    returned = lax.all_to_all(send_part, "expert", split_axis=0, concat_axis=0, tiled=True)
    weighted = own_weights.reshape(-1)[:, None] * returned.reshape(-1, width).astype(jnp.float32)
    term = (
        jnp.zeros((group_rows + 1, width), jnp.float32)
        .at[own_slots.reshape(-1)]
        .add(weighted)[:group_rows]
    )
    expert_sum = lax.psum_scatter(
        term.astype(jnp.bfloat16), "tensor", scatter_dimension=0, tiled=True
    ).astype(jnp.float32)
    next_residual = (first_residual.astype(jnp.float32) + expert_sum).astype(jnp.bfloat16)
    own_normed = normalize(next_residual.astype(jnp.float32), input_gain).astype(jnp.bfloat16)
    next_normed = lax.all_gather(own_normed, "tensor", axis=0, tiled=True)
    query_cols = q_weight.shape[1]
    kv_cols = kv_weight.shape[1]
    query_raw = jnp.dot(
        next_normed,
        lax.all_gather(q_weight, "expert", axis=0, tiled=True),
        preferred_element_type=jnp.float32,
    )
    kv_raw = jnp.dot(
        next_normed,
        lax.all_gather(kv_weight, "expert", axis=0, tiled=True),
        preferred_element_type=jnp.float32,
    )
    head_size = q_gain.shape[0]
    queries = (
        normalize(query_raw.reshape(group_rows, -1, head_size), q_gain)
        .reshape(group_rows, query_cols)
        .astype(jnp.bfloat16)
    )
    heads_here = kv_cols // head_size
    head_number = tensor_index * heads_here + jnp.arange(heads_here, dtype=jnp.int32)
    is_key = head_number < KV_HEADS
    kv_shaped = kv_raw.reshape(group_rows, heads_here, head_size)
    keys_values = (
        jnp.where(is_key[None, :, None], normalize(kv_shaped, k_gain), kv_shaped)
        .reshape(group_rows, kv_cols)
        .astype(jnp.bfloat16)
    )
    return (next_residual, queries, keys_values)


def solution(mesh):
    small = mesh.shape["tensor"] == 2 and mesh.shape["expert"] == 4 * PLANE
    return jax.shard_map(
        per_device_dense if small else per_device,
        mesh=mesh,
        in_specs=(
            P("expert", "tensor"),
            P("tensor", None),
            P(("expert", "tensor"), None),
            P(),
            P("expert", None),
            P("expert", None),
            P("expert", None, "tensor"),
            P("expert", None, "tensor"),
            P("expert", "tensor", None),
            P(),
            P("expert", "tensor"),
            P("expert", "tensor"),
            P(),
            P(),
        ),
        out_specs=(P(("expert", "tensor"), None), P("expert", "tensor"), P("expert", "tensor")),
        check_vma=False,
    )
```

```python
import functools

import jax
import jax.numpy as jnp
from jax import lax
from jax.experimental import pallas as pl
from jax.experimental.pallas import tpu as pltpu
from jax.sharding import PartitionSpec as P

KV_HEADS = 4
TOP = 8
PLANE = 4
META = 128


EPSILON = 1e-06

SMALL = pl.CostEstimate(flops=0, bytes_accessed=0, transcendentals=0)
VMEM = pl.BlockSpec(memory_space=pltpu.VMEM)
HBM = pl.BlockSpec(memory_space=pltpu.HBM)


def normalize(values, gain):
    return values * lax.rsqrt(jnp.mean(values * values, axis=-1, keepdims=True) + EPSILON) * gain


def params(mebibytes):
    return pltpu.CompilerParams(vmem_limit_bytes=mebibytes << 20)


def lanes(start, size):
    return pl.ds(pl.multiple_of(start, size), size)


def in_hbm(value):
    return pltpu.with_memory_space_constraint(value, pltpu.HBM)


def in_vmem(value):
    return pltpu.with_memory_space_constraint(value, pltpu.VMEM)


def out_projection_kernel(chunk, a_hbm, w_hbm, mine_ref, theirs_ref, a_buf, w_buf, a_sem, sems):
    depth = w_buf.shape[0]
    count = depth // chunk
    half = mine_ref.shape[0]
    a_copy = pltpu.make_async_copy(a_hbm, a_buf, a_sem)
    a_copy.start()
    copies = []
    for i in range(count):
        rows = pl.ds(i * chunk, chunk)
        copies.append(pltpu.make_async_copy(w_hbm.at[rows], w_buf.at[rows], sems.at[i]))
    for copy in copies:
        copy.start()
    tensor = lax.axis_index("tensor")
    own = lanes(tensor * half, half)
    other = lanes((1 - tensor) * half, half)
    a_copy.wait()
    for i in range(count):
        copies[i].wait()
        at = pl.ds(i * chunk, chunk)
        both = jnp.concatenate([a_buf[own, at], a_buf[other, at]], axis=0)
        product = jnp.dot(both, w_buf[at, :], preferred_element_type=jnp.float32)
        if i == 0:
            mine_ref[...] = product[:half]
            theirs_ref[...] = product[half:]
        else:
            mine_ref[...] += product[:half]
            theirs_ref[...] += product[half:]


def out_projection(attn_out, out_weight):
    rows, depth = attn_out.shape
    width = out_weight.shape[1]
    chunk = 256
    half = pltpu.VMEM((rows // 2, width), jnp.float32)
    return pl.pallas_call(
        functools.partial(out_projection_kernel, chunk),
        out_shape=(half, half),
        in_specs=[HBM, HBM],
        out_specs=(VMEM, VMEM),
        scratch_shapes=[
            pltpu.VMEM((rows, depth), jnp.bfloat16),
            pltpu.VMEM((depth, width), jnp.bfloat16),
            pltpu.SemaphoreType.DMA,
            pltpu.SemaphoreType.DMA((depth // chunk,)),
        ],
        compiler_params=params(14),
        cost_estimate=SMALL,
        name="out_projection",
    )(in_hbm(attn_out), in_hbm(out_weight))


def first_norm_kernel(depth, count, *refs):
    mine, theirs = refs[:count], refs[count : 2 * count]
    residual_ref, gain_ref, meta_ref, tokens_ref = refs[2 * count : 2 * count + 4]
    slice_refs, first_ref = refs[2 * count + 4 : -1], refs[-1]
    rows, width = residual_ref.shape
    sub = width // (PLANE * depth)
    start = 0
    for mine_ref, theirs_ref in zip(mine, theirs):
        cols = slice(start, start + mine_ref.shape[1])
        start += mine_ref.shape[1]
        first_ref[:, cols] = (
            residual_ref[:, cols].astype(jnp.float32) + (mine_ref[...] + theirs_ref[...])
        ).astype(jnp.bfloat16)
    first = first_ref[...]
    tokens_ref[:, :width] = normalize(first.astype(jnp.float32), gain_ref[...]).astype(jnp.bfloat16)
    tokens_ref[:, width:] = meta_ref[...]
    plane = lax.axis_index("expert") % PLANE
    for d in range(PLANE):
        for z in range(depth):
            slice_refs[d][z * rows : (z + 1) * rows, :] = first_ref[
                :, lanes((z * PLANE + (plane ^ d)) * sub, sub)
            ]


def first_norm(mine, theirs, residual, gain, meta, depth):
    rows, width = residual.shape
    piece = jax.ShapeDtypeStruct((depth * rows, width // (PLANE * depth)), jnp.bfloat16)
    return pl.pallas_call(
        functools.partial(first_norm_kernel, depth, len(mine)),
        out_shape=(jax.ShapeDtypeStruct((rows, width + META), jnp.bfloat16),) + (piece,) * PLANE,
        in_specs=[VMEM] * (2 * len(mine) + 3),
        out_specs=(VMEM,) * (1 + PLANE),
        scratch_shapes=[pltpu.VMEM((rows, width), jnp.bfloat16)],
        compiler_params=params(2),
        name="first_norm",
    )(*mine, *theirs, residual, gain, meta)


def pack_kernel(depth, *refs):
    line, pieces, out_refs = refs[:depth], refs[depth : depth + PLANE], refs[depth + PLANE :]
    rows, extended = line[0].shape
    sub = pieces[0].shape[1]
    for d, ref in enumerate(out_refs):
        for z in range(depth):
            ref[z * rows : (z + 1) * rows, :extended] = line[z][...]
        ref[:, extended : extended + sub] = pieces[d][...]
        ref[:, extended + sub :] = pieces[PLANE - 1][...]


def pack(line, pieces):
    depth = len(line)
    rows, extended = line[0].shape
    shape = pltpu.VMEM((depth * rows, extended + 2 * pieces[0].shape[1]), jnp.bfloat16)
    return pl.pallas_call(
        functools.partial(pack_kernel, depth),
        out_shape=(shape,) * (PLANE - 1),
        in_specs=[VMEM] * (depth + PLANE),
        out_specs=(VMEM,) * (PLANE - 1),
        compiler_params=params(2),
        name="pack_tokens",
    )(*line, *pieces)


def load_kernel(count, *refs):
    sources, targets, sems = refs[:count], refs[-count - 1 : -1], refs[-1]
    copies = [
        pltpu.make_async_copy(source, target, sems.at[i])
        for i, (source, target) in enumerate(zip(sources, targets))
    ]
    for copy in copies:
        copy.start()
    for copy in copies:
        copy.wait()


def load(weights, after):
    count = len(weights)
    return pl.pallas_call(
        functools.partial(load_kernel, count),
        out_shape=tuple(pltpu.VMEM(w.shape, w.dtype) for w in weights),
        in_specs=[HBM] * count + [pl.BlockSpec(memory_space=pl.ANY)] * len(after),
        out_specs=(VMEM,) * count,
        scratch_shapes=[pltpu.SemaphoreType.DMA((count,))],
        compiler_params=params(2),
        cost_estimate=SMALL,
        name="load_weights",
    )(*map(in_hbm, weights), *after)


def expert_kernel(depth, chunk, count, *refs):
    block_refs, (gate_ref, up_ref, down_ref) = refs[:count], refs[count : count + 3]
    mine_ref, *theirs_refs, x_buf, act_buf = refs[count + 3 :]
    width, hidden = gate_ref.shape[1:]
    extended = x_buf.shape[1]
    start = 0
    for ref in block_refs:
        rows = ref.shape[0]
        x_buf[start : start + rows, :] = ref[:, :extended]
        start += rows
    meta = x_buf[:, width:].astype(jnp.float32)
    lane = lax.broadcasted_iota(jnp.int32, meta.shape, 1)
    chip = lax.axis_index("expert")
    expert = 2 * chip + lax.axis_index("tensor")
    chosen = (lane == expert) | (lane == expert + META // 2)
    route = 0.5 * jnp.sum(jnp.where(chosen, meta, 0.0), axis=1, keepdims=True)
    for i in range(hidden // chunk):
        cols = pl.ds(i * chunk, chunk)
        x = x_buf[:, :width]
        gate = jnp.dot(x, gate_ref[0, :, cols], preferred_element_type=jnp.float32)
        up = jnp.dot(x, up_ref[0, :, cols], preferred_element_type=jnp.float32)
        act = gate * (1.0 + jnp.tanh(0.5 * gate)) * (up * route)
        act_buf[:, i * chunk : (i + 1) * chunk] = act.astype(jnp.bfloat16)
    sub = width // (PLANE * depth)
    part = sub * depth
    half = mine_ref.shape[0]
    plane = chip % PLANE
    for d in range(PLANE):
        weight = jnp.concatenate(
            [down_ref[0, :, lanes((z * PLANE + (plane ^ d)) * sub, sub)] for z in range(depth)],
            axis=1,
        )
        out = jnp.dot(act_buf[...], weight, preferred_element_type=jnp.float32)
        cols = slice(d * part, (d + 1) * part)
        mine_ref[:, cols] = out[:half].astype(jnp.bfloat16)
        start = half
        for ref in theirs_refs:
            stop = start + ref.shape[0]
            ref[:, cols] = out[start:stop].astype(jnp.bfloat16)
            start = stop


def experts(blocks, weights, depth, pieces):
    width, hidden = weights[0].shape[1:]
    chunk = 256
    extended = width + META
    total = sum(block.shape[0] for block in blocks)
    rows = [total // 2] + [total // 2 // pieces] * pieces
    return pl.pallas_call(
        functools.partial(expert_kernel, depth, chunk, len(blocks)),
        out_shape=tuple(pltpu.VMEM((size, width), jnp.bfloat16) for size in rows),
        in_specs=[VMEM] * (len(blocks) + 3),
        out_specs=(VMEM,) * (1 + pieces),
        scratch_shapes=[
            pltpu.VMEM((total, extended), jnp.bfloat16),
            pltpu.VMEM((total, hidden), jnp.bfloat16),
        ],
        compiler_params=params(16),
        cost_estimate=pl.CostEstimate(
            flops=6 * total * width * hidden, bytes_accessed=0, transcendentals=0
        ),
        name="experts",
    )(*blocks, *weights)


def chip_sum_kernel(count, *refs):
    mine, theirs, out_refs = refs[:2], refs[2 : 2 + count], refs[2 + count :]
    part = out_refs[0].shape[1]
    start = 0
    for own_ref in mine:
        first = start
        while start < first + own_ref.shape[0]:
            ref, theirs = theirs[0], theirs[1:]
            size = ref.shape[0]
            own = slice(start - first, start - first + size)
            for d, out_ref in enumerate(out_refs):
                at = slice(d * part, (d + 1) * part)
                total = own_ref[own, at].astype(jnp.float32) + ref[:, at].astype(jnp.float32)
                out_ref[start : start + size, :] = total.astype(jnp.bfloat16)
            start += size


def chip_sum(mine, theirs):
    rows, width = sum(value.shape[0] for value in mine), mine[0].shape[1]
    return pl.pallas_call(
        functools.partial(chip_sum_kernel, len(theirs)),
        out_shape=(pltpu.VMEM((rows, width // PLANE), jnp.bfloat16),) * PLANE,
        in_specs=[VMEM] * (2 + len(theirs)),
        out_specs=(VMEM,) * PLANE,
        compiler_params=params(4),
        name="chip_sum",
    )(*mine, *theirs)


def plane_sum_kernel(depth, *refs):
    in_refs, out_refs = refs[:PLANE], refs[PLANE:]
    group = in_refs[0].shape[0] // PLANE
    rows = group // depth
    for k in range(PLANE):
        for z in range(depth):
            total = 0.0
            for d in range(PLANE):
                start = (k ^ d) * group + z * rows
                total = total + in_refs[d][start : start + rows, :].astype(jnp.float32)
            out_refs[z][k * rows : (k + 1) * rows, :] = total.astype(jnp.bfloat16)


def plane_sum(parts, depth):
    rows, part = parts[0].shape
    return pl.pallas_call(
        functools.partial(plane_sum_kernel, depth),
        out_shape=(pltpu.VMEM((rows // depth, part), jnp.bfloat16),) * depth,
        in_specs=[VMEM] * PLANE,
        out_specs=(VMEM,) * depth,
        compiler_params=params(4),
        name="plane_sum",
    )(*parts)


def second_norm_kernel(depth, *refs):
    parts, packed = refs[:depth], refs[depth : depth + PLANE + 1]
    gain_ref, scaled_ref, next_ref = refs[depth + PLANE + 1 :]
    rows = packed[0].shape[0] // depth
    part = parts[0].shape[1]
    sub = part // depth
    skip = packed[0].shape[1] - 2 * sub
    lane = lax.broadcasted_iota(jnp.int32, (rows, META), 1)
    plane = lax.axis_index("expert") % PLANE
    gain = jnp.concatenate(
        [gain_ref[:, lanes((z * PLANE + plane) * sub, sub)] for z in range(depth)], axis=1
    )
    for d in range(PLANE):
        at = slice(d * rows, (d + 1) * rows)
        total = parts[0][at, :].astype(jnp.float32)
        for ref in parts[1:]:
            total = total + ref[at, :].astype(jnp.float32)
        if d < PLANE - 1:
            first = packed[d][:, skip : skip + sub]
        else:
            first = jnp.concatenate([ref[:, skip + sub :] for ref in packed[d:]], axis=0)
        first = jnp.concatenate([first[z * rows : (z + 1) * rows] for z in range(depth)], axis=1)
        following = (first.astype(jnp.float32) + total).astype(jnp.bfloat16)
        next_ref[at, :] = following
        wide = following.astype(jnp.float32)
        scaled_ref[at, :part] = (wide * gain).astype(jnp.bfloat16)
        squares = jnp.sum(wide * wide, axis=1, keepdims=True)
        high = squares.astype(jnp.bfloat16).astype(jnp.float32)
        low = squares - high
        scaled_ref[at, part:] = jnp.where(
            lane == 0, high, jnp.where(lane == 1, low, 0.0)
        ).astype(jnp.bfloat16)


def second_norm(parts, packed, gain):
    depth = len(parts)
    rows, part = parts[0].shape
    return pl.pallas_call(
        functools.partial(second_norm_kernel, depth),
        out_shape=(
            jax.ShapeDtypeStruct((rows, part + META), jnp.bfloat16),
            jax.ShapeDtypeStruct((rows, part), jnp.bfloat16),
        ),
        in_specs=[VMEM] * (depth + PLANE + 2),
        out_specs=(VMEM, VMEM),
        compiler_params=params(4),
        name="second_norm",
    )(*parts, *packed, gain)


def projection_kernel(chunk, mine_ref, theirs_ref, next_ref, q_ref, *refs):
    kv_refs, out_refs, kv_buf = refs[: -PLANE - 1], refs[-PLANE - 1 : -1], refs[-1]
    depth = len(kv_refs)
    rows, extended = mine_ref.shape
    part = extended - META
    sub = part // depth
    q_cols, kv_cols = q_ref.shape[1], kv_buf.shape[1]
    cols = q_cols + kv_cols
    line = lax.axis_index("expert") // PLANE
    for d, ref in enumerate(kv_refs):
        kv_buf[lanes((line ^ d) * sub, sub), :] = ref[...]
    block = rows // PLANE
    tensor = lax.axis_index("tensor")
    own = lanes(tensor * block, block)
    other = lanes((1 - tensor) * block, block)
    for d in range(PLANE):
        at = slice(d * block, (d + 1) * block)
        out_refs[d][own, cols : cols + META] = mine_ref[at, part:]
        out_refs[d][other, cols : cols + META] = theirs_ref[at, part:]
        out_refs[d][:block, cols + META :] = next_ref[at, : part // 2]
        out_refs[d][block:, cols + META :] = next_ref[at, part // 2 :]
    both = jnp.concatenate([mine_ref[:, :part], theirs_ref[:, :part]], axis=0)

    def multiply(weight, target):
        product = jnp.dot(both, weight, preferred_element_type=jnp.float32).astype(jnp.bfloat16)
        at = slice(target, target + weight.shape[1])
        for d in range(PLANE):
            out_refs[d][own, at] = product[d * block : (d + 1) * block]
            out_refs[d][other, at] = product[rows + d * block : rows + (d + 1) * block]

    multiply(kv_buf[...], q_cols)
    for start in range(0, q_cols, chunk):
        multiply(q_ref[:, start : start + chunk], start)


def projection(mine, theirs, following, q_weight, kv_weights):
    rows, part = following.shape
    q_cols, kv_cols = q_weight.shape[1], kv_weights[0].shape[1]
    chunk = 512
    shape = pltpu.VMEM((2 * rows // PLANE, q_cols + kv_cols + META + part // 2), jnp.bfloat16)
    return pl.pallas_call(
        functools.partial(projection_kernel, chunk),
        out_shape=(shape,) * PLANE,
        in_specs=[VMEM] * (4 + len(kv_weights)),
        out_specs=(VMEM,) * PLANE,
        scratch_shapes=[pltpu.VMEM((part, kv_cols), jnp.bfloat16)],
        compiler_params=params(8),
        cost_estimate=SMALL,
        name="qkv_projection",
    )(mine, theirs, following, q_weight, *kv_weights)


def head_norm_kernel(depth, *refs):
    parts, q_gain_ref, k_gain_ref = refs[:PLANE], refs[PLANE], refs[PLANE + 1]
    next_ref, q_ref, kv_ref = refs[PLANE + 2 :]
    width = next_ref.shape[1]
    q_cols, kv_cols = q_ref.shape[1], kv_ref.shape[1]
    cols = q_cols + kv_cols
    head = q_gain_ref.shape[1]

    def total(at):
        value = parts[0][:, at].astype(jnp.float32)
        for ref in parts[1:]:
            value = value + ref[:, at].astype(jnp.float32)
        return value

    squares = jnp.sum(total(slice(cols, cols + META)), axis=1, keepdims=True)
    scale = lax.rsqrt(squares / width + EPSILON)
    for h in range(q_cols // head):
        at = slice(h * head, (h + 1) * head)
        q_ref[:, at] = normalize(total(at) * scale, q_gain_ref[...]).astype(jnp.bfloat16)
    tensor = lax.axis_index("tensor")
    for h in range(kv_cols // head):
        at = slice(h * head, (h + 1) * head)
        raw = total(slice(q_cols + h * head, q_cols + (h + 1) * head)) * scale
        is_key = tensor * (kv_cols // head) + h < KV_HEADS
        kv_ref[:, at] = jnp.where(is_key, normalize(raw, k_gain_ref[...]), raw).astype(
            jnp.bfloat16
        )
    plane = lax.axis_index("expert") % PLANE
    rows = next_ref.shape[0]
    sub = width // (PLANE * depth)
    for d in range(PLANE):
        for z in range(depth):
            top = z * sub * 2 // (depth * sub)
            start = cols + META + z * sub - top * (depth * sub // 2)
            next_ref[:, lanes((z * PLANE + (plane ^ d)) * sub, sub)] = parts[d][
                top * rows : (top + 1) * rows, start : start + sub
            ]


def head_norm(parts, q_gain, k_gain, q_cols, kv_cols, rows, width, depth):
    both = parts[0].shape[0]
    return pl.pallas_call(
        functools.partial(head_norm_kernel, depth),
        out_shape=(
            jax.ShapeDtypeStruct((rows, width), jnp.bfloat16),
            jax.ShapeDtypeStruct((both, q_cols), jnp.bfloat16),
            jax.ShapeDtypeStruct((both, kv_cols), jnp.bfloat16),
        ),
        in_specs=[VMEM] * (PLANE + 2),
        out_specs=(VMEM, VMEM, VMEM),
        compiler_params=params(4),
        name="head_norm",
    )(*parts, q_gain, k_gain)


def per_device_dense(
    attn_out,
    out_weight,
    residual,
    attn_gain,
    expert_ids,
    route_weights,
    w_gate,
    w_up,
    w_down,
    input_gain,
    q_weight,
    kv_weight,
    q_gain,
    k_gain,
):
    n_expert = lax.axis_size("expert")
    depth = n_expert // PLANE
    rows, width = residual.shape
    tensor_index = lax.axis_index("tensor").astype(jnp.int32)

    def to_core(value):
        return lax.ppermute(value, "tensor", [(0, 1), (1, 0)])

    def to_expert(value, offset):
        return lax.ppermute(value, "expert", [(i, i ^ offset) for i in range(n_expert)])

    def to_z(values):
        return [to_expert(v, d * PLANE) if d else v for d, v in enumerate(values)]

    def to_plane(values):
        return [to_expert(v, d) if d else v for d, v in enumerate(values)]

    own_ids = lax.dynamic_slice_in_dim(expert_ids, tensor_index * rows, rows, 0)
    own_route = lax.dynamic_slice_in_dim(route_weights, tensor_index * rows, rows, 0)
    chosen = own_ids[:, :, None] == jnp.arange(META // 2, dtype=jnp.int32)[None, None, :]
    dense = jnp.sum(jnp.where(chosen, own_route[:, :, None], 0.0), axis=1)
    high = lax.reduce_precision(dense, 8, 7)
    meta = jnp.concatenate([high, dense - high], axis=1).astype(jnp.bfloat16)

    lines = [list(range(i, n_expert, PLANE)) for i in range(PLANE)]
    mine, theirs = out_projection(attn_out, out_weight)
    tokens, *firsts = first_norm(
        (mine,), (to_core(theirs),), residual, attn_gain[None, :], meta, depth
    )
    tokens, q_own, kv_own = lax.optimization_barrier((tokens, q_weight, kv_weight))
    kv_rows = [kv_own, to_expert(kv_own, PLANE)]
    q_rows = lax.all_gather(q_own, "expert", axis=0, tiled=True, axis_index_groups=lines)
    weights = load((w_gate, w_up, w_down), (tokens,))
    line = to_z([tokens] * depth)
    *line, gate, up, down, kv_rows[1] = lax.optimization_barrier((*line, *weights, kv_rows[1]))
    weights = (gate, up, down)
    near = to_plane(pack(line, firsts))
    cut = near[0].shape[0] // 2
    one, two = near[1][:cut], near[2][cut:]
    far = [to_expert(one, 2), to_expert(two, 1)]
    near_mine, *near_theirs = experts((*near, *map(to_core, near)), weights, depth, len(near))
    theirs = list(map(to_core, near_theirs))
    near_mine, *far = lax.optimization_barrier((near_mine, *far))
    far_both = [*far, *map(to_core, far)]
    far_mine, *far_theirs = experts(far_both, weights, depth, 1)
    theirs += map(to_core, far_theirs)
    *sums, kv_own = lax.optimization_barrier((*chip_sum((near_mine, far_mine), theirs), kv_own))
    parts = to_plane(sums)
    kv_rows.append(to_expert(kv_own, 2 * PLANE))
    parts = plane_sum(parts, depth)
    kv_rows.append(to_expert(kv_rows[2], PLANE))
    (q_rows,) = load((q_rows,), parts)
    parts = to_z(parts)
    *parts, q_rows = lax.optimization_barrier((*parts, q_rows))
    scaled, following = second_norm(parts, (*near, *far), input_gain[None, :])
    products = to_plane(projection(scaled, to_core(scaled), following, q_rows, kv_rows))
    return head_norm(
        products,
        q_gain[None, :],
        k_gain[None, :],
        q_weight.shape[1],
        kv_weight.shape[1],
        rows,
        width,
        depth,
    )


def per_device(
    attn_out,
    out_weight,
    residual,
    attn_gain,
    expert_ids,
    route_weights,
    w_gate,
    w_up,
    w_down,
    input_gain,
    q_weight,
    kv_weight,
    q_gain,
    k_gain,
):
    n_expert = lax.axis_size("expert")
    n_tensor = lax.axis_size("tensor")
    share = n_tensor // 2
    tensor_index = lax.axis_index("tensor")
    group_rows = attn_out.shape[0]
    width = residual.shape[1]
    half = tensor_index // share
    capacity = 3 * group_rows * TOP // (4 * n_expert)
    all_experts = 2 * n_expert
    attn_rows = lax.psum_scatter(
        jnp.dot(attn_out, out_weight, preferred_element_type=jnp.float32),
        "tensor",
        scatter_dimension=0,
        tiled=True,
    )
    first_residual = (residual.astype(jnp.float32) + attn_rows).astype(jnp.bfloat16)
    normed = normalize(first_residual.astype(jnp.float32), attn_gain).astype(jnp.bfloat16)
    group_normed = lax.all_gather(normed, "tensor", axis=0, tiled=True)
    flat_ids = expert_ids.reshape(-1)
    onehot = (flat_ids[:, None] == jnp.arange(all_experts, dtype=jnp.int32)[None, :]).astype(
        jnp.int32
    )
    earlier = jnp.cumsum(onehot, axis=0) - onehot
    rank = jnp.sum(earlier * onehot, axis=1)
    dest = flat_ids * capacity + rank
    row_owner = jnp.arange(flat_ids.shape[0], dtype=jnp.int32) // TOP
    slot_row = jnp.full((all_experts * capacity,), group_rows, jnp.int32).at[dest].set(row_owner)
    slot_weight = (
        jnp.zeros((all_experts * capacity,), jnp.float32).at[dest].set(route_weights.reshape(-1))
    )
    own_slots = lax.dynamic_index_in_dim(
        slot_row.reshape(n_expert, 2, capacity), half, 1, keepdims=False
    )
    own_weights = lax.dynamic_index_in_dim(
        slot_weight.reshape(n_expert, 2, capacity), half, 1, keepdims=False
    )
    padded_rows = jnp.concatenate([group_normed, jnp.zeros((1, width), jnp.bfloat16)], axis=0)
    gate_w = w_gate[0]
    up_w = w_up[0]
    down_w = w_down[0]
    outgoing = jnp.take(padded_rows, own_slots, axis=0)
    arrived = lax.all_to_all(outgoing, "expert", split_axis=0, concat_axis=0, tiled=True)
    flat = arrived.reshape(-1, width)
    gate = jnp.dot(flat, gate_w, preferred_element_type=jnp.float32)
    up = jnp.dot(flat, up_w, preferred_element_type=jnp.float32)
    act = (jax.nn.silu(gate) * up).astype(jnp.bfloat16)
    part = jnp.dot(act, down_w, preferred_element_type=jnp.float32).astype(jnp.bfloat16)
    send_part = part.reshape(arrived.shape)
    returned = lax.all_to_all(send_part, "expert", split_axis=0, concat_axis=0, tiled=True)
    weighted = own_weights.reshape(-1)[:, None] * returned.reshape(-1, width).astype(jnp.float32)
    term = (
        jnp.zeros((group_rows + 1, width), jnp.float32)
        .at[own_slots.reshape(-1)]
        .add(weighted)[:group_rows]
    )
    expert_sum = lax.psum_scatter(
        term.astype(jnp.bfloat16), "tensor", scatter_dimension=0, tiled=True
    ).astype(jnp.float32)
    next_residual = (first_residual.astype(jnp.float32) + expert_sum).astype(jnp.bfloat16)
    own_normed = normalize(next_residual.astype(jnp.float32), input_gain).astype(jnp.bfloat16)
    next_normed = lax.all_gather(own_normed, "tensor", axis=0, tiled=True)
    query_cols = q_weight.shape[1]
    kv_cols = kv_weight.shape[1]
    query_raw = jnp.dot(
        next_normed,
        lax.all_gather(q_weight, "expert", axis=0, tiled=True),
        preferred_element_type=jnp.float32,
    )
    kv_raw = jnp.dot(
        next_normed,
        lax.all_gather(kv_weight, "expert", axis=0, tiled=True),
        preferred_element_type=jnp.float32,
    )
    head_size = q_gain.shape[0]
    queries = (
        normalize(query_raw.reshape(group_rows, -1, head_size), q_gain)
        .reshape(group_rows, query_cols)
        .astype(jnp.bfloat16)
    )
    heads_here = kv_cols // head_size
    head_number = tensor_index * heads_here + jnp.arange(heads_here, dtype=jnp.int32)
    is_key = head_number < KV_HEADS
    kv_shaped = kv_raw.reshape(group_rows, heads_here, head_size)
    keys_values = (
        jnp.where(is_key[None, :, None], normalize(kv_shaped, k_gain), kv_shaped)
        .reshape(group_rows, kv_cols)
        .astype(jnp.bfloat16)
    )
    return (next_residual, queries, keys_values)


def solution(mesh):
    small = mesh.shape["tensor"] == 2 and mesh.shape["expert"] == 4 * PLANE
    return jax.shard_map(
        per_device_dense if small else per_device,
        mesh=mesh,
        in_specs=(
            P("expert", "tensor"),
            P("tensor", None),
            P(("expert", "tensor"), None),
            P(),
            P("expert", None),
            P("expert", None),
            P("expert", None, "tensor"),
            P("expert", None, "tensor"),
            P("expert", "tensor", None),
            P(),
            P("expert", "tensor"),
            P("expert", "tensor"),
            P(),
            P(),
        ),
        out_specs=(P(("expert", "tensor"), None), P("expert", "tensor"), P("expert", "tensor")),
        check_vma=False,
    )
```

```python
import functools

import jax
import jax.numpy as jnp
from jax import lax
from jax.experimental import pallas as pl
from jax.experimental.pallas import tpu as pltpu
from jax.sharding import PartitionSpec as P

KV_HEADS = 4
TOP = 8
PLANE = 4
META = 128


EPSILON = 1e-06

SMALL = pl.CostEstimate(flops=0, bytes_accessed=0, transcendentals=0)
VMEM = pl.BlockSpec(memory_space=pltpu.VMEM)
HBM = pl.BlockSpec(memory_space=pltpu.HBM)


def normalize(values, gain):
    return values * lax.rsqrt(jnp.mean(values * values, axis=-1, keepdims=True) + EPSILON) * gain


def params(mebibytes):
    return pltpu.CompilerParams(vmem_limit_bytes=mebibytes << 20)


def lanes(start, size):
    return pl.ds(pl.multiple_of(start, size), size)


def in_hbm(value):
    return pltpu.with_memory_space_constraint(value, pltpu.HBM)


def in_vmem(value):
    return pltpu.with_memory_space_constraint(value, pltpu.VMEM)


def out_projection_kernel(chunk, a_hbm, w_hbm, mine_ref, theirs_ref, a_buf, w_buf, a_sem, sems):
    depth = w_buf.shape[0]
    count = depth // chunk
    half = mine_ref.shape[0]
    a_copy = pltpu.make_async_copy(a_hbm, a_buf, a_sem)
    a_copy.start()
    copies = []
    for i in range(count):
        rows = pl.ds(i * chunk, chunk)
        copies.append(pltpu.make_async_copy(w_hbm.at[rows], w_buf.at[rows], sems.at[i]))
    for copy in copies:
        copy.start()
    tensor = lax.axis_index("tensor")
    own = lanes(tensor * half, half)
    other = lanes((1 - tensor) * half, half)
    a_copy.wait()
    for i in range(count):
        copies[i].wait()
        at = pl.ds(i * chunk, chunk)
        both = jnp.concatenate([a_buf[own, at], a_buf[other, at]], axis=0)
        product = jnp.dot(both, w_buf[at, :], preferred_element_type=jnp.float32)
        if i == 0:
            mine_ref[...] = product[:half]
            theirs_ref[...] = product[half:]
        else:
            mine_ref[...] += product[:half]
            theirs_ref[...] += product[half:]


def out_projection(attn_out, out_weight):
    rows, depth = attn_out.shape
    width = out_weight.shape[1]
    chunk = 256
    half = pltpu.VMEM((rows // 2, width), jnp.float32)
    return pl.pallas_call(
        functools.partial(out_projection_kernel, chunk),
        out_shape=(half, half),
        in_specs=[HBM, HBM],
        out_specs=(VMEM, VMEM),
        scratch_shapes=[
            pltpu.VMEM((rows, depth), jnp.bfloat16),
            pltpu.VMEM((depth, width), jnp.bfloat16),
            pltpu.SemaphoreType.DMA,
            pltpu.SemaphoreType.DMA((depth // chunk,)),
        ],
        compiler_params=params(14),
        cost_estimate=SMALL,
        name="out_projection",
    )(in_hbm(attn_out), in_hbm(out_weight))


def first_norm_kernel(depth, count, *refs):
    mine, theirs = refs[:count], refs[count : 2 * count]
    residual_ref, gain_ref, meta_ref, tokens_ref = refs[2 * count : 2 * count + 4]
    slice_refs, first_ref = refs[2 * count + 4 : -1], refs[-1]
    rows, width = residual_ref.shape
    sub = width // (PLANE * depth)
    start = 0
    for mine_ref, theirs_ref in zip(mine, theirs):
        cols = slice(start, start + mine_ref.shape[1])
        start += mine_ref.shape[1]
        first_ref[:, cols] = (
            residual_ref[:, cols].astype(jnp.float32) + (mine_ref[...] + theirs_ref[...])
        ).astype(jnp.bfloat16)
    first = first_ref[...]
    tokens_ref[:, :width] = normalize(first.astype(jnp.float32), gain_ref[...]).astype(jnp.bfloat16)
    tokens_ref[:, width:] = meta_ref[...]
    plane = lax.axis_index("expert") % PLANE
    for d in range(PLANE):
        for z in range(depth):
            slice_refs[d][z * rows : (z + 1) * rows, :] = first_ref[
                :, lanes((z * PLANE + (plane ^ d)) * sub, sub)
            ]


def first_norm(mine, theirs, residual, gain, meta, depth):
    rows, width = residual.shape
    piece = jax.ShapeDtypeStruct((depth * rows, width // (PLANE * depth)), jnp.bfloat16)
    return pl.pallas_call(
        functools.partial(first_norm_kernel, depth, len(mine)),
        out_shape=(jax.ShapeDtypeStruct((rows, width + META), jnp.bfloat16),) + (piece,) * PLANE,
        in_specs=[VMEM] * (2 * len(mine) + 3),
        out_specs=(VMEM,) * (1 + PLANE),
        scratch_shapes=[pltpu.VMEM((rows, width), jnp.bfloat16)],
        compiler_params=params(2),
        name="first_norm",
    )(*mine, *theirs, residual, gain, meta)


def pack_kernel(depth, *refs):
    line, pieces, out_refs = refs[:depth], refs[depth : depth + PLANE], refs[depth + PLANE :]
    rows, extended = line[0].shape
    sub = pieces[0].shape[1]
    for d, ref in enumerate(out_refs):
        for z in range(depth):
            ref[z * rows : (z + 1) * rows, :extended] = line[z][...]
        ref[:, extended : extended + sub] = pieces[d][...]
        ref[:, extended + sub :] = pieces[PLANE - 1][...]


def pack(line, pieces):
    depth = len(line)
    rows, extended = line[0].shape
    shape = pltpu.VMEM((depth * rows, extended + 2 * pieces[0].shape[1]), jnp.bfloat16)
    return pl.pallas_call(
        functools.partial(pack_kernel, depth),
        out_shape=(shape,) * (PLANE - 1),
        in_specs=[VMEM] * (depth + PLANE),
        out_specs=(VMEM,) * (PLANE - 1),
        compiler_params=params(2),
        name="pack_tokens",
    )(*line, *pieces)


def load_kernel(count, *refs):
    sources, targets, sems = refs[:count], refs[-count - 1 : -1], refs[-1]
    copies = [
        pltpu.make_async_copy(source, target, sems.at[i])
        for i, (source, target) in enumerate(zip(sources, targets))
    ]
    for copy in copies:
        copy.start()
    for copy in copies:
        copy.wait()


def load(weights, after):
    count = len(weights)
    return pl.pallas_call(
        functools.partial(load_kernel, count),
        out_shape=tuple(pltpu.VMEM(w.shape, w.dtype) for w in weights),
        in_specs=[HBM] * count + [pl.BlockSpec(memory_space=pl.ANY)] * len(after),
        out_specs=(VMEM,) * count,
        scratch_shapes=[pltpu.SemaphoreType.DMA((count,))],
        compiler_params=params(2),
        cost_estimate=SMALL,
        name="load_weights",
    )(*map(in_hbm, weights), *after)


def expert_kernel(depth, chunk, count, *refs):
    block_refs, (gate_ref, up_ref, down_ref) = refs[:count], refs[count : count + 3]
    mine_ref, *theirs_refs, x_buf, act_buf = refs[count + 3 :]
    width, hidden = gate_ref.shape[1:]
    extended = x_buf.shape[1]
    start = 0
    for ref in block_refs:
        rows = ref.shape[0]
        x_buf[start : start + rows, :] = ref[:, :extended]
        start += rows
    meta = x_buf[:, width:].astype(jnp.float32)
    lane = lax.broadcasted_iota(jnp.int32, meta.shape, 1)
    chip = lax.axis_index("expert")
    expert = 2 * chip + lax.axis_index("tensor")
    chosen = (lane == expert) | (lane == expert + META // 2)
    route = 0.5 * jnp.sum(jnp.where(chosen, meta, 0.0), axis=1, keepdims=True)
    for i in range(hidden // chunk):
        cols = pl.ds(i * chunk, chunk)
        x = x_buf[:, :width]
        gate = jnp.dot(x, gate_ref[0, :, cols], preferred_element_type=jnp.float32)
        up = jnp.dot(x, up_ref[0, :, cols], preferred_element_type=jnp.float32)
        act = gate * (1.0 + jnp.tanh(0.5 * gate)) * (up * route)
        act_buf[:, i * chunk : (i + 1) * chunk] = act.astype(jnp.bfloat16)
    sub = width // (PLANE * depth)
    part = sub * depth
    half = mine_ref.shape[0]
    plane = chip % PLANE
    for d in range(PLANE):
        weight = jnp.concatenate(
            [down_ref[0, :, lanes((z * PLANE + (plane ^ d)) * sub, sub)] for z in range(depth)],
            axis=1,
        )
        out = jnp.dot(act_buf[...], weight, preferred_element_type=jnp.float32)
        cols = slice(d * part, (d + 1) * part)
        mine_ref[:, cols] = out[:half].astype(jnp.bfloat16)
        start = half
        for ref in theirs_refs:
            stop = start + ref.shape[0]
            ref[:, cols] = out[start:stop].astype(jnp.bfloat16)
            start = stop


def experts(blocks, weights, depth, pieces):
    width, hidden = weights[0].shape[1:]
    chunk = 256
    extended = width + META
    total = sum(block.shape[0] for block in blocks)
    rows = [total // 2] + [total // 2 // pieces] * pieces
    return pl.pallas_call(
        functools.partial(expert_kernel, depth, chunk, len(blocks)),
        out_shape=tuple(pltpu.VMEM((size, width), jnp.bfloat16) for size in rows),
        in_specs=[VMEM] * (len(blocks) + 3),
        out_specs=(VMEM,) * (1 + pieces),
        scratch_shapes=[
            pltpu.VMEM((total, extended), jnp.bfloat16),
            pltpu.VMEM((total, hidden), jnp.bfloat16),
        ],
        compiler_params=params(16),
        cost_estimate=pl.CostEstimate(
            flops=6 * total * width * hidden, bytes_accessed=0, transcendentals=0
        ),
        name="experts",
    )(*blocks, *weights)


def chip_sum_kernel(count, *refs):
    mine, theirs, out_refs = refs[:2], refs[2 : 2 + count], refs[2 + count :]
    part = out_refs[0].shape[1]
    start = 0
    for own_ref in mine:
        first = start
        while start < first + own_ref.shape[0]:
            ref, theirs = theirs[0], theirs[1:]
            size = ref.shape[0]
            own = slice(start - first, start - first + size)
            for d, out_ref in enumerate(out_refs):
                at = slice(d * part, (d + 1) * part)
                total = own_ref[own, at].astype(jnp.float32) + ref[:, at].astype(jnp.float32)
                out_ref[start : start + size, :] = total.astype(jnp.bfloat16)
            start += size


def chip_sum(mine, theirs):
    rows, width = sum(value.shape[0] for value in mine), mine[0].shape[1]
    return pl.pallas_call(
        functools.partial(chip_sum_kernel, len(theirs)),
        out_shape=(pltpu.VMEM((rows, width // PLANE), jnp.bfloat16),) * PLANE,
        in_specs=[VMEM] * (2 + len(theirs)),
        out_specs=(VMEM,) * PLANE,
        compiler_params=params(4),
        name="chip_sum",
    )(*mine, *theirs)


def plane_sum_kernel(depth, *refs):
    in_refs, out_refs = refs[:PLANE], refs[PLANE:]
    group = in_refs[0].shape[0] // PLANE
    rows = group // depth
    for k in range(PLANE):
        for z in range(depth):
            total = 0.0
            for d in range(PLANE):
                start = (k ^ d) * group + z * rows
                total = total + in_refs[d][start : start + rows, :].astype(jnp.float32)
            out_refs[z][k * rows : (k + 1) * rows, :] = total.astype(jnp.bfloat16)


def plane_sum(parts, depth):
    rows, part = parts[0].shape
    return pl.pallas_call(
        functools.partial(plane_sum_kernel, depth),
        out_shape=(pltpu.VMEM((rows // depth, part), jnp.bfloat16),) * depth,
        in_specs=[VMEM] * PLANE,
        out_specs=(VMEM,) * depth,
        compiler_params=params(4),
        name="plane_sum",
    )(*parts)


def second_norm_kernel(depth, *refs):
    parts, packed = refs[:depth], refs[depth : depth + PLANE + 1]
    gain_ref, scaled_ref, next_ref = refs[depth + PLANE + 1 :]
    rows = packed[0].shape[0] // depth
    part = parts[0].shape[1]
    sub = part // depth
    skip = packed[0].shape[1] - 2 * sub
    lane = lax.broadcasted_iota(jnp.int32, (rows, META), 1)
    plane = lax.axis_index("expert") % PLANE
    gain = jnp.concatenate(
        [gain_ref[:, lanes((z * PLANE + plane) * sub, sub)] for z in range(depth)], axis=1
    )
    for d in range(PLANE):
        at = slice(d * rows, (d + 1) * rows)
        total = parts[0][at, :].astype(jnp.float32)
        for ref in parts[1:]:
            total = total + ref[at, :].astype(jnp.float32)
        if d < PLANE - 1:
            first = packed[d][:, skip : skip + sub]
        else:
            first = jnp.concatenate([ref[:, skip + sub :] for ref in packed[d:]], axis=0)
        first = jnp.concatenate([first[z * rows : (z + 1) * rows] for z in range(depth)], axis=1)
        following = (first.astype(jnp.float32) + total).astype(jnp.bfloat16)
        next_ref[at, :] = following
        wide = following.astype(jnp.float32)
        scaled_ref[at, :part] = (wide * gain).astype(jnp.bfloat16)
        squares = jnp.sum(wide * wide, axis=1, keepdims=True)
        high = squares.astype(jnp.bfloat16).astype(jnp.float32)
        low = squares - high
        scaled_ref[at, part:] = jnp.where(
            lane == 0, high, jnp.where(lane == 1, low, 0.0)
        ).astype(jnp.bfloat16)


def second_norm(parts, packed, gain):
    depth = len(parts)
    rows, part = parts[0].shape
    return pl.pallas_call(
        functools.partial(second_norm_kernel, depth),
        out_shape=(
            jax.ShapeDtypeStruct((rows, part + META), jnp.bfloat16),
            jax.ShapeDtypeStruct((rows, part), jnp.bfloat16),
        ),
        in_specs=[VMEM] * (depth + PLANE + 2),
        out_specs=(VMEM, VMEM),
        compiler_params=params(4),
        name="second_norm",
    )(*parts, *packed, gain)


def projection_kernel(chunk, count, mine_ref, theirs_ref, next_ref, *refs):
    weight_refs, out_refs, order_buf = refs[:count], refs[count:-1], refs[-1]
    rows, extended = mine_ref.shape
    part = extended - META
    sub = part // count
    cols = weight_refs[0].shape[1]
    line = lax.axis_index("expert") // PLANE
    for d in range(count):
        at = lanes((line ^ d) * sub, sub)
        here = slice(d * sub, (d + 1) * sub)
        order_buf[:rows, here] = mine_ref[:, at]
        order_buf[rows:, here] = theirs_ref[:, at]
    block = rows // PLANE
    tensor = lax.axis_index("tensor")
    own = lanes(tensor * block, block)
    other = lanes((1 - tensor) * block, block)
    for d in range(PLANE):
        at = slice(d * block, (d + 1) * block)
        out_refs[d][own, cols : cols + META] = mine_ref[at, part:]
        out_refs[d][other, cols : cols + META] = theirs_ref[at, part:]
        out_refs[d][:block, cols + META :] = next_ref[at, : part // 2]
        out_refs[d][block:, cols + META :] = next_ref[at, part // 2 :]
    for start in range(0, cols, chunk):
        at = slice(start, start + chunk)
        weight = jnp.concatenate([ref[:, at] for ref in weight_refs], axis=0)
        product = jnp.dot(order_buf[...], weight, preferred_element_type=jnp.float32)
        product = product.astype(jnp.bfloat16)
        for d in range(PLANE):
            out_refs[d][own, at] = product[d * block : (d + 1) * block]
            out_refs[d][other, at] = product[rows + d * block : rows + (d + 1) * block]


def projection(mine, theirs, following, weights):
    rows, part = following.shape
    cols = weights[0].shape[1]
    chunk = 512
    shape = pltpu.VMEM((2 * rows // PLANE, cols + META + part // 2), jnp.bfloat16)
    return pl.pallas_call(
        functools.partial(projection_kernel, chunk, len(weights)),
        out_shape=(shape,) * PLANE,
        in_specs=[VMEM] * (3 + len(weights)),
        out_specs=(VMEM,) * PLANE,
        scratch_shapes=[pltpu.VMEM((2 * rows, part), jnp.bfloat16)],
        compiler_params=params(8),
        cost_estimate=SMALL,
        name="qkv_projection",
    )(mine, theirs, following, *map(in_vmem, weights))


def head_norm_kernel(depth, *refs):
    parts, q_gain_ref, k_gain_ref = refs[:PLANE], refs[PLANE], refs[PLANE + 1]
    next_ref, q_ref, kv_ref = refs[PLANE + 2 :]
    width = next_ref.shape[1]
    q_cols, kv_cols = q_ref.shape[1], kv_ref.shape[1]
    cols = q_cols + kv_cols
    head = q_gain_ref.shape[1]

    def total(at):
        value = parts[0][:, at].astype(jnp.float32)
        for ref in parts[1:]:
            value = value + ref[:, at].astype(jnp.float32)
        return value

    squares = jnp.sum(total(slice(cols, cols + META)), axis=1, keepdims=True)
    scale = lax.rsqrt(squares / width + EPSILON)
    for h in range(q_cols // head):
        at = slice(h * head, (h + 1) * head)
        q_ref[:, at] = normalize(total(at) * scale, q_gain_ref[...]).astype(jnp.bfloat16)
    tensor = lax.axis_index("tensor")
    for h in range(kv_cols // head):
        at = slice(h * head, (h + 1) * head)
        raw = total(slice(q_cols + h * head, q_cols + (h + 1) * head)) * scale
        is_key = tensor * (kv_cols // head) + h < KV_HEADS
        kv_ref[:, at] = jnp.where(is_key, normalize(raw, k_gain_ref[...]), raw).astype(
            jnp.bfloat16
        )
    plane = lax.axis_index("expert") % PLANE
    rows = next_ref.shape[0]
    sub = width // (PLANE * depth)
    for d in range(PLANE):
        for z in range(depth):
            top = z * sub * 2 // (depth * sub)
            start = cols + META + z * sub - top * (depth * sub // 2)
            next_ref[:, lanes((z * PLANE + (plane ^ d)) * sub, sub)] = parts[d][
                top * rows : (top + 1) * rows, start : start + sub
            ]


def head_norm(parts, q_gain, k_gain, q_cols, kv_cols, rows, width, depth):
    both = parts[0].shape[0]
    return pl.pallas_call(
        functools.partial(head_norm_kernel, depth),
        out_shape=(
            jax.ShapeDtypeStruct((rows, width), jnp.bfloat16),
            jax.ShapeDtypeStruct((both, q_cols), jnp.bfloat16),
            jax.ShapeDtypeStruct((both, kv_cols), jnp.bfloat16),
        ),
        in_specs=[VMEM] * (PLANE + 2),
        out_specs=(VMEM, VMEM, VMEM),
        compiler_params=params(4),
        name="head_norm",
    )(*parts, q_gain, k_gain)


def per_device_dense(
    attn_out,
    out_weight,
    residual,
    attn_gain,
    expert_ids,
    route_weights,
    w_gate,
    w_up,
    w_down,
    input_gain,
    q_weight,
    kv_weight,
    q_gain,
    k_gain,
):
    n_expert = lax.axis_size("expert")
    depth = n_expert // PLANE
    rows, width = residual.shape
    tensor_index = lax.axis_index("tensor").astype(jnp.int32)

    def to_core(value):
        return lax.ppermute(value, "tensor", [(0, 1), (1, 0)])

    def to_expert(value, offset):
        return lax.ppermute(value, "expert", [(i, i ^ offset) for i in range(n_expert)])

    def to_z(values):
        return [to_expert(v, d * PLANE) if d else v for d, v in enumerate(values)]

    def to_plane(values):
        return [to_expert(v, d) if d else v for d, v in enumerate(values)]

    own_ids = lax.dynamic_slice_in_dim(expert_ids, tensor_index * rows, rows, 0)
    own_route = lax.dynamic_slice_in_dim(route_weights, tensor_index * rows, rows, 0)
    chosen = own_ids[:, :, None] == jnp.arange(META // 2, dtype=jnp.int32)[None, None, :]
    dense = jnp.sum(jnp.where(chosen, own_route[:, :, None], 0.0), axis=1)
    high = lax.reduce_precision(dense, 8, 7)
    meta = jnp.concatenate([high, dense - high], axis=1).astype(jnp.bfloat16)

    mine, theirs = out_projection(attn_out, out_weight)
    mine, q_own, kv_own = lax.optimization_barrier((mine, q_weight, kv_weight))
    joined = jnp.concatenate([q_own, kv_own], axis=1)
    tokens, *firsts = first_norm(
        (mine,), (to_core(theirs),), residual, attn_gain[None, :], meta, depth
    )
    tokens, joined = lax.optimization_barrier((tokens, joined))
    far_line = n_expert // 2
    pairs = [[i, i + far_line] for i in range(far_line)]
    pair_rows = lax.all_gather(joined, "expert", axis=0, axis_index_groups=pairs)
    rows_of = [joined, to_expert(joined, PLANE)]
    weights = load((w_gate, w_up, w_down), (tokens,))
    line = to_z([tokens] * depth)
    *line, gate, up, down = lax.optimization_barrier((*line, *weights))
    weights = (gate, up, down)
    near = to_plane(pack(line, firsts))
    cut = near[0].shape[0] // 2
    one, two = near[1][:cut], near[2][cut:]
    far = [to_expert(one, 2), to_expert(two, 1)]
    near_mine, *near_theirs = experts((*near, *map(to_core, near)), weights, depth, len(near))
    theirs = list(map(to_core, near_theirs))
    near_mine, rows_of[1], *far = lax.optimization_barrier((near_mine, rows_of[1], *far))
    far_both = [*far, *map(to_core, far)]
    far_mine, *far_theirs = experts(far_both, weights, depth, 1)
    theirs += map(to_core, far_theirs)
    parts = to_plane(chip_sum((near_mine, far_mine), theirs))
    parts[0], pair_rows = lax.optimization_barrier((parts[0], pair_rows))
    other_half = 1 - lax.axis_index("expert").astype(jnp.int32) // far_line
    rows_of.append(lax.dynamic_index_in_dim(pair_rows, other_half, 0, keepdims=False))
    rows_of.append(to_expert(rows_of[2], PLANE))
    parts = to_z(plane_sum(parts, depth))
    scaled, following = second_norm(parts, (*near, *far), input_gain[None, :])
    products = to_plane(projection(scaled, to_core(scaled), following, rows_of))
    return head_norm(
        products,
        q_gain[None, :],
        k_gain[None, :],
        q_weight.shape[1],
        kv_weight.shape[1],
        rows,
        width,
        depth,
    )


def per_device(
    attn_out,
    out_weight,
    residual,
    attn_gain,
    expert_ids,
    route_weights,
    w_gate,
    w_up,
    w_down,
    input_gain,
    q_weight,
    kv_weight,
    q_gain,
    k_gain,
):
    n_expert = lax.axis_size("expert")
    n_tensor = lax.axis_size("tensor")
    share = n_tensor // 2
    tensor_index = lax.axis_index("tensor")
    group_rows = attn_out.shape[0]
    width = residual.shape[1]
    half = tensor_index // share
    capacity = 3 * group_rows * TOP // (4 * n_expert)
    all_experts = 2 * n_expert
    attn_rows = lax.psum_scatter(
        jnp.dot(attn_out, out_weight, preferred_element_type=jnp.float32),
        "tensor",
        scatter_dimension=0,
        tiled=True,
    )
    first_residual = (residual.astype(jnp.float32) + attn_rows).astype(jnp.bfloat16)
    normed = normalize(first_residual.astype(jnp.float32), attn_gain).astype(jnp.bfloat16)
    group_normed = lax.all_gather(normed, "tensor", axis=0, tiled=True)
    flat_ids = expert_ids.reshape(-1)
    onehot = (flat_ids[:, None] == jnp.arange(all_experts, dtype=jnp.int32)[None, :]).astype(
        jnp.int32
    )
    earlier = jnp.cumsum(onehot, axis=0) - onehot
    rank = jnp.sum(earlier * onehot, axis=1)
    dest = flat_ids * capacity + rank
    row_owner = jnp.arange(flat_ids.shape[0], dtype=jnp.int32) // TOP
    slot_row = jnp.full((all_experts * capacity,), group_rows, jnp.int32).at[dest].set(row_owner)
    slot_weight = (
        jnp.zeros((all_experts * capacity,), jnp.float32).at[dest].set(route_weights.reshape(-1))
    )
    own_slots = lax.dynamic_index_in_dim(
        slot_row.reshape(n_expert, 2, capacity), half, 1, keepdims=False
    )
    own_weights = lax.dynamic_index_in_dim(
        slot_weight.reshape(n_expert, 2, capacity), half, 1, keepdims=False
    )
    padded_rows = jnp.concatenate([group_normed, jnp.zeros((1, width), jnp.bfloat16)], axis=0)
    gate_w = w_gate[0]
    up_w = w_up[0]
    down_w = w_down[0]
    outgoing = jnp.take(padded_rows, own_slots, axis=0)
    arrived = lax.all_to_all(outgoing, "expert", split_axis=0, concat_axis=0, tiled=True)
    flat = arrived.reshape(-1, width)
    gate = jnp.dot(flat, gate_w, preferred_element_type=jnp.float32)
    up = jnp.dot(flat, up_w, preferred_element_type=jnp.float32)
    act = (jax.nn.silu(gate) * up).astype(jnp.bfloat16)
    part = jnp.dot(act, down_w, preferred_element_type=jnp.float32).astype(jnp.bfloat16)
    send_part = part.reshape(arrived.shape)
    returned = lax.all_to_all(send_part, "expert", split_axis=0, concat_axis=0, tiled=True)
    weighted = own_weights.reshape(-1)[:, None] * returned.reshape(-1, width).astype(jnp.float32)
    term = (
        jnp.zeros((group_rows + 1, width), jnp.float32)
        .at[own_slots.reshape(-1)]
        .add(weighted)[:group_rows]
    )
    expert_sum = lax.psum_scatter(
        term.astype(jnp.bfloat16), "tensor", scatter_dimension=0, tiled=True
    ).astype(jnp.float32)
    next_residual = (first_residual.astype(jnp.float32) + expert_sum).astype(jnp.bfloat16)
    own_normed = normalize(next_residual.astype(jnp.float32), input_gain).astype(jnp.bfloat16)
    next_normed = lax.all_gather(own_normed, "tensor", axis=0, tiled=True)
    query_cols = q_weight.shape[1]
    kv_cols = kv_weight.shape[1]
    query_raw = jnp.dot(
        next_normed,
        lax.all_gather(q_weight, "expert", axis=0, tiled=True),
        preferred_element_type=jnp.float32,
    )
    kv_raw = jnp.dot(
        next_normed,
        lax.all_gather(kv_weight, "expert", axis=0, tiled=True),
        preferred_element_type=jnp.float32,
    )
    head_size = q_gain.shape[0]
    queries = (
        normalize(query_raw.reshape(group_rows, -1, head_size), q_gain)
        .reshape(group_rows, query_cols)
        .astype(jnp.bfloat16)
    )
    heads_here = kv_cols // head_size
    head_number = tensor_index * heads_here + jnp.arange(heads_here, dtype=jnp.int32)
    is_key = head_number < KV_HEADS
    kv_shaped = kv_raw.reshape(group_rows, heads_here, head_size)
    keys_values = (
        jnp.where(is_key[None, :, None], normalize(kv_shaped, k_gain), kv_shaped)
        .reshape(group_rows, kv_cols)
        .astype(jnp.bfloat16)
    )
    return (next_residual, queries, keys_values)


def solution(mesh):
    small = mesh.shape["tensor"] == 2 and mesh.shape["expert"] == 4 * PLANE
    return jax.shard_map(
        per_device_dense if small else per_device,
        mesh=mesh,
        in_specs=(
            P("expert", "tensor"),
            P("tensor", None),
            P(("expert", "tensor"), None),
            P(),
            P("expert", None),
            P("expert", None),
            P("expert", None, "tensor"),
            P("expert", None, "tensor"),
            P("expert", "tensor", None),
            P(),
            P("expert", "tensor"),
            P("expert", "tensor"),
            P(),
            P(),
        ),
        out_specs=(P(("expert", "tensor"), None), P("expert", "tensor"), P("expert", "tensor")),
        check_vma=False,
    )
```

```python
import functools

import jax
import jax.numpy as jnp
from jax import lax
from jax.experimental import pallas as pl
from jax.experimental.pallas import tpu as pltpu
from jax.sharding import PartitionSpec as P

KV_HEADS = 4
TOP = 8
PLANE = 4
META = 128


EPSILON = 1e-06

SMALL = pl.CostEstimate(flops=0, bytes_accessed=0, transcendentals=0)
VMEM = pl.BlockSpec(memory_space=pltpu.VMEM)
HBM = pl.BlockSpec(memory_space=pltpu.HBM)


def normalize(values, gain):
    return values * lax.rsqrt(jnp.mean(values * values, axis=-1, keepdims=True) + EPSILON) * gain


def params(mebibytes):
    return pltpu.CompilerParams(vmem_limit_bytes=mebibytes << 20)


def lanes(start, size):
    return pl.ds(pl.multiple_of(start, size), size)


def in_hbm(value):
    return pltpu.with_memory_space_constraint(value, pltpu.HBM)


def in_vmem(value):
    return pltpu.with_memory_space_constraint(value, pltpu.VMEM)


def out_projection_kernel(chunk, a_hbm, w_hbm, mine_ref, theirs_ref, a_buf, w_buf, a_sem, sems):
    depth = w_buf.shape[0]
    count = depth // chunk
    half = mine_ref.shape[0]
    a_copy = pltpu.make_async_copy(a_hbm, a_buf, a_sem)
    a_copy.start()
    copies = []
    for i in range(count):
        rows = pl.ds(i * chunk, chunk)
        copies.append(pltpu.make_async_copy(w_hbm.at[rows], w_buf.at[rows], sems.at[i]))
    for copy in copies:
        copy.start()
    tensor = lax.axis_index("tensor")
    own = lanes(tensor * half, half)
    other = lanes((1 - tensor) * half, half)
    a_copy.wait()
    for i in range(count):
        copies[i].wait()
        at = pl.ds(i * chunk, chunk)
        both = jnp.concatenate([a_buf[own, at], a_buf[other, at]], axis=0)
        product = jnp.dot(both, w_buf[at, :], preferred_element_type=jnp.float32)
        if i == 0:
            mine_ref[...] = product[:half]
            theirs_ref[...] = product[half:]
        else:
            mine_ref[...] += product[:half]
            theirs_ref[...] += product[half:]


def out_projection(attn_out, out_weight):
    rows, depth = attn_out.shape
    width = out_weight.shape[1]
    chunk = 256
    half = pltpu.VMEM((rows // 2, width), jnp.float32)
    return pl.pallas_call(
        functools.partial(out_projection_kernel, chunk),
        out_shape=(half, half),
        in_specs=[HBM, HBM],
        out_specs=(VMEM, VMEM),
        scratch_shapes=[
            pltpu.VMEM((rows, depth), jnp.bfloat16),
            pltpu.VMEM((depth, width), jnp.bfloat16),
            pltpu.SemaphoreType.DMA,
            pltpu.SemaphoreType.DMA((depth // chunk,)),
        ],
        compiler_params=params(14),
        cost_estimate=SMALL,
        name="out_projection",
    )(in_hbm(attn_out), in_hbm(out_weight))


def first_norm_kernel(mine_ref, theirs_ref, residual_ref, gain_ref, meta_ref, tokens_ref, first_ref):
    width = residual_ref.shape[1]
    first = (residual_ref[...].astype(jnp.float32) + (mine_ref[...] + theirs_ref[...])).astype(
        jnp.bfloat16
    )
    first_ref[...] = first
    tokens_ref[:, :width] = normalize(first.astype(jnp.float32), gain_ref[...]).astype(jnp.bfloat16)
    tokens_ref[:, width:] = meta_ref[...]


def first_norm(mine, theirs, residual, gain, meta):
    rows, width = residual.shape
    return pl.pallas_call(
        first_norm_kernel,
        out_shape=(
            pltpu.VMEM((rows, width + META), jnp.bfloat16),
            pltpu.VMEM((rows, width), jnp.bfloat16),
        ),
        in_specs=[VMEM] * 5,
        out_specs=(VMEM, VMEM),
        compiler_params=params(2),
        name="first_norm",
    )(mine, theirs, residual, gain, meta)


def pack_kernel(depth, *refs):
    line, out_ref = refs[:depth], refs[depth]
    rows = line[0].shape[0]
    for z in range(depth):
        out_ref[z * rows : (z + 1) * rows, :] = line[z][...]


def pack(line):
    depth = len(line)
    rows, extended = line[0].shape
    return pl.pallas_call(
        functools.partial(pack_kernel, depth),
        out_shape=pltpu.VMEM((depth * rows, extended), jnp.bfloat16),
        in_specs=[VMEM] * depth,
        out_specs=VMEM,
        compiler_params=params(2),
        name="pack_tokens",
    )(*line)


def load_kernel(count, *refs):
    sources, targets, sems = refs[:count], refs[-count - 1 : -1], refs[-1]
    copies = [
        pltpu.make_async_copy(source, target, sems.at[i])
        for i, (source, target) in enumerate(zip(sources, targets))
    ]
    for copy in copies:
        copy.start()
    for copy in copies:
        copy.wait()


def load(weights, after):
    count = len(weights)
    return pl.pallas_call(
        functools.partial(load_kernel, count),
        out_shape=tuple(pltpu.VMEM(w.shape, w.dtype) for w in weights),
        in_specs=[HBM] * count + [pl.BlockSpec(memory_space=pl.ANY)] * len(after),
        out_specs=(VMEM,) * count,
        scratch_shapes=[pltpu.SemaphoreType.DMA((count,))],
        compiler_params=params(2),
        cost_estimate=SMALL,
        name="load_weights",
    )(*map(in_hbm, weights), *after)


def expert_kernel(depth, chunk, count, *refs):
    block_refs, (gate_ref, up_ref, down_ref) = refs[:count], refs[count : count + 3]
    mine_ref, *theirs_refs, x_buf, act_buf = refs[count + 3 :]
    width, hidden = gate_ref.shape[1:]
    extended = x_buf.shape[1]
    start = 0
    for ref in block_refs:
        rows = ref.shape[0]
        x_buf[start : start + rows, :] = ref[:, :extended]
        start += rows
    meta = x_buf[:, width:].astype(jnp.float32)
    lane = lax.broadcasted_iota(jnp.int32, meta.shape, 1)
    chip = lax.axis_index("expert")
    expert = 2 * chip + lax.axis_index("tensor")
    chosen = (lane == expert) | (lane == expert + META // 2)
    route = 0.5 * jnp.sum(jnp.where(chosen, meta, 0.0), axis=1, keepdims=True)
    for i in range(hidden // chunk):
        cols = pl.ds(i * chunk, chunk)
        x = x_buf[:, :width]
        gate = jnp.dot(x, gate_ref[0, :, cols], preferred_element_type=jnp.float32)
        up = jnp.dot(x, up_ref[0, :, cols], preferred_element_type=jnp.float32)
        act = gate * (1.0 + jnp.tanh(0.5 * gate)) * (up * route)
        act_buf[:, i * chunk : (i + 1) * chunk] = act.astype(jnp.bfloat16)
    sub = width // (PLANE * depth)
    part = sub * depth
    half = mine_ref.shape[0]
    plane = chip % PLANE
    for d in range(PLANE):
        weight = jnp.concatenate(
            [down_ref[0, :, lanes((z * PLANE + (plane ^ d)) * sub, sub)] for z in range(depth)],
            axis=1,
        )
        out = jnp.dot(act_buf[...], weight, preferred_element_type=jnp.float32)
        cols = slice(d * part, (d + 1) * part)
        mine_ref[:, cols] = out[:half].astype(jnp.bfloat16)
        start = half
        for ref in theirs_refs:
            stop = start + ref.shape[0]
            ref[:, cols] = out[start:stop].astype(jnp.bfloat16)
            start = stop


def experts(blocks, weights, depth, pieces):
    width, hidden = weights[0].shape[1:]
    chunk = 256
    extended = width + META
    total = sum(block.shape[0] for block in blocks)
    rows = [total // 2] + [total // 2 // pieces] * pieces
    return pl.pallas_call(
        functools.partial(expert_kernel, depth, chunk, len(blocks)),
        out_shape=tuple(pltpu.VMEM((size, width), jnp.bfloat16) for size in rows),
        in_specs=[VMEM] * (len(blocks) + 3),
        out_specs=(VMEM,) * (1 + pieces),
        scratch_shapes=[
            pltpu.VMEM((total, extended), jnp.bfloat16),
            pltpu.VMEM((total, hidden), jnp.bfloat16),
        ],
        compiler_params=params(16),
        cost_estimate=pl.CostEstimate(
            flops=6 * total * width * hidden, bytes_accessed=0, transcendentals=0
        ),
        name="experts",
    )(*blocks, *weights)


def chip_sum_kernel(depth, count, first_ref, *refs):
    mine, theirs, out_refs = refs[:2], refs[2 : 2 + count], refs[2 + count :]
    part = out_refs[0].shape[1]
    sub = part // depth
    held = first_ref.shape[0]
    plane = lax.axis_index("expert") % PLANE
    start = 0
    for own_ref in mine:
        first = start
        while start < first + own_ref.shape[0]:
            ref, theirs = theirs[0], theirs[1:]
            size = ref.shape[0]
            own = slice(start - first, start - first + size)
            for d, out_ref in enumerate(out_refs):
                at = slice(d * part, (d + 1) * part)
                total = own_ref[own, at].astype(jnp.float32) + ref[:, at].astype(jnp.float32)
                if start == 0:
                    residual = jnp.concatenate(
                        [
                            first_ref[:, lanes((z * PLANE + (plane ^ d)) * sub, sub)]
                            for z in range(depth)
                        ],
                        axis=1,
                    )
                    with_first = total[:held] + residual.astype(jnp.float32)
                    total = jnp.concatenate([with_first, total[held:]], axis=0)
                out_ref[start : start + size, :] = total.astype(jnp.bfloat16)
            start += size


def chip_sum(mine, theirs, first, depth):
    rows, width = sum(value.shape[0] for value in mine), mine[0].shape[1]
    return pl.pallas_call(
        functools.partial(chip_sum_kernel, depth, len(theirs)),
        out_shape=(pltpu.VMEM((rows, width // PLANE), jnp.bfloat16),) * PLANE,
        in_specs=[VMEM] * (3 + len(theirs)),
        out_specs=(VMEM,) * PLANE,
        compiler_params=params(4),
        name="chip_sum",
    )(first, *mine, *theirs)


def plane_sum_kernel(depth, *refs):
    in_refs, out_refs = refs[:PLANE], refs[PLANE:]
    group = in_refs[0].shape[0] // PLANE
    rows = group // depth
    for k in range(PLANE):
        for z in range(depth):
            total = 0.0
            for d in range(PLANE):
                start = (k ^ d) * group + z * rows
                total = total + in_refs[d][start : start + rows, :].astype(jnp.float32)
            out_refs[z][k * rows : (k + 1) * rows, :] = total.astype(jnp.bfloat16)


def plane_sum(parts, depth):
    rows, part = parts[0].shape
    return pl.pallas_call(
        functools.partial(plane_sum_kernel, depth),
        out_shape=(pltpu.VMEM((rows // depth, part), jnp.bfloat16),) * depth,
        in_specs=[VMEM] * PLANE,
        out_specs=(VMEM,) * depth,
        compiler_params=params(4),
        name="plane_sum",
    )(*parts)


def second_norm_kernel(depth, *refs):
    parts, (gain_ref, scaled_ref, next_ref) = refs[:depth], refs[depth:]
    rows, part = next_ref.shape
    sub = part // depth
    plane = lax.axis_index("expert") % PLANE
    gain = jnp.concatenate(
        [gain_ref[:, lanes((z * PLANE + plane) * sub, sub)] for z in range(depth)], axis=1
    )
    total = parts[0][...].astype(jnp.float32)
    for ref in parts[1:]:
        total = total + ref[...].astype(jnp.float32)
    following = total.astype(jnp.bfloat16)
    next_ref[...] = following
    wide = following.astype(jnp.float32)
    scaled_ref[:, :part] = (wide * gain).astype(jnp.bfloat16)
    squares = jnp.sum(wide * wide, axis=1, keepdims=True)
    high = squares.astype(jnp.bfloat16).astype(jnp.float32)
    lane = lax.broadcasted_iota(jnp.int32, (rows, META), 1)
    scaled_ref[:, part:] = jnp.where(
        lane == 0, high, jnp.where(lane == 1, squares - high, 0.0)
    ).astype(jnp.bfloat16)


def second_norm(parts, gain):
    depth = len(parts)
    rows, part = parts[0].shape
    return pl.pallas_call(
        functools.partial(second_norm_kernel, depth),
        out_shape=(
            pltpu.VMEM((rows, part + META), jnp.bfloat16),
            pltpu.VMEM((rows, part), jnp.bfloat16),
        ),
        in_specs=[VMEM] * (depth + 1),
        out_specs=(VMEM, VMEM),
        compiler_params=params(4),
        name="second_norm",
    )(*parts, gain)


def projection_kernel(chunk, mine_ref, theirs_ref, next_ref, q_ref, *refs):
    kv_refs, out_refs, kv_buf = refs[: -PLANE - 1], refs[-PLANE - 1 : -1], refs[-1]
    depth = len(kv_refs)
    rows, extended = mine_ref.shape
    part = extended - META
    sub = part // depth
    q_cols, kv_cols = q_ref.shape[1], kv_buf.shape[1]
    cols = q_cols + kv_cols
    line = lax.axis_index("expert") // PLANE
    for d, ref in enumerate(kv_refs):
        kv_buf[lanes((line ^ d) * sub, sub), :] = ref[...]
    block = rows // PLANE
    tensor = lax.axis_index("tensor")
    own = lanes(tensor * block, block)
    other = lanes((1 - tensor) * block, block)
    for d in range(PLANE):
        at = slice(d * block, (d + 1) * block)
        out_refs[d][own, cols : cols + META] = mine_ref[at, part:]
        out_refs[d][other, cols : cols + META] = theirs_ref[at, part:]
        out_refs[d][:block, cols + META :] = next_ref[at, : part // 2]
        out_refs[d][block:, cols + META :] = next_ref[at, part // 2 :]
    both = jnp.concatenate([mine_ref[:, :part], theirs_ref[:, :part]], axis=0)

    def multiply(weight, target):
        product = jnp.dot(both, weight, preferred_element_type=jnp.float32).astype(jnp.bfloat16)
        at = slice(target, target + weight.shape[1])
        for d in range(PLANE):
            out_refs[d][own, at] = product[d * block : (d + 1) * block]
            out_refs[d][other, at] = product[rows + d * block : rows + (d + 1) * block]

    multiply(kv_buf[...], q_cols)
    for start in range(0, q_cols, chunk):
        multiply(q_ref[:, start : start + chunk], start)


def projection(mine, theirs, following, q_weight, kv_weights):
    rows, part = following.shape
    q_cols, kv_cols = q_weight.shape[1], kv_weights[0].shape[1]
    chunk = 512
    shape = pltpu.VMEM((2 * rows // PLANE, q_cols + kv_cols + META + part // 2), jnp.bfloat16)
    return pl.pallas_call(
        functools.partial(projection_kernel, chunk),
        out_shape=(shape,) * PLANE,
        in_specs=[VMEM] * (4 + len(kv_weights)),
        out_specs=(VMEM,) * PLANE,
        scratch_shapes=[pltpu.VMEM((part, kv_cols), jnp.bfloat16)],
        compiler_params=params(8),
        cost_estimate=SMALL,
        name="qkv_projection",
    )(mine, theirs, following, q_weight, *kv_weights)


def head_norm_kernel(depth, *refs):
    parts, q_gain_ref, k_gain_ref = refs[:PLANE], refs[PLANE], refs[PLANE + 1]
    next_ref, q_ref, kv_ref = refs[PLANE + 2 :]
    width = next_ref.shape[1]
    q_cols, kv_cols = q_ref.shape[1], kv_ref.shape[1]
    cols = q_cols + kv_cols
    head = q_gain_ref.shape[1]

    def total(at):
        value = parts[0][:, at].astype(jnp.float32)
        for ref in parts[1:]:
            value = value + ref[:, at].astype(jnp.float32)
        return value

    squares = jnp.sum(total(slice(cols, cols + META)), axis=1, keepdims=True)
    scale = lax.rsqrt(squares / width + EPSILON)
    for h in range(q_cols // head):
        at = slice(h * head, (h + 1) * head)
        q_ref[:, at] = normalize(total(at) * scale, q_gain_ref[...]).astype(jnp.bfloat16)
    tensor = lax.axis_index("tensor")
    for h in range(kv_cols // head):
        at = slice(h * head, (h + 1) * head)
        raw = total(slice(q_cols + h * head, q_cols + (h + 1) * head)) * scale
        is_key = tensor * (kv_cols // head) + h < KV_HEADS
        kv_ref[:, at] = jnp.where(is_key, normalize(raw, k_gain_ref[...]), raw).astype(
            jnp.bfloat16
        )
    plane = lax.axis_index("expert") % PLANE
    rows = next_ref.shape[0]
    sub = width // (PLANE * depth)
    for d in range(PLANE):
        for z in range(depth):
            top = z * sub * 2 // (depth * sub)
            start = cols + META + z * sub - top * (depth * sub // 2)
            next_ref[:, lanes((z * PLANE + (plane ^ d)) * sub, sub)] = parts[d][
                top * rows : (top + 1) * rows, start : start + sub
            ]


def head_norm(parts, q_gain, k_gain, q_cols, kv_cols, rows, width, depth):
    both = parts[0].shape[0]
    return pl.pallas_call(
        functools.partial(head_norm_kernel, depth),
        out_shape=(
            jax.ShapeDtypeStruct((rows, width), jnp.bfloat16),
            jax.ShapeDtypeStruct((both, q_cols), jnp.bfloat16),
            jax.ShapeDtypeStruct((both, kv_cols), jnp.bfloat16),
        ),
        in_specs=[VMEM] * (PLANE + 2),
        out_specs=(VMEM, VMEM, VMEM),
        compiler_params=params(4),
        name="head_norm",
    )(*parts, q_gain, k_gain)


def per_device_dense(
    attn_out,
    out_weight,
    residual,
    attn_gain,
    expert_ids,
    route_weights,
    w_gate,
    w_up,
    w_down,
    input_gain,
    q_weight,
    kv_weight,
    q_gain,
    k_gain,
):
    n_expert = lax.axis_size("expert")
    depth = n_expert // PLANE
    rows, width = residual.shape
    tensor_index = lax.axis_index("tensor").astype(jnp.int32)

    def to_core(value):
        return lax.ppermute(value, "tensor", [(0, 1), (1, 0)])

    def to_expert(value, offset):
        return lax.ppermute(value, "expert", [(i, i ^ offset) for i in range(n_expert)])

    def to_z(values):
        return [to_expert(v, d * PLANE) if d else v for d, v in enumerate(values)]

    def to_plane(values):
        return [to_expert(v, d) if d else v for d, v in enumerate(values)]

    own_ids = lax.dynamic_slice_in_dim(expert_ids, tensor_index * rows, rows, 0)
    own_route = lax.dynamic_slice_in_dim(route_weights, tensor_index * rows, rows, 0)
    chosen = own_ids[:, :, None] == jnp.arange(META // 2, dtype=jnp.int32)[None, None, :]
    dense = jnp.sum(jnp.where(chosen, own_route[:, :, None], 0.0), axis=1)
    high = lax.reduce_precision(dense, 8, 7)
    meta = jnp.concatenate([high, dense - high], axis=1).astype(jnp.bfloat16)

    lines = [list(range(i, n_expert, PLANE)) for i in range(PLANE)]
    mine, theirs = out_projection(attn_out, out_weight)
    tokens, first = first_norm(mine, to_core(theirs), residual, attn_gain[None, :], meta)
    tokens, q_own = lax.optimization_barrier((tokens, q_weight))
    q_rows = lax.all_gather(q_own, "expert", axis=0, tiled=True, axis_index_groups=lines)
    weights = load((w_gate, w_up, w_down), (tokens,))
    line = to_z([tokens] * depth)
    *line, gate, up, down = lax.optimization_barrier((*line, *weights))
    weights = (gate, up, down)
    near = to_plane([pack(line)] * (PLANE - 1))
    cut = near[0].shape[0] // 2
    one, two = near[1][:cut], near[2][cut:]
    far = [to_expert(one, 2), to_expert(two, 1)]
    near_mine, *near_theirs = experts((*near, *map(to_core, near)), weights, depth, len(near))
    theirs = list(map(to_core, near_theirs))
    near_mine, *far = lax.optimization_barrier((near_mine, *far))
    far_both = [*far, *map(to_core, far)]
    far_mine, *far_theirs = experts(far_both, weights, depth, 1)
    theirs += map(to_core, far_theirs)
    *sums, kv_own = lax.optimization_barrier((*chip_sum((near_mine, far_mine), theirs, first, depth), kv_weight))
    parts = to_plane(sums)
    kv_rows = [kv_own, to_expert(kv_own, PLANE), to_expert(kv_own, 2 * PLANE)]
    *parts, kv_rows[1], kv_rows[2] = lax.optimization_barrier(
        (*plane_sum(parts, depth), *kv_rows[1:])
    )
    kv_rows.append(to_expert(kv_rows[2], PLANE))
    (q_rows,) = load((q_rows,), parts)
    parts = to_z(parts)
    *parts, q_rows = lax.optimization_barrier((*parts, q_rows))
    scaled, following = second_norm(parts, input_gain[None, :])
    products = to_plane(projection(scaled, to_core(scaled), following, q_rows, kv_rows))
    return head_norm(
        products,
        q_gain[None, :],
        k_gain[None, :],
        q_weight.shape[1],
        kv_weight.shape[1],
        rows,
        width,
        depth,
    )


def per_device(
    attn_out,
    out_weight,
    residual,
    attn_gain,
    expert_ids,
    route_weights,
    w_gate,
    w_up,
    w_down,
    input_gain,
    q_weight,
    kv_weight,
    q_gain,
    k_gain,
):
    n_expert = lax.axis_size("expert")
    n_tensor = lax.axis_size("tensor")
    share = n_tensor // 2
    tensor_index = lax.axis_index("tensor")
    group_rows = attn_out.shape[0]
    width = residual.shape[1]
    half = tensor_index // share
    capacity = 3 * group_rows * TOP // (4 * n_expert)
    all_experts = 2 * n_expert
    attn_rows = lax.psum_scatter(
        jnp.dot(attn_out, out_weight, preferred_element_type=jnp.float32),
        "tensor",
        scatter_dimension=0,
        tiled=True,
    )
    first_residual = (residual.astype(jnp.float32) + attn_rows).astype(jnp.bfloat16)
    normed = normalize(first_residual.astype(jnp.float32), attn_gain).astype(jnp.bfloat16)
    group_normed = lax.all_gather(normed, "tensor", axis=0, tiled=True)
    flat_ids = expert_ids.reshape(-1)
    onehot = (flat_ids[:, None] == jnp.arange(all_experts, dtype=jnp.int32)[None, :]).astype(
        jnp.int32
    )
    earlier = jnp.cumsum(onehot, axis=0) - onehot
    rank = jnp.sum(earlier * onehot, axis=1)
    dest = flat_ids * capacity + rank
    row_owner = jnp.arange(flat_ids.shape[0], dtype=jnp.int32) // TOP
    slot_row = jnp.full((all_experts * capacity,), group_rows, jnp.int32).at[dest].set(row_owner)
    slot_weight = (
        jnp.zeros((all_experts * capacity,), jnp.float32).at[dest].set(route_weights.reshape(-1))
    )
    own_slots = lax.dynamic_index_in_dim(
        slot_row.reshape(n_expert, 2, capacity), half, 1, keepdims=False
    )
    own_weights = lax.dynamic_index_in_dim(
        slot_weight.reshape(n_expert, 2, capacity), half, 1, keepdims=False
    )
    padded_rows = jnp.concatenate([group_normed, jnp.zeros((1, width), jnp.bfloat16)], axis=0)
    gate_w = w_gate[0]
    up_w = w_up[0]
    down_w = w_down[0]
    outgoing = jnp.take(padded_rows, own_slots, axis=0)
    arrived = lax.all_to_all(outgoing, "expert", split_axis=0, concat_axis=0, tiled=True)
    flat = arrived.reshape(-1, width)
    gate = jnp.dot(flat, gate_w, preferred_element_type=jnp.float32)
    up = jnp.dot(flat, up_w, preferred_element_type=jnp.float32)
    act = (jax.nn.silu(gate) * up).astype(jnp.bfloat16)
    part = jnp.dot(act, down_w, preferred_element_type=jnp.float32).astype(jnp.bfloat16)
    send_part = part.reshape(arrived.shape)
    returned = lax.all_to_all(send_part, "expert", split_axis=0, concat_axis=0, tiled=True)
    weighted = own_weights.reshape(-1)[:, None] * returned.reshape(-1, width).astype(jnp.float32)
    term = (
        jnp.zeros((group_rows + 1, width), jnp.float32)
        .at[own_slots.reshape(-1)]
        .add(weighted)[:group_rows]
    )
    expert_sum = lax.psum_scatter(
        term.astype(jnp.bfloat16), "tensor", scatter_dimension=0, tiled=True
    ).astype(jnp.float32)
    next_residual = (first_residual.astype(jnp.float32) + expert_sum).astype(jnp.bfloat16)
    own_normed = normalize(next_residual.astype(jnp.float32), input_gain).astype(jnp.bfloat16)
    next_normed = lax.all_gather(own_normed, "tensor", axis=0, tiled=True)
    query_cols = q_weight.shape[1]
    kv_cols = kv_weight.shape[1]
    query_raw = jnp.dot(
        next_normed,
        lax.all_gather(q_weight, "expert", axis=0, tiled=True),
        preferred_element_type=jnp.float32,
    )
    kv_raw = jnp.dot(
        next_normed,
        lax.all_gather(kv_weight, "expert", axis=0, tiled=True),
        preferred_element_type=jnp.float32,
    )
    head_size = q_gain.shape[0]
    queries = (
        normalize(query_raw.reshape(group_rows, -1, head_size), q_gain)
        .reshape(group_rows, query_cols)
        .astype(jnp.bfloat16)
    )
    heads_here = kv_cols // head_size
    head_number = tensor_index * heads_here + jnp.arange(heads_here, dtype=jnp.int32)
    is_key = head_number < KV_HEADS
    kv_shaped = kv_raw.reshape(group_rows, heads_here, head_size)
    keys_values = (
        jnp.where(is_key[None, :, None], normalize(kv_shaped, k_gain), kv_shaped)
        .reshape(group_rows, kv_cols)
        .astype(jnp.bfloat16)
    )
    return (next_residual, queries, keys_values)


def solution(mesh):
    small = mesh.shape["tensor"] == 2 and mesh.shape["expert"] == 4 * PLANE
    return jax.shard_map(
        per_device_dense if small else per_device,
        mesh=mesh,
        in_specs=(
            P("expert", "tensor"),
            P("tensor", None),
            P(("expert", "tensor"), None),
            P(),
            P("expert", None),
            P("expert", None),
            P("expert", None, "tensor"),
            P("expert", None, "tensor"),
            P("expert", "tensor", None),
            P(),
            P("expert", "tensor"),
            P("expert", "tensor"),
            P(),
            P(),
        ),
        out_specs=(P(("expert", "tensor"), None), P("expert", "tensor"), P("expert", "tensor")),
        check_vma=False,
    )
```

```python
import functools

import jax
import jax.numpy as jnp
from jax import lax
from jax.experimental import pallas as pl
from jax.experimental.pallas import tpu as pltpu
from jax.sharding import PartitionSpec as P

KV_HEADS = 4
TOP = 8
PLANE = 4
META = 128


EPSILON = 1e-06

SMALL = pl.CostEstimate(flops=0, bytes_accessed=0, transcendentals=0)
VMEM = pl.BlockSpec(memory_space=pltpu.VMEM)
HBM = pl.BlockSpec(memory_space=pltpu.HBM)


def normalize(values, gain):
    return values * lax.rsqrt(jnp.mean(values * values, axis=-1, keepdims=True) + EPSILON) * gain


def params(mebibytes):
    return pltpu.CompilerParams(vmem_limit_bytes=mebibytes << 20)


def far_first(values):
    return [values[0], *reversed(values[1:])]


def lanes(start, size):
    return pl.ds(pl.multiple_of(start, size), size)


def in_hbm(value):
    return pltpu.with_memory_space_constraint(value, pltpu.HBM)


def in_vmem(value):
    return pltpu.with_memory_space_constraint(value, pltpu.VMEM)


def out_projection_kernel(chunk, a_hbm, w_hbm, mine_ref, theirs_ref, a_buf, w_buf, a_sem, sems):
    depth = w_buf.shape[0]
    count = depth // chunk
    half = mine_ref.shape[0]
    a_copy = pltpu.make_async_copy(a_hbm, a_buf, a_sem)
    a_copy.start()
    copies = []
    for i in range(count):
        rows = pl.ds(i * chunk, chunk)
        copies.append(pltpu.make_async_copy(w_hbm.at[rows], w_buf.at[rows], sems.at[i]))
    for copy in copies:
        copy.start()
    tensor = lax.axis_index("tensor")
    own = lanes(tensor * half, half)
    other = lanes((1 - tensor) * half, half)
    a_copy.wait()
    for i in range(count):
        copies[i].wait()
        at = pl.ds(i * chunk, chunk)
        both = jnp.concatenate([a_buf[own, at], a_buf[other, at]], axis=0)
        product = jnp.dot(both, w_buf[at, :], preferred_element_type=jnp.float32)
        if i == 0:
            mine_ref[...] = product[:half]
            theirs_ref[...] = product[half:]
        else:
            mine_ref[...] += product[:half]
            theirs_ref[...] += product[half:]


def out_projection(attn_out, out_weight):
    rows, depth = attn_out.shape
    width = out_weight.shape[1]
    chunk = 256
    half = pltpu.VMEM((rows // 2, width), jnp.float32)
    return pl.pallas_call(
        functools.partial(out_projection_kernel, chunk),
        out_shape=(half, half),
        in_specs=[HBM, HBM],
        out_specs=(VMEM, VMEM),
        scratch_shapes=[
            pltpu.VMEM((rows, depth), jnp.bfloat16),
            pltpu.VMEM((depth, width), jnp.bfloat16),
            pltpu.SemaphoreType.DMA,
            pltpu.SemaphoreType.DMA((depth // chunk,)),
        ],
        compiler_params=params(14),
        cost_estimate=SMALL,
        name="out_projection",
    )(in_hbm(attn_out), in_hbm(out_weight))


def first_norm_kernel(mine_ref, theirs_ref, residual_ref, gain_ref, meta_ref, tokens_ref, first_ref):
    width = residual_ref.shape[1]
    first = (residual_ref[...].astype(jnp.float32) + (mine_ref[...] + theirs_ref[...])).astype(
        jnp.bfloat16
    )
    first_ref[...] = first
    tokens_ref[:, :width] = normalize(first.astype(jnp.float32), gain_ref[...]).astype(jnp.bfloat16)
    tokens_ref[:, width:] = meta_ref[...]


def first_norm(mine, theirs, residual, gain, meta):
    rows, width = residual.shape
    return pl.pallas_call(
        first_norm_kernel,
        out_shape=(
            pltpu.VMEM((rows, width + META), jnp.bfloat16),
            pltpu.VMEM((rows, width), jnp.bfloat16),
        ),
        in_specs=[VMEM] * 5,
        out_specs=(VMEM, VMEM),
        compiler_params=params(2),
        name="first_norm",
    )(mine, theirs, residual, gain, meta)


def pack_kernel(depth, *refs):
    line, out_ref = far_first(refs[:depth]), refs[depth]
    rows = line[0].shape[0]
    for z in range(depth):
        out_ref[z * rows : (z + 1) * rows, :] = line[z][...]


def pack(line):
    depth = len(line)
    rows, extended = line[0].shape
    return pl.pallas_call(
        functools.partial(pack_kernel, depth),
        out_shape=pltpu.VMEM((depth * rows, extended), jnp.bfloat16),
        in_specs=[VMEM] * depth,
        out_specs=VMEM,
        compiler_params=params(2),
        name="pack_tokens",
    )(*far_first(line))


def load_kernel(count, *refs):
    sources, targets, sems = refs[:count], refs[-count - 1 : -1], refs[-1]
    copies = [
        pltpu.make_async_copy(source, target, sems.at[i])
        for i, (source, target) in enumerate(zip(sources, targets))
    ]
    for copy in copies:
        copy.start()
    for copy in copies:
        copy.wait()


def load(weights, after):
    count = len(weights)
    return pl.pallas_call(
        functools.partial(load_kernel, count),
        out_shape=tuple(pltpu.VMEM(w.shape, w.dtype) for w in weights),
        in_specs=[HBM] * count + [pl.BlockSpec(memory_space=pl.ANY)] * len(after),
        out_specs=(VMEM,) * count,
        scratch_shapes=[pltpu.SemaphoreType.DMA((count,))],
        compiler_params=params(2),
        cost_estimate=SMALL,
        name="load_weights",
    )(*map(in_hbm, weights), *after)


def expert_kernel(depth, chunk, count, *refs):
    block_refs, (gate_ref, up_ref, down_ref) = refs[:count], refs[count : count + 3]
    mine_ref, *theirs_refs, x_buf, act_buf = refs[count + 3 :]
    width, hidden = gate_ref.shape[1:]
    extended = x_buf.shape[1]
    start = 0
    for ref in block_refs:
        rows = ref.shape[0]
        x_buf[start : start + rows, :] = ref[:, :extended]
        start += rows
    meta = x_buf[:, width:].astype(jnp.float32)
    lane = lax.broadcasted_iota(jnp.int32, meta.shape, 1)
    chip = lax.axis_index("expert")
    expert = 2 * chip + lax.axis_index("tensor")
    chosen = (lane == expert) | (lane == expert + META // 2)
    route = 0.5 * jnp.sum(jnp.where(chosen, meta, 0.0), axis=1, keepdims=True)
    for i in range(hidden // chunk):
        cols = pl.ds(i * chunk, chunk)
        x = x_buf[:, :width]
        gate = jnp.dot(x, gate_ref[0, :, cols], preferred_element_type=jnp.float32)
        up = jnp.dot(x, up_ref[0, :, cols], preferred_element_type=jnp.float32)
        act = gate * (1.0 + jnp.tanh(0.5 * gate)) * (up * route)
        act_buf[:, i * chunk : (i + 1) * chunk] = act.astype(jnp.bfloat16)
    sub = width // (PLANE * depth)
    part = sub * depth
    half = mine_ref.shape[0]
    plane = chip % PLANE
    for d in range(PLANE):
        weight = jnp.concatenate(
            [down_ref[0, :, lanes((z * PLANE + (plane ^ d)) * sub, sub)] for z in range(depth)],
            axis=1,
        )
        out = jnp.dot(act_buf[...], weight, preferred_element_type=jnp.float32)
        cols = slice(d * part, (d + 1) * part)
        mine_ref[:, cols] = out[:half].astype(jnp.bfloat16)
        start = half
        for ref in theirs_refs:
            stop = start + ref.shape[0]
            ref[:, cols] = out[start:stop].astype(jnp.bfloat16)
            start = stop


def experts(blocks, weights, depth, pieces):
    width, hidden = weights[0].shape[1:]
    chunk = 256
    extended = width + META
    total = sum(block.shape[0] for block in blocks)
    rows = [total // 2] + [total // 2 // pieces] * pieces
    return pl.pallas_call(
        functools.partial(expert_kernel, depth, chunk, len(blocks)),
        out_shape=tuple(pltpu.VMEM((size, width), jnp.bfloat16) for size in rows),
        in_specs=[VMEM] * (len(blocks) + 3),
        out_specs=(VMEM,) * (1 + pieces),
        scratch_shapes=[
            pltpu.VMEM((total, extended), jnp.bfloat16),
            pltpu.VMEM((total, hidden), jnp.bfloat16),
        ],
        compiler_params=params(16),
        cost_estimate=pl.CostEstimate(
            flops=6 * total * width * hidden, bytes_accessed=0, transcendentals=0
        ),
        name="experts",
    )(*blocks, *weights)


def chip_sum_kernel(depth, count, first_ref, *refs):
    mine, theirs, out_refs = refs[:2], refs[2 : 2 + count], refs[2 + count :]
    part = out_refs[0].shape[1]
    sub = part // depth
    held = first_ref.shape[0]
    plane = lax.axis_index("expert") % PLANE
    start = 0
    for own_ref in mine:
        first = start
        while start < first + own_ref.shape[0]:
            ref, theirs = theirs[0], theirs[1:]
            size = ref.shape[0]
            own = slice(start - first, start - first + size)
            for d, out_ref in enumerate(out_refs):
                at = slice(d * part, (d + 1) * part)
                total = own_ref[own, at].astype(jnp.float32) + ref[:, at].astype(jnp.float32)
                if start == 0:
                    residual = jnp.concatenate(
                        [
                            first_ref[:, lanes((z * PLANE + (plane ^ d)) * sub, sub)]
                            for z in range(depth)
                        ],
                        axis=1,
                    )
                    with_first = total[:held] + residual.astype(jnp.float32)
                    total = jnp.concatenate([with_first, total[held:]], axis=0)
                out_ref[start : start + size, :] = total.astype(jnp.bfloat16)
            start += size


def chip_sum(mine, theirs, first, depth):
    rows, width = sum(value.shape[0] for value in mine), mine[0].shape[1]
    return pl.pallas_call(
        functools.partial(chip_sum_kernel, depth, len(theirs)),
        out_shape=(pltpu.VMEM((rows, width // PLANE), jnp.bfloat16),) * PLANE,
        in_specs=[VMEM] * (3 + len(theirs)),
        out_specs=(VMEM,) * PLANE,
        compiler_params=params(4),
        name="chip_sum",
    )(first, *mine, *theirs)


def plane_sum_kernel(depth, *refs):
    in_refs, out_refs = far_first(refs[:PLANE]), refs[PLANE:]
    group = in_refs[0].shape[0] // PLANE
    rows = group // depth
    for k in range(PLANE):
        for z in range(depth):
            total = 0.0
            for d in range(PLANE):
                start = (k ^ d) * group + z * rows
                total = total + in_refs[d][start : start + rows, :].astype(jnp.float32)
            out_refs[z][k * rows : (k + 1) * rows, :] = total.astype(jnp.bfloat16)


def plane_sum(parts, depth):
    rows, part = parts[0].shape
    return pl.pallas_call(
        functools.partial(plane_sum_kernel, depth),
        out_shape=(pltpu.VMEM((rows // depth, part), jnp.bfloat16),) * depth,
        in_specs=[VMEM] * PLANE,
        out_specs=(VMEM,) * depth,
        compiler_params=params(4),
        name="plane_sum",
    )(*far_first(parts))


def second_norm_kernel(depth, *refs):
    parts, (gain_ref, scaled_ref, next_ref) = refs[:depth], refs[depth:]
    rows, part = next_ref.shape
    sub = part // depth
    plane = lax.axis_index("expert") % PLANE
    gain = jnp.concatenate(
        [gain_ref[:, lanes((z * PLANE + plane) * sub, sub)] for z in range(depth)], axis=1
    )
    total = parts[0][...].astype(jnp.float32)
    for ref in parts[1:]:
        total = total + ref[...].astype(jnp.float32)
    following = total.astype(jnp.bfloat16)
    next_ref[...] = following
    wide = following.astype(jnp.float32)
    scaled_ref[:, :part] = (wide * gain).astype(jnp.bfloat16)
    squares = jnp.sum(wide * wide, axis=1, keepdims=True)
    high = squares.astype(jnp.bfloat16).astype(jnp.float32)
    lane = lax.broadcasted_iota(jnp.int32, (rows, META), 1)
    scaled_ref[:, part:] = jnp.where(
        lane == 0, high, jnp.where(lane == 1, squares - high, 0.0)
    ).astype(jnp.bfloat16)


def second_norm(parts, gain):
    depth = len(parts)
    rows, part = parts[0].shape
    return pl.pallas_call(
        functools.partial(second_norm_kernel, depth),
        out_shape=(
            pltpu.VMEM((rows, part + META), jnp.bfloat16),
            pltpu.VMEM((rows, part), jnp.bfloat16),
        ),
        in_specs=[VMEM] * (depth + 1),
        out_specs=(VMEM, VMEM),
        compiler_params=params(4),
        name="second_norm",
    )(*far_first(parts), gain)


def projection_kernel(chunk, mine_ref, theirs_ref, next_ref, q_ref, *refs):
    kv_refs, out_refs, kv_buf = refs[: -PLANE - 1], refs[-PLANE - 1 : -1], refs[-1]
    depth = len(kv_refs)
    rows, extended = mine_ref.shape
    part = extended - META
    sub = part // depth
    q_cols, kv_cols = q_ref.shape[1], kv_buf.shape[1]
    cols = q_cols + kv_cols
    line = lax.axis_index("expert") // PLANE
    for d, ref in enumerate(kv_refs):
        kv_buf[lanes((line ^ d) * sub, sub), :] = ref[...]
    block = rows // PLANE
    tensor = lax.axis_index("tensor")
    own = lanes(tensor * block, block)
    other = lanes((1 - tensor) * block, block)
    for d in range(PLANE):
        at = slice(d * block, (d + 1) * block)
        out_refs[d][own, cols : cols + META] = mine_ref[at, part:]
        out_refs[d][other, cols : cols + META] = theirs_ref[at, part:]
        out_refs[d][:block, cols + META :] = next_ref[at, : part // 2]
        out_refs[d][block:, cols + META :] = next_ref[at, part // 2 :]
    both = jnp.concatenate([mine_ref[:, :part], theirs_ref[:, :part]], axis=0)

    def multiply(weight, target):
        product = jnp.dot(both, weight, preferred_element_type=jnp.float32).astype(jnp.bfloat16)
        at = slice(target, target + weight.shape[1])
        for d in range(PLANE):
            out_refs[d][own, at] = product[d * block : (d + 1) * block]
            out_refs[d][other, at] = product[rows + d * block : rows + (d + 1) * block]

    multiply(kv_buf[...], q_cols)
    for start in range(0, q_cols, chunk):
        multiply(q_ref[:, start : start + chunk], start)


def projection(mine, theirs, following, q_weight, kv_weights):
    rows, part = following.shape
    q_cols, kv_cols = q_weight.shape[1], kv_weights[0].shape[1]
    chunk = 512
    shape = pltpu.VMEM((2 * rows // PLANE, q_cols + kv_cols + META + part // 2), jnp.bfloat16)
    return pl.pallas_call(
        functools.partial(projection_kernel, chunk),
        out_shape=(shape,) * PLANE,
        in_specs=[VMEM] * (4 + len(kv_weights)),
        out_specs=(VMEM,) * PLANE,
        scratch_shapes=[pltpu.VMEM((part, kv_cols), jnp.bfloat16)],
        compiler_params=params(8),
        cost_estimate=SMALL,
        name="qkv_projection",
    )(mine, theirs, following, q_weight, *kv_weights)


def head_norm_kernel(depth, *refs):
    parts, q_gain_ref, k_gain_ref = far_first(refs[:PLANE]), refs[PLANE], refs[PLANE + 1]
    next_ref, q_ref, kv_ref = refs[PLANE + 2 :]
    width = next_ref.shape[1]
    q_cols, kv_cols = q_ref.shape[1], kv_ref.shape[1]
    cols = q_cols + kv_cols
    head = q_gain_ref.shape[1]

    def total(at):
        value = parts[0][:, at].astype(jnp.float32)
        for ref in parts[1:]:
            value = value + ref[:, at].astype(jnp.float32)
        return value

    squares = jnp.sum(total(slice(cols, cols + META)), axis=1, keepdims=True)
    scale = lax.rsqrt(squares / width + EPSILON)
    for h in range(q_cols // head):
        at = slice(h * head, (h + 1) * head)
        q_ref[:, at] = normalize(total(at) * scale, q_gain_ref[...]).astype(jnp.bfloat16)
    tensor = lax.axis_index("tensor")
    for h in range(kv_cols // head):
        at = slice(h * head, (h + 1) * head)
        raw = total(slice(q_cols + h * head, q_cols + (h + 1) * head)) * scale
        is_key = tensor * (kv_cols // head) + h < KV_HEADS
        kv_ref[:, at] = jnp.where(is_key, normalize(raw, k_gain_ref[...]), raw).astype(
            jnp.bfloat16
        )
    plane = lax.axis_index("expert") % PLANE
    rows = next_ref.shape[0]
    sub = width // (PLANE * depth)
    for d in range(PLANE):
        for z in range(depth):
            top = z * sub * 2 // (depth * sub)
            start = cols + META + z * sub - top * (depth * sub // 2)
            next_ref[:, lanes((z * PLANE + (plane ^ d)) * sub, sub)] = parts[d][
                top * rows : (top + 1) * rows, start : start + sub
            ]


def head_norm(parts, q_gain, k_gain, q_cols, kv_cols, rows, width, depth):
    both = parts[0].shape[0]
    return pl.pallas_call(
        functools.partial(head_norm_kernel, depth),
        out_shape=(
            jax.ShapeDtypeStruct((rows, width), jnp.bfloat16),
            jax.ShapeDtypeStruct((both, q_cols), jnp.bfloat16),
            jax.ShapeDtypeStruct((both, kv_cols), jnp.bfloat16),
        ),
        in_specs=[VMEM] * (PLANE + 2),
        out_specs=(VMEM, VMEM, VMEM),
        compiler_params=params(4),
        name="head_norm",
    )(*far_first(parts), q_gain, k_gain)


def per_device_dense(
    attn_out,
    out_weight,
    residual,
    attn_gain,
    expert_ids,
    route_weights,
    w_gate,
    w_up,
    w_down,
    input_gain,
    q_weight,
    kv_weight,
    q_gain,
    k_gain,
):
    n_expert = lax.axis_size("expert")
    depth = n_expert // PLANE
    rows, width = residual.shape
    tensor_index = lax.axis_index("tensor").astype(jnp.int32)

    def to_core(value):
        return lax.ppermute(value, "tensor", [(0, 1), (1, 0)])

    def to_expert(value, offset):
        return lax.ppermute(value, "expert", [(i, i ^ offset) for i in range(n_expert)])

    def to_z(values):
        return [to_expert(v, d * PLANE) if d else v for d, v in enumerate(values)]

    def to_plane(values):
        return [to_expert(v, d) if d else v for d, v in enumerate(values)]

    own_ids = lax.dynamic_slice_in_dim(expert_ids, tensor_index * rows, rows, 0)
    own_route = lax.dynamic_slice_in_dim(route_weights, tensor_index * rows, rows, 0)
    chosen = own_ids[:, :, None] == jnp.arange(META // 2, dtype=jnp.int32)[None, None, :]
    dense = jnp.sum(jnp.where(chosen, own_route[:, :, None], 0.0), axis=1)
    high = lax.reduce_precision(dense, 8, 7)
    meta = jnp.concatenate([high, dense - high], axis=1).astype(jnp.bfloat16)

    lines = [list(range(i, n_expert, PLANE)) for i in range(PLANE)]
    mine, theirs = out_projection(attn_out, out_weight)
    tokens, first = first_norm(mine, to_core(theirs), residual, attn_gain[None, :], meta)
    tokens, q_own = lax.optimization_barrier((tokens, q_weight))
    q_rows = lax.all_gather(q_own, "expert", axis=0, tiled=True, axis_index_groups=lines)
    weights = load((w_gate, w_up, w_down), (tokens,))
    line = to_z([tokens] * depth)
    *line, gate, up, down = lax.optimization_barrier((*line, *weights))
    weights = (gate, up, down)
    near = to_plane([pack(line)] * (PLANE - 1))
    cut = near[0].shape[0] // 2
    one, two = near[1][:cut], near[2][cut:]
    far = [to_expert(one, 2), to_expert(two, 1)]
    near_mine, *near_theirs = experts((*near, *map(to_core, near)), weights, depth, len(near))
    theirs = list(map(to_core, near_theirs))
    near_mine, *far = lax.optimization_barrier((near_mine, *far))
    far_both = [*far, *map(to_core, far)]
    far_mine, *far_theirs = experts(far_both, weights, depth, 1)
    theirs += map(to_core, far_theirs)
    *sums, kv_own = lax.optimization_barrier((*chip_sum((near_mine, far_mine), theirs, first, depth), kv_weight))
    parts = to_plane(sums)
    kv_rows = [kv_own, to_expert(kv_own, PLANE), to_expert(kv_own, 2 * PLANE)]
    *parts, kv_rows[1], kv_rows[2] = lax.optimization_barrier(
        (*plane_sum(parts, depth), *kv_rows[1:])
    )
    kv_rows.append(to_expert(kv_rows[2], PLANE))
    (q_rows,) = load((q_rows,), parts)
    parts = to_z(parts)
    *parts, q_rows = lax.optimization_barrier((*parts, q_rows))
    scaled, following = second_norm(parts, input_gain[None, :])
    products = to_plane(projection(scaled, to_core(scaled), following, q_rows, kv_rows))
    return head_norm(
        products,
        q_gain[None, :],
        k_gain[None, :],
        q_weight.shape[1],
        kv_weight.shape[1],
        rows,
        width,
        depth,
    )


def per_device(
    attn_out,
    out_weight,
    residual,
    attn_gain,
    expert_ids,
    route_weights,
    w_gate,
    w_up,
    w_down,
    input_gain,
    q_weight,
    kv_weight,
    q_gain,
    k_gain,
):
    n_expert = lax.axis_size("expert")
    n_tensor = lax.axis_size("tensor")
    share = n_tensor // 2
    tensor_index = lax.axis_index("tensor")
    group_rows = attn_out.shape[0]
    width = residual.shape[1]
    half = tensor_index // share
    capacity = 3 * group_rows * TOP // (4 * n_expert)
    all_experts = 2 * n_expert
    attn_rows = lax.psum_scatter(
        jnp.dot(attn_out, out_weight, preferred_element_type=jnp.float32),
        "tensor",
        scatter_dimension=0,
        tiled=True,
    )
    first_residual = (residual.astype(jnp.float32) + attn_rows).astype(jnp.bfloat16)
    normed = normalize(first_residual.astype(jnp.float32), attn_gain).astype(jnp.bfloat16)
    group_normed = lax.all_gather(normed, "tensor", axis=0, tiled=True)
    flat_ids = expert_ids.reshape(-1)
    onehot = (flat_ids[:, None] == jnp.arange(all_experts, dtype=jnp.int32)[None, :]).astype(
        jnp.int32
    )
    earlier = jnp.cumsum(onehot, axis=0) - onehot
    rank = jnp.sum(earlier * onehot, axis=1)
    dest = flat_ids * capacity + rank
    row_owner = jnp.arange(flat_ids.shape[0], dtype=jnp.int32) // TOP
    slot_row = jnp.full((all_experts * capacity,), group_rows, jnp.int32).at[dest].set(row_owner)
    slot_weight = (
        jnp.zeros((all_experts * capacity,), jnp.float32).at[dest].set(route_weights.reshape(-1))
    )
    own_slots = lax.dynamic_index_in_dim(
        slot_row.reshape(n_expert, 2, capacity), half, 1, keepdims=False
    )
    own_weights = lax.dynamic_index_in_dim(
        slot_weight.reshape(n_expert, 2, capacity), half, 1, keepdims=False
    )
    padded_rows = jnp.concatenate([group_normed, jnp.zeros((1, width), jnp.bfloat16)], axis=0)
    gate_w = w_gate[0]
    up_w = w_up[0]
    down_w = w_down[0]
    outgoing = jnp.take(padded_rows, own_slots, axis=0)
    arrived = lax.all_to_all(outgoing, "expert", split_axis=0, concat_axis=0, tiled=True)
    flat = arrived.reshape(-1, width)
    gate = jnp.dot(flat, gate_w, preferred_element_type=jnp.float32)
    up = jnp.dot(flat, up_w, preferred_element_type=jnp.float32)
    act = (jax.nn.silu(gate) * up).astype(jnp.bfloat16)
    part = jnp.dot(act, down_w, preferred_element_type=jnp.float32).astype(jnp.bfloat16)
    send_part = part.reshape(arrived.shape)
    returned = lax.all_to_all(send_part, "expert", split_axis=0, concat_axis=0, tiled=True)
    weighted = own_weights.reshape(-1)[:, None] * returned.reshape(-1, width).astype(jnp.float32)
    term = (
        jnp.zeros((group_rows + 1, width), jnp.float32)
        .at[own_slots.reshape(-1)]
        .add(weighted)[:group_rows]
    )
    expert_sum = lax.psum_scatter(
        term.astype(jnp.bfloat16), "tensor", scatter_dimension=0, tiled=True
    ).astype(jnp.float32)
    next_residual = (first_residual.astype(jnp.float32) + expert_sum).astype(jnp.bfloat16)
    own_normed = normalize(next_residual.astype(jnp.float32), input_gain).astype(jnp.bfloat16)
    next_normed = lax.all_gather(own_normed, "tensor", axis=0, tiled=True)
    query_cols = q_weight.shape[1]
    kv_cols = kv_weight.shape[1]
    query_raw = jnp.dot(
        next_normed,
        lax.all_gather(q_weight, "expert", axis=0, tiled=True),
        preferred_element_type=jnp.float32,
    )
    kv_raw = jnp.dot(
        next_normed,
        lax.all_gather(kv_weight, "expert", axis=0, tiled=True),
        preferred_element_type=jnp.float32,
    )
    head_size = q_gain.shape[0]
    queries = (
        normalize(query_raw.reshape(group_rows, -1, head_size), q_gain)
        .reshape(group_rows, query_cols)
        .astype(jnp.bfloat16)
    )
    heads_here = kv_cols // head_size
    head_number = tensor_index * heads_here + jnp.arange(heads_here, dtype=jnp.int32)
    is_key = head_number < KV_HEADS
    kv_shaped = kv_raw.reshape(group_rows, heads_here, head_size)
    keys_values = (
        jnp.where(is_key[None, :, None], normalize(kv_shaped, k_gain), kv_shaped)
        .reshape(group_rows, kv_cols)
        .astype(jnp.bfloat16)
    )
    return (next_residual, queries, keys_values)


def solution(mesh):
    small = mesh.shape["tensor"] == 2 and mesh.shape["expert"] == 4 * PLANE
    return jax.shard_map(
        per_device_dense if small else per_device,
        mesh=mesh,
        in_specs=(
            P("expert", "tensor"),
            P("tensor", None),
            P(("expert", "tensor"), None),
            P(),
            P("expert", None),
            P("expert", None),
            P("expert", None, "tensor"),
            P("expert", None, "tensor"),
            P("expert", "tensor", None),
            P(),
            P("expert", "tensor"),
            P("expert", "tensor"),
            P(),
            P(),
        ),
        out_specs=(P(("expert", "tensor"), None), P("expert", "tensor"), P("expert", "tensor")),
        check_vma=False,
    )
```

```python
import functools

import jax
import jax.numpy as jnp
from jax import lax
from jax.experimental import pallas as pl
from jax.experimental.pallas import tpu as pltpu
from jax.sharding import PartitionSpec as P

KV_HEADS = 4
TOP = 8
PLANE = 4
META = 128


EPSILON = 1e-06

SMALL = pl.CostEstimate(flops=0, bytes_accessed=0, transcendentals=0)
VMEM = pl.BlockSpec(memory_space=pltpu.VMEM)
HBM = pl.BlockSpec(memory_space=pltpu.HBM)


def normalize(values, gain):
    return values * lax.rsqrt(jnp.mean(values * values, axis=-1, keepdims=True) + EPSILON) * gain


def params(mebibytes):
    return pltpu.CompilerParams(vmem_limit_bytes=mebibytes << 20)


def lanes(start, size):
    return pl.ds(pl.multiple_of(start, size), size)


def in_hbm(value):
    return pltpu.with_memory_space_constraint(value, pltpu.HBM)


def in_vmem(value):
    return pltpu.with_memory_space_constraint(value, pltpu.VMEM)


def out_projection_kernel(chunk, a_hbm, w_hbm, mine_ref, theirs_ref, a_buf, w_buf, a_sem, sems):
    depth = w_buf.shape[0]
    count = depth // chunk
    half = mine_ref.shape[0]
    a_copy = pltpu.make_async_copy(a_hbm, a_buf, a_sem)
    a_copy.start()
    copies = []
    for i in range(count):
        rows = pl.ds(i * chunk, chunk)
        copies.append(pltpu.make_async_copy(w_hbm.at[rows], w_buf.at[rows], sems.at[i]))
    for copy in copies:
        copy.start()
    tensor = lax.axis_index("tensor")
    own = lanes(tensor * half, half)
    other = lanes((1 - tensor) * half, half)
    a_copy.wait()
    for i in range(count):
        copies[i].wait()
        at = pl.ds(i * chunk, chunk)
        both = jnp.concatenate([a_buf[own, at], a_buf[other, at]], axis=0)
        product = jnp.dot(both, w_buf[at, :], preferred_element_type=jnp.float32)
        if i == 0:
            mine_ref[...] = product[:half]
            theirs_ref[...] = product[half:]
        else:
            mine_ref[...] += product[:half]
            theirs_ref[...] += product[half:]


def out_projection(attn_out, out_weight):
    rows, depth = attn_out.shape
    width = out_weight.shape[1]
    chunk = 256
    half = pltpu.VMEM((rows // 2, width), jnp.float32)
    return pl.pallas_call(
        functools.partial(out_projection_kernel, chunk),
        out_shape=(half, half),
        in_specs=[HBM, HBM],
        out_specs=(VMEM, VMEM),
        scratch_shapes=[
            pltpu.VMEM((rows, depth), jnp.bfloat16),
            pltpu.VMEM((depth, width), jnp.bfloat16),
            pltpu.SemaphoreType.DMA,
            pltpu.SemaphoreType.DMA((depth // chunk,)),
        ],
        compiler_params=params(14),
        cost_estimate=SMALL,
        name="out_projection",
    )(in_hbm(attn_out), in_hbm(out_weight))


def first_norm_kernel(mine_ref, theirs_ref, residual_ref, gain_ref, meta_ref, tokens_ref, first_ref):
    width = residual_ref.shape[1]
    first = (residual_ref[...].astype(jnp.float32) + (mine_ref[...] + theirs_ref[...])).astype(
        jnp.bfloat16
    )
    first_ref[...] = first
    tokens_ref[:, :width] = normalize(first.astype(jnp.float32), gain_ref[...]).astype(jnp.bfloat16)
    tokens_ref[:, width:] = meta_ref[...]


def first_norm(mine, theirs, residual, gain, meta):
    rows, width = residual.shape
    return pl.pallas_call(
        first_norm_kernel,
        out_shape=(
            pltpu.VMEM((rows, width + META), jnp.bfloat16),
            pltpu.VMEM((rows, width), jnp.bfloat16),
        ),
        in_specs=[VMEM] * 5,
        out_specs=(VMEM, VMEM),
        compiler_params=params(2),
        name="first_norm",
    )(mine, theirs, residual, gain, meta)


def pack_kernel(depth, *refs):
    line, out_ref = refs[:depth], refs[depth]
    rows = line[0].shape[0]
    for z in range(depth):
        out_ref[z * rows : (z + 1) * rows, :] = line[z][...]


def pack(line):
    depth = len(line)
    rows, extended = line[0].shape
    return pl.pallas_call(
        functools.partial(pack_kernel, depth),
        out_shape=pltpu.VMEM((depth * rows, extended), jnp.bfloat16),
        in_specs=[VMEM] * depth,
        out_specs=VMEM,
        compiler_params=params(2),
        name="pack_tokens",
    )(*line)


def load_kernel(count, *refs):
    sources, targets, sems = refs[:count], refs[-count - 1 : -1], refs[-1]
    copies = [
        pltpu.make_async_copy(source, target, sems.at[i])
        for i, (source, target) in enumerate(zip(sources, targets))
    ]
    for copy in copies:
        copy.start()
    for copy in copies:
        copy.wait()


def load(weights, after):
    count = len(weights)
    return pl.pallas_call(
        functools.partial(load_kernel, count),
        out_shape=tuple(pltpu.VMEM(w.shape, w.dtype) for w in weights),
        in_specs=[HBM] * count + [pl.BlockSpec(memory_space=pl.ANY)] * len(after),
        out_specs=(VMEM,) * count,
        scratch_shapes=[pltpu.SemaphoreType.DMA((count,))],
        compiler_params=params(2),
        cost_estimate=SMALL,
        name="load_weights",
    )(*map(in_hbm, weights), *after)


def expert_kernel(depth, chunk, count, *refs):
    block_refs, (gate_ref, up_ref, down_ref) = refs[:count], refs[count : count + 3]
    mine_ref, *theirs_refs, x_buf, act_buf = refs[count + 3 :]
    width, hidden = gate_ref.shape[1:]
    extended = x_buf.shape[1]
    start = 0
    for ref in block_refs:
        rows = ref.shape[0]
        x_buf[start : start + rows, :] = ref[:, :extended]
        start += rows
    meta = x_buf[:, width:].astype(jnp.float32)
    lane = lax.broadcasted_iota(jnp.int32, meta.shape, 1)
    chip = lax.axis_index("expert")
    expert = 2 * chip + lax.axis_index("tensor")
    chosen = (lane == expert) | (lane == expert + META // 2)
    route = 0.5 * jnp.sum(jnp.where(chosen, meta, 0.0), axis=1, keepdims=True)
    for i in range(hidden // chunk):
        cols = pl.ds(i * chunk, chunk)
        x = x_buf[:, :width]
        gate = jnp.dot(x, gate_ref[0, :, cols], preferred_element_type=jnp.float32)
        up = jnp.dot(x, up_ref[0, :, cols], preferred_element_type=jnp.float32)
        act = gate * (1.0 + jnp.tanh(0.5 * gate)) * (up * route)
        act_buf[:, i * chunk : (i + 1) * chunk] = act.astype(jnp.bfloat16)
    sub = width // (PLANE * depth)
    part = sub * depth
    half = mine_ref.shape[0]
    plane = chip % PLANE
    for d in range(PLANE):
        weight = jnp.concatenate(
            [down_ref[0, :, lanes((z * PLANE + (plane ^ d)) * sub, sub)] for z in range(depth)],
            axis=1,
        )
        out = jnp.dot(act_buf[...], weight, preferred_element_type=jnp.float32)
        cols = slice(d * part, (d + 1) * part)
        mine_ref[:, cols] = out[:half].astype(jnp.bfloat16)
        start = half
        for ref in theirs_refs:
            stop = start + ref.shape[0]
            ref[:, cols] = out[start:stop].astype(jnp.bfloat16)
            start = stop


def experts(blocks, weights, depth, pieces):
    width, hidden = weights[0].shape[1:]
    chunk = 256
    extended = width + META
    total = sum(block.shape[0] for block in blocks)
    rows = [total // 2] + [total // 2 // pieces] * pieces
    return pl.pallas_call(
        functools.partial(expert_kernel, depth, chunk, len(blocks)),
        out_shape=tuple(pltpu.VMEM((size, width), jnp.bfloat16) for size in rows),
        in_specs=[VMEM] * (len(blocks) + 3),
        out_specs=(VMEM,) * (1 + pieces),
        scratch_shapes=[
            pltpu.VMEM((total, extended), jnp.bfloat16),
            pltpu.VMEM((total, hidden), jnp.bfloat16),
        ],
        compiler_params=params(16),
        cost_estimate=pl.CostEstimate(
            flops=6 * total * width * hidden, bytes_accessed=0, transcendentals=0
        ),
        name="experts",
    )(*blocks, *weights)


def chip_sum_kernel(depth, count, first_ref, *refs):
    mine, theirs, out_refs = refs[:2], refs[2 : 2 + count], refs[2 + count :]
    part = out_refs[0].shape[1]
    sub = part // depth
    held = first_ref.shape[0]
    plane = lax.axis_index("expert") % PLANE
    start = 0
    for own_ref in mine:
        first = start
        while start < first + own_ref.shape[0]:
            ref, theirs = theirs[0], theirs[1:]
            size = ref.shape[0]
            own = slice(start - first, start - first + size)
            for d, out_ref in enumerate(out_refs):
                at = slice(d * part, (d + 1) * part)
                total = own_ref[own, at].astype(jnp.float32) + ref[:, at].astype(jnp.float32)
                if start == 0:
                    residual = jnp.concatenate(
                        [
                            first_ref[:, lanes((z * PLANE + (plane ^ d)) * sub, sub)]
                            for z in range(depth)
                        ],
                        axis=1,
                    )
                    with_first = total[:held] + residual.astype(jnp.float32)
                    total = jnp.concatenate([with_first, total[held:]], axis=0)
                out_ref[start : start + size, :] = total.astype(jnp.bfloat16)
            start += size


def chip_sum(mine, theirs, first, depth):
    rows, width = sum(value.shape[0] for value in mine), mine[0].shape[1]
    return pl.pallas_call(
        functools.partial(chip_sum_kernel, depth, len(theirs)),
        out_shape=(pltpu.VMEM((rows, width // PLANE), jnp.bfloat16),) * PLANE,
        in_specs=[VMEM] * (3 + len(theirs)),
        out_specs=(VMEM,) * PLANE,
        compiler_params=params(4),
        name="chip_sum",
    )(first, *mine, *theirs)


def plane_sum_kernel(depth, *refs):
    in_refs, out_refs = refs[:PLANE], refs[PLANE:]
    group = in_refs[0].shape[0] // PLANE
    rows = group // depth
    for k in range(PLANE):
        for z in range(depth):
            total = 0.0
            for d in range(PLANE):
                start = (k ^ d) * group + z * rows
                total = total + in_refs[d][start : start + rows, :].astype(jnp.float32)
            out_refs[z][k * rows : (k + 1) * rows, :] = total.astype(jnp.bfloat16)


def plane_sum(parts, depth):
    rows, part = parts[0].shape
    return pl.pallas_call(
        functools.partial(plane_sum_kernel, depth),
        out_shape=(pltpu.VMEM((rows // depth, part), jnp.bfloat16),) * depth,
        in_specs=[VMEM] * PLANE,
        out_specs=(VMEM,) * depth,
        compiler_params=params(4),
        name="plane_sum",
    )(*parts)


def second_norm_kernel(depth, *refs):
    parts, (gain_ref, scaled_ref, next_ref) = refs[:depth], refs[depth:]
    rows, part = next_ref.shape
    sub = part // depth
    plane = lax.axis_index("expert") % PLANE
    gain = jnp.concatenate(
        [gain_ref[:, lanes((z * PLANE + plane) * sub, sub)] for z in range(depth)], axis=1
    )
    total = parts[0][...].astype(jnp.float32)
    for ref in parts[1:]:
        total = total + ref[...].astype(jnp.float32)
    following = total.astype(jnp.bfloat16)
    next_ref[...] = following
    wide = following.astype(jnp.float32)
    scaled_ref[:, :part] = (wide * gain).astype(jnp.bfloat16)
    squares = jnp.sum(wide * wide, axis=1, keepdims=True)
    high = squares.astype(jnp.bfloat16).astype(jnp.float32)
    lane = lax.broadcasted_iota(jnp.int32, (rows, META), 1)
    scaled_ref[:, part:] = jnp.where(
        lane == 0, high, jnp.where(lane == 1, squares - high, 0.0)
    ).astype(jnp.bfloat16)


def second_norm(parts, gain):
    depth = len(parts)
    rows, part = parts[0].shape
    return pl.pallas_call(
        functools.partial(second_norm_kernel, depth),
        out_shape=(
            pltpu.VMEM((rows, part + META), jnp.bfloat16),
            pltpu.VMEM((rows, part), jnp.bfloat16),
        ),
        in_specs=[VMEM] * (depth + 1),
        out_specs=(VMEM, VMEM),
        compiler_params=params(4),
        name="second_norm",
    )(*parts, gain)


def projection_kernel(chunk, mine_ref, theirs_ref, next_ref, q_ref, *refs):
    kv_refs, out_refs, kv_buf = refs[: -PLANE - 1], refs[-PLANE - 1 : -1], refs[-1]
    depth = len(kv_refs)
    rows, extended = mine_ref.shape
    part = extended - META
    sub = part // depth
    q_cols, kv_cols = q_ref.shape[1], kv_buf.shape[1]
    cols = q_cols + kv_cols
    line = lax.axis_index("expert") // PLANE
    for d, ref in enumerate(kv_refs):
        kv_buf[lanes((line ^ d) * sub, sub), :] = ref[...]
    block = rows // PLANE
    tensor = lax.axis_index("tensor")
    own = lanes(tensor * block, block)
    other = lanes((1 - tensor) * block, block)
    for d in range(PLANE):
        at = slice(d * block, (d + 1) * block)
        out_refs[d][own, cols : cols + META] = mine_ref[at, part:]
        out_refs[d][other, cols : cols + META] = theirs_ref[at, part:]
        out_refs[d][:block, cols + META :] = next_ref[at, : part // 2]
        out_refs[d][block:, cols + META :] = next_ref[at, part // 2 :]
    both = jnp.concatenate([mine_ref[:, :part], theirs_ref[:, :part]], axis=0)

    def multiply(weight, target):
        product = jnp.dot(both, weight, preferred_element_type=jnp.float32).astype(jnp.bfloat16)
        at = slice(target, target + weight.shape[1])
        for d in range(PLANE):
            out_refs[d][own, at] = product[d * block : (d + 1) * block]
            out_refs[d][other, at] = product[rows + d * block : rows + (d + 1) * block]

    multiply(kv_buf[...], q_cols)
    for start in range(0, q_cols, chunk):
        multiply(q_ref[:, start : start + chunk], start)


def projection(mine, theirs, following, q_weight, kv_weights):
    rows, part = following.shape
    q_cols, kv_cols = q_weight.shape[1], kv_weights[0].shape[1]
    chunk = 512
    shape = pltpu.VMEM((2 * rows // PLANE, q_cols + kv_cols + META + part // 2), jnp.bfloat16)
    return pl.pallas_call(
        functools.partial(projection_kernel, chunk),
        out_shape=(shape,) * PLANE,
        in_specs=[VMEM] * (4 + len(kv_weights)),
        out_specs=(VMEM,) * PLANE,
        scratch_shapes=[pltpu.VMEM((part, kv_cols), jnp.bfloat16)],
        compiler_params=params(8),
        cost_estimate=SMALL,
        name="qkv_projection",
    )(mine, theirs, following, q_weight, *kv_weights)


def head_norm_kernel(depth, *refs):
    parts, q_gain_ref, k_gain_ref = refs[:PLANE], refs[PLANE], refs[PLANE + 1]
    next_ref, q_ref, kv_ref = refs[PLANE + 2 :]
    width = next_ref.shape[1]
    q_cols, kv_cols = q_ref.shape[1], kv_ref.shape[1]
    cols = q_cols + kv_cols
    head = q_gain_ref.shape[1]

    def total(at):
        value = parts[0][:, at].astype(jnp.float32)
        for ref in parts[1:]:
            value = value + ref[:, at].astype(jnp.float32)
        return value

    squares = jnp.sum(total(slice(cols, cols + META)), axis=1, keepdims=True)
    scale = lax.rsqrt(squares / width + EPSILON)
    for h in range(q_cols // head):
        at = slice(h * head, (h + 1) * head)
        q_ref[:, at] = normalize(total(at) * scale, q_gain_ref[...]).astype(jnp.bfloat16)
    tensor = lax.axis_index("tensor")
    for h in range(kv_cols // head):
        at = slice(h * head, (h + 1) * head)
        raw = total(slice(q_cols + h * head, q_cols + (h + 1) * head)) * scale
        is_key = tensor * (kv_cols // head) + h < KV_HEADS
        kv_ref[:, at] = jnp.where(is_key, normalize(raw, k_gain_ref[...]), raw).astype(
            jnp.bfloat16
        )
    plane = lax.axis_index("expert") % PLANE
    rows = next_ref.shape[0]
    sub = width // (PLANE * depth)
    for d in range(PLANE):
        for z in range(depth):
            top = z * sub * 2 // (depth * sub)
            start = cols + META + z * sub - top * (depth * sub // 2)
            next_ref[:, lanes((z * PLANE + (plane ^ d)) * sub, sub)] = parts[d][
                top * rows : (top + 1) * rows, start : start + sub
            ]


def head_norm(parts, q_gain, k_gain, q_cols, kv_cols, rows, width, depth):
    both = parts[0].shape[0]
    return pl.pallas_call(
        functools.partial(head_norm_kernel, depth),
        out_shape=(
            jax.ShapeDtypeStruct((rows, width), jnp.bfloat16),
            jax.ShapeDtypeStruct((both, q_cols), jnp.bfloat16),
            jax.ShapeDtypeStruct((both, kv_cols), jnp.bfloat16),
        ),
        in_specs=[VMEM] * (PLANE + 2),
        out_specs=(VMEM, VMEM, VMEM),
        compiler_params=params(4),
        name="head_norm",
    )(*parts, q_gain, k_gain)


def per_device_dense(
    attn_out,
    out_weight,
    residual,
    attn_gain,
    expert_ids,
    route_weights,
    w_gate,
    w_up,
    w_down,
    input_gain,
    q_weight,
    kv_weight,
    q_gain,
    k_gain,
):
    n_expert = lax.axis_size("expert")
    depth = n_expert // PLANE
    rows, width = residual.shape
    tensor_index = lax.axis_index("tensor").astype(jnp.int32)

    def to_core(value):
        return lax.ppermute(value, "tensor", [(0, 1), (1, 0)])

    def to_expert(value, offset):
        return lax.ppermute(value, "expert", [(i, i ^ offset) for i in range(n_expert)])

    def to_z(values):
        return [to_expert(v, d * PLANE) if d else v for d, v in enumerate(values)]

    def to_plane(values):
        return [to_expert(v, d) if d else v for d, v in enumerate(values)]

    own_ids = lax.dynamic_slice_in_dim(expert_ids, tensor_index * rows, rows, 0)
    own_route = lax.dynamic_slice_in_dim(route_weights, tensor_index * rows, rows, 0)
    chosen = own_ids[:, :, None] == jnp.arange(META // 2, dtype=jnp.int32)[None, None, :]
    dense = jnp.sum(jnp.where(chosen, own_route[:, :, None], 0.0), axis=1)
    high = lax.reduce_precision(dense, 8, 7)
    meta = jnp.concatenate([high, dense - high], axis=1).astype(jnp.bfloat16)

    lines = [list(range(i, n_expert, PLANE)) for i in range(PLANE)]
    mine, theirs = out_projection(attn_out, out_weight)
    tokens, first = first_norm(mine, to_core(theirs), residual, attn_gain[None, :], meta)
    tokens, q_own = lax.optimization_barrier((tokens, q_weight))
    q_rows = lax.all_gather(q_own, "expert", axis=0, tiled=True, axis_index_groups=lines)
    weights = load((w_gate, w_up, w_down), (tokens,))
    line = to_z([tokens] * depth)
    *line, gate, up, down = lax.optimization_barrier((*line, *weights))
    weights = (gate, up, down)
    near = to_plane([pack(line)] * (PLANE - 1))
    cut = near[0].shape[0] // 2
    one, two = near[1][:cut], near[2][cut:]
    far = [to_expert(one, 2), to_expert(two, 1)]
    near_mine, *near_theirs = experts((*near, *map(to_core, near)), weights, depth, len(near))
    theirs = list(map(to_core, near_theirs))
    near_mine, *far = lax.optimization_barrier((near_mine, *far))
    far_both = [*far, *map(to_core, far)]
    far_mine, *far_theirs = experts(far_both, weights, depth, 1)
    theirs += map(to_core, far_theirs)
    *sums, kv_own = lax.optimization_barrier((*chip_sum((near_mine, far_mine), theirs, first, depth), kv_weight))
    parts = to_plane(sums)
    kv_rows = [kv_own, to_expert(kv_own, PLANE), to_expert(kv_own, 2 * PLANE)]
    parts = plane_sum(parts, depth)
    kv_rows.append(to_expert(kv_rows[2], PLANE))
    (q_rows,) = load((q_rows,), (*parts, *kv_rows[1:3]))
    parts = to_z(parts)
    *parts, q_rows = lax.optimization_barrier((*parts, q_rows))
    scaled, following = second_norm(parts, input_gain[None, :])
    products = to_plane(projection(scaled, to_core(scaled), following, q_rows, kv_rows))
    return head_norm(
        products,
        q_gain[None, :],
        k_gain[None, :],
        q_weight.shape[1],
        kv_weight.shape[1],
        rows,
        width,
        depth,
    )


def per_device(
    attn_out,
    out_weight,
    residual,
    attn_gain,
    expert_ids,
    route_weights,
    w_gate,
    w_up,
    w_down,
    input_gain,
    q_weight,
    kv_weight,
    q_gain,
    k_gain,
):
    n_expert = lax.axis_size("expert")
    n_tensor = lax.axis_size("tensor")
    share = n_tensor // 2
    tensor_index = lax.axis_index("tensor")
    group_rows = attn_out.shape[0]
    width = residual.shape[1]
    half = tensor_index // share
    capacity = 3 * group_rows * TOP // (4 * n_expert)
    all_experts = 2 * n_expert
    attn_rows = lax.psum_scatter(
        jnp.dot(attn_out, out_weight, preferred_element_type=jnp.float32),
        "tensor",
        scatter_dimension=0,
        tiled=True,
    )
    first_residual = (residual.astype(jnp.float32) + attn_rows).astype(jnp.bfloat16)
    normed = normalize(first_residual.astype(jnp.float32), attn_gain).astype(jnp.bfloat16)
    group_normed = lax.all_gather(normed, "tensor", axis=0, tiled=True)
    flat_ids = expert_ids.reshape(-1)
    onehot = (flat_ids[:, None] == jnp.arange(all_experts, dtype=jnp.int32)[None, :]).astype(
        jnp.int32
    )
    earlier = jnp.cumsum(onehot, axis=0) - onehot
    rank = jnp.sum(earlier * onehot, axis=1)
    dest = flat_ids * capacity + rank
    row_owner = jnp.arange(flat_ids.shape[0], dtype=jnp.int32) // TOP
    slot_row = jnp.full((all_experts * capacity,), group_rows, jnp.int32).at[dest].set(row_owner)
    slot_weight = (
        jnp.zeros((all_experts * capacity,), jnp.float32).at[dest].set(route_weights.reshape(-1))
    )
    own_slots = lax.dynamic_index_in_dim(
        slot_row.reshape(n_expert, 2, capacity), half, 1, keepdims=False
    )
    own_weights = lax.dynamic_index_in_dim(
        slot_weight.reshape(n_expert, 2, capacity), half, 1, keepdims=False
    )
    padded_rows = jnp.concatenate([group_normed, jnp.zeros((1, width), jnp.bfloat16)], axis=0)
    gate_w = w_gate[0]
    up_w = w_up[0]
    down_w = w_down[0]
    outgoing = jnp.take(padded_rows, own_slots, axis=0)
    arrived = lax.all_to_all(outgoing, "expert", split_axis=0, concat_axis=0, tiled=True)
    flat = arrived.reshape(-1, width)
    gate = jnp.dot(flat, gate_w, preferred_element_type=jnp.float32)
    up = jnp.dot(flat, up_w, preferred_element_type=jnp.float32)
    act = (jax.nn.silu(gate) * up).astype(jnp.bfloat16)
    part = jnp.dot(act, down_w, preferred_element_type=jnp.float32).astype(jnp.bfloat16)
    send_part = part.reshape(arrived.shape)
    returned = lax.all_to_all(send_part, "expert", split_axis=0, concat_axis=0, tiled=True)
    weighted = own_weights.reshape(-1)[:, None] * returned.reshape(-1, width).astype(jnp.float32)
    term = (
        jnp.zeros((group_rows + 1, width), jnp.float32)
        .at[own_slots.reshape(-1)]
        .add(weighted)[:group_rows]
    )
    expert_sum = lax.psum_scatter(
        term.astype(jnp.bfloat16), "tensor", scatter_dimension=0, tiled=True
    ).astype(jnp.float32)
    next_residual = (first_residual.astype(jnp.float32) + expert_sum).astype(jnp.bfloat16)
    own_normed = normalize(next_residual.astype(jnp.float32), input_gain).astype(jnp.bfloat16)
    next_normed = lax.all_gather(own_normed, "tensor", axis=0, tiled=True)
    query_cols = q_weight.shape[1]
    kv_cols = kv_weight.shape[1]
    query_raw = jnp.dot(
        next_normed,
        lax.all_gather(q_weight, "expert", axis=0, tiled=True),
        preferred_element_type=jnp.float32,
    )
    kv_raw = jnp.dot(
        next_normed,
        lax.all_gather(kv_weight, "expert", axis=0, tiled=True),
        preferred_element_type=jnp.float32,
    )
    head_size = q_gain.shape[0]
    queries = (
        normalize(query_raw.reshape(group_rows, -1, head_size), q_gain)
        .reshape(group_rows, query_cols)
        .astype(jnp.bfloat16)
    )
    heads_here = kv_cols // head_size
    head_number = tensor_index * heads_here + jnp.arange(heads_here, dtype=jnp.int32)
    is_key = head_number < KV_HEADS
    kv_shaped = kv_raw.reshape(group_rows, heads_here, head_size)
    keys_values = (
        jnp.where(is_key[None, :, None], normalize(kv_shaped, k_gain), kv_shaped)
        .reshape(group_rows, kv_cols)
        .astype(jnp.bfloat16)
    )
    return (next_residual, queries, keys_values)


def solution(mesh):
    small = mesh.shape["tensor"] == 2 and mesh.shape["expert"] == 4 * PLANE
    return jax.shard_map(
        per_device_dense if small else per_device,
        mesh=mesh,
        in_specs=(
            P("expert", "tensor"),
            P("tensor", None),
            P(("expert", "tensor"), None),
            P(),
            P("expert", None),
            P("expert", None),
            P("expert", None, "tensor"),
            P("expert", None, "tensor"),
            P("expert", "tensor", None),
            P(),
            P("expert", "tensor"),
            P("expert", "tensor"),
            P(),
            P(),
        ),
        out_specs=(P(("expert", "tensor"), None), P("expert", "tensor"), P("expert", "tensor")),
        check_vma=False,
    )
```

```python
import functools

import jax
import jax.numpy as jnp
from jax import lax
from jax.experimental import pallas as pl
from jax.experimental.pallas import tpu as pltpu
from jax.sharding import PartitionSpec as P

KV_HEADS = 4
TOP = 8
PLANE = 4
META = 128


EPSILON = 1e-06

SMALL = pl.CostEstimate(flops=0, bytes_accessed=0, transcendentals=0)
VMEM = pl.BlockSpec(memory_space=pltpu.VMEM)
HBM = pl.BlockSpec(memory_space=pltpu.HBM)


def normalize(values, gain):
    return values * lax.rsqrt(jnp.mean(values * values, axis=-1, keepdims=True) + EPSILON) * gain


def params(mebibytes):
    return pltpu.CompilerParams(vmem_limit_bytes=mebibytes << 20)


def lanes(start, size):
    return pl.ds(pl.multiple_of(start, size), size)


def in_hbm(value):
    return pltpu.with_memory_space_constraint(value, pltpu.HBM)


def in_vmem(value):
    return pltpu.with_memory_space_constraint(value, pltpu.VMEM)


def out_projection_kernel(chunk, a_hbm, w_hbm, mine_ref, theirs_ref, a_buf, w_buf, a_sem, sems):
    depth = w_buf.shape[0]
    count = depth // chunk
    half = mine_ref.shape[0]
    a_copy = pltpu.make_async_copy(a_hbm, a_buf, a_sem)
    a_copy.start()
    copies = []
    for i in range(count):
        rows = pl.ds(i * chunk, chunk)
        copies.append(pltpu.make_async_copy(w_hbm.at[rows], w_buf.at[rows], sems.at[i]))
    for copy in copies:
        copy.start()
    tensor = lax.axis_index("tensor")
    own = lanes(tensor * half, half)
    other = lanes((1 - tensor) * half, half)
    a_copy.wait()
    for i in range(count):
        copies[i].wait()
        at = pl.ds(i * chunk, chunk)
        both = jnp.concatenate([a_buf[own, at], a_buf[other, at]], axis=0)
        product = jnp.dot(both, w_buf[at, :], preferred_element_type=jnp.float32)
        if i == 0:
            mine_ref[...] = product[:half]
            theirs_ref[...] = product[half:]
        else:
            mine_ref[...] += product[:half]
            theirs_ref[...] += product[half:]


def out_projection(attn_out, out_weight):
    rows, depth = attn_out.shape
    width = out_weight.shape[1]
    chunk = 512
    half = pltpu.VMEM((rows // 2, width), jnp.float32)
    return pl.pallas_call(
        functools.partial(out_projection_kernel, chunk),
        out_shape=(half, half),
        in_specs=[HBM, HBM],
        out_specs=(VMEM, VMEM),
        scratch_shapes=[
            pltpu.VMEM((rows, depth), jnp.bfloat16),
            pltpu.VMEM((depth, width), jnp.bfloat16),
            pltpu.SemaphoreType.DMA,
            pltpu.SemaphoreType.DMA((depth // chunk,)),
        ],
        compiler_params=params(14),
        cost_estimate=SMALL,
        name="out_projection",
    )(in_hbm(attn_out), in_hbm(out_weight))


def first_norm_kernel(mine_ref, theirs_ref, residual_ref, gain_ref, meta_ref, tokens_ref, first_ref):
    width = residual_ref.shape[1]
    first = (residual_ref[...].astype(jnp.float32) + (mine_ref[...] + theirs_ref[...])).astype(
        jnp.bfloat16
    )
    first_ref[...] = first
    tokens_ref[:, :width] = normalize(first.astype(jnp.float32), gain_ref[...]).astype(jnp.bfloat16)
    tokens_ref[:, width:] = meta_ref[...]


def first_norm(mine, theirs, residual, gain, meta):
    rows, width = residual.shape
    return pl.pallas_call(
        first_norm_kernel,
        out_shape=(
            pltpu.VMEM((rows, width + META), jnp.bfloat16),
            pltpu.VMEM((rows, width), jnp.bfloat16),
        ),
        in_specs=[VMEM] * 5,
        out_specs=(VMEM, VMEM),
        compiler_params=params(2),
        name="first_norm",
    )(mine, theirs, residual, gain, meta)


def pack_kernel(depth, *refs):
    line, out_ref = refs[:depth], refs[depth]
    rows = line[0].shape[0]
    for z in range(depth):
        out_ref[z * rows : (z + 1) * rows, :] = line[z][...]


def pack(line):
    depth = len(line)
    rows, extended = line[0].shape
    return pl.pallas_call(
        functools.partial(pack_kernel, depth),
        out_shape=pltpu.VMEM((depth * rows, extended), jnp.bfloat16),
        in_specs=[VMEM] * depth,
        out_specs=VMEM,
        compiler_params=params(2),
        name="pack_tokens",
    )(*line)


def load_kernel(count, *refs):
    sources, targets, sems = refs[:count], refs[-count - 1 : -1], refs[-1]
    copies = [
        pltpu.make_async_copy(source, target, sems.at[i])
        for i, (source, target) in enumerate(zip(sources, targets))
    ]
    for copy in copies:
        copy.start()
    for copy in copies:
        copy.wait()


def load(weights, after):
    count = len(weights)
    return pl.pallas_call(
        functools.partial(load_kernel, count),
        out_shape=tuple(pltpu.VMEM(w.shape, w.dtype) for w in weights),
        in_specs=[HBM] * count + [pl.BlockSpec(memory_space=pl.ANY)] * len(after),
        out_specs=(VMEM,) * count,
        scratch_shapes=[pltpu.SemaphoreType.DMA((count,))],
        compiler_params=params(2),
        cost_estimate=SMALL,
        name="load_weights",
    )(*map(in_hbm, weights), *after)


def expert_kernel(depth, chunk, count, *refs):
    block_refs, (gate_ref, up_ref, down_ref) = refs[:count], refs[count : count + 3]
    mine_ref, *theirs_refs, x_buf, act_buf = refs[count + 3 :]
    width, hidden = gate_ref.shape[1:]
    extended = x_buf.shape[1]
    start = 0
    for ref in block_refs:
        rows = ref.shape[0]
        x_buf[start : start + rows, :] = ref[:, :extended]
        start += rows
    meta = x_buf[:, width:].astype(jnp.float32)
    lane = lax.broadcasted_iota(jnp.int32, meta.shape, 1)
    chip = lax.axis_index("expert")
    expert = 2 * chip + lax.axis_index("tensor")
    chosen = (lane == expert) | (lane == expert + META // 2)
    route = 0.5 * jnp.sum(jnp.where(chosen, meta, 0.0), axis=1, keepdims=True)
    for i in range(hidden // chunk):
        cols = pl.ds(i * chunk, chunk)
        x = x_buf[:, :width]
        gate = jnp.dot(x, gate_ref[0, :, cols], preferred_element_type=jnp.float32)
        up = jnp.dot(x, up_ref[0, :, cols], preferred_element_type=jnp.float32)
        act = gate * (1.0 + jnp.tanh(0.5 * gate)) * (up * route)
        act_buf[:, i * chunk : (i + 1) * chunk] = act.astype(jnp.bfloat16)
    sub = width // (PLANE * depth)
    part = sub * depth
    half = mine_ref.shape[0]
    plane = chip % PLANE
    for d in range(PLANE):
        weight = jnp.concatenate(
            [down_ref[0, :, lanes((z * PLANE + (plane ^ d)) * sub, sub)] for z in range(depth)],
            axis=1,
        )
        out = jnp.dot(act_buf[...], weight, preferred_element_type=jnp.float32)
        cols = slice(d * part, (d + 1) * part)
        mine_ref[:, cols] = out[:half].astype(jnp.bfloat16)
        start = half
        for ref in theirs_refs:
            stop = start + ref.shape[0]
            ref[:, cols] = out[start:stop].astype(jnp.bfloat16)
            start = stop


def experts(blocks, weights, depth, pieces):
    width, hidden = weights[0].shape[1:]
    chunk = 256
    extended = width + META
    total = sum(block.shape[0] for block in blocks)
    rows = [total // 2] + [total // 2 // pieces] * pieces
    return pl.pallas_call(
        functools.partial(expert_kernel, depth, chunk, len(blocks)),
        out_shape=tuple(pltpu.VMEM((size, width), jnp.bfloat16) for size in rows),
        in_specs=[VMEM] * (len(blocks) + 3),
        out_specs=(VMEM,) * (1 + pieces),
        scratch_shapes=[
            pltpu.VMEM((total, extended), jnp.bfloat16),
            pltpu.VMEM((total, hidden), jnp.bfloat16),
        ],
        compiler_params=params(16),
        cost_estimate=pl.CostEstimate(
            flops=6 * total * width * hidden, bytes_accessed=0, transcendentals=0
        ),
        name="experts",
    )(*blocks, *weights)


def chip_sum_kernel(depth, count, first_ref, *refs):
    mine, theirs, out_refs = refs[:2], refs[2 : 2 + count], refs[2 + count :]
    part = out_refs[0].shape[1]
    sub = part // depth
    held = first_ref.shape[0]
    plane = lax.axis_index("expert") % PLANE
    start = 0
    for own_ref in mine:
        first = start
        while start < first + own_ref.shape[0]:
            ref, theirs = theirs[0], theirs[1:]
            size = ref.shape[0]
            own = slice(start - first, start - first + size)
            for d, out_ref in enumerate(out_refs):
                at = slice(d * part, (d + 1) * part)
                total = own_ref[own, at].astype(jnp.float32) + ref[:, at].astype(jnp.float32)
                if start == 0:
                    residual = jnp.concatenate(
                        [
                            first_ref[:, lanes((z * PLANE + (plane ^ d)) * sub, sub)]
                            for z in range(depth)
                        ],
                        axis=1,
                    )
                    with_first = total[:held] + residual.astype(jnp.float32)
                    total = jnp.concatenate([with_first, total[held:]], axis=0)
                out_ref[start : start + size, :] = total.astype(jnp.bfloat16)
            start += size


def chip_sum(mine, theirs, first, depth):
    rows, width = sum(value.shape[0] for value in mine), mine[0].shape[1]
    return pl.pallas_call(
        functools.partial(chip_sum_kernel, depth, len(theirs)),
        out_shape=(pltpu.VMEM((rows, width // PLANE), jnp.bfloat16),) * PLANE,
        in_specs=[VMEM] * (3 + len(theirs)),
        out_specs=(VMEM,) * PLANE,
        compiler_params=params(4),
        name="chip_sum",
    )(first, *mine, *theirs)


def plane_sum_kernel(depth, *refs):
    in_refs, out_refs = refs[:PLANE], refs[PLANE:]
    group = in_refs[0].shape[0] // PLANE
    rows = group // depth
    for k in range(PLANE):
        for z in range(depth):
            total = 0.0
            for d in range(PLANE):
                start = (k ^ d) * group + z * rows
                total = total + in_refs[d][start : start + rows, :].astype(jnp.float32)
            out_refs[z][k * rows : (k + 1) * rows, :] = total.astype(jnp.bfloat16)


def plane_sum(parts, depth):
    rows, part = parts[0].shape
    return pl.pallas_call(
        functools.partial(plane_sum_kernel, depth),
        out_shape=(pltpu.VMEM((rows // depth, part), jnp.bfloat16),) * depth,
        in_specs=[VMEM] * PLANE,
        out_specs=(VMEM,) * depth,
        compiler_params=params(4),
        name="plane_sum",
    )(*parts)


def second_norm_kernel(depth, *refs):
    parts, (gain_ref, scaled_ref, next_ref) = refs[:depth], refs[depth:]
    rows, part = next_ref.shape
    sub = part // depth
    plane = lax.axis_index("expert") % PLANE
    gain = jnp.concatenate(
        [gain_ref[:, lanes((z * PLANE + plane) * sub, sub)] for z in range(depth)], axis=1
    )
    total = parts[0][...].astype(jnp.float32)
    for ref in parts[1:]:
        total = total + ref[...].astype(jnp.float32)
    following = total.astype(jnp.bfloat16)
    next_ref[...] = following
    wide = following.astype(jnp.float32)
    scaled_ref[:, :part] = (wide * gain).astype(jnp.bfloat16)
    squares = jnp.sum(wide * wide, axis=1, keepdims=True)
    high = squares.astype(jnp.bfloat16).astype(jnp.float32)
    lane = lax.broadcasted_iota(jnp.int32, (rows, META), 1)
    scaled_ref[:, part:] = jnp.where(
        lane == 0, high, jnp.where(lane == 1, squares - high, 0.0)
    ).astype(jnp.bfloat16)


def second_norm(parts, gain):
    depth = len(parts)
    rows, part = parts[0].shape
    return pl.pallas_call(
        functools.partial(second_norm_kernel, depth),
        out_shape=(
            pltpu.VMEM((rows, part + META), jnp.bfloat16),
            pltpu.VMEM((rows, part), jnp.bfloat16),
        ),
        in_specs=[VMEM] * (depth + 1),
        out_specs=(VMEM, VMEM),
        compiler_params=params(4),
        name="second_norm",
    )(*parts, gain)


def projection_kernel(chunk, mine_ref, theirs_ref, next_ref, q_ref, *refs):
    kv_refs, out_refs, kv_buf = refs[: -PLANE - 1], refs[-PLANE - 1 : -1], refs[-1]
    depth = len(kv_refs)
    rows, extended = mine_ref.shape
    part = extended - META
    sub = part // depth
    q_cols, kv_cols = q_ref.shape[1], kv_buf.shape[1]
    cols = q_cols + kv_cols
    line = lax.axis_index("expert") // PLANE
    for d, ref in enumerate(kv_refs):
        kv_buf[lanes((line ^ d) * sub, sub), :] = ref[...]
    block = rows // PLANE
    tensor = lax.axis_index("tensor")
    own = lanes(tensor * block, block)
    other = lanes((1 - tensor) * block, block)
    for d in range(PLANE):
        at = slice(d * block, (d + 1) * block)
        out_refs[d][own, cols : cols + META] = mine_ref[at, part:]
        out_refs[d][other, cols : cols + META] = theirs_ref[at, part:]
        out_refs[d][:block, cols + META :] = next_ref[at, : part // 2]
        out_refs[d][block:, cols + META :] = next_ref[at, part // 2 :]
    both = jnp.concatenate([mine_ref[:, :part], theirs_ref[:, :part]], axis=0)

    def multiply(weight, target):
        product = jnp.dot(both, weight, preferred_element_type=jnp.float32).astype(jnp.bfloat16)
        at = slice(target, target + weight.shape[1])
        for d in range(PLANE):
            out_refs[d][own, at] = product[d * block : (d + 1) * block]
            out_refs[d][other, at] = product[rows + d * block : rows + (d + 1) * block]

    multiply(kv_buf[...], q_cols)
    for start in range(0, q_cols, chunk):
        multiply(q_ref[:, start : start + chunk], start)


def projection(mine, theirs, following, q_weight, kv_weights):
    rows, part = following.shape
    q_cols, kv_cols = q_weight.shape[1], kv_weights[0].shape[1]
    chunk = 512
    shape = pltpu.VMEM((2 * rows // PLANE, q_cols + kv_cols + META + part // 2), jnp.bfloat16)
    return pl.pallas_call(
        functools.partial(projection_kernel, chunk),
        out_shape=(shape,) * PLANE,
        in_specs=[VMEM] * (4 + len(kv_weights)),
        out_specs=(VMEM,) * PLANE,
        scratch_shapes=[pltpu.VMEM((part, kv_cols), jnp.bfloat16)],
        compiler_params=params(8),
        cost_estimate=SMALL,
        name="qkv_projection",
    )(mine, theirs, following, q_weight, *kv_weights)


def head_norm_kernel(depth, *refs):
    parts, q_gain_ref, k_gain_ref = refs[:PLANE], refs[PLANE], refs[PLANE + 1]
    next_ref, q_ref, kv_ref = refs[PLANE + 2 :]
    width = next_ref.shape[1]
    q_cols, kv_cols = q_ref.shape[1], kv_ref.shape[1]
    cols = q_cols + kv_cols
    head = q_gain_ref.shape[1]

    def total(at):
        value = parts[0][:, at].astype(jnp.float32)
        for ref in parts[1:]:
            value = value + ref[:, at].astype(jnp.float32)
        return value

    squares = jnp.sum(total(slice(cols, cols + META)), axis=1, keepdims=True)
    scale = lax.rsqrt(squares / width + EPSILON)
    for h in range(q_cols // head):
        at = slice(h * head, (h + 1) * head)
        q_ref[:, at] = normalize(total(at) * scale, q_gain_ref[...]).astype(jnp.bfloat16)
    tensor = lax.axis_index("tensor")
    for h in range(kv_cols // head):
        at = slice(h * head, (h + 1) * head)
        raw = total(slice(q_cols + h * head, q_cols + (h + 1) * head)) * scale
        is_key = tensor * (kv_cols // head) + h < KV_HEADS
        kv_ref[:, at] = jnp.where(is_key, normalize(raw, k_gain_ref[...]), raw).astype(
            jnp.bfloat16
        )
    plane = lax.axis_index("expert") % PLANE
    rows = next_ref.shape[0]
    sub = width // (PLANE * depth)
    for d in range(PLANE):
        for z in range(depth):
            top = z * sub * 2 // (depth * sub)
            start = cols + META + z * sub - top * (depth * sub // 2)
            next_ref[:, lanes((z * PLANE + (plane ^ d)) * sub, sub)] = parts[d][
                top * rows : (top + 1) * rows, start : start + sub
            ]


def head_norm(parts, q_gain, k_gain, q_cols, kv_cols, rows, width, depth):
    both = parts[0].shape[0]
    return pl.pallas_call(
        functools.partial(head_norm_kernel, depth),
        out_shape=(
            jax.ShapeDtypeStruct((rows, width), jnp.bfloat16),
            jax.ShapeDtypeStruct((both, q_cols), jnp.bfloat16),
            jax.ShapeDtypeStruct((both, kv_cols), jnp.bfloat16),
        ),
        in_specs=[VMEM] * (PLANE + 2),
        out_specs=(VMEM, VMEM, VMEM),
        compiler_params=params(4),
        name="head_norm",
    )(*parts, q_gain, k_gain)


def per_device_dense(
    attn_out,
    out_weight,
    residual,
    attn_gain,
    expert_ids,
    route_weights,
    w_gate,
    w_up,
    w_down,
    input_gain,
    q_weight,
    kv_weight,
    q_gain,
    k_gain,
):
    n_expert = lax.axis_size("expert")
    depth = n_expert // PLANE
    rows, width = residual.shape
    tensor_index = lax.axis_index("tensor").astype(jnp.int32)

    def to_core(value):
        return lax.ppermute(value, "tensor", [(0, 1), (1, 0)])

    def to_expert(value, offset):
        return lax.ppermute(value, "expert", [(i, i ^ offset) for i in range(n_expert)])

    def to_z(values):
        return [to_expert(v, d * PLANE) if d else v for d, v in enumerate(values)]

    def to_plane(values):
        return [to_expert(v, d) if d else v for d, v in enumerate(values)]

    own_ids = lax.dynamic_slice_in_dim(expert_ids, tensor_index * rows, rows, 0)
    own_route = lax.dynamic_slice_in_dim(route_weights, tensor_index * rows, rows, 0)
    chosen = own_ids[:, :, None] == jnp.arange(META // 2, dtype=jnp.int32)[None, None, :]
    dense = jnp.sum(jnp.where(chosen, own_route[:, :, None], 0.0), axis=1)
    high = lax.reduce_precision(dense, 8, 7)
    meta = jnp.concatenate([high, dense - high], axis=1).astype(jnp.bfloat16)

    lines = [list(range(i, n_expert, PLANE)) for i in range(PLANE)]
    mine, theirs = out_projection(attn_out, out_weight)
    tokens, first = first_norm(mine, to_core(theirs), residual, attn_gain[None, :], meta)
    tokens, q_own = lax.optimization_barrier((tokens, q_weight))
    q_rows = lax.all_gather(q_own, "expert", axis=0, tiled=True, axis_index_groups=lines)
    weights = load((w_gate, w_up, w_down), (tokens,))
    line = to_z([tokens] * depth)
    *line, gate, up, down = lax.optimization_barrier((*line, *weights))
    weights = (gate, up, down)
    near = to_plane([pack(line)] * (PLANE - 1))
    cut = near[0].shape[0] // 2
    one, two = near[1][:cut], near[2][cut:]
    far = [to_expert(one, 2), to_expert(two, 1)]
    near_mine, *near_theirs = experts((*near, *map(to_core, near)), weights, depth, 2)
    theirs = list(map(to_core, near_theirs))
    near_mine, *far = lax.optimization_barrier((near_mine, *far))
    far_both = [*far, *map(to_core, far)]
    far_mine, *far_theirs = experts(far_both, weights, depth, 1)
    theirs += map(to_core, far_theirs)
    *sums, kv_own = lax.optimization_barrier((*chip_sum((near_mine, far_mine), theirs, first, depth), kv_weight))
    parts = to_plane(sums)
    kv_rows = [kv_own, to_expert(kv_own, PLANE), to_expert(kv_own, 2 * PLANE)]
    parts = plane_sum(parts, depth)
    kv_rows.append(to_expert(kv_rows[2], PLANE))
    (q_rows,) = load((q_rows,), (*parts, *kv_rows[1:3]))
    parts = to_z(parts)
    *parts, q_rows = lax.optimization_barrier((*parts, q_rows))
    scaled, following = second_norm(parts, input_gain[None, :])
    products = to_plane(projection(scaled, to_core(scaled), following, q_rows, kv_rows))
    return head_norm(
        products,
        q_gain[None, :],
        k_gain[None, :],
        q_weight.shape[1],
        kv_weight.shape[1],
        rows,
        width,
        depth,
    )


def per_device(
    attn_out,
    out_weight,
    residual,
    attn_gain,
    expert_ids,
    route_weights,
    w_gate,
    w_up,
    w_down,
    input_gain,
    q_weight,
    kv_weight,
    q_gain,
    k_gain,
):
    n_expert = lax.axis_size("expert")
    n_tensor = lax.axis_size("tensor")
    share = n_tensor // 2
    tensor_index = lax.axis_index("tensor")
    group_rows = attn_out.shape[0]
    width = residual.shape[1]
    half = tensor_index // share
    capacity = 3 * group_rows * TOP // (4 * n_expert)
    all_experts = 2 * n_expert
    attn_rows = lax.psum_scatter(
        jnp.dot(attn_out, out_weight, preferred_element_type=jnp.float32),
        "tensor",
        scatter_dimension=0,
        tiled=True,
    )
    first_residual = (residual.astype(jnp.float32) + attn_rows).astype(jnp.bfloat16)
    normed = normalize(first_residual.astype(jnp.float32), attn_gain).astype(jnp.bfloat16)
    group_normed = lax.all_gather(normed, "tensor", axis=0, tiled=True)
    flat_ids = expert_ids.reshape(-1)
    onehot = (flat_ids[:, None] == jnp.arange(all_experts, dtype=jnp.int32)[None, :]).astype(
        jnp.int32
    )
    earlier = jnp.cumsum(onehot, axis=0) - onehot
    rank = jnp.sum(earlier * onehot, axis=1)
    dest = flat_ids * capacity + rank
    row_owner = jnp.arange(flat_ids.shape[0], dtype=jnp.int32) // TOP
    slot_row = jnp.full((all_experts * capacity,), group_rows, jnp.int32).at[dest].set(row_owner)
    slot_weight = (
        jnp.zeros((all_experts * capacity,), jnp.float32).at[dest].set(route_weights.reshape(-1))
    )
    own_slots = lax.dynamic_index_in_dim(
        slot_row.reshape(n_expert, 2, capacity), half, 1, keepdims=False
    )
    own_weights = lax.dynamic_index_in_dim(
        slot_weight.reshape(n_expert, 2, capacity), half, 1, keepdims=False
    )
    padded_rows = jnp.concatenate([group_normed, jnp.zeros((1, width), jnp.bfloat16)], axis=0)
    gate_w = w_gate[0]
    up_w = w_up[0]
    down_w = w_down[0]
    outgoing = jnp.take(padded_rows, own_slots, axis=0)
    arrived = lax.all_to_all(outgoing, "expert", split_axis=0, concat_axis=0, tiled=True)
    flat = arrived.reshape(-1, width)
    gate = jnp.dot(flat, gate_w, preferred_element_type=jnp.float32)
    up = jnp.dot(flat, up_w, preferred_element_type=jnp.float32)
    act = (jax.nn.silu(gate) * up).astype(jnp.bfloat16)
    part = jnp.dot(act, down_w, preferred_element_type=jnp.float32).astype(jnp.bfloat16)
    send_part = part.reshape(arrived.shape)
    returned = lax.all_to_all(send_part, "expert", split_axis=0, concat_axis=0, tiled=True)
    weighted = own_weights.reshape(-1)[:, None] * returned.reshape(-1, width).astype(jnp.float32)
    term = (
        jnp.zeros((group_rows + 1, width), jnp.float32)
        .at[own_slots.reshape(-1)]
        .add(weighted)[:group_rows]
    )
    expert_sum = lax.psum_scatter(
        term.astype(jnp.bfloat16), "tensor", scatter_dimension=0, tiled=True
    ).astype(jnp.float32)
    next_residual = (first_residual.astype(jnp.float32) + expert_sum).astype(jnp.bfloat16)
    own_normed = normalize(next_residual.astype(jnp.float32), input_gain).astype(jnp.bfloat16)
    next_normed = lax.all_gather(own_normed, "tensor", axis=0, tiled=True)
    query_cols = q_weight.shape[1]
    kv_cols = kv_weight.shape[1]
    query_raw = jnp.dot(
        next_normed,
        lax.all_gather(q_weight, "expert", axis=0, tiled=True),
        preferred_element_type=jnp.float32,
    )
    kv_raw = jnp.dot(
        next_normed,
        lax.all_gather(kv_weight, "expert", axis=0, tiled=True),
        preferred_element_type=jnp.float32,
    )
    head_size = q_gain.shape[0]
    queries = (
        normalize(query_raw.reshape(group_rows, -1, head_size), q_gain)
        .reshape(group_rows, query_cols)
        .astype(jnp.bfloat16)
    )
    heads_here = kv_cols // head_size
    head_number = tensor_index * heads_here + jnp.arange(heads_here, dtype=jnp.int32)
    is_key = head_number < KV_HEADS
    kv_shaped = kv_raw.reshape(group_rows, heads_here, head_size)
    keys_values = (
        jnp.where(is_key[None, :, None], normalize(kv_shaped, k_gain), kv_shaped)
        .reshape(group_rows, kv_cols)
        .astype(jnp.bfloat16)
    )
    return (next_residual, queries, keys_values)


def solution(mesh):
    small = mesh.shape["tensor"] == 2 and mesh.shape["expert"] == 4 * PLANE
    return jax.shard_map(
        per_device_dense if small else per_device,
        mesh=mesh,
        in_specs=(
            P("expert", "tensor"),
            P("tensor", None),
            P(("expert", "tensor"), None),
            P(),
            P("expert", None),
            P("expert", None),
            P("expert", None, "tensor"),
            P("expert", None, "tensor"),
            P("expert", "tensor", None),
            P(),
            P("expert", "tensor"),
            P("expert", "tensor"),
            P(),
            P(),
        ),
        out_specs=(P(("expert", "tensor"), None), P("expert", "tensor"), P("expert", "tensor")),
        check_vma=False,
    )
```

```python
import functools

import jax
import jax.numpy as jnp
from jax import lax
from jax.experimental import pallas as pl
from jax.experimental.pallas import tpu as pltpu
from jax.sharding import PartitionSpec as P

KV_HEADS = 4
TOP = 8
PLANE = 4
META = 128


EPSILON = 1e-06

SMALL = pl.CostEstimate(flops=0, bytes_accessed=0, transcendentals=0)
VMEM = pl.BlockSpec(memory_space=pltpu.VMEM)
HBM = pl.BlockSpec(memory_space=pltpu.HBM)


def normalize(values, gain):
    return values * lax.rsqrt(jnp.mean(values * values, axis=-1, keepdims=True) + EPSILON) * gain


def params(mebibytes):
    return pltpu.CompilerParams(vmem_limit_bytes=mebibytes << 20)


def far_first(values):
    return [values[0], *reversed(values[1:])]


def lanes(start, size):
    return pl.ds(pl.multiple_of(start, size), size)


def in_hbm(value):
    return pltpu.with_memory_space_constraint(value, pltpu.HBM)


def in_vmem(value):
    return pltpu.with_memory_space_constraint(value, pltpu.VMEM)


def out_projection_kernel(chunk, a_hbm, w_hbm, mine_ref, theirs_ref, a_buf, w_buf, a_sem, sems):
    depth = w_buf.shape[0]
    count = depth // chunk
    half = mine_ref.shape[0]
    a_copy = pltpu.make_async_copy(a_hbm, a_buf, a_sem)
    a_copy.start()
    copies = []
    for i in range(count):
        rows = pl.ds(i * chunk, chunk)
        copies.append(pltpu.make_async_copy(w_hbm.at[rows], w_buf.at[rows], sems.at[i]))
    for copy in copies:
        copy.start()
    tensor = lax.axis_index("tensor")
    own = lanes(tensor * half, half)
    other = lanes((1 - tensor) * half, half)
    a_copy.wait()
    for i in range(count):
        copies[i].wait()
        at = pl.ds(i * chunk, chunk)
        both = jnp.concatenate([a_buf[own, at], a_buf[other, at]], axis=0)
        product = jnp.dot(both, w_buf[at, :], preferred_element_type=jnp.float32)
        if i == 0:
            mine_ref[...] = product[:half]
            theirs_ref[...] = product[half:]
        else:
            mine_ref[...] += product[:half]
            theirs_ref[...] += product[half:]


def out_projection(attn_out, out_weight):
    rows, depth = attn_out.shape
    width = out_weight.shape[1]
    chunk = 512
    half = pltpu.VMEM((rows // 2, width), jnp.float32)
    return pl.pallas_call(
        functools.partial(out_projection_kernel, chunk),
        out_shape=(half, half),
        in_specs=[HBM, HBM],
        out_specs=(VMEM, VMEM),
        scratch_shapes=[
            pltpu.VMEM((rows, depth), jnp.bfloat16),
            pltpu.VMEM((depth, width), jnp.bfloat16),
            pltpu.SemaphoreType.DMA,
            pltpu.SemaphoreType.DMA((depth // chunk,)),
        ],
        compiler_params=params(14),
        cost_estimate=SMALL,
        name="out_projection",
    )(in_hbm(attn_out), in_hbm(out_weight))


def first_norm_kernel(mine_ref, theirs_ref, residual_ref, gain_ref, meta_ref, tokens_ref, first_ref):
    width = residual_ref.shape[1]
    first = (residual_ref[...].astype(jnp.float32) + (mine_ref[...] + theirs_ref[...])).astype(
        jnp.bfloat16
    )
    first_ref[...] = first
    tokens_ref[:, :width] = normalize(first.astype(jnp.float32), gain_ref[...]).astype(jnp.bfloat16)
    tokens_ref[:, width:] = meta_ref[...]


def first_norm(mine, theirs, residual, gain, meta):
    rows, width = residual.shape
    return pl.pallas_call(
        first_norm_kernel,
        out_shape=(
            pltpu.VMEM((rows, width + META), jnp.bfloat16),
            pltpu.VMEM((rows, width), jnp.bfloat16),
        ),
        in_specs=[VMEM] * 5,
        out_specs=(VMEM, VMEM),
        compiler_params=params(2),
        name="first_norm",
    )(mine, theirs, residual, gain, meta)


def pack_kernel(depth, *refs):
    line, out_ref = far_first(refs[:depth]), refs[depth]
    rows = line[0].shape[0]
    for z in range(depth):
        out_ref[z * rows : (z + 1) * rows, :] = line[z][...]


def pack(line):
    depth = len(line)
    rows, extended = line[0].shape
    return pl.pallas_call(
        functools.partial(pack_kernel, depth),
        out_shape=pltpu.VMEM((depth * rows, extended), jnp.bfloat16),
        in_specs=[VMEM] * depth,
        out_specs=VMEM,
        compiler_params=params(2),
        name="pack_tokens",
    )(*far_first(line))


def load_kernel(count, *refs):
    sources, targets, sems = refs[:count], refs[-count - 1 : -1], refs[-1]
    copies = [
        pltpu.make_async_copy(source, target, sems.at[i])
        for i, (source, target) in enumerate(zip(sources, targets))
    ]
    for copy in copies:
        copy.start()
    for copy in copies:
        copy.wait()


def load(weights, after):
    count = len(weights)
    return pl.pallas_call(
        functools.partial(load_kernel, count),
        out_shape=tuple(pltpu.VMEM(w.shape, w.dtype) for w in weights),
        in_specs=[HBM] * count + [pl.BlockSpec(memory_space=pl.ANY)] * len(after),
        out_specs=(VMEM,) * count,
        scratch_shapes=[pltpu.SemaphoreType.DMA((count,))],
        compiler_params=params(2),
        cost_estimate=SMALL,
        name="load_weights",
    )(*map(in_hbm, weights), *after)


def expert_kernel(depth, chunk, count, *refs):
    block_refs, (gate_ref, up_ref, down_ref) = refs[:count], refs[count : count + 3]
    mine_ref, *theirs_refs, x_buf, act_buf = refs[count + 3 :]
    width, hidden = gate_ref.shape[1:]
    extended = x_buf.shape[1]
    start = 0
    for ref in block_refs:
        rows = ref.shape[0]
        x_buf[start : start + rows, :] = ref[:, :extended]
        start += rows
    meta = x_buf[:, width:].astype(jnp.float32)
    lane = lax.broadcasted_iota(jnp.int32, meta.shape, 1)
    chip = lax.axis_index("expert")
    expert = 2 * chip + lax.axis_index("tensor")
    chosen = (lane == expert) | (lane == expert + META // 2)
    route = 0.5 * jnp.sum(jnp.where(chosen, meta, 0.0), axis=1, keepdims=True)
    for i in range(hidden // chunk):
        cols = pl.ds(i * chunk, chunk)
        x = x_buf[:, :width]
        gate = jnp.dot(x, gate_ref[0, :, cols], preferred_element_type=jnp.float32)
        up = jnp.dot(x, up_ref[0, :, cols], preferred_element_type=jnp.float32)
        act = gate * (1.0 + jnp.tanh(0.5 * gate)) * (up * route)
        act_buf[:, i * chunk : (i + 1) * chunk] = act.astype(jnp.bfloat16)
    sub = width // (PLANE * depth)
    part = sub * depth
    half = mine_ref.shape[0]
    plane = chip % PLANE
    for d in range(PLANE):
        weight = jnp.concatenate(
            [down_ref[0, :, lanes((z * PLANE + (plane ^ d)) * sub, sub)] for z in range(depth)],
            axis=1,
        )
        out = jnp.dot(act_buf[...], weight, preferred_element_type=jnp.float32)
        cols = slice(d * part, (d + 1) * part)
        mine_ref[:, cols] = out[:half].astype(jnp.bfloat16)
        start = half
        for ref in theirs_refs:
            stop = start + ref.shape[0]
            ref[:, cols] = out[start:stop].astype(jnp.bfloat16)
            start = stop


def experts(blocks, weights, depth, pieces):
    width, hidden = weights[0].shape[1:]
    chunk = 256
    extended = width + META
    total = sum(block.shape[0] for block in blocks)
    rows = [total // 2] + [total // 2 // pieces] * pieces
    return pl.pallas_call(
        functools.partial(expert_kernel, depth, chunk, len(blocks)),
        out_shape=tuple(pltpu.VMEM((size, width), jnp.bfloat16) for size in rows),
        in_specs=[VMEM] * (len(blocks) + 3),
        out_specs=(VMEM,) * (1 + pieces),
        scratch_shapes=[
            pltpu.VMEM((total, extended), jnp.bfloat16),
            pltpu.VMEM((total, hidden), jnp.bfloat16),
        ],
        compiler_params=params(16),
        cost_estimate=pl.CostEstimate(
            flops=6 * total * width * hidden, bytes_accessed=0, transcendentals=0
        ),
        name="experts",
    )(*blocks, *weights)


def chip_sum_kernel(depth, count, first_ref, *refs):
    mine, theirs, out_refs = refs[:2], refs[2 : 2 + count], refs[2 + count :]
    part = out_refs[0].shape[1]
    sub = part // depth
    held = first_ref.shape[0]
    plane = lax.axis_index("expert") % PLANE
    start = 0
    for own_ref in mine:
        first = start
        while start < first + own_ref.shape[0]:
            ref, theirs = theirs[0], theirs[1:]
            size = ref.shape[0]
            own = slice(start - first, start - first + size)
            for d, out_ref in enumerate(out_refs):
                at = slice(d * part, (d + 1) * part)
                total = own_ref[own, at].astype(jnp.float32) + ref[:, at].astype(jnp.float32)
                if start == 0:
                    residual = jnp.concatenate(
                        [
                            first_ref[:, lanes((z * PLANE + (plane ^ d)) * sub, sub)]
                            for z in range(depth)
                        ],
                        axis=1,
                    )
                    with_first = total[:held] + residual.astype(jnp.float32)
                    total = jnp.concatenate([with_first, total[held:]], axis=0)
                out_ref[start : start + size, :] = total.astype(jnp.bfloat16)
            start += size


def chip_sum(mine, theirs, first, depth):
    rows, width = sum(value.shape[0] for value in mine), mine[0].shape[1]
    return pl.pallas_call(
        functools.partial(chip_sum_kernel, depth, len(theirs)),
        out_shape=(pltpu.VMEM((rows, width // PLANE), jnp.bfloat16),) * PLANE,
        in_specs=[VMEM] * (3 + len(theirs)),
        out_specs=(VMEM,) * PLANE,
        compiler_params=params(4),
        name="chip_sum",
    )(first, *mine, *theirs)


def plane_sum_kernel(depth, *refs):
    in_refs, out_refs = refs[:PLANE], refs[PLANE:]
    group = in_refs[0].shape[0] // PLANE
    rows = group // depth
    for k in range(PLANE):
        for z in range(depth):
            total = 0.0
            for d in range(PLANE):
                start = (k ^ d) * group + z * rows
                total = total + in_refs[d][start : start + rows, :].astype(jnp.float32)
            out_refs[z][k * rows : (k + 1) * rows, :] = total.astype(jnp.bfloat16)


def plane_sum(parts, depth):
    rows, part = parts[0].shape
    return pl.pallas_call(
        functools.partial(plane_sum_kernel, depth),
        out_shape=(pltpu.VMEM((rows // depth, part), jnp.bfloat16),) * depth,
        in_specs=[VMEM] * PLANE,
        out_specs=(VMEM,) * depth,
        compiler_params=params(4),
        name="plane_sum",
    )(*parts)


def second_norm_kernel(depth, *refs):
    parts, (gain_ref, scaled_ref, next_ref) = refs[:depth], refs[depth:]
    rows, part = next_ref.shape
    sub = part // depth
    plane = lax.axis_index("expert") % PLANE
    gain = jnp.concatenate(
        [gain_ref[:, lanes((z * PLANE + plane) * sub, sub)] for z in range(depth)], axis=1
    )
    total = parts[0][...].astype(jnp.float32)
    for ref in parts[1:]:
        total = total + ref[...].astype(jnp.float32)
    following = total.astype(jnp.bfloat16)
    next_ref[...] = following
    wide = following.astype(jnp.float32)
    scaled_ref[:, :part] = (wide * gain).astype(jnp.bfloat16)
    squares = jnp.sum(wide * wide, axis=1, keepdims=True)
    high = squares.astype(jnp.bfloat16).astype(jnp.float32)
    lane = lax.broadcasted_iota(jnp.int32, (rows, META), 1)
    scaled_ref[:, part:] = jnp.where(
        lane == 0, high, jnp.where(lane == 1, squares - high, 0.0)
    ).astype(jnp.bfloat16)


def second_norm(parts, gain):
    depth = len(parts)
    rows, part = parts[0].shape
    return pl.pallas_call(
        functools.partial(second_norm_kernel, depth),
        out_shape=(
            pltpu.VMEM((rows, part + META), jnp.bfloat16),
            pltpu.VMEM((rows, part), jnp.bfloat16),
        ),
        in_specs=[VMEM] * (depth + 1),
        out_specs=(VMEM, VMEM),
        compiler_params=params(4),
        name="second_norm",
    )(*far_first(parts), gain)


def projection_kernel(chunk, mine_ref, theirs_ref, next_ref, q_ref, *refs):
    kv_refs, out_refs, kv_buf = refs[: -PLANE - 1], refs[-PLANE - 1 : -1], refs[-1]
    depth = len(kv_refs)
    rows, extended = mine_ref.shape
    part = extended - META
    sub = part // depth
    q_cols, kv_cols = q_ref.shape[1], kv_buf.shape[1]
    cols = q_cols + kv_cols
    line = lax.axis_index("expert") // PLANE
    for d, ref in enumerate(kv_refs):
        kv_buf[lanes((line ^ d) * sub, sub), :] = ref[...]
    block = rows // PLANE
    tensor = lax.axis_index("tensor")
    own = lanes(tensor * block, block)
    other = lanes((1 - tensor) * block, block)
    for d in range(PLANE):
        at = slice(d * block, (d + 1) * block)
        out_refs[d][own, cols : cols + META] = mine_ref[at, part:]
        out_refs[d][other, cols : cols + META] = theirs_ref[at, part:]
        out_refs[d][:block, cols + META :] = next_ref[at, : part // 2]
        out_refs[d][block:, cols + META :] = next_ref[at, part // 2 :]
    both = jnp.concatenate([mine_ref[:, :part], theirs_ref[:, :part]], axis=0)

    def multiply(weight, target):
        product = jnp.dot(both, weight, preferred_element_type=jnp.float32).astype(jnp.bfloat16)
        at = slice(target, target + weight.shape[1])
        for d in range(PLANE):
            out_refs[d][own, at] = product[d * block : (d + 1) * block]
            out_refs[d][other, at] = product[rows + d * block : rows + (d + 1) * block]

    multiply(kv_buf[...], q_cols)
    for start in range(0, q_cols, chunk):
        multiply(q_ref[:, start : start + chunk], start)


def projection(mine, theirs, following, q_weight, kv_weights):
    rows, part = following.shape
    q_cols, kv_cols = q_weight.shape[1], kv_weights[0].shape[1]
    chunk = 512
    shape = pltpu.VMEM((2 * rows // PLANE, q_cols + kv_cols + META + part // 2), jnp.bfloat16)
    return pl.pallas_call(
        functools.partial(projection_kernel, chunk),
        out_shape=(shape,) * PLANE,
        in_specs=[VMEM] * (4 + len(kv_weights)),
        out_specs=(VMEM,) * PLANE,
        scratch_shapes=[pltpu.VMEM((part, kv_cols), jnp.bfloat16)],
        compiler_params=params(8),
        cost_estimate=SMALL,
        name="qkv_projection",
    )(mine, theirs, following, q_weight, *kv_weights)


def head_norm_kernel(depth, *refs):
    parts, q_gain_ref, k_gain_ref = refs[:PLANE], refs[PLANE], refs[PLANE + 1]
    next_ref, q_ref, kv_ref = refs[PLANE + 2 :]
    width = next_ref.shape[1]
    q_cols, kv_cols = q_ref.shape[1], kv_ref.shape[1]
    cols = q_cols + kv_cols
    head = q_gain_ref.shape[1]

    def total(at):
        value = parts[0][:, at].astype(jnp.float32)
        for ref in parts[1:]:
            value = value + ref[:, at].astype(jnp.float32)
        return value

    squares = jnp.sum(total(slice(cols, cols + META)), axis=1, keepdims=True)
    scale = lax.rsqrt(squares / width + EPSILON)
    for h in range(q_cols // head):
        at = slice(h * head, (h + 1) * head)
        q_ref[:, at] = normalize(total(at) * scale, q_gain_ref[...]).astype(jnp.bfloat16)
    tensor = lax.axis_index("tensor")
    for h in range(kv_cols // head):
        at = slice(h * head, (h + 1) * head)
        raw = total(slice(q_cols + h * head, q_cols + (h + 1) * head)) * scale
        is_key = tensor * (kv_cols // head) + h < KV_HEADS
        kv_ref[:, at] = jnp.where(is_key, normalize(raw, k_gain_ref[...]), raw).astype(
            jnp.bfloat16
        )
    plane = lax.axis_index("expert") % PLANE
    rows = next_ref.shape[0]
    sub = width // (PLANE * depth)
    for d in range(PLANE):
        for z in range(depth):
            top = z * sub * 2 // (depth * sub)
            start = cols + META + z * sub - top * (depth * sub // 2)
            next_ref[:, lanes((z * PLANE + (plane ^ d)) * sub, sub)] = parts[d][
                top * rows : (top + 1) * rows, start : start + sub
            ]


def head_norm(parts, q_gain, k_gain, q_cols, kv_cols, rows, width, depth):
    both = parts[0].shape[0]
    return pl.pallas_call(
        functools.partial(head_norm_kernel, depth),
        out_shape=(
            jax.ShapeDtypeStruct((rows, width), jnp.bfloat16),
            jax.ShapeDtypeStruct((both, q_cols), jnp.bfloat16),
            jax.ShapeDtypeStruct((both, kv_cols), jnp.bfloat16),
        ),
        in_specs=[VMEM] * (PLANE + 2),
        out_specs=(VMEM, VMEM, VMEM),
        compiler_params=params(4),
        name="head_norm",
    )(*parts, q_gain, k_gain)


def per_device_dense(
    attn_out,
    out_weight,
    residual,
    attn_gain,
    expert_ids,
    route_weights,
    w_gate,
    w_up,
    w_down,
    input_gain,
    q_weight,
    kv_weight,
    q_gain,
    k_gain,
):
    n_expert = lax.axis_size("expert")
    depth = n_expert // PLANE
    rows, width = residual.shape
    tensor_index = lax.axis_index("tensor").astype(jnp.int32)

    def to_core(value):
        return lax.ppermute(value, "tensor", [(0, 1), (1, 0)])

    def to_expert(value, offset):
        return lax.ppermute(value, "expert", [(i, i ^ offset) for i in range(n_expert)])

    def to_z(values):
        return [to_expert(v, d * PLANE) if d else v for d, v in enumerate(values)]

    def to_plane(values):
        return [to_expert(v, d) if d else v for d, v in enumerate(values)]

    own_ids = lax.dynamic_slice_in_dim(expert_ids, tensor_index * rows, rows, 0)
    own_route = lax.dynamic_slice_in_dim(route_weights, tensor_index * rows, rows, 0)
    chosen = own_ids[:, :, None] == jnp.arange(META // 2, dtype=jnp.int32)[None, None, :]
    dense = jnp.sum(jnp.where(chosen, own_route[:, :, None], 0.0), axis=1)
    high = lax.reduce_precision(dense, 8, 7)
    meta = jnp.concatenate([high, dense - high], axis=1).astype(jnp.bfloat16)

    lines = [list(range(i, n_expert, PLANE)) for i in range(PLANE)]
    mine, theirs = out_projection(attn_out, out_weight)
    tokens, first = first_norm(mine, to_core(theirs), residual, attn_gain[None, :], meta)
    tokens, q_own = lax.optimization_barrier((tokens, q_weight))
    q_rows = lax.all_gather(q_own, "expert", axis=0, tiled=True, axis_index_groups=lines)
    weights = load((w_gate, w_up, w_down), (tokens,))
    line = to_z([tokens] * depth)
    tied = lax.optimization_barrier((*far_first(line), *weights))
    line, weights = far_first(tied[:depth]), tied[depth:]
    near = to_plane([pack(line)] * (PLANE - 1))
    cut = near[0].shape[0] // 2
    one, two = near[1][:cut], near[2][cut:]
    far = [to_expert(one, 2), to_expert(two, 1)]
    near_mine, *near_theirs = experts((*near, *map(to_core, near)), weights, depth, 2)
    theirs = list(map(to_core, near_theirs))
    near_mine, *far = lax.optimization_barrier((near_mine, *far))
    far_both = [*far, *map(to_core, far)]
    far_mine, *far_theirs = experts(far_both, weights, depth, 1)
    theirs += map(to_core, far_theirs)
    *sums, kv_own = lax.optimization_barrier((*chip_sum((near_mine, far_mine), theirs, first, depth), kv_weight))
    parts = to_plane(sums)
    kv_rows = [kv_own, to_expert(kv_own, PLANE), to_expert(kv_own, 2 * PLANE)]
    parts = plane_sum(parts, depth)
    kv_rows.append(to_expert(kv_rows[2], PLANE))
    (q_rows,) = load((q_rows,), (*parts, *kv_rows[1:3]))
    parts = to_z(parts)
    *parts, q_rows = lax.optimization_barrier((*far_first(parts), q_rows))
    parts = far_first(parts)
    scaled, following = second_norm(parts, input_gain[None, :])
    products = to_plane(projection(scaled, to_core(scaled), following, q_rows, kv_rows))
    return head_norm(
        products,
        q_gain[None, :],
        k_gain[None, :],
        q_weight.shape[1],
        kv_weight.shape[1],
        rows,
        width,
        depth,
    )


def per_device(
    attn_out,
    out_weight,
    residual,
    attn_gain,
    expert_ids,
    route_weights,
    w_gate,
    w_up,
    w_down,
    input_gain,
    q_weight,
    kv_weight,
    q_gain,
    k_gain,
):
    n_expert = lax.axis_size("expert")
    n_tensor = lax.axis_size("tensor")
    share = n_tensor // 2
    tensor_index = lax.axis_index("tensor")
    group_rows = attn_out.shape[0]
    width = residual.shape[1]
    half = tensor_index // share
    capacity = 3 * group_rows * TOP // (4 * n_expert)
    all_experts = 2 * n_expert
    attn_rows = lax.psum_scatter(
        jnp.dot(attn_out, out_weight, preferred_element_type=jnp.float32),
        "tensor",
        scatter_dimension=0,
        tiled=True,
    )
    first_residual = (residual.astype(jnp.float32) + attn_rows).astype(jnp.bfloat16)
    normed = normalize(first_residual.astype(jnp.float32), attn_gain).astype(jnp.bfloat16)
    group_normed = lax.all_gather(normed, "tensor", axis=0, tiled=True)
    flat_ids = expert_ids.reshape(-1)
    onehot = (flat_ids[:, None] == jnp.arange(all_experts, dtype=jnp.int32)[None, :]).astype(
        jnp.int32
    )
    earlier = jnp.cumsum(onehot, axis=0) - onehot
    rank = jnp.sum(earlier * onehot, axis=1)
    dest = flat_ids * capacity + rank
    row_owner = jnp.arange(flat_ids.shape[0], dtype=jnp.int32) // TOP
    slot_row = jnp.full((all_experts * capacity,), group_rows, jnp.int32).at[dest].set(row_owner)
    slot_weight = (
        jnp.zeros((all_experts * capacity,), jnp.float32).at[dest].set(route_weights.reshape(-1))
    )
    own_slots = lax.dynamic_index_in_dim(
        slot_row.reshape(n_expert, 2, capacity), half, 1, keepdims=False
    )
    own_weights = lax.dynamic_index_in_dim(
        slot_weight.reshape(n_expert, 2, capacity), half, 1, keepdims=False
    )
    padded_rows = jnp.concatenate([group_normed, jnp.zeros((1, width), jnp.bfloat16)], axis=0)
    gate_w = w_gate[0]
    up_w = w_up[0]
    down_w = w_down[0]
    outgoing = jnp.take(padded_rows, own_slots, axis=0)
    arrived = lax.all_to_all(outgoing, "expert", split_axis=0, concat_axis=0, tiled=True)
    flat = arrived.reshape(-1, width)
    gate = jnp.dot(flat, gate_w, preferred_element_type=jnp.float32)
    up = jnp.dot(flat, up_w, preferred_element_type=jnp.float32)
    act = (jax.nn.silu(gate) * up).astype(jnp.bfloat16)
    part = jnp.dot(act, down_w, preferred_element_type=jnp.float32).astype(jnp.bfloat16)
    send_part = part.reshape(arrived.shape)
    returned = lax.all_to_all(send_part, "expert", split_axis=0, concat_axis=0, tiled=True)
    weighted = own_weights.reshape(-1)[:, None] * returned.reshape(-1, width).astype(jnp.float32)
    term = (
        jnp.zeros((group_rows + 1, width), jnp.float32)
        .at[own_slots.reshape(-1)]
        .add(weighted)[:group_rows]
    )
    expert_sum = lax.psum_scatter(
        term.astype(jnp.bfloat16), "tensor", scatter_dimension=0, tiled=True
    ).astype(jnp.float32)
    next_residual = (first_residual.astype(jnp.float32) + expert_sum).astype(jnp.bfloat16)
    own_normed = normalize(next_residual.astype(jnp.float32), input_gain).astype(jnp.bfloat16)
    next_normed = lax.all_gather(own_normed, "tensor", axis=0, tiled=True)
    query_cols = q_weight.shape[1]
    kv_cols = kv_weight.shape[1]
    query_raw = jnp.dot(
        next_normed,
        lax.all_gather(q_weight, "expert", axis=0, tiled=True),
        preferred_element_type=jnp.float32,
    )
    kv_raw = jnp.dot(
        next_normed,
        lax.all_gather(kv_weight, "expert", axis=0, tiled=True),
        preferred_element_type=jnp.float32,
    )
    head_size = q_gain.shape[0]
    queries = (
        normalize(query_raw.reshape(group_rows, -1, head_size), q_gain)
        .reshape(group_rows, query_cols)
        .astype(jnp.bfloat16)
    )
    heads_here = kv_cols // head_size
    head_number = tensor_index * heads_here + jnp.arange(heads_here, dtype=jnp.int32)
    is_key = head_number < KV_HEADS
    kv_shaped = kv_raw.reshape(group_rows, heads_here, head_size)
    keys_values = (
        jnp.where(is_key[None, :, None], normalize(kv_shaped, k_gain), kv_shaped)
        .reshape(group_rows, kv_cols)
        .astype(jnp.bfloat16)
    )
    return (next_residual, queries, keys_values)


def solution(mesh):
    small = mesh.shape["tensor"] == 2 and mesh.shape["expert"] == 4 * PLANE
    return jax.shard_map(
        per_device_dense if small else per_device,
        mesh=mesh,
        in_specs=(
            P("expert", "tensor"),
            P("tensor", None),
            P(("expert", "tensor"), None),
            P(),
            P("expert", None),
            P("expert", None),
            P("expert", None, "tensor"),
            P("expert", None, "tensor"),
            P("expert", "tensor", None),
            P(),
            P("expert", "tensor"),
            P("expert", "tensor"),
            P(),
            P(),
        ),
        out_specs=(P(("expert", "tensor"), None), P("expert", "tensor"), P("expert", "tensor")),
        check_vma=False,
    )
```

```python
import functools

import jax
import jax.numpy as jnp
from jax import lax
from jax.experimental import pallas as pl
from jax.experimental.pallas import tpu as pltpu
from jax.sharding import PartitionSpec as P

KV_HEADS = 4
TOP = 8
PLANE = 4
META = 128


EPSILON = 1e-06

SMALL = pl.CostEstimate(flops=0, bytes_accessed=0, transcendentals=0)
VMEM = pl.BlockSpec(memory_space=pltpu.VMEM)
HBM = pl.BlockSpec(memory_space=pltpu.HBM)


def normalize(values, gain):
    return values * lax.rsqrt(jnp.mean(values * values, axis=-1, keepdims=True) + EPSILON) * gain


def params(mebibytes):
    return pltpu.CompilerParams(vmem_limit_bytes=mebibytes << 20)


def far_first(values):
    return [values[0], *reversed(values[1:])]


def lanes(start, size):
    return pl.ds(pl.multiple_of(start, size), size)


def in_hbm(value):
    return pltpu.with_memory_space_constraint(value, pltpu.HBM)


def in_vmem(value):
    return pltpu.with_memory_space_constraint(value, pltpu.VMEM)


def out_projection_kernel(chunk, a_hbm, w_hbm, mine_ref, theirs_ref, a_buf, w_buf, a_sem, sems):
    depth = w_buf.shape[0]
    count = depth // chunk
    half = mine_ref.shape[0]
    a_copy = pltpu.make_async_copy(a_hbm, a_buf, a_sem)
    a_copy.start()
    copies = []
    for i in range(count):
        rows = pl.ds(i * chunk, chunk)
        copies.append(pltpu.make_async_copy(w_hbm.at[rows], w_buf.at[rows], sems.at[i]))
    for copy in copies:
        copy.start()
    tensor = lax.axis_index("tensor")
    own = lanes(tensor * half, half)
    other = lanes((1 - tensor) * half, half)
    a_copy.wait()
    for i in range(count):
        copies[i].wait()
        at = pl.ds(i * chunk, chunk)
        both = jnp.concatenate([a_buf[own, at], a_buf[other, at]], axis=0)
        product = jnp.dot(both, w_buf[at, :], preferred_element_type=jnp.float32)
        if i == 0:
            mine_ref[...] = product[:half]
            theirs_ref[...] = product[half:]
        else:
            mine_ref[...] += product[:half]
            theirs_ref[...] += product[half:]


def out_projection(attn_out, out_weight):
    rows, depth = attn_out.shape
    width = out_weight.shape[1]
    chunk = 512
    half = pltpu.VMEM((rows // 2, width), jnp.float32)
    return pl.pallas_call(
        functools.partial(out_projection_kernel, chunk),
        out_shape=(half, half),
        in_specs=[HBM, HBM],
        out_specs=(VMEM, VMEM),
        scratch_shapes=[
            pltpu.VMEM((rows, depth), jnp.bfloat16),
            pltpu.VMEM((depth, width), jnp.bfloat16),
            pltpu.SemaphoreType.DMA,
            pltpu.SemaphoreType.DMA((depth // chunk,)),
        ],
        compiler_params=params(14),
        cost_estimate=SMALL,
        name="out_projection",
    )(in_hbm(attn_out), in_hbm(out_weight))


def first_norm_kernel(mine_ref, theirs_ref, residual_ref, gain_ref, meta_ref, tokens_ref, first_ref):
    width = residual_ref.shape[1]
    first = (residual_ref[...].astype(jnp.float32) + (mine_ref[...] + theirs_ref[...])).astype(
        jnp.bfloat16
    )
    first_ref[...] = first
    tokens_ref[:, :width] = normalize(first.astype(jnp.float32), gain_ref[...]).astype(jnp.bfloat16)
    tokens_ref[:, width:] = meta_ref[...]


def first_norm(mine, theirs, residual, gain, meta):
    rows, width = residual.shape
    return pl.pallas_call(
        first_norm_kernel,
        out_shape=(
            pltpu.VMEM((rows, width + META), jnp.bfloat16),
            pltpu.VMEM((rows, width), jnp.bfloat16),
        ),
        in_specs=[VMEM] * 5,
        out_specs=(VMEM, VMEM),
        compiler_params=params(2),
        name="first_norm",
    )(mine, theirs, residual, gain, meta)


def pack_kernel(depth, *refs):
    line, out_ref = far_first(refs[:depth]), refs[depth]
    rows = line[0].shape[0]
    for z in range(depth):
        out_ref[z * rows : (z + 1) * rows, :] = line[z][...]


def pack(line):
    depth = len(line)
    rows, extended = line[0].shape
    return pl.pallas_call(
        functools.partial(pack_kernel, depth),
        out_shape=pltpu.VMEM((depth * rows, extended), jnp.bfloat16),
        in_specs=[VMEM] * depth,
        out_specs=VMEM,
        compiler_params=params(2),
        name="pack_tokens",
    )(*far_first(line))


def load_kernel(count, *refs):
    sources, targets, sems = refs[:count], refs[-count - 1 : -1], refs[-1]
    copies = [
        pltpu.make_async_copy(source, target, sems.at[i])
        for i, (source, target) in enumerate(zip(sources, targets))
    ]
    for copy in copies:
        copy.start()
    for copy in copies:
        copy.wait()


def load(weights, after):
    count = len(weights)
    return pl.pallas_call(
        functools.partial(load_kernel, count),
        out_shape=tuple(pltpu.VMEM(w.shape, w.dtype) for w in weights),
        in_specs=[HBM] * count + [pl.BlockSpec(memory_space=pl.ANY)] * len(after),
        out_specs=(VMEM,) * count,
        scratch_shapes=[pltpu.SemaphoreType.DMA((count,))],
        compiler_params=params(2),
        cost_estimate=SMALL,
        name="load_weights",
    )(*map(in_hbm, weights), *after)


def expert_kernel(depth, chunk, count, *refs):
    block_refs, (gate_ref, up_ref, down_ref) = refs[:count], refs[count : count + 3]
    mine_ref, *theirs_refs, x_buf, act_buf = refs[count + 3 :]
    width, hidden = gate_ref.shape[1:]
    extended = x_buf.shape[1]
    start = 0
    for ref in block_refs:
        rows = ref.shape[0]
        x_buf[start : start + rows, :] = ref[:, :extended]
        start += rows
    meta = x_buf[:, width:].astype(jnp.float32)
    lane = lax.broadcasted_iota(jnp.int32, meta.shape, 1)
    chip = lax.axis_index("expert")
    expert = 2 * chip + lax.axis_index("tensor")
    chosen = (lane == expert) | (lane == expert + META // 2)
    route = 0.5 * jnp.sum(jnp.where(chosen, meta, 0.0), axis=1, keepdims=True)
    for i in range(hidden // chunk):
        cols = pl.ds(i * chunk, chunk)
        x = x_buf[:, :width]
        gate = jnp.dot(x, gate_ref[0, :, cols], preferred_element_type=jnp.float32)
        up = jnp.dot(x, up_ref[0, :, cols], preferred_element_type=jnp.float32)
        act = gate * (1.0 + jnp.tanh(0.5 * gate)) * (up * route)
        act_buf[:, i * chunk : (i + 1) * chunk] = act.astype(jnp.bfloat16)
    sub = width // (PLANE * depth)
    part = sub * depth
    half = mine_ref.shape[0]
    plane = chip % PLANE
    for d in range(PLANE):
        weight = jnp.concatenate(
            [down_ref[0, :, lanes((z * PLANE + (plane ^ d)) * sub, sub)] for z in range(depth)],
            axis=1,
        )
        out = jnp.dot(act_buf[...], weight, preferred_element_type=jnp.float32)
        cols = slice(d * part, (d + 1) * part)
        mine_ref[:, cols] = out[:half].astype(jnp.bfloat16)
        start = half
        for ref in theirs_refs:
            stop = start + ref.shape[0]
            ref[:, cols] = out[start:stop].astype(jnp.bfloat16)
            start = stop


def experts(blocks, weights, depth, pieces):
    width, hidden = weights[0].shape[1:]
    chunk = 256
    extended = width + META
    total = sum(block.shape[0] for block in blocks)
    rows = [total // 2] + [total // 2 // pieces] * pieces
    return pl.pallas_call(
        functools.partial(expert_kernel, depth, chunk, len(blocks)),
        out_shape=tuple(pltpu.VMEM((size, width), jnp.bfloat16) for size in rows),
        in_specs=[VMEM] * (len(blocks) + 3),
        out_specs=(VMEM,) * (1 + pieces),
        scratch_shapes=[
            pltpu.VMEM((total, extended), jnp.bfloat16),
            pltpu.VMEM((total, hidden), jnp.bfloat16),
        ],
        compiler_params=params(16),
        cost_estimate=pl.CostEstimate(
            flops=6 * total * width * hidden, bytes_accessed=0, transcendentals=0
        ),
        name="experts",
    )(*blocks, *weights)


def chip_sum_kernel(depth, count, first_ref, *refs):
    mine, theirs, out_refs = refs[:2], refs[2 : 2 + count], refs[2 + count :]
    part = out_refs[0].shape[1]
    sub = part // depth
    held = first_ref.shape[0]
    plane = lax.axis_index("expert") % PLANE
    start = 0
    for own_ref in mine:
        first = start
        while start < first + own_ref.shape[0]:
            ref, theirs = theirs[0], theirs[1:]
            size = ref.shape[0]
            own = slice(start - first, start - first + size)
            for d, out_ref in enumerate(out_refs):
                at = slice(d * part, (d + 1) * part)
                total = own_ref[own, at].astype(jnp.float32) + ref[:, at].astype(jnp.float32)
                if start == 0:
                    residual = jnp.concatenate(
                        [
                            first_ref[:, lanes((z * PLANE + (plane ^ d)) * sub, sub)]
                            for z in range(depth)
                        ],
                        axis=1,
                    )
                    with_first = total[:held] + residual.astype(jnp.float32)
                    total = jnp.concatenate([with_first, total[held:]], axis=0)
                out_ref[start : start + size, :] = total.astype(jnp.bfloat16)
            start += size


def chip_sum(mine, theirs, first, depth):
    rows, width = sum(value.shape[0] for value in mine), mine[0].shape[1]
    return pl.pallas_call(
        functools.partial(chip_sum_kernel, depth, len(theirs)),
        out_shape=(pltpu.VMEM((rows, width // PLANE), jnp.bfloat16),) * PLANE,
        in_specs=[VMEM] * (3 + len(theirs)),
        out_specs=(VMEM,) * PLANE,
        compiler_params=params(4),
        name="chip_sum",
    )(first, *mine, *theirs)


def plane_sum_kernel(depth, *refs):
    in_refs, out_refs = refs[:PLANE], refs[PLANE:]
    group = in_refs[0].shape[0] // PLANE
    rows = group // depth
    for k in range(PLANE):
        for z in range(depth):
            total = 0.0
            for d in range(PLANE):
                start = (k ^ d) * group + z * rows
                total = total + in_refs[d][start : start + rows, :].astype(jnp.float32)
            out_refs[z][k * rows : (k + 1) * rows, :] = total.astype(jnp.bfloat16)


def plane_sum(parts, depth):
    rows, part = parts[0].shape
    return pl.pallas_call(
        functools.partial(plane_sum_kernel, depth),
        out_shape=(pltpu.VMEM((rows // depth, part), jnp.bfloat16),) * depth,
        in_specs=[VMEM] * PLANE,
        out_specs=(VMEM,) * depth,
        compiler_params=params(4),
        name="plane_sum",
    )(*parts)


def second_norm_kernel(depth, *refs):
    parts, (gain_ref, scaled_ref, next_ref) = refs[:depth], refs[depth:]
    rows, part = next_ref.shape
    sub = part // depth
    plane = lax.axis_index("expert") % PLANE
    gain = jnp.concatenate(
        [gain_ref[:, lanes((z * PLANE + plane) * sub, sub)] for z in range(depth)], axis=1
    )
    total = parts[0][...].astype(jnp.float32)
    for ref in parts[1:]:
        total = total + ref[...].astype(jnp.float32)
    following = total.astype(jnp.bfloat16)
    next_ref[...] = following
    wide = following.astype(jnp.float32)
    scaled_ref[:, :part] = (wide * gain).astype(jnp.bfloat16)
    squares = jnp.sum(wide * wide, axis=1, keepdims=True)
    high = squares.astype(jnp.bfloat16).astype(jnp.float32)
    lane = lax.broadcasted_iota(jnp.int32, (rows, META), 1)
    scaled_ref[:, part:] = jnp.where(
        lane == 0, high, jnp.where(lane == 1, squares - high, 0.0)
    ).astype(jnp.bfloat16)


def second_norm(parts, gain):
    depth = len(parts)
    rows, part = parts[0].shape
    return pl.pallas_call(
        functools.partial(second_norm_kernel, depth),
        out_shape=(
            pltpu.VMEM((rows, part + META), jnp.bfloat16),
            pltpu.VMEM((rows, part), jnp.bfloat16),
        ),
        in_specs=[VMEM] * (depth + 1),
        out_specs=(VMEM, VMEM),
        compiler_params=params(4),
        name="second_norm",
    )(*parts, gain)


def projection_kernel(chunk, mine_ref, theirs_ref, next_ref, q_ref, *refs):
    kv_refs, out_refs, kv_buf = refs[: -PLANE - 1], refs[-PLANE - 1 : -1], refs[-1]
    depth = len(kv_refs)
    rows, extended = mine_ref.shape
    part = extended - META
    sub = part // depth
    q_cols, kv_cols = q_ref.shape[1], kv_buf.shape[1]
    cols = q_cols + kv_cols
    line = lax.axis_index("expert") // PLANE
    for d, ref in enumerate(kv_refs):
        kv_buf[lanes((line ^ d) * sub, sub), :] = ref[...]
    block = rows // PLANE
    tensor = lax.axis_index("tensor")
    own = lanes(tensor * block, block)
    other = lanes((1 - tensor) * block, block)
    for d in range(PLANE):
        at = slice(d * block, (d + 1) * block)
        out_refs[d][own, cols : cols + META] = mine_ref[at, part:]
        out_refs[d][other, cols : cols + META] = theirs_ref[at, part:]
        out_refs[d][:block, cols + META :] = next_ref[at, : part // 2]
        out_refs[d][block:, cols + META :] = next_ref[at, part // 2 :]
    both = jnp.concatenate([mine_ref[:, :part], theirs_ref[:, :part]], axis=0)

    def multiply(weight, target):
        product = jnp.dot(both, weight, preferred_element_type=jnp.float32).astype(jnp.bfloat16)
        at = slice(target, target + weight.shape[1])
        for d in range(PLANE):
            out_refs[d][own, at] = product[d * block : (d + 1) * block]
            out_refs[d][other, at] = product[rows + d * block : rows + (d + 1) * block]

    multiply(kv_buf[...], q_cols)
    for start in range(0, q_cols, chunk):
        multiply(q_ref[:, start : start + chunk], start)


def projection(mine, theirs, following, q_weight, kv_weights):
    rows, part = following.shape
    q_cols, kv_cols = q_weight.shape[1], kv_weights[0].shape[1]
    chunk = 512
    shape = pltpu.VMEM((2 * rows // PLANE, q_cols + kv_cols + META + part // 2), jnp.bfloat16)
    return pl.pallas_call(
        functools.partial(projection_kernel, chunk),
        out_shape=(shape,) * PLANE,
        in_specs=[VMEM] * (4 + len(kv_weights)),
        out_specs=(VMEM,) * PLANE,
        scratch_shapes=[pltpu.VMEM((part, kv_cols), jnp.bfloat16)],
        compiler_params=params(8),
        cost_estimate=SMALL,
        name="qkv_projection",
    )(mine, theirs, following, q_weight, *kv_weights)


def head_norm_kernel(depth, *refs):
    parts, q_gain_ref, k_gain_ref = refs[:PLANE], refs[PLANE], refs[PLANE + 1]
    next_ref, q_ref, kv_ref = refs[PLANE + 2 :]
    width = next_ref.shape[1]
    q_cols, kv_cols = q_ref.shape[1], kv_ref.shape[1]
    cols = q_cols + kv_cols
    head = q_gain_ref.shape[1]

    def total(at):
        value = parts[0][:, at].astype(jnp.float32)
        for ref in parts[1:]:
            value = value + ref[:, at].astype(jnp.float32)
        return value

    squares = jnp.sum(total(slice(cols, cols + META)), axis=1, keepdims=True)
    scale = lax.rsqrt(squares / width + EPSILON)
    for h in range(q_cols // head):
        at = slice(h * head, (h + 1) * head)
        q_ref[:, at] = normalize(total(at) * scale, q_gain_ref[...]).astype(jnp.bfloat16)
    tensor = lax.axis_index("tensor")
    for h in range(kv_cols // head):
        at = slice(h * head, (h + 1) * head)
        raw = total(slice(q_cols + h * head, q_cols + (h + 1) * head)) * scale
        is_key = tensor * (kv_cols // head) + h < KV_HEADS
        kv_ref[:, at] = jnp.where(is_key, normalize(raw, k_gain_ref[...]), raw).astype(
            jnp.bfloat16
        )
    plane = lax.axis_index("expert") % PLANE
    rows = next_ref.shape[0]
    sub = width // (PLANE * depth)
    for d in range(PLANE):
        for z in range(depth):
            top = z * sub * 2 // (depth * sub)
            start = cols + META + z * sub - top * (depth * sub // 2)
            next_ref[:, lanes((z * PLANE + (plane ^ d)) * sub, sub)] = parts[d][
                top * rows : (top + 1) * rows, start : start + sub
            ]


def head_norm(parts, q_gain, k_gain, q_cols, kv_cols, rows, width, depth):
    both = parts[0].shape[0]
    return pl.pallas_call(
        functools.partial(head_norm_kernel, depth),
        out_shape=(
            jax.ShapeDtypeStruct((rows, width), jnp.bfloat16),
            jax.ShapeDtypeStruct((both, q_cols), jnp.bfloat16),
            jax.ShapeDtypeStruct((both, kv_cols), jnp.bfloat16),
        ),
        in_specs=[VMEM] * (PLANE + 2),
        out_specs=(VMEM, VMEM, VMEM),
        compiler_params=params(4),
        name="head_norm",
    )(*parts, q_gain, k_gain)


def per_device_dense(
    attn_out,
    out_weight,
    residual,
    attn_gain,
    expert_ids,
    route_weights,
    w_gate,
    w_up,
    w_down,
    input_gain,
    q_weight,
    kv_weight,
    q_gain,
    k_gain,
):
    n_expert = lax.axis_size("expert")
    depth = n_expert // PLANE
    rows, width = residual.shape
    tensor_index = lax.axis_index("tensor").astype(jnp.int32)

    def to_core(value):
        return lax.ppermute(value, "tensor", [(0, 1), (1, 0)])

    def to_expert(value, offset):
        return lax.ppermute(value, "expert", [(i, i ^ offset) for i in range(n_expert)])

    def to_z(values):
        return [to_expert(v, d * PLANE) if d else v for d, v in enumerate(values)]

    def to_plane(values):
        return [to_expert(v, d) if d else v for d, v in enumerate(values)]

    own_ids = lax.dynamic_slice_in_dim(expert_ids, tensor_index * rows, rows, 0)
    own_route = lax.dynamic_slice_in_dim(route_weights, tensor_index * rows, rows, 0)
    chosen = own_ids[:, :, None] == jnp.arange(META // 2, dtype=jnp.int32)[None, None, :]
    dense = jnp.sum(jnp.where(chosen, own_route[:, :, None], 0.0), axis=1)
    high = lax.reduce_precision(dense, 8, 7)
    meta = jnp.concatenate([high, dense - high], axis=1).astype(jnp.bfloat16)

    lines = [list(range(i, n_expert, PLANE)) for i in range(PLANE)]
    mine, theirs = out_projection(attn_out, out_weight)
    tokens, first = first_norm(mine, to_core(theirs), residual, attn_gain[None, :], meta)
    tokens, q_own = lax.optimization_barrier((tokens, q_weight))
    q_rows = lax.all_gather(q_own, "expert", axis=0, tiled=True, axis_index_groups=lines)
    weights = load((w_gate, w_up, w_down), (tokens,))
    line = to_z([tokens] * depth)
    tied = lax.optimization_barrier((*far_first(line), *weights))
    line, weights = far_first(tied[:depth]), tied[depth:]
    near = to_plane([pack(line)] * (PLANE - 1))
    cut = near[0].shape[0] // 2
    one, two = near[1][:cut], near[2][cut:]
    far = [to_expert(one, 2), to_expert(two, 1)]
    near_mine, *near_theirs = experts((*near, *map(to_core, near)), weights, depth, 2)
    theirs = list(map(to_core, near_theirs))
    near_mine, *far = lax.optimization_barrier((near_mine, *far))
    far_both = [*far, *map(to_core, far)]
    far_mine, *far_theirs = experts(far_both, weights, depth, 1)
    theirs += map(to_core, far_theirs)
    *sums, kv_own = lax.optimization_barrier((*chip_sum((near_mine, far_mine), theirs, first, depth), kv_weight))
    parts = to_plane(sums)
    kv_rows = [kv_own, to_expert(kv_own, PLANE), to_expert(kv_own, 2 * PLANE)]
    parts = plane_sum(parts, depth)
    kv_rows.append(to_expert(kv_rows[2], PLANE))
    (q_rows,) = load((q_rows,), (*parts, *kv_rows[1:3]))
    parts = to_z(parts)
    *parts, q_rows = lax.optimization_barrier((*parts, q_rows))
    scaled, following = second_norm(parts, input_gain[None, :])
    products = to_plane(projection(scaled, to_core(scaled), following, q_rows, kv_rows))
    return head_norm(
        products,
        q_gain[None, :],
        k_gain[None, :],
        q_weight.shape[1],
        kv_weight.shape[1],
        rows,
        width,
        depth,
    )


def per_device(
    attn_out,
    out_weight,
    residual,
    attn_gain,
    expert_ids,
    route_weights,
    w_gate,
    w_up,
    w_down,
    input_gain,
    q_weight,
    kv_weight,
    q_gain,
    k_gain,
):
    n_expert = lax.axis_size("expert")
    n_tensor = lax.axis_size("tensor")
    share = n_tensor // 2
    tensor_index = lax.axis_index("tensor")
    group_rows = attn_out.shape[0]
    width = residual.shape[1]
    half = tensor_index // share
    capacity = 3 * group_rows * TOP // (4 * n_expert)
    all_experts = 2 * n_expert
    attn_rows = lax.psum_scatter(
        jnp.dot(attn_out, out_weight, preferred_element_type=jnp.float32),
        "tensor",
        scatter_dimension=0,
        tiled=True,
    )
    first_residual = (residual.astype(jnp.float32) + attn_rows).astype(jnp.bfloat16)
    normed = normalize(first_residual.astype(jnp.float32), attn_gain).astype(jnp.bfloat16)
    group_normed = lax.all_gather(normed, "tensor", axis=0, tiled=True)
    flat_ids = expert_ids.reshape(-1)
    onehot = (flat_ids[:, None] == jnp.arange(all_experts, dtype=jnp.int32)[None, :]).astype(
        jnp.int32
    )
    earlier = jnp.cumsum(onehot, axis=0) - onehot
    rank = jnp.sum(earlier * onehot, axis=1)
    dest = flat_ids * capacity + rank
    row_owner = jnp.arange(flat_ids.shape[0], dtype=jnp.int32) // TOP
    slot_row = jnp.full((all_experts * capacity,), group_rows, jnp.int32).at[dest].set(row_owner)
    slot_weight = (
        jnp.zeros((all_experts * capacity,), jnp.float32).at[dest].set(route_weights.reshape(-1))
    )
    own_slots = lax.dynamic_index_in_dim(
        slot_row.reshape(n_expert, 2, capacity), half, 1, keepdims=False
    )
    own_weights = lax.dynamic_index_in_dim(
        slot_weight.reshape(n_expert, 2, capacity), half, 1, keepdims=False
    )
    padded_rows = jnp.concatenate([group_normed, jnp.zeros((1, width), jnp.bfloat16)], axis=0)
    gate_w = w_gate[0]
    up_w = w_up[0]
    down_w = w_down[0]
    outgoing = jnp.take(padded_rows, own_slots, axis=0)
    arrived = lax.all_to_all(outgoing, "expert", split_axis=0, concat_axis=0, tiled=True)
    flat = arrived.reshape(-1, width)
    gate = jnp.dot(flat, gate_w, preferred_element_type=jnp.float32)
    up = jnp.dot(flat, up_w, preferred_element_type=jnp.float32)
    act = (jax.nn.silu(gate) * up).astype(jnp.bfloat16)
    part = jnp.dot(act, down_w, preferred_element_type=jnp.float32).astype(jnp.bfloat16)
    send_part = part.reshape(arrived.shape)
    returned = lax.all_to_all(send_part, "expert", split_axis=0, concat_axis=0, tiled=True)
    weighted = own_weights.reshape(-1)[:, None] * returned.reshape(-1, width).astype(jnp.float32)
    term = (
        jnp.zeros((group_rows + 1, width), jnp.float32)
        .at[own_slots.reshape(-1)]
        .add(weighted)[:group_rows]
    )
    expert_sum = lax.psum_scatter(
        term.astype(jnp.bfloat16), "tensor", scatter_dimension=0, tiled=True
    ).astype(jnp.float32)
    next_residual = (first_residual.astype(jnp.float32) + expert_sum).astype(jnp.bfloat16)
    own_normed = normalize(next_residual.astype(jnp.float32), input_gain).astype(jnp.bfloat16)
    next_normed = lax.all_gather(own_normed, "tensor", axis=0, tiled=True)
    query_cols = q_weight.shape[1]
    kv_cols = kv_weight.shape[1]
    query_raw = jnp.dot(
        next_normed,
        lax.all_gather(q_weight, "expert", axis=0, tiled=True),
        preferred_element_type=jnp.float32,
    )
    kv_raw = jnp.dot(
        next_normed,
        lax.all_gather(kv_weight, "expert", axis=0, tiled=True),
        preferred_element_type=jnp.float32,
    )
    head_size = q_gain.shape[0]
    queries = (
        normalize(query_raw.reshape(group_rows, -1, head_size), q_gain)
        .reshape(group_rows, query_cols)
        .astype(jnp.bfloat16)
    )
    heads_here = kv_cols // head_size
    head_number = tensor_index * heads_here + jnp.arange(heads_here, dtype=jnp.int32)
    is_key = head_number < KV_HEADS
    kv_shaped = kv_raw.reshape(group_rows, heads_here, head_size)
    keys_values = (
        jnp.where(is_key[None, :, None], normalize(kv_shaped, k_gain), kv_shaped)
        .reshape(group_rows, kv_cols)
        .astype(jnp.bfloat16)
    )
    return (next_residual, queries, keys_values)


def solution(mesh):
    small = mesh.shape["tensor"] == 2 and mesh.shape["expert"] == 4 * PLANE
    return jax.shard_map(
        per_device_dense if small else per_device,
        mesh=mesh,
        in_specs=(
            P("expert", "tensor"),
            P("tensor", None),
            P(("expert", "tensor"), None),
            P(),
            P("expert", None),
            P("expert", None),
            P("expert", None, "tensor"),
            P("expert", None, "tensor"),
            P("expert", "tensor", None),
            P(),
            P("expert", "tensor"),
            P("expert", "tensor"),
            P(),
            P(),
        ),
        out_specs=(P(("expert", "tensor"), None), P("expert", "tensor"), P("expert", "tensor")),
        check_vma=False,
    )
```

```python
import functools

import jax
import jax.numpy as jnp
from jax import lax
from jax.experimental import pallas as pl
from jax.experimental.pallas import tpu as pltpu
from jax.sharding import PartitionSpec as P

KV_HEADS = 4
TOP = 8
PLANE = 4
META = 128


EPSILON = 1e-06

SMALL = pl.CostEstimate(flops=0, bytes_accessed=0, transcendentals=0)
VMEM = pl.BlockSpec(memory_space=pltpu.VMEM)
HBM = pl.BlockSpec(memory_space=pltpu.HBM)


def normalize(values, gain):
    return values * lax.rsqrt(jnp.mean(values * values, axis=-1, keepdims=True) + EPSILON) * gain


def params(mebibytes):
    return pltpu.CompilerParams(vmem_limit_bytes=mebibytes << 20)


def lanes(start, size):
    return pl.ds(pl.multiple_of(start, size), size)


def in_hbm(value):
    return pltpu.with_memory_space_constraint(value, pltpu.HBM)


def in_vmem(value):
    return pltpu.with_memory_space_constraint(value, pltpu.VMEM)


def out_projection_kernel(chunk, a_hbm, w_hbm, mine_ref, theirs_ref, a_buf, w_buf, a_sem, sems):
    depth = w_buf.shape[0]
    count = depth // chunk
    half = mine_ref.shape[0]
    a_copy = pltpu.make_async_copy(a_hbm, a_buf, a_sem)
    a_copy.start()
    copies = []
    for i in range(count):
        rows = pl.ds(i * chunk, chunk)
        copies.append(pltpu.make_async_copy(w_hbm.at[rows], w_buf.at[rows], sems.at[i]))
    for copy in copies:
        copy.start()
    tensor = lax.axis_index("tensor")
    own = lanes(tensor * half, half)
    other = lanes((1 - tensor) * half, half)
    a_copy.wait()
    for i in range(count):
        copies[i].wait()
        at = pl.ds(i * chunk, chunk)
        both = jnp.concatenate([a_buf[own, at], a_buf[other, at]], axis=0)
        product = jnp.dot(both, w_buf[at, :], preferred_element_type=jnp.float32)
        if i == 0:
            mine_ref[...] = product[:half]
            theirs_ref[...] = product[half:]
        else:
            mine_ref[...] += product[:half]
            theirs_ref[...] += product[half:]


def out_projection(attn_out, out_weight):
    rows, depth = attn_out.shape
    width = out_weight.shape[1]
    chunk = 512
    half = pltpu.VMEM((rows // 2, width), jnp.float32)
    return pl.pallas_call(
        functools.partial(out_projection_kernel, chunk),
        out_shape=(half, half),
        in_specs=[HBM, HBM],
        out_specs=(VMEM, VMEM),
        scratch_shapes=[
            pltpu.VMEM((rows, depth), jnp.bfloat16),
            pltpu.VMEM((depth, width), jnp.bfloat16),
            pltpu.SemaphoreType.DMA,
            pltpu.SemaphoreType.DMA((depth // chunk,)),
        ],
        compiler_params=params(14),
        cost_estimate=SMALL,
        name="out_projection",
    )(in_hbm(attn_out), in_hbm(out_weight))


def first_norm_kernel(mine_ref, theirs_ref, residual_ref, gain_ref, meta_ref, tokens_ref, first_ref):
    width = residual_ref.shape[1]
    first = (residual_ref[...].astype(jnp.float32) + (mine_ref[...] + theirs_ref[...])).astype(
        jnp.bfloat16
    )
    first_ref[...] = first
    tokens_ref[:, :width] = normalize(first.astype(jnp.float32), gain_ref[...]).astype(jnp.bfloat16)
    tokens_ref[:, width:] = meta_ref[...]


def first_norm(mine, theirs, residual, gain, meta):
    rows, width = residual.shape
    return pl.pallas_call(
        first_norm_kernel,
        out_shape=(
            pltpu.VMEM((rows, width + META), jnp.bfloat16),
            pltpu.VMEM((rows, width), jnp.bfloat16),
        ),
        in_specs=[VMEM] * 5,
        out_specs=(VMEM, VMEM),
        compiler_params=params(2),
        name="first_norm",
    )(mine, theirs, residual, gain, meta)


def pack_kernel(depth, *refs):
    line, out_ref = refs[:depth], refs[depth]
    rows = line[0].shape[0]
    for z in range(depth):
        out_ref[z * rows : (z + 1) * rows, :] = line[z][...]


def pack(line):
    depth = len(line)
    rows, extended = line[0].shape
    return pl.pallas_call(
        functools.partial(pack_kernel, depth),
        out_shape=pltpu.VMEM((depth * rows, extended), jnp.bfloat16),
        in_specs=[VMEM] * depth,
        out_specs=VMEM,
        compiler_params=params(2),
        name="pack_tokens",
    )(*line)


def load_kernel(count, *refs):
    sources, targets, sems = refs[:count], refs[-count - 1 : -1], refs[-1]
    copies = [
        pltpu.make_async_copy(source, target, sems.at[i])
        for i, (source, target) in enumerate(zip(sources, targets))
    ]
    for copy in copies:
        copy.start()
    for copy in copies:
        copy.wait()


def load(weights, after):
    count = len(weights)
    return pl.pallas_call(
        functools.partial(load_kernel, count),
        out_shape=tuple(pltpu.VMEM(w.shape, w.dtype) for w in weights),
        in_specs=[HBM] * count + [pl.BlockSpec(memory_space=pl.ANY)] * len(after),
        out_specs=(VMEM,) * count,
        scratch_shapes=[pltpu.SemaphoreType.DMA((count,))],
        compiler_params=params(2),
        cost_estimate=SMALL,
        name="load_weights",
    )(*map(in_hbm, weights), *after)


def expert_kernel(depth, chunk, count, *refs):
    block_refs, (gate_ref, up_ref, down_ref) = refs[:count], refs[count : count + 3]
    mine_ref, *theirs_refs, x_buf, act_buf = refs[count + 3 :]
    width, hidden = gate_ref.shape[1:]
    extended = x_buf.shape[1]
    start = 0
    for ref in block_refs:
        rows = ref.shape[0]
        x_buf[start : start + rows, :] = ref[:, :extended]
        start += rows
    meta = x_buf[:, width:].astype(jnp.float32)
    lane = lax.broadcasted_iota(jnp.int32, meta.shape, 1)
    chip = lax.axis_index("expert")
    expert = 2 * chip + lax.axis_index("tensor")
    chosen = (lane == expert) | (lane == expert + META // 2)
    route = 0.5 * jnp.sum(jnp.where(chosen, meta, 0.0), axis=1, keepdims=True)
    for i in range(hidden // chunk):
        cols = pl.ds(i * chunk, chunk)
        x = x_buf[:, :width]
        gate = jnp.dot(x, gate_ref[0, :, cols], preferred_element_type=jnp.float32)
        up = jnp.dot(x, up_ref[0, :, cols], preferred_element_type=jnp.float32)
        act = gate * (1.0 + jnp.tanh(0.5 * gate)) * (up * route)
        act_buf[:, i * chunk : (i + 1) * chunk] = act.astype(jnp.bfloat16)
    sub = width // (PLANE * depth)
    part = sub * depth
    half = mine_ref.shape[0]
    plane = chip % PLANE
    for d in range(PLANE):
        weight = jnp.concatenate(
            [down_ref[0, :, lanes((z * PLANE + (plane ^ d)) * sub, sub)] for z in range(depth)],
            axis=1,
        )
        out = jnp.dot(act_buf[...], weight, preferred_element_type=jnp.float32)
        cols = slice(d * part, (d + 1) * part)
        mine_ref[:, cols] = out[:half].astype(jnp.bfloat16)
        start = half
        for ref in theirs_refs:
            stop = start + ref.shape[0]
            ref[:, cols] = out[start:stop].astype(jnp.bfloat16)
            start = stop


def experts(blocks, weights, depth, pieces):
    width, hidden = weights[0].shape[1:]
    chunk = 256
    extended = width + META
    total = sum(block.shape[0] for block in blocks)
    rows = [total // 2] + [total // 2 // pieces] * pieces
    return pl.pallas_call(
        functools.partial(expert_kernel, depth, chunk, len(blocks)),
        out_shape=tuple(pltpu.VMEM((size, width), jnp.bfloat16) for size in rows),
        in_specs=[VMEM] * (len(blocks) + 3),
        out_specs=(VMEM,) * (1 + pieces),
        scratch_shapes=[
            pltpu.VMEM((total, extended), jnp.bfloat16),
            pltpu.VMEM((total, hidden), jnp.bfloat16),
        ],
        compiler_params=params(16),
        cost_estimate=pl.CostEstimate(
            flops=6 * total * width * hidden, bytes_accessed=0, transcendentals=0
        ),
        name="experts",
    )(*blocks, *weights)


def chip_sum_kernel(depth, count, first_ref, *refs):
    mine, theirs, out_refs = refs[:2], refs[2 : 2 + count], refs[2 + count :]
    part = out_refs[0].shape[1]
    sub = part // depth
    held = first_ref.shape[0]
    plane = lax.axis_index("expert") % PLANE
    start = 0
    for own_ref in mine:
        first = start
        while start < first + own_ref.shape[0]:
            ref, theirs = theirs[0], theirs[1:]
            size = ref.shape[0]
            own = slice(start - first, start - first + size)
            for d, out_ref in enumerate(out_refs):
                at = slice(d * part, (d + 1) * part)
                total = own_ref[own, at].astype(jnp.float32) + ref[:, at].astype(jnp.float32)
                if start == 0:
                    residual = jnp.concatenate(
                        [
                            first_ref[:, lanes((z * PLANE + (plane ^ d)) * sub, sub)]
                            for z in range(depth)
                        ],
                        axis=1,
                    )
                    with_first = total[:held] + residual.astype(jnp.float32)
                    total = jnp.concatenate([with_first, total[held:]], axis=0)
                out_ref[start : start + size, :] = total.astype(jnp.bfloat16)
            start += size


def chip_sum(mine, theirs, first, depth):
    rows, width = sum(value.shape[0] for value in mine), mine[0].shape[1]
    return pl.pallas_call(
        functools.partial(chip_sum_kernel, depth, len(theirs)),
        out_shape=(pltpu.VMEM((rows, width // PLANE), jnp.bfloat16),) * PLANE,
        in_specs=[VMEM] * (3 + len(theirs)),
        out_specs=(VMEM,) * PLANE,
        compiler_params=params(4),
        name="chip_sum",
    )(first, *mine, *theirs)


def plane_sum_kernel(depth, *refs):
    in_refs, out_refs = refs[:PLANE], refs[PLANE:]
    group = in_refs[0].shape[0] // PLANE
    rows = group // depth
    for k in range(PLANE):
        for z in range(depth):
            total = 0.0
            for d in range(PLANE):
                start = (k ^ d) * group + z * rows
                total = total + in_refs[d][start : start + rows, :].astype(jnp.float32)
            out_refs[z][k * rows : (k + 1) * rows, :] = total.astype(jnp.bfloat16)


def plane_sum(parts, depth):
    rows, part = parts[0].shape
    return pl.pallas_call(
        functools.partial(plane_sum_kernel, depth),
        out_shape=(pltpu.VMEM((rows // depth, part), jnp.bfloat16),) * depth,
        in_specs=[VMEM] * PLANE,
        out_specs=(VMEM,) * depth,
        compiler_params=params(4),
        name="plane_sum",
    )(*parts)


def second_norm_kernel(depth, *refs):
    parts, (gain_ref, scaled_ref, next_ref) = refs[:depth], refs[depth:]
    rows, part = next_ref.shape
    sub = part // depth
    plane = lax.axis_index("expert") % PLANE
    gain = jnp.concatenate(
        [gain_ref[:, lanes((z * PLANE + plane) * sub, sub)] for z in range(depth)], axis=1
    )
    total = parts[0][...].astype(jnp.float32)
    for ref in parts[1:]:
        total = total + ref[...].astype(jnp.float32)
    following = total.astype(jnp.bfloat16)
    next_ref[...] = following
    wide = following.astype(jnp.float32)
    scaled_ref[:, :part] = (wide * gain).astype(jnp.bfloat16)
    squares = jnp.sum(wide * wide, axis=1, keepdims=True)
    high = squares.astype(jnp.bfloat16).astype(jnp.float32)
    lane = lax.broadcasted_iota(jnp.int32, (rows, META), 1)
    scaled_ref[:, part:] = jnp.where(
        lane == 0, high, jnp.where(lane == 1, squares - high, 0.0)
    ).astype(jnp.bfloat16)


def second_norm(parts, gain):
    depth = len(parts)
    rows, part = parts[0].shape
    return pl.pallas_call(
        functools.partial(second_norm_kernel, depth),
        out_shape=(
            pltpu.VMEM((rows, part + META), jnp.bfloat16),
            pltpu.VMEM((rows, part), jnp.bfloat16),
        ),
        in_specs=[VMEM] * (depth + 1),
        out_specs=(VMEM, VMEM),
        compiler_params=params(4),
        name="second_norm",
    )(*parts, gain)


def projection_kernel(chunk, mine_ref, theirs_ref, next_ref, q_ref, *refs):
    kv_refs, out_refs, kv_buf = refs[: -PLANE - 1], refs[-PLANE - 1 : -1], refs[-1]
    depth = len(kv_refs)
    rows, extended = mine_ref.shape
    part = extended - META
    sub = part // depth
    q_cols, kv_cols = q_ref.shape[1], kv_buf.shape[1]
    cols = q_cols + kv_cols
    line = lax.axis_index("expert") // PLANE
    for d, ref in enumerate(kv_refs):
        kv_buf[lanes((line ^ d) * sub, sub), :] = ref[...]
    block = rows // PLANE
    tensor = lax.axis_index("tensor")
    own = lanes(tensor * block, block)
    other = lanes((1 - tensor) * block, block)
    for d in range(PLANE):
        at = slice(d * block, (d + 1) * block)
        out_refs[d][own, cols : cols + META] = mine_ref[at, part:]
        out_refs[d][other, cols : cols + META] = theirs_ref[at, part:]
        out_refs[d][:block, cols + META :] = next_ref[at, : part // 2]
        out_refs[d][block:, cols + META :] = next_ref[at, part // 2 :]
    both = jnp.concatenate([mine_ref[:, :part], theirs_ref[:, :part]], axis=0)

    def multiply(weight, target):
        product = jnp.dot(both, weight, preferred_element_type=jnp.float32).astype(jnp.bfloat16)
        at = slice(target, target + weight.shape[1])
        for d in range(PLANE):
            out_refs[d][own, at] = product[d * block : (d + 1) * block]
            out_refs[d][other, at] = product[rows + d * block : rows + (d + 1) * block]

    multiply(kv_buf[...], q_cols)
    for start in range(0, q_cols, chunk):
        multiply(q_ref[:, start : start + chunk], start)


def projection(mine, theirs, following, q_weight, kv_weights):
    rows, part = following.shape
    q_cols, kv_cols = q_weight.shape[1], kv_weights[0].shape[1]
    chunk = 512
    shape = pltpu.VMEM((2 * rows // PLANE, q_cols + kv_cols + META + part // 2), jnp.bfloat16)
    return pl.pallas_call(
        functools.partial(projection_kernel, chunk),
        out_shape=(shape,) * PLANE,
        in_specs=[VMEM] * (4 + len(kv_weights)),
        out_specs=(VMEM,) * PLANE,
        scratch_shapes=[pltpu.VMEM((part, kv_cols), jnp.bfloat16)],
        compiler_params=params(8),
        cost_estimate=SMALL,
        name="qkv_projection",
    )(mine, theirs, following, q_weight, *kv_weights)


def head_norm_kernel(depth, *refs):
    parts, q_gain_ref, k_gain_ref = refs[:PLANE], refs[PLANE], refs[PLANE + 1]
    next_ref, q_ref, kv_ref = refs[PLANE + 2 :]
    width = next_ref.shape[1]
    q_cols, kv_cols = q_ref.shape[1], kv_ref.shape[1]
    cols = q_cols + kv_cols
    head = q_gain_ref.shape[1]

    def total(at):
        value = parts[0][:, at].astype(jnp.float32)
        for ref in parts[1:]:
            value = value + ref[:, at].astype(jnp.float32)
        return value

    squares = jnp.sum(total(slice(cols, cols + META)), axis=1, keepdims=True)
    scale = lax.rsqrt(squares / width + EPSILON)
    for h in range(q_cols // head):
        at = slice(h * head, (h + 1) * head)
        q_ref[:, at] = normalize(total(at) * scale, q_gain_ref[...]).astype(jnp.bfloat16)
    tensor = lax.axis_index("tensor")
    for h in range(kv_cols // head):
        at = slice(h * head, (h + 1) * head)
        raw = total(slice(q_cols + h * head, q_cols + (h + 1) * head)) * scale
        is_key = tensor * (kv_cols // head) + h < KV_HEADS
        kv_ref[:, at] = jnp.where(is_key, normalize(raw, k_gain_ref[...]), raw).astype(
            jnp.bfloat16
        )
    plane = lax.axis_index("expert") % PLANE
    rows = next_ref.shape[0]
    sub = width // (PLANE * depth)
    for d in range(PLANE):
        for z in range(depth):
            top = z * sub * 2 // (depth * sub)
            start = cols + META + z * sub - top * (depth * sub // 2)
            next_ref[:, lanes((z * PLANE + (plane ^ d)) * sub, sub)] = parts[d][
                top * rows : (top + 1) * rows, start : start + sub
            ]


def head_norm(parts, q_gain, k_gain, q_cols, kv_cols, rows, width, depth):
    both = parts[0].shape[0]
    return pl.pallas_call(
        functools.partial(head_norm_kernel, depth),
        out_shape=(
            jax.ShapeDtypeStruct((rows, width), jnp.bfloat16),
            jax.ShapeDtypeStruct((both, q_cols), jnp.bfloat16),
            jax.ShapeDtypeStruct((both, kv_cols), jnp.bfloat16),
        ),
        in_specs=[VMEM] * (PLANE + 2),
        out_specs=(VMEM, VMEM, VMEM),
        compiler_params=params(4),
        name="head_norm",
    )(*parts, q_gain, k_gain)


def per_device_dense(
    attn_out,
    out_weight,
    residual,
    attn_gain,
    expert_ids,
    route_weights,
    w_gate,
    w_up,
    w_down,
    input_gain,
    q_weight,
    kv_weight,
    q_gain,
    k_gain,
):
    n_expert = lax.axis_size("expert")
    depth = n_expert // PLANE
    rows, width = residual.shape
    tensor_index = lax.axis_index("tensor").astype(jnp.int32)

    def to_core(value):
        return lax.ppermute(value, "tensor", [(0, 1), (1, 0)])

    def to_expert(value, offset):
        return lax.ppermute(value, "expert", [(i, i ^ offset) for i in range(n_expert)])

    def to_z(values):
        return [to_expert(v, d * PLANE) if d else v for d, v in enumerate(values)]

    def to_plane(values):
        return [to_expert(v, d) if d else v for d, v in enumerate(values)]

    own_ids = lax.dynamic_slice_in_dim(expert_ids, tensor_index * rows, rows, 0)
    own_route = lax.dynamic_slice_in_dim(route_weights, tensor_index * rows, rows, 0)
    chosen = own_ids[:, :, None] == jnp.arange(META // 2, dtype=jnp.int32)[None, None, :]
    dense = jnp.sum(jnp.where(chosen, own_route[:, :, None], 0.0), axis=1)
    high = lax.reduce_precision(dense, 8, 7)
    meta = jnp.concatenate([high, dense - high], axis=1).astype(jnp.bfloat16)

    lines = [list(range(i, n_expert, PLANE)) for i in range(PLANE)]
    mine, theirs = out_projection(attn_out, out_weight)
    tokens, first = first_norm(mine, to_core(theirs), residual, attn_gain[None, :], meta)
    tokens, q_own = lax.optimization_barrier((tokens, q_weight))
    q_rows = lax.all_gather(q_own, "expert", axis=0, tiled=True, axis_index_groups=lines)
    weights = load((w_gate, w_up, w_down), (tokens,))
    line = to_z([tokens] * depth)
    *line, gate, up, down = lax.optimization_barrier((*line, *weights))
    weights = (gate, up, down)
    near = to_plane([pack(line)] * (PLANE - 1))
    cut = near[0].shape[0] // 2
    one, two = near[1][:cut], near[2][cut:]
    far = [to_expert(one, 2), to_expert(two, 1)]
    near_mine, *near_theirs = experts((*near, *map(to_core, near)), weights, depth, 2)
    theirs = list(map(to_core, near_theirs))
    near_mine, *far = lax.optimization_barrier((near_mine, *far))
    far_both = [*far, *map(to_core, far)]
    far_mine, *far_theirs = experts(far_both, weights, depth, 1)
    theirs += map(to_core, far_theirs)
    *sums, kv_own = lax.optimization_barrier((*chip_sum((near_mine, far_mine), theirs, first, depth), kv_weight))
    parts = to_plane(sums)
    kv_rows = [kv_own, to_expert(kv_own, PLANE), to_expert(kv_own, 2 * PLANE)]
    parts = plane_sum(parts, depth)
    kv_rows.append(to_expert(kv_own, 3 * PLANE))
    (q_rows,) = load((q_rows,), (*parts, *kv_rows[1:]))
    parts = to_z(parts)
    *parts, q_rows = lax.optimization_barrier((*parts, q_rows))
    scaled, following = second_norm(parts, input_gain[None, :])
    products = to_plane(projection(scaled, to_core(scaled), following, q_rows, kv_rows))
    return head_norm(
        products,
        q_gain[None, :],
        k_gain[None, :],
        q_weight.shape[1],
        kv_weight.shape[1],
        rows,
        width,
        depth,
    )


def per_device(
    attn_out,
    out_weight,
    residual,
    attn_gain,
    expert_ids,
    route_weights,
    w_gate,
    w_up,
    w_down,
    input_gain,
    q_weight,
    kv_weight,
    q_gain,
    k_gain,
):
    n_expert = lax.axis_size("expert")
    n_tensor = lax.axis_size("tensor")
    share = n_tensor // 2
    tensor_index = lax.axis_index("tensor")
    group_rows = attn_out.shape[0]
    width = residual.shape[1]
    half = tensor_index // share
    capacity = 3 * group_rows * TOP // (4 * n_expert)
    all_experts = 2 * n_expert
    attn_rows = lax.psum_scatter(
        jnp.dot(attn_out, out_weight, preferred_element_type=jnp.float32),
        "tensor",
        scatter_dimension=0,
        tiled=True,
    )
    first_residual = (residual.astype(jnp.float32) + attn_rows).astype(jnp.bfloat16)
    normed = normalize(first_residual.astype(jnp.float32), attn_gain).astype(jnp.bfloat16)
    group_normed = lax.all_gather(normed, "tensor", axis=0, tiled=True)
    flat_ids = expert_ids.reshape(-1)
    onehot = (flat_ids[:, None] == jnp.arange(all_experts, dtype=jnp.int32)[None, :]).astype(
        jnp.int32
    )
    earlier = jnp.cumsum(onehot, axis=0) - onehot
    rank = jnp.sum(earlier * onehot, axis=1)
    dest = flat_ids * capacity + rank
    row_owner = jnp.arange(flat_ids.shape[0], dtype=jnp.int32) // TOP
    slot_row = jnp.full((all_experts * capacity,), group_rows, jnp.int32).at[dest].set(row_owner)
    slot_weight = (
        jnp.zeros((all_experts * capacity,), jnp.float32).at[dest].set(route_weights.reshape(-1))
    )
    own_slots = lax.dynamic_index_in_dim(
        slot_row.reshape(n_expert, 2, capacity), half, 1, keepdims=False
    )
    own_weights = lax.dynamic_index_in_dim(
        slot_weight.reshape(n_expert, 2, capacity), half, 1, keepdims=False
    )
    padded_rows = jnp.concatenate([group_normed, jnp.zeros((1, width), jnp.bfloat16)], axis=0)
    gate_w = w_gate[0]
    up_w = w_up[0]
    down_w = w_down[0]
    outgoing = jnp.take(padded_rows, own_slots, axis=0)
    arrived = lax.all_to_all(outgoing, "expert", split_axis=0, concat_axis=0, tiled=True)
    flat = arrived.reshape(-1, width)
    gate = jnp.dot(flat, gate_w, preferred_element_type=jnp.float32)
    up = jnp.dot(flat, up_w, preferred_element_type=jnp.float32)
    act = (jax.nn.silu(gate) * up).astype(jnp.bfloat16)
    part = jnp.dot(act, down_w, preferred_element_type=jnp.float32).astype(jnp.bfloat16)
    send_part = part.reshape(arrived.shape)
    returned = lax.all_to_all(send_part, "expert", split_axis=0, concat_axis=0, tiled=True)
    weighted = own_weights.reshape(-1)[:, None] * returned.reshape(-1, width).astype(jnp.float32)
    term = (
        jnp.zeros((group_rows + 1, width), jnp.float32)
        .at[own_slots.reshape(-1)]
        .add(weighted)[:group_rows]
    )
    expert_sum = lax.psum_scatter(
        term.astype(jnp.bfloat16), "tensor", scatter_dimension=0, tiled=True
    ).astype(jnp.float32)
    next_residual = (first_residual.astype(jnp.float32) + expert_sum).astype(jnp.bfloat16)
    own_normed = normalize(next_residual.astype(jnp.float32), input_gain).astype(jnp.bfloat16)
    next_normed = lax.all_gather(own_normed, "tensor", axis=0, tiled=True)
    query_cols = q_weight.shape[1]
    kv_cols = kv_weight.shape[1]
    query_raw = jnp.dot(
        next_normed,
        lax.all_gather(q_weight, "expert", axis=0, tiled=True),
        preferred_element_type=jnp.float32,
    )
    kv_raw = jnp.dot(
        next_normed,
        lax.all_gather(kv_weight, "expert", axis=0, tiled=True),
        preferred_element_type=jnp.float32,
    )
    head_size = q_gain.shape[0]
    queries = (
        normalize(query_raw.reshape(group_rows, -1, head_size), q_gain)
        .reshape(group_rows, query_cols)
        .astype(jnp.bfloat16)
    )
    heads_here = kv_cols // head_size
    head_number = tensor_index * heads_here + jnp.arange(heads_here, dtype=jnp.int32)
    is_key = head_number < KV_HEADS
    kv_shaped = kv_raw.reshape(group_rows, heads_here, head_size)
    keys_values = (
        jnp.where(is_key[None, :, None], normalize(kv_shaped, k_gain), kv_shaped)
        .reshape(group_rows, kv_cols)
        .astype(jnp.bfloat16)
    )
    return (next_residual, queries, keys_values)


def solution(mesh):
    small = mesh.shape["tensor"] == 2 and mesh.shape["expert"] == 4 * PLANE
    return jax.shard_map(
        per_device_dense if small else per_device,
        mesh=mesh,
        in_specs=(
            P("expert", "tensor"),
            P("tensor", None),
            P(("expert", "tensor"), None),
            P(),
            P("expert", None),
            P("expert", None),
            P("expert", None, "tensor"),
            P("expert", None, "tensor"),
            P("expert", "tensor", None),
            P(),
            P("expert", "tensor"),
            P("expert", "tensor"),
            P(),
            P(),
        ),
        out_specs=(P(("expert", "tensor"), None), P("expert", "tensor"), P("expert", "tensor")),
        check_vma=False,
    )
```
